32 devices in a mesh: dp: 4 (over y, x), ctx: 8 (over z, core).
Axes of the slice: x: 2, y: 2, z: 4, core: 2. Of those that a mesh axis runs over, the one named last changes fastest.
Arguments:
- projections: bfloat16 [3072, 8192], P(None, ('dp', 'ctx')), may hold values from -6 to 6
- short_filter: bfloat16 [7, 3072], replicated, may hold values from -2 to 2
- long_filter: bfloat16 [256, 8192], P(('dp', 'ctx')), may hold values from -6 to 6
- out_grad: bfloat16 [1024, 8192], P(None, ('dp', 'ctx')), may hold values from -3 to 3
Outputs:
- mixed: bfloat16 [1024, 8192], P(None, ('dp', 'ctx'))
- proj_grad: bfloat16 [3072, 8192], P(None, ('dp', 'ctx'))
- filter_grad: float32 [256, 8192], P(('dp', 'ctx'))
The draws below stay inside these ranges and needn't reach their ends.
All inputs are finite; a program needn't handle non-finite values.
Results may differ from the reference program's by a relative error of at most 0.01.
Values may be sent and summed in bfloat16 or wider, within the bound.
No kernel may reach another device: no remote copies, remote signals or barrier semaphores. Data moves between devices by JAX's collectives and lax.ppermute only.
A program may use at most 64 MiB of HBM per device.

```python
import math
import jax
import jax.numpy as jnp
from jax import lax

CH = 1024
CPG = 4
TAPS = 7
SEQ = 8192
GROUPS = 256


def steps_of(rng, extent, cuts, low, largest):
    gain = 1.0
    for position, parts in cuts:
        draws = jax.random.uniform(jax.random.fold_in(jax.random.fold_in(rng, 6), position), (parts,), jnp.float32, low / len(cuts), largest / len(cuts))
        gain = gain * jnp.repeat(jnp.exp(draws), extent[position] // parts).reshape((-1,) + (1,) * (len(extent) - 1 - position))
    return gain


def normal_values(stream_key, extent, spread, bound, shards=(), kind=jnp.bfloat16):
    level = steps_of(stream_key, extent, shards, -0.22, 0.18) if shards else 1.0
    array = jax.random.normal(stream_key, extent, jnp.float32) * spread * level
    return jnp.minimum(jnp.maximum(array, -bound), bound).astype(kind)


def setup_inputs(seed: int = 0) -> dict:
    keys = jax.random.split(jax.random.key(seed), 5)
    projections = normal_values(keys[0], (3 * CH, SEQ), 1.0, 6.0, ((1, 32),))
    short_filter = normal_values(keys[1], (TAPS, 3 * CH), TAPS ** -0.5, 2.0)
    long_filter = normal_values(keys[2], (GROUPS, SEQ), 1.0, 6.0, ((0, 32),))
    out_grad = normal_values(keys[3], (CH, SEQ), 0.5, 3.0, ((1, 32),))
    return {"projections": projections, "short_filter": short_filter, "long_filter": long_filter, "out_grad": out_grad}


def contract(form, first, second):
    return jnp.einsum(form, first.astype(jnp.float32), second.astype(jnp.float32), precision=lax.Precision.HIGHEST)


def rounded(values):
    return lax.optimization_barrier(values.astype(jnp.bfloat16)).astype(jnp.float32)


def dft_table(count_out, count_in, period):
    left_index = jnp.arange(count_out, dtype=jnp.int32)[:, None]
    right_index = jnp.arange(count_in, dtype=jnp.int32)[None, :]
    angle = ((left_index * right_index) % period).astype(jnp.float32) * (2.0 * math.pi / period)
    return jnp.cos(angle), jnp.sin(angle)


def make_tables():
    padded_len = 2 * SEQ
    inner_len = max(divisor for divisor in range(1, SEQ + 1) if SEQ % divisor == 0 and divisor * divisor <= padded_len)
    outer_len = padded_len // inner_len
    cos_outer, sin_outer = dft_table(outer_len, outer_len // 2, outer_len)
    cos_inner, sin_inner = dft_table(inner_len, inner_len, inner_len)
    return ((rounded(cos_outer), rounded(sin_outer)), dft_table(outer_len, inner_len, padded_len), (rounded(cos_inner), rounded(sin_inner)), padded_len)


def forward_dft(signal, tables):
    (cos_outer, sin_outer), (cos_twist, sin_twist), (cos_inner, sin_inner), padded_len = tables
    count = signal.shape[0]
    folded = signal.astype(jnp.float32).reshape(count, cos_outer.shape[1], cos_inner.shape[0])
    first_re = contract("db,rba->rda", cos_outer, folded)
    first_im = -contract("db,rba->rda", sin_outer, folded)
    twist_re = rounded(first_re * cos_twist + first_im * sin_twist)
    twist_im = rounded(first_im * cos_twist - first_re * sin_twist)
    spec_re = contract("rda,ae->rde", twist_re, cos_inner) + contract("rda,ae->rde", twist_im, sin_inner)
    spec_im = contract("rda,ae->rde", twist_im, cos_inner) - contract("rda,ae->rde", twist_re, sin_inner)
    return spec_re, spec_im


def inverse_dft(spec_re, spec_im, tables):
    (cos_outer, sin_outer), (cos_twist, sin_twist), (cos_inner, sin_inner), padded_len = tables
    count = spec_re.shape[0]
    back_re = contract("rde,ea->rda", spec_re, cos_inner) - contract("rde,ea->rda", spec_im, sin_inner)
    back_im = contract("rde,ea->rda", spec_im, cos_inner) + contract("rde,ea->rda", spec_re, sin_inner)
    turn_re = rounded(back_re * cos_twist - back_im * sin_twist)
    turn_im = rounded(back_im * cos_twist + back_re * sin_twist)
    signal = contract("db,rda->rba", cos_outer, turn_re) - contract("db,rda->rba", sin_outer, turn_im)
    return signal.reshape(count, -1) / padded_len


def reference(projections, short_filter, long_filter, out_grad):
    scale = SEQ ** -0.5
    tables = make_tables()
    weights = short_filter.astype(jnp.float32)
    source = projections.astype(jnp.float32)
    total = jnp.zeros((3 * CH, SEQ), jnp.float32)
    for lag in range(TAPS):
        total = total + weights[lag][:, None] * jnp.pad(source, ((0, 0), (lag, 0)))[:, :SEQ]
    features = total.astype(jnp.bfloat16)
    query = features[:CH].astype(jnp.float32)
    key_part = features[CH:2 * CH].astype(jnp.float32)
    value_part = features[2 * CH:].astype(jnp.float32)
    product = (key_part * value_part).astype(jnp.bfloat16)
    cot = out_grad.astype(jnp.float32)
    conv_grad = (cot * query).astype(jnp.bfloat16)

    block_groups = math.gcd(GROUPS, 16)
    block_count = GROUPS // block_groups
    block_chan = block_groups * CPG

    def per_block(triple):
        prod_block, grad_block, filt_block = triple
        filt_re, filt_im = forward_dft(filt_block, tables)
        filt_re = filt_re[:, None]
        filt_im = filt_im[:, None]
        prod_re, prod_im = forward_dft(prod_block, tables)
        grad_re, grad_im = forward_dft(grad_block, tables)
        shape = (block_groups, CPG) + prod_re.shape[1:]
        prod_re = prod_re.reshape(shape)
        prod_im = prod_im.reshape(shape)
        grad_re = grad_re.reshape(shape)
        grad_im = grad_im.reshape(shape)
        flat = (-1,) + prod_re.shape[2:]
        conv_re = rounded((filt_re * prod_re - filt_im * prod_im) * scale).reshape(flat)
        conv_im = rounded((filt_re * prod_im + filt_im * prod_re) * scale).reshape(flat)
        conv = inverse_dft(conv_re, conv_im, tables).astype(jnp.bfloat16)
        back_re = rounded((filt_re * grad_re + filt_im * grad_im) * scale).reshape(flat)
        back_im = rounded((filt_re * grad_im - filt_im * grad_re) * scale).reshape(flat)
        back = inverse_dft(back_re, back_im, tables).astype(jnp.bfloat16)
        cross_re = rounded(jnp.sum(prod_re * grad_re + prod_im * grad_im, axis=1))
        cross_im = rounded(jnp.sum(prod_re * grad_im - prod_im * grad_re, axis=1))
        filter_part = inverse_dft(cross_re, cross_im, tables) * scale
        return conv, back, filter_part

    conv_b, back_b, filter_b = lax.map(per_block, (product.reshape(block_count, block_chan, SEQ), conv_grad.reshape(block_count, block_chan, SEQ), long_filter.reshape(block_count, block_groups, SEQ)))
    conv = conv_b.reshape(CH, SEQ).astype(jnp.float32)
    back = back_b.reshape(CH, SEQ).astype(jnp.float32)
    filter_grad = filter_b.reshape(GROUPS, SEQ)
    mixed = (query * conv).astype(jnp.bfloat16)
    query_grad = (cot * conv).astype(jnp.bfloat16)
    key_grad = (back * value_part).astype(jnp.bfloat16)
    value_grad = (back * key_part).astype(jnp.bfloat16)
    feat_grad = jnp.concatenate([query_grad, key_grad, value_grad], axis=0).astype(jnp.float32)
    gathered = jnp.zeros((3 * CH, SEQ), jnp.float32)
    for lag in range(TAPS):
        gathered = gathered + weights[lag][:, None] * jnp.pad(feat_grad, ((0, 0), (0, lag)))[:, lag:]
    return mixed, gathered.astype(jnp.bfloat16), filter_grad
```

```python
import math

import jax
import jax.numpy as jnp
from jax import lax
from jax.sharding import PartitionSpec as P

CPG = 4
TAPS = 7


def shifted(value, axis, steps):
    count = lax.axis_size(axis)
    first, last = (max(0, -steps), min(count, count - steps))
    return lax.ppermute(value, axis, [(source, source + steps) for source in range(first, last)])


def contract(form, first, second):
    return jnp.einsum(form, first, second, preferred_element_type=jnp.float32)


def dft_table(count_out, count_in, period):
    left_index = jnp.arange(count_out, dtype=jnp.int32)[:, None]
    right_index = jnp.arange(count_in, dtype=jnp.int32)[None, :]
    angle = (left_index * right_index % period).astype(jnp.float32) * (2.0 * math.pi / period)
    return (jnp.cos(angle), jnp.sin(angle))


def make_tables(seq_len):
    padded_len = 2 * seq_len
    inner_len = max(
        (
            divisor
            for divisor in range(1, seq_len + 1)
            if seq_len % divisor == 0 and divisor * divisor <= padded_len
        )
    )
    outer_len = padded_len // inner_len
    cos_outer, sin_outer = dft_table(outer_len, outer_len // 2, outer_len)
    cos_inner, sin_inner = dft_table(inner_len, inner_len, inner_len)
    return (
        (cos_outer.astype(jnp.bfloat16), sin_outer.astype(jnp.bfloat16)),
        dft_table(outer_len, inner_len, padded_len),
        (cos_inner.astype(jnp.bfloat16), sin_inner.astype(jnp.bfloat16)),
        padded_len,
    )


def forward_dft(signal, tables):
    (cos_outer, sin_outer), (cos_twist, sin_twist), (cos_inner, sin_inner), padded_len = tables
    count = signal.shape[0]
    folded = signal.reshape(count, cos_outer.shape[1], cos_inner.shape[0])
    first_re = contract("db,rba->rda", cos_outer, folded)
    first_im = -contract("db,rba->rda", sin_outer, folded)
    twist_re = (first_re * cos_twist + first_im * sin_twist).astype(jnp.bfloat16)
    twist_im = (first_im * cos_twist - first_re * sin_twist).astype(jnp.bfloat16)
    spec_re = contract("rda,ae->rde", twist_re, cos_inner) + contract(
        "rda,ae->rde", twist_im, sin_inner
    )
    spec_im = contract("rda,ae->rde", twist_im, cos_inner) - contract(
        "rda,ae->rde", twist_re, sin_inner
    )
    return (spec_re, spec_im)


def inverse_dft(spec_re, spec_im, tables):
    (cos_outer, sin_outer), (cos_twist, sin_twist), (cos_inner, sin_inner), padded_len = tables
    count = spec_re.shape[0]
    back_re = contract("rde,ea->rda", spec_re, cos_inner) - contract(
        "rde,ea->rda", spec_im, sin_inner
    )
    back_im = contract("rde,ea->rda", spec_im, cos_inner) + contract(
        "rde,ea->rda", spec_re, sin_inner
    )
    turn_re = (back_re * cos_twist - back_im * sin_twist).astype(jnp.bfloat16)
    turn_im = (back_im * cos_twist + back_re * sin_twist).astype(jnp.bfloat16)
    signal = contract("db,rda->rba", cos_outer, turn_re) - contract(
        "db,rda->rba", sin_outer, turn_im
    )
    return signal.reshape(count, -1) / padded_len


def shards(projections, short_filter, long_filter, out_grad):
    width = out_grad.shape[0]
    local_len = out_grad.shape[1]
    lanes_dp = lax.axis_size("dp")
    lanes_ctx = lax.axis_size("ctx")
    seq_len = local_len * lanes_dp * lanes_ctx
    groups = width // CPG
    local_groups = long_filter.shape[0]
    tables = make_tables(seq_len)
    weights = short_filter.astype(jnp.float32)
    rim_len = TAPS - 1
    earlier = shifted(projections[:, local_len - rim_len :], ("dp", "ctx"), 1)
    extended = jnp.concatenate([earlier, projections], axis=1).astype(jnp.float32)
    total = jnp.zeros(projections.shape, jnp.float32)
    for lag in range(TAPS):
        total = (
            total + weights[lag][:, None] * extended[:, rim_len - lag : rim_len - lag + local_len]
        )
    features = total.astype(jnp.bfloat16)
    query = features[:width].astype(jnp.float32)
    key_part = features[width : 2 * width].astype(jnp.float32)
    value_part = features[2 * width :].astype(jnp.float32)
    product = (key_part * value_part).astype(jnp.bfloat16)
    cotangent = out_grad.astype(jnp.float32)
    conv_grad = (cotangent * query).astype(jnp.bfloat16)
    scale = seq_len ** (-0.5)
    filt_re, filt_im = forward_dft(long_filter, tables)
    filt_re = filt_re[:, None]
    filt_im = filt_im[:, None]

    def spectra(whole):
        spec_re, spec_im = forward_dft(whole.reshape(-1, seq_len), tables)
        shape = (local_groups, CPG) + spec_re.shape[1:]
        return (spec_re.reshape(shape), spec_im.reshape(shape))

    def inverse_block(spec_re, spec_im):
        flat_shape = (-1,) + spec_re.shape[2:]
        signal = inverse_dft(spec_re.reshape(flat_shape), spec_im.reshape(flat_shape), tables)
        return signal.reshape(local_groups, CPG, seq_len).astype(jnp.bfloat16)

    devices = lanes_dp * lanes_ctx
    owned = local_groups * CPG
    everyone = ("dp", "ctx")

    def to_owners(block):
        pieces = block.reshape(devices, owned, local_len)
        arrived = lax.all_to_all(pieces, everyone, split_axis=0, concat_axis=0, tiled=True)
        return arrived.transpose(1, 0, 2)

    def to_positions(block):
        pieces = block.reshape(owned, devices, local_len).transpose(1, 0, 2)
        return lax.all_to_all(pieces, everyone, split_axis=0, concat_axis=0, tiled=True)

    prod_chan = to_owners(product)
    prod_re, prod_im = spectra(prod_chan)
    conv_re = ((filt_re * prod_re - filt_im * prod_im) * scale).astype(jnp.bfloat16)
    conv_im = ((filt_re * prod_im + filt_im * prod_re) * scale).astype(jnp.bfloat16)
    conv_chan = inverse_block(conv_re, conv_im)
    conv_tok = to_positions(conv_chan)
    grad_chan = to_owners(conv_grad)
    grad_re, grad_im = spectra(grad_chan)
    back_re = ((filt_re * grad_re + filt_im * grad_im) * scale).astype(jnp.bfloat16)
    back_im = ((filt_re * grad_im - filt_im * grad_re) * scale).astype(jnp.bfloat16)
    back_chan = inverse_block(back_re, back_im)
    back_tok = to_positions(back_chan)
    cross_re = jnp.sum(prod_re * grad_re + prod_im * grad_im, axis=1).astype(jnp.bfloat16)
    cross_im = jnp.sum(prod_re * grad_im - prod_im * grad_re, axis=1).astype(jnp.bfloat16)
    filter_grad = inverse_dft(cross_re, cross_im, tables) * scale
    conv = conv_tok.reshape(width, local_len).astype(jnp.float32)
    back = back_tok.reshape(width, local_len).astype(jnp.float32)
    mixed = (query * conv).astype(jnp.bfloat16)
    query_grad = (cotangent * conv).astype(jnp.bfloat16)
    key_grad = (back * value_part).astype(jnp.bfloat16)
    value_grad = (back * key_part).astype(jnp.bfloat16)
    feat_grad = jnp.concatenate([query_grad, key_grad, value_grad], axis=0)
    later = shifted(feat_grad[:, :rim_len], ("dp", "ctx"), -1)
    extended_grad = jnp.concatenate([feat_grad, later], axis=1).astype(jnp.float32)
    gathered = jnp.zeros(projections.shape, jnp.float32)
    for lag in range(TAPS):
        gathered = gathered + weights[lag][:, None] * extended_grad[:, lag : lag + local_len]
    proj_grad = gathered.astype(jnp.bfloat16)
    return (mixed, proj_grad, filter_grad)


def solution(mesh):
    placed = (P(None, ("dp", "ctx")), P(), P(("dp", "ctx"), None), P(None, ("dp", "ctx")))
    return jax.shard_map(
        shards,
        mesh=mesh,
        in_specs=placed,
        out_specs=(P(None, ("dp", "ctx")), P(None, ("dp", "ctx")), P(("dp", "ctx"), None)),
        check_vma=False,
    )
```

```python
import math

import jax
import jax.numpy as jnp
import numpy as np
from jax import lax
from jax.experimental import pallas as pl
from jax.experimental.pallas import tpu as pltpu
from jax.sharding import PartitionSpec as P

CPG = 4
TAPS = 7
PAIRS = CPG // 2
EVERYONE = ("dp", "ctx")
VMEM_LIMIT = 40 * 1024 * 1024


def shifted(value, axis, steps):
    count = lax.axis_size(axis)
    first, last = (max(0, -steps), min(count, count - steps))
    return lax.ppermute(value, axis, [(source, source + steps) for source in range(first, last)])


def sizes_of(seq_len):
    padded = 2 * seq_len
    inner = max(d for d in range(1, seq_len + 1) if seq_len % d == 0 and d * d <= padded)
    return padded, inner, padded // inner


def table(count_out, count_in, period):
    turns = np.arange(count_out, dtype=np.int64)[:, None] * np.arange(count_in, dtype=np.int64)
    angle = (turns % period).astype(np.float64) * (2.0 * math.pi / period)
    return np.cos(angle), np.sin(angle)


def make_tables(seq_len, sources):
    padded, inner, outer = sizes_of(seq_len)
    half = outer // 2
    fold = half // sources
    order = np.arange(half).reshape(sources, fold).T.reshape(-1)
    cos_o, sin_o = table(outer, half, outer)
    cos_i, sin_i = table(inner, inner, inner)
    cos_p, sin_p = cos_o[:, order], sin_o[:, order]
    narrow = lambda blocks: jnp.asarray(np.block(blocks).astype(np.float32)).astype(jnp.bfloat16)
    twist = [jnp.asarray(t.astype(np.float32)) for t in table(outer, inner, padded)]
    return {
        "first": narrow([[cos_p, sin_p], [-sin_p, cos_p]]),
        "second": narrow([[cos_i, -sin_i], [sin_i, cos_i]]),
        "third": narrow([[cos_i, sin_i], [-sin_i, cos_i]]),
        "fourth": narrow([[cos_p.T, -sin_p.T], [sin_p.T, cos_p.T]]),
        "first_real": narrow([[cos_o], [-sin_o]]),
        "fourth_real": narrow([[cos_o.T, -sin_o.T]]),
        "twist_re": twist[0],
        "twist_im": twist[1],
    }


LANES = 128


def spread(tall, count, stride, first, height, width):
    tiles = [tall[pl.ds(t * height + first, count, stride=stride), :] for t in range(width[0] // LANES, width[1] // LANES)]
    return tiles[0] if len(tiles) == 1 else jnp.concatenate(tiles, axis=1)


def put_spread(tall, values, stride, first, height, width):
    for i, t in enumerate(range(width[0] // LANES, width[1] // LANES)):
        tall[pl.ds(t * height + first, values.shape[0], stride=stride), :] = values[:, i * LANES : (i + 1) * LANES]


def dot(left, right):
    return jnp.dot(left, right, preferred_element_type=jnp.float32)


def transform_filters(long_filter, tables, seq_len):
    padded, inner, outer = sizes_of(seq_len)
    half = outer // 2
    groups = long_filter.shape[0]
    scale = seq_len ** -0.5

    def kernel(x_ref, first_ref, second_ref, tr_ref, ti_ref, out_ref, tall):
        height = half * groups
        for b in range(half):
            for t in range(inner // LANES):
                at = t * height + b * groups
                lanes = slice(b * inner + t * LANES, b * inner + (t + 1) * LANES)
                tall[at : at + groups, :] = x_ref[:, lanes].astype(jnp.float32)
        for g in range(groups):
            x = spread(tall, half, groups, g, height, (0, inner)).astype(jnp.bfloat16)
            f = dot(first_ref[...], x)
            f_re, f_im = f[:outer], f[outer:]
            g_re = (f_re * tr_ref[...] + f_im * ti_ref[...]).astype(jnp.bfloat16)
            g_im = (f_im * tr_ref[...] - f_re * ti_ref[...]).astype(jnp.bfloat16)
            spec = dot(g_re, second_ref[:inner]) + dot(g_im, second_ref[inner:])
            out_ref[g * outer : (g + 1) * outer, :] = spec * scale

    return pl.pallas_call(
        kernel,
        name="filter_dft",
        out_shape=jax.ShapeDtypeStruct((groups * outer, 2 * inner), jnp.float32),
        scratch_shapes=[pltpu.VMEM((half * groups * inner // LANES, LANES), jnp.float32)],
        compiler_params=pltpu.CompilerParams(vmem_limit_bytes=VMEM_LIMIT),
        cost_estimate=pl.CostEstimate(flops=200_000_000, bytes_accessed=2_000_000, transcendentals=0),
    )(long_filter, tables["first_real"], tables["second"], tables["twist_re"], tables["twist_im"])


def filtered(arrived, filters, tables, seq_len, other=None):
    padded, inner, outer = sizes_of(seq_len)
    half = outer // 2
    sources, channels, local = arrived.shape
    fold = local // inner
    groups = channels // CPG
    backward = other is not None

    def kernel(*refs):
        if backward:
            (x_ref, f_ref, k_ref, first_ref, second_ref, third_ref, fourth_ref, tr_ref, ti_ref,
             y_ref, cross_ref, tall, wide, stage, turn) = refs
        else:
            (x_ref, f_ref, first_ref, second_ref, third_ref, fourth_ref, tr_ref, ti_ref,
             y_ref, z_ref, tall, wide, stage, turn) = refs
        height = sources * channels
        for t in range(local // LANES):
            block = x_ref[:, :, t * LANES : (t + 1) * LANES].astype(jnp.float32)
            tall[t * height : (t + 1) * height, :] = block.reshape(height, LANES)
        for c in range(channels):
            pair, part = divmod(c, 2)
            for h in range(fold):
                rows = spread(tall, sources, channels, c, height, (h * inner, (h + 1) * inner))
                at = part * half + h * sources
                wide[at : at + sources, pair * inner : (pair + 1) * inner] = rows.astype(jnp.bfloat16)
        for g in range(groups):
            span = PAIRS * inner
            f = dot(first_ref[...], wide[:, g * span : (g + 1) * span])
            for p in range(PAIRS):
                f_re = f[:outer, p * inner : (p + 1) * inner]
                f_im = f[outer:, p * inner : (p + 1) * inner]
                at = (g * PAIRS + p) * outer
                stage[at : at + outer, :inner] = (f_re * tr_ref[...] + f_im * ti_ref[...]).astype(jnp.bfloat16)
                stage[at : at + outer, inner:] = (f_im * tr_ref[...] - f_re * ti_ref[...]).astype(jnp.bfloat16)
        for g in range(groups):
            s_re = f_ref[g * outer : (g + 1) * outer, :inner]
            s_im = f_ref[g * outer : (g + 1) * outer, inner:]
            cross_re = cross_im = None
            for p in range(PAIRS):
                at = (g * PAIRS + p) * outer
                z = dot(stage[at : at + outer, :], second_ref[...])
                z_re, z_im = z[:, :inner], z[:, inner:]
                if backward:
                    k_re = k_ref[at : at + outer, :inner].astype(jnp.float32)
                    k_im = k_ref[at : at + outer, inner:].astype(jnp.float32)
                    part_re = k_re * z_re + k_im * z_im
                    part_im = k_re * z_im - k_im * z_re
                    cross_re = part_re if cross_re is None else cross_re + part_re
                    cross_im = part_im if cross_im is None else cross_im + part_im
                    o_re = s_re * z_re + s_im * z_im
                    o_im = s_re * z_im - s_im * z_re
                else:
                    z_ref[at : at + outer, :] = z
                    o_re = s_re * z_re - s_im * z_im
                    o_im = s_re * z_im + s_im * z_re
                stage[at : at + outer, :inner] = o_re.astype(jnp.bfloat16)
                stage[at : at + outer, inner:] = o_im.astype(jnp.bfloat16)
            if backward:
                cross_ref[g * outer : (g + 1) * outer, :inner] = cross_re.astype(jnp.bfloat16)
                cross_ref[g * outer : (g + 1) * outer, inner:] = cross_im.astype(jnp.bfloat16)
        for pair in range(groups * PAIRS):
            at = pair * outer
            h = dot(stage[at : at + outer, :], third_ref[...])
            h_re, h_im = h[:, :inner], h[:, inner:]
            lanes = slice(pair * inner, (pair + 1) * inner)
            turn[:outer, lanes] = (h_re * tr_ref[...] - h_im * ti_ref[...]).astype(jnp.bfloat16)
            turn[outer:, lanes] = (h_im * tr_ref[...] + h_re * ti_ref[...]).astype(jnp.bfloat16)
        for g in range(groups):
            span = PAIRS * inner
            y = dot(fourth_ref[...], turn[:, g * span : (g + 1) * span]) * (1.0 / padded)
            for p in range(PAIRS):
                for part in range(2):
                    c = (g * PAIRS + p) * 2 + part
                    for h in range(fold):
                        at = part * half + h * sources
                        rows = y[at : at + sources, p * inner : (p + 1) * inner]
                        put_spread(tall, rows, channels, c, height, (h * inner, (h + 1) * inner))
        for t in range(local // LANES):
            block = tall[t * height : (t + 1) * height, :].reshape(sources, channels, LANES)
            y_ref[:, :, t * LANES : (t + 1) * LANES] = block.astype(jnp.bfloat16)

    pairs = groups * PAIRS
    if backward:
        extra = jax.ShapeDtypeStruct((groups * outer, 2 * inner), jnp.bfloat16)
    else:
        extra = jax.ShapeDtypeStruct((pairs * outer, 2 * inner), jnp.float32)
    operands = [arrived, filters] + ([other] if backward else [])
    operands += [tables[n] for n in ("first", "second", "third", "fourth", "twist_re", "twist_im")]
    return pl.pallas_call(
        kernel,
        name="correlate" if backward else "convolve",
        out_shape=(jax.ShapeDtypeStruct(arrived.shape, jnp.bfloat16), extra),
        scratch_shapes=[
            pltpu.VMEM((sources * channels * local // LANES, LANES), jnp.float32),
            pltpu.VMEM((outer, pairs * inner), jnp.bfloat16),
            pltpu.VMEM((pairs * outer, 2 * inner), jnp.bfloat16),
            pltpu.VMEM((2 * outer, pairs * inner), jnp.bfloat16),
        ],
        compiler_params=pltpu.CompilerParams(vmem_limit_bytes=VMEM_LIMIT),
        cost_estimate=pl.CostEstimate(flops=2_000_000_000, bytes_accessed=5_000_000, transcendentals=0),
    )(*operands)


def filter_gradient(cross, tables, seq_len):
    padded, inner, outer = sizes_of(seq_len)
    half = outer // 2
    groups = cross.shape[0] // outer
    scale = seq_len ** -0.5 / padded

    def kernel(s_ref, third_ref, fourth_ref, tr_ref, ti_ref, out_ref, tall, turn):
        for g in range(groups):
            h = dot(s_ref[g * outer : (g + 1) * outer, :], third_ref[...])
            h_re, h_im = h[:, :inner], h[:, inner:]
            turn[:outer, g * inner : (g + 1) * inner] = (h_re * tr_ref[...] - h_im * ti_ref[...]).astype(jnp.bfloat16)
            turn[outer:, g * inner : (g + 1) * inner] = (h_im * tr_ref[...] + h_re * ti_ref[...]).astype(jnp.bfloat16)
        for g in range(groups):
            y = dot(fourth_ref[...], turn[:, g * inner : (g + 1) * inner]) * scale
            put_spread(tall, y, groups, g, half * groups, (0, inner))
        for b in range(half):
            for t in range(inner // LANES):
                at = (t * half + b) * groups
                out_ref[:, b * inner + t * LANES : b * inner + (t + 1) * LANES] = tall[at : at + groups, :]

    return pl.pallas_call(
        kernel,
        name="filter_gradient",
        out_shape=jax.ShapeDtypeStruct((groups, seq_len), jnp.float32),
        scratch_shapes=[
            pltpu.VMEM((half * groups * inner // LANES, LANES), jnp.float32),
            pltpu.VMEM((2 * outer, groups * inner), jnp.bfloat16),
        ],
        compiler_params=pltpu.CompilerParams(vmem_limit_bytes=VMEM_LIMIT),
        cost_estimate=pl.CostEstimate(flops=200_000_000, bytes_accessed=2_000_000, transcendentals=0),
    )(cross, tables["third"], tables["fourth_real"], tables["twist_re"], tables["twist_im"])


def shards(projections, short_filter, long_filter, out_grad):
    width, local_len = out_grad.shape
    devices = lax.axis_size(EVERYONE)
    seq_len = local_len * devices
    owned = width // devices
    tables = make_tables(seq_len, devices)
    weights = short_filter.astype(jnp.float32)
    rim_len = TAPS - 1
    earlier = shifted(projections[:, local_len - rim_len :], EVERYONE, 1)
    extended = jnp.concatenate([earlier, projections], axis=1).astype(jnp.float32)
    total = jnp.zeros(projections.shape, jnp.float32)
    for lag in range(TAPS):
        total = (
            total + weights[lag][:, None] * extended[:, rim_len - lag : rim_len - lag + local_len]
        )
    features = total.astype(jnp.bfloat16)
    query = features[:width].astype(jnp.float32)
    key_part = features[width : 2 * width].astype(jnp.float32)
    value_part = features[2 * width :].astype(jnp.float32)
    product = (key_part * value_part).astype(jnp.bfloat16)
    cotangent = out_grad.astype(jnp.float32)
    conv_grad = (cotangent * query).astype(jnp.bfloat16)

    def exchange(block):
        pieces = block.reshape(devices, owned, local_len)
        return lax.all_to_all(pieces, EVERYONE, split_axis=0, concat_axis=0, tiled=True)

    filters = transform_filters(long_filter, tables, seq_len)
    prod_chan = exchange(product)
    conv_grad, prod_chan = lax.optimization_barrier((conv_grad, prod_chan))
    grad_chan = exchange(conv_grad)
    conv_chan, prod_spec = filtered(prod_chan, filters, tables, seq_len)
    conv_chan, grad_chan = lax.optimization_barrier((conv_chan, grad_chan))
    conv_tok = exchange(conv_chan)
    back_chan, cross = filtered(grad_chan, filters, tables, seq_len, prod_spec)
    back_chan, conv_tok = lax.optimization_barrier((back_chan, conv_tok))
    back_tok = exchange(back_chan)
    filter_grad = filter_gradient(cross, tables, seq_len)

    conv = conv_tok.reshape(width, local_len).astype(jnp.float32)
    back = back_tok.reshape(width, local_len).astype(jnp.float32)
    mixed = (query * conv).astype(jnp.bfloat16)
    query_grad = (cotangent * conv).astype(jnp.bfloat16)
    key_grad = (back * value_part).astype(jnp.bfloat16)
    value_grad = (back * key_part).astype(jnp.bfloat16)
    feat_grad = jnp.concatenate([query_grad, key_grad, value_grad], axis=0)
    later = shifted(feat_grad[:, :rim_len], EVERYONE, -1)
    extended_grad = jnp.concatenate([feat_grad, later], axis=1).astype(jnp.float32)
    gathered = jnp.zeros(projections.shape, jnp.float32)
    for lag in range(TAPS):
        gathered = gathered + weights[lag][:, None] * extended_grad[:, lag : lag + local_len]
    proj_grad = gathered.astype(jnp.bfloat16)
    return (mixed, proj_grad, filter_grad)


def solution(mesh):
    placed = (P(None, EVERYONE), P(), P(EVERYONE, None), P(None, EVERYONE))
    return jax.shard_map(
        shards,
        mesh=mesh,
        in_specs=placed,
        out_specs=(P(None, EVERYONE), P(None, EVERYONE), P(EVERYONE, None)),
        check_vma=False,
    )
```

```python
import math

import jax
import jax.numpy as jnp
import numpy as np
from jax import lax
from jax.experimental import pallas as pl
from jax.experimental.pallas import tpu as pltpu
from jax.sharding import PartitionSpec as P

CPG = 4
TAPS = 7
PAIRS = CPG // 2
EVERYONE = ("dp", "ctx")
VMEM_LIMIT = 40 * 1024 * 1024


def shifted(value, axis, steps):
    count = lax.axis_size(axis)
    first, last = (max(0, -steps), min(count, count - steps))
    return lax.ppermute(value, axis, [(source, source + steps) for source in range(first, last)])


def sizes_of(seq_len):
    padded = 2 * seq_len
    inner = max(d for d in range(1, seq_len + 1) if seq_len % d == 0 and d * d <= padded)
    return padded, inner, padded // inner


def table(count_out, count_in, period):
    turns = np.arange(count_out, dtype=np.int64)[:, None] * np.arange(count_in, dtype=np.int64)
    angle = (turns % period).astype(np.float64) * (2.0 * math.pi / period)
    return np.cos(angle), np.sin(angle)


def make_tables(seq_len, sources):
    padded, inner, outer = sizes_of(seq_len)
    half = outer // 2
    fold = half // sources
    order = np.arange(half).reshape(sources, fold).T.reshape(-1)
    cos_o, sin_o = table(outer, half, outer)
    cos_i, sin_i = table(inner, inner, inner)
    cos_p, sin_p = cos_o[:, order], sin_o[:, order]
    narrow = lambda blocks: jnp.asarray(np.block(blocks).astype(np.float32)).astype(jnp.bfloat16)
    twist = [jnp.asarray(t.astype(np.float32)) for t in table(outer, inner, padded)]
    return {
        "first": narrow([[cos_p, sin_p], [-sin_p, cos_p]]),
        "second": narrow([[cos_i, -sin_i], [sin_i, cos_i]]),
        "third": narrow([[cos_i, sin_i], [-sin_i, cos_i]]),
        "fourth": narrow([[cos_p.T, -sin_p.T], [sin_p.T, cos_p.T]]),
        "first_real": narrow([[cos_o], [-sin_o]]),
        "fourth_real": narrow([[cos_o.T, -sin_o.T]]),
        "twist_re": twist[0],
        "twist_im": twist[1],
    }


LANES = 128


def spread(tall, count, stride, first, height, width):
    tiles = [tall[pl.ds(t * height + first, count, stride=stride), :] for t in range(width[0] // LANES, width[1] // LANES)]
    return tiles[0] if len(tiles) == 1 else jnp.concatenate(tiles, axis=1)


def put_spread(tall, values, stride, first, height, width):
    for i, t in enumerate(range(width[0] // LANES, width[1] // LANES)):
        tall[pl.ds(t * height + first, values.shape[0], stride=stride), :] = values[:, i * LANES : (i + 1) * LANES]


def dot(left, right):
    return jnp.dot(left, right, preferred_element_type=jnp.float32)


def transform_filters(long_filter, tables, seq_len):
    padded, inner, outer = sizes_of(seq_len)
    half = outer // 2
    groups = long_filter.shape[0]
    scale = seq_len ** -0.5

    def kernel(x_ref, first_ref, second_ref, tr_ref, ti_ref, out_ref, tall):
        height = half * groups
        for b in range(half):
            for t in range(inner // LANES):
                at = t * height + b * groups
                lanes = slice(b * inner + t * LANES, b * inner + (t + 1) * LANES)
                tall[at : at + groups, :] = x_ref[:, lanes].astype(jnp.float32)
        for g in range(groups):
            x = spread(tall, half, groups, g, height, (0, inner)).astype(jnp.bfloat16)
            f = dot(first_ref[...], x)
            f_re, f_im = f[:outer], f[outer:]
            g_re = (f_re * tr_ref[...] + f_im * ti_ref[...]).astype(jnp.bfloat16)
            g_im = (f_im * tr_ref[...] - f_re * ti_ref[...]).astype(jnp.bfloat16)
            spec = dot(g_re, second_ref[:inner]) + dot(g_im, second_ref[inner:])
            out_ref[g * outer : (g + 1) * outer, :] = spec * scale

    return pl.pallas_call(
        kernel,
        name="filter_dft",
        out_shape=jax.ShapeDtypeStruct((groups * outer, 2 * inner), jnp.float32),
        scratch_shapes=[pltpu.VMEM((half * groups * inner // LANES, LANES), jnp.float32)],
        compiler_params=pltpu.CompilerParams(vmem_limit_bytes=VMEM_LIMIT),
        cost_estimate=pl.CostEstimate(flops=200_000_000, bytes_accessed=2_000_000, transcendentals=0),
    )(long_filter, tables["first_real"], tables["second"], tables["twist_re"], tables["twist_im"])


def filtered(arrived, filters, tables, seq_len, other=None):
    padded, inner, outer = sizes_of(seq_len)
    half = outer // 2
    sources, channels, local = arrived.shape
    fold = local // inner
    groups = channels // CPG
    backward = other is not None

    def kernel(*refs):
        if backward:
            (x_ref, f_ref, k_ref, first_ref, second_ref, third_ref, fourth_ref, tr_ref, ti_ref,
             y_ref, cross_ref, tall, wide, stage, turn) = refs
        else:
            (x_ref, f_ref, first_ref, second_ref, third_ref, fourth_ref, tr_ref, ti_ref,
             y_ref, z_ref, tall, wide, stage, turn) = refs
        height = sources * channels
        for t in range(local // LANES):
            block = x_ref[:, :, t * LANES : (t + 1) * LANES].astype(jnp.float32)
            tall[t * height : (t + 1) * height, :] = block.reshape(height, LANES)
        for c in range(channels):
            pair, part = divmod(c, 2)
            for h in range(fold):
                rows = spread(tall, sources, channels, c, height, (h * inner, (h + 1) * inner))
                at = part * half + h * sources
                wide[at : at + sources, pair * inner : (pair + 1) * inner] = rows.astype(jnp.bfloat16)
        for g in range(groups):
            span = PAIRS * inner
            f = dot(first_ref[...], wide[:, g * span : (g + 1) * span])
            for p in range(PAIRS):
                f_re = f[:outer, p * inner : (p + 1) * inner]
                f_im = f[outer:, p * inner : (p + 1) * inner]
                at = (g * PAIRS + p) * outer
                stage[at : at + outer, :inner] = (f_re * tr_ref[...] + f_im * ti_ref[...]).astype(jnp.bfloat16)
                stage[at : at + outer, inner:] = (f_im * tr_ref[...] - f_re * ti_ref[...]).astype(jnp.bfloat16)
        for g in range(groups):
            s_re = f_ref[g * outer : (g + 1) * outer, :inner]
            s_im = f_ref[g * outer : (g + 1) * outer, inner:]
            cross_re = cross_im = None
            for p in range(PAIRS):
                at = (g * PAIRS + p) * outer
                z = dot(stage[at : at + outer, :], second_ref[...])
                z_re, z_im = z[:, :inner], z[:, inner:]
                if backward:
                    k_re = k_ref[at : at + outer, :inner].astype(jnp.float32)
                    k_im = k_ref[at : at + outer, inner:].astype(jnp.float32)
                    part_re = k_re * z_re + k_im * z_im
                    part_im = k_re * z_im - k_im * z_re
                    cross_re = part_re if cross_re is None else cross_re + part_re
                    cross_im = part_im if cross_im is None else cross_im + part_im
                    o_re = s_re * z_re + s_im * z_im
                    o_im = s_re * z_im - s_im * z_re
                else:
                    z_ref[at : at + outer, :] = z
                    o_re = s_re * z_re - s_im * z_im
                    o_im = s_re * z_im + s_im * z_re
                stage[at : at + outer, :inner] = o_re.astype(jnp.bfloat16)
                stage[at : at + outer, inner:] = o_im.astype(jnp.bfloat16)
            if backward:
                cross_ref[g * outer : (g + 1) * outer, :inner] = cross_re.astype(jnp.bfloat16)
                cross_ref[g * outer : (g + 1) * outer, inner:] = cross_im.astype(jnp.bfloat16)
        for pair in range(groups * PAIRS):
            at = pair * outer
            h = dot(stage[at : at + outer, :], third_ref[...])
            h_re, h_im = h[:, :inner], h[:, inner:]
            lanes = slice(pair * inner, (pair + 1) * inner)
            turn[:outer, lanes] = (h_re * tr_ref[...] - h_im * ti_ref[...]).astype(jnp.bfloat16)
            turn[outer:, lanes] = (h_im * tr_ref[...] + h_re * ti_ref[...]).astype(jnp.bfloat16)
        for g in range(groups):
            span = PAIRS * inner
            y = dot(fourth_ref[...], turn[:, g * span : (g + 1) * span]) * (1.0 / padded)
            for p in range(PAIRS):
                for part in range(2):
                    c = (g * PAIRS + p) * 2 + part
                    for h in range(fold):
                        at = part * half + h * sources
                        rows = y[at : at + sources, p * inner : (p + 1) * inner]
                        put_spread(tall, rows, channels, c, height, (h * inner, (h + 1) * inner))
        for t in range(local // LANES):
            block = tall[t * height : (t + 1) * height, :].reshape(sources, channels, LANES)
            y_ref[:, :, t * LANES : (t + 1) * LANES] = block.astype(jnp.bfloat16)

    pairs = groups * PAIRS
    if backward:
        extra = jax.ShapeDtypeStruct((groups * outer, 2 * inner), jnp.bfloat16)
    else:
        extra = jax.ShapeDtypeStruct((pairs * outer, 2 * inner), jnp.float32)
    operands = [arrived, filters] + ([other] if backward else [])
    operands += [tables[n] for n in ("first", "second", "third", "fourth", "twist_re", "twist_im")]
    return pl.pallas_call(
        kernel,
        name="correlate" if backward else "convolve",
        out_shape=(jax.ShapeDtypeStruct(arrived.shape, jnp.bfloat16), extra),
        scratch_shapes=[
            pltpu.VMEM((sources * channels * local // LANES, LANES), jnp.float32),
            pltpu.VMEM((outer, pairs * inner), jnp.bfloat16),
            pltpu.VMEM((pairs * outer, 2 * inner), jnp.bfloat16),
            pltpu.VMEM((2 * outer, pairs * inner), jnp.bfloat16),
        ],
        compiler_params=pltpu.CompilerParams(vmem_limit_bytes=VMEM_LIMIT),
        cost_estimate=pl.CostEstimate(flops=2_000_000_000, bytes_accessed=5_000_000, transcendentals=0),
    )(*operands)


def filter_gradient(cross, tables, seq_len):
    padded, inner, outer = sizes_of(seq_len)
    half = outer // 2
    groups = cross.shape[0] // outer
    scale = seq_len ** -0.5 / padded

    def kernel(s_ref, third_ref, fourth_ref, tr_ref, ti_ref, out_ref, tall, turn):
        for g in range(groups):
            h = dot(s_ref[g * outer : (g + 1) * outer, :], third_ref[...])
            h_re, h_im = h[:, :inner], h[:, inner:]
            turn[:outer, g * inner : (g + 1) * inner] = (h_re * tr_ref[...] - h_im * ti_ref[...]).astype(jnp.bfloat16)
            turn[outer:, g * inner : (g + 1) * inner] = (h_im * tr_ref[...] + h_re * ti_ref[...]).astype(jnp.bfloat16)
        for g in range(groups):
            y = dot(fourth_ref[...], turn[:, g * inner : (g + 1) * inner]) * scale
            put_spread(tall, y, groups, g, half * groups, (0, inner))
        for b in range(half):
            for t in range(inner // LANES):
                at = (t * half + b) * groups
                out_ref[:, b * inner + t * LANES : b * inner + (t + 1) * LANES] = tall[at : at + groups, :]

    return pl.pallas_call(
        kernel,
        name="filter_gradient",
        out_shape=jax.ShapeDtypeStruct((groups, seq_len), jnp.float32),
        scratch_shapes=[
            pltpu.VMEM((half * groups * inner // LANES, LANES), jnp.float32),
            pltpu.VMEM((2 * outer, groups * inner), jnp.bfloat16),
        ],
        compiler_params=pltpu.CompilerParams(vmem_limit_bytes=VMEM_LIMIT),
        cost_estimate=pl.CostEstimate(flops=200_000_000, bytes_accessed=2_000_000, transcendentals=0),
    )(cross, tables["third"], tables["fourth_real"], tables["twist_re"], tables["twist_im"])


RIM = 8
ROWS = 256


def rims(arrays, first):
    kind, rows_all, local = arrays[0].shape[0], arrays[0].shape[1], arrays[0].shape[2]
    start = 0 if first else LANES - RIM
    pick = np.zeros((RIM, LANES), np.float32)
    pick[np.arange(RIM), start + np.arange(RIM)] = 1.0

    def kernel(pick_ref, *refs):
        out_ref = refs[-1]
        value = refs[0][0]
        for ref in refs[1:-1]:
            value = (value.astype(jnp.float32) * ref[0].astype(jnp.float32)).astype(jnp.bfloat16)
        out_ref[...] = lax.dot_general(
            pick_ref[...], value, (((1,), (1,)), ((), ())), preferred_element_type=jnp.float32
        ).astype(jnp.bfloat16)

    tile = 0 if first else local // LANES - 1
    return kernel, pick, tile


def call_rims(name, count, width, tile, pick, kernel, operands, maps):
    return pl.pallas_call(
        kernel,
        name=name,
        grid=(count,),
        in_specs=[pl.BlockSpec((RIM, LANES), lambda i: (0, 0))]
        + [pl.BlockSpec((1, width, LANES), m) for m in maps],
        out_specs=pl.BlockSpec((RIM, width), lambda i: (0, i)),
        out_shape=jax.ShapeDtypeStruct((RIM, count * width), jnp.bfloat16),
        cost_estimate=pl.CostEstimate(flops=10_000_000, bytes_accessed=1_000_000, transcendentals=0),
    )(jnp.asarray(pick).astype(jnp.bfloat16), *operands)


def edge_columns(rim, weights, forward):
    spot = lax.broadcasted_iota(jnp.int32, (RIM, LANES), 0)
    added = jnp.zeros((RIM, LANES), jnp.float32)
    for lag in range(1, TAPS):
        moved = pltpu.roll(rim, lag if forward else RIM - lag, 0)
        inside = spot < lag if forward else spot >= RIM - lag
        added = added + jnp.where(inside, moved, 0.0) * weights[lag : lag + 1]
    taps = jnp.concatenate([weights, jnp.zeros((RIM - TAPS, LANES), jnp.float32)], axis=0)
    rest = jnp.zeros((LANES - 2 * RIM, LANES), jnp.float32)
    rows = [added, taps, rest] if forward else [taps, rest, added]
    return jnp.concatenate(rows, axis=0).T


def seven_taps(tiles, rim, weights, forward):
    columns = edge_columns(rim, weights, forward)
    lane = lax.broadcasted_iota(jnp.int32, (LANES, LANES), 1)
    offset = RIM if forward else 0
    edge = jnp.where(lane < RIM, columns, 0.0) if forward else jnp.where(lane >= LANES - RIM, columns, 0.0)
    tap = [columns[:, offset + lag : offset + lag + 1] for lag in range(TAPS)]
    total = [tile * tap[0] for tile in tiles]
    last = len(tiles) - 1
    for lag in range(1, TAPS):
        if forward:
            moved = [pltpu.roll(tile, lag, 1) for tile in tiles]
            inside = lane >= lag
            for t in range(len(tiles)):
                total[t] = total[t] + tap[lag] * jnp.where(inside, moved[t], moved[t - 1] if t else 0.0)
        else:
            moved = [pltpu.roll(tile, LANES - lag, 1) for tile in tiles]
            inside = lane < LANES - lag
            for t in range(len(tiles)):
                total[t] = total[t] + tap[lag] * jnp.where(inside, moved[t], moved[t + 1] if t < last else 0.0)
    if forward:
        total[0] = total[0] + edge
    else:
        total[last] = total[last] + edge
    return total


def features_of(projections, rim, short_filter, out_grad):
    width, local = out_grad.shape
    steps = width // ROWS

    def kernel(x_ref, rim_q, rim_k, rim_v, w_q, w_k, w_v, og_ref, f_ref, kv_ref, dconv_ref):
        for r in range(ROWS // LANES):
            rows = slice(r * LANES, (r + 1) * LANES)
            made = []
            for part, (rim_ref, w_ref) in enumerate(((rim_q, w_q), (rim_k, w_k), (rim_v, w_v))):
                tiles = [
                    x_ref[part, rows, t * LANES : (t + 1) * LANES].astype(jnp.float32)
                    for t in range(local // LANES)
                ]
                total = seven_taps(
                    tiles, rim_ref[:, rows].astype(jnp.float32), w_ref[:, rows].astype(jnp.float32), True
                )
                total = [value.astype(jnp.bfloat16) for value in total]
                for t, value in enumerate(total):
                    f_ref[part, rows, t * LANES : (t + 1) * LANES] = value
                made.append([value.astype(jnp.float32) for value in total])
            for t in range(local // LANES):
                lanes = slice(t * LANES, (t + 1) * LANES)
                kv_ref[rows, lanes] = (made[1][t] * made[2][t]).astype(jnp.bfloat16)
                og = og_ref[rows, lanes].astype(jnp.float32)
                dconv_ref[rows, lanes] = (og * made[0][t]).astype(jnp.bfloat16)

    third = lambda part: (lambda i: (0, part * steps + i))
    pair = pl.BlockSpec((ROWS, local), lambda i: (i, 0))
    triple = pl.BlockSpec((3, ROWS, local), lambda i: (0, i, 0))
    return pl.pallas_call(
        kernel,
        name="features",
        grid=(steps,),
        in_specs=[triple]
        + [pl.BlockSpec((RIM, ROWS), third(p)) for p in range(3)]
        + [pl.BlockSpec((TAPS, ROWS), third(p)) for p in range(3)]
        + [pair],
        out_specs=(triple, pair, pair),
        out_shape=(
            jax.ShapeDtypeStruct((3, width, local), jnp.bfloat16),
            jax.ShapeDtypeStruct((width, local), jnp.bfloat16),
            jax.ShapeDtypeStruct((width, local), jnp.bfloat16),
        ),
        cost_estimate=pl.CostEstimate(flops=20_000_000, bytes_accessed=5_000_000, transcendentals=0),
    )(projections, rim, rim, rim, short_filter, short_filter, short_filter, out_grad)


def query_side(feats, conv, out_grad, rim, short_filter):
    width, local = out_grad.shape
    steps = width // ROWS

    def kernel(q_ref, conv_ref, og_ref, rim_ref, w_ref, mixed_ref, grad_ref):
        for r in range(ROWS // LANES):
            rows = slice(r * LANES, (r + 1) * LANES)
            tiles = []
            for t in range(local // LANES):
                lanes = slice(t * LANES, (t + 1) * LANES)
                conv_here = conv_ref[0, rows, lanes].astype(jnp.float32)
                mixed_ref[rows, lanes] = (q_ref[0, rows, lanes].astype(jnp.float32) * conv_here).astype(jnp.bfloat16)
                grad = (og_ref[rows, lanes].astype(jnp.float32) * conv_here).astype(jnp.bfloat16)
                tiles.append(grad.astype(jnp.float32))
            total = seven_taps(tiles, rim_ref[:, rows].astype(jnp.float32), w_ref[:, rows].astype(jnp.float32), False)
            for t, value in enumerate(total):
                grad_ref[0, rows, t * LANES : (t + 1) * LANES] = value.astype(jnp.bfloat16)

    pair = pl.BlockSpec((ROWS, local), lambda i: (i, 0))
    one = pl.BlockSpec((1, ROWS, local), lambda i: (0, i, 0))
    return pl.pallas_call(
        kernel,
        name="query_side",
        grid=(steps,),
        in_specs=[one, one, pair, pl.BlockSpec((RIM, ROWS), lambda i: (0, i)), pl.BlockSpec((TAPS, ROWS), lambda i: (0, i))],
        out_specs=(pair, one),
        out_shape=(
            jax.ShapeDtypeStruct((width, local), jnp.bfloat16),
            jax.ShapeDtypeStruct((3, width, local), jnp.bfloat16),
        ),
        cost_estimate=pl.CostEstimate(flops=10_000_000, bytes_accessed=3_000_000, transcendentals=0),
    )(feats, conv, out_grad, rim, short_filter)


def key_value_side(grad, feats, back, rim, short_filter):
    width, local = back.shape[1:]
    steps = width // ROWS

    def kernel(_, f_ref, back_ref, rim_ref, w_ref, grad_ref):
        for r in range(ROWS // LANES):
            rows = slice(r * LANES, (r + 1) * LANES)
            tiles = []
            for t in range(local // LANES):
                lanes = slice(t * LANES, (t + 1) * LANES)
                value = back_ref[0, rows, lanes].astype(jnp.float32) * f_ref[0, rows, lanes].astype(jnp.float32)
                tiles.append(value.astype(jnp.bfloat16).astype(jnp.float32))
            total = seven_taps(tiles, rim_ref[:, rows].astype(jnp.float32), w_ref[:, rows].astype(jnp.float32), False)
            for t, value in enumerate(total):
                grad_ref[0, rows, t * LANES : (t + 1) * LANES] = value.astype(jnp.bfloat16)

    return pl.pallas_call(
        kernel,
        name="key_value_side",
        grid=(2, steps),
        in_specs=[
            pl.BlockSpec(memory_space=pl.ANY),
            pl.BlockSpec((1, ROWS, local), lambda p, i: (2 - p, i, 0)),
            pl.BlockSpec((1, ROWS, local), lambda p, i: (0, i, 0)),
            pl.BlockSpec((RIM, ROWS), lambda p, i: (0, p * steps + i)),
            pl.BlockSpec((TAPS, ROWS), lambda p, i: (0, (1 + p) * steps + i)),
        ],
        out_specs=pl.BlockSpec((1, ROWS, local), lambda p, i: (1 + p, i, 0)),
        out_shape=jax.ShapeDtypeStruct((3, width, local), jnp.bfloat16),
        input_output_aliases={0: 0},
        cost_estimate=pl.CostEstimate(flops=20_000_000, bytes_accessed=4_000_000, transcendentals=0),
    )(grad, feats, back, rim, short_filter)


def shards(projections, short_filter, long_filter, out_grad):
    width, local_len = out_grad.shape
    devices = lax.axis_size(EVERYONE)
    seq_len = local_len * devices
    owned = width // devices
    tables = make_tables(seq_len, devices)
    tripled = projections.reshape(3, width, local_len)

    kernel, pick, tile = rims([tripled], False)
    own_rim = call_rims("last_positions", 3, width, tile, pick, kernel, [tripled], [lambda i: (i, 0, tile)])
    left_rim = shifted(own_rim, EVERYONE, 1)
    feats, product, conv_grad = features_of(tripled, left_rim, short_filter, out_grad)

    def exchange(block):
        pieces = block.reshape(devices, owned, local_len)
        return lax.all_to_all(pieces, EVERYONE, split_axis=0, concat_axis=0, tiled=True)

    filters = transform_filters(long_filter, tables, seq_len)
    prod_chan = exchange(product)
    conv_grad, prod_chan = lax.optimization_barrier((conv_grad, prod_chan))
    grad_chan = exchange(conv_grad)
    conv_chan, prod_spec = filtered(prod_chan, filters, tables, seq_len)
    conv_chan, grad_chan = lax.optimization_barrier((conv_chan, grad_chan))
    conv_tok = exchange(conv_chan)
    back_chan, cross = filtered(grad_chan, filters, tables, seq_len, prod_spec)
    back_chan, conv_tok = lax.optimization_barrier((back_chan, conv_tok))
    back_tok = exchange(back_chan)
    filter_grad = filter_gradient(cross, tables, seq_len)

    conv = conv_tok.reshape(1, width, local_len)
    cotangent = out_grad.reshape(1, width, local_len)
    here = lambda i: (0, 0, 0)
    kernel, pick, tile = rims([conv, cotangent], True)
    query_rim = call_rims("query_rim", 1, width, tile, pick, kernel, [conv, cotangent], [here, here])
    query_rim = shifted(query_rim, EVERYONE, -1)
    mixed, grad = query_side(feats, conv, out_grad, query_rim, short_filter)

    back = back_tok.reshape(1, width, local_len)
    kernel, pick, tile = rims([back, feats], True)
    side_rim = call_rims(
        "key_value_rim", 2, width, tile, pick, kernel, [back, feats], [here, lambda i: (2 - i, 0, 0)]
    )
    side_rim = shifted(side_rim, EVERYONE, -1)
    grad = key_value_side(grad, feats, back, side_rim, short_filter)
    return (mixed, grad.reshape(3 * width, local_len), filter_grad)


def solution(mesh):
    placed = (P(None, EVERYONE), P(), P(EVERYONE, None), P(None, EVERYONE))
    return jax.shard_map(
        shards,
        mesh=mesh,
        in_specs=placed,
        out_specs=(P(None, EVERYONE), P(None, EVERYONE), P(EVERYONE, None)),
        check_vma=False,
    )
```

```python
import math

import jax
import jax.numpy as jnp
import numpy as np
from jax import lax
from jax.experimental import pallas as pl
from jax.experimental.pallas import tpu as pltpu
from jax.sharding import PartitionSpec as P

CPG = 4
TAPS = 7
PAIRS = CPG // 2
EVERYONE = ("dp", "ctx")
VMEM_LIMIT = 40 * 1024 * 1024


def shifted(value, axis, steps):
    count = lax.axis_size(axis)
    first, last = (max(0, -steps), min(count, count - steps))
    return lax.ppermute(value, axis, [(source, source + steps) for source in range(first, last)])


def sizes_of(seq_len):
    padded = 2 * seq_len
    inner = max(d for d in range(1, seq_len + 1) if seq_len % d == 0 and d * d <= padded)
    return padded, inner, padded // inner


def table(count_out, count_in, period):
    turns = np.arange(count_out, dtype=np.int64)[:, None] * np.arange(count_in, dtype=np.int64)
    angle = (turns % period).astype(np.float64) * (2.0 * math.pi / period)
    return np.cos(angle), np.sin(angle)


def make_tables(seq_len, sources):
    padded, inner, outer = sizes_of(seq_len)
    half = outer // 2
    fold = half // sources
    order = np.arange(half).reshape(sources, fold).T.reshape(-1)
    cos_o, sin_o = table(outer, half, outer)
    cos_i, sin_i = table(inner, inner, inner)
    cos_p, sin_p = cos_o[:, order], sin_o[:, order]
    narrow = lambda blocks: jnp.asarray(np.block(blocks).astype(np.float32)).astype(jnp.bfloat16)
    twist = [jnp.asarray(t.astype(np.float32)) for t in table(outer, inner, padded)]
    return {
        "first": narrow([[cos_p, sin_p], [-sin_p, cos_p]]),
        "second": narrow([[cos_i, -sin_i], [sin_i, cos_i]]),
        "third": narrow([[cos_i, sin_i], [-sin_i, cos_i]]),
        "fourth": narrow([[cos_p.T, -sin_p.T], [sin_p.T, cos_p.T]]),
        "first_real": narrow([[cos_o], [-sin_o]]),
        "fourth_real": narrow([[cos_o.T, -sin_o.T]]),
        "twist_re": twist[0],
        "twist_im": twist[1],
    }


LANES = 128


def spread(tall, count, stride, first, height, width):
    tiles = [tall[pl.ds(t * height + first, count, stride=stride), :] for t in range(width[0] // LANES, width[1] // LANES)]
    return tiles[0] if len(tiles) == 1 else jnp.concatenate(tiles, axis=1)


def put_spread(tall, values, stride, first, height, width):
    for i, t in enumerate(range(width[0] // LANES, width[1] // LANES)):
        tall[pl.ds(t * height + first, values.shape[0], stride=stride), :] = values[:, i * LANES : (i + 1) * LANES]


def dot(left, right):
    return jnp.dot(left, right, preferred_element_type=jnp.float32)


def transform_filters(long_filter, tables, seq_len):
    padded, inner, outer = sizes_of(seq_len)
    half = outer // 2
    groups = long_filter.shape[0]
    scale = seq_len ** -0.5

    def kernel(x_ref, first_ref, second_ref, tr_ref, ti_ref, out_ref, tall):
        height = half * groups
        for b in range(half):
            for t in range(inner // LANES):
                at = t * height + b * groups
                lanes = slice(b * inner + t * LANES, b * inner + (t + 1) * LANES)
                tall[at : at + groups, :] = x_ref[:, lanes].astype(jnp.float32)
        for g in range(groups):
            x = spread(tall, half, groups, g, height, (0, inner)).astype(jnp.bfloat16)
            f = dot(first_ref[...], x)
            f_re, f_im = f[:outer], f[outer:]
            g_re = (f_re * tr_ref[...] + f_im * ti_ref[...]).astype(jnp.bfloat16)
            g_im = (f_im * tr_ref[...] - f_re * ti_ref[...]).astype(jnp.bfloat16)
            spec = dot(g_re, second_ref[:inner]) + dot(g_im, second_ref[inner:])
            out_ref[g * outer : (g + 1) * outer, :] = spec * scale

    return pl.pallas_call(
        kernel,
        name="filter_dft",
        out_shape=jax.ShapeDtypeStruct((groups * outer, 2 * inner), jnp.float32),
        scratch_shapes=[pltpu.VMEM((half * groups * inner // LANES, LANES), jnp.float32)],
        compiler_params=pltpu.CompilerParams(vmem_limit_bytes=VMEM_LIMIT),
        cost_estimate=pl.CostEstimate(flops=200_000_000, bytes_accessed=2_000_000, transcendentals=0),
    )(long_filter, tables["first_real"], tables["second"], tables["twist_re"], tables["twist_im"])


def filtered(arrived, filters, tables, seq_len, other=None):
    padded, inner, outer = sizes_of(seq_len)
    half = outer // 2
    sources, channels, local = arrived.shape
    fold = local // inner
    groups = channels // CPG
    backward = other is not None

    def kernel(*refs):
        if backward:
            (x_ref, f_ref, k_ref, first_ref, second_ref, third_ref, fourth_ref, tr_ref, ti_ref,
             y_ref, cross_ref, tall, wide, stage, turn) = refs
        else:
            (x_ref, f_ref, first_ref, second_ref, third_ref, fourth_ref, tr_ref, ti_ref,
             y_ref, z_ref, tall, wide, stage, turn) = refs
        height = sources * channels
        for t in range(local // LANES):
            block = x_ref[:, :, t * LANES : (t + 1) * LANES].astype(jnp.float32)
            tall[t * height : (t + 1) * height, :] = block.reshape(height, LANES)
        for c in range(channels):
            pair, part = divmod(c, 2)
            for h in range(fold):
                rows = spread(tall, sources, channels, c, height, (h * inner, (h + 1) * inner))
                at = part * half + h * sources
                wide[at : at + sources, pair * inner : (pair + 1) * inner] = rows.astype(jnp.bfloat16)
        for g in range(groups):
            span = PAIRS * inner
            f = dot(first_ref[...], wide[:, g * span : (g + 1) * span])
            for p in range(PAIRS):
                f_re = f[:outer, p * inner : (p + 1) * inner]
                f_im = f[outer:, p * inner : (p + 1) * inner]
                at = (g * PAIRS + p) * outer
                stage[at : at + outer, :inner] = (f_re * tr_ref[...] + f_im * ti_ref[...]).astype(jnp.bfloat16)
                stage[at : at + outer, inner:] = (f_im * tr_ref[...] - f_re * ti_ref[...]).astype(jnp.bfloat16)
        for g in range(groups):
            s_re = f_ref[g * outer : (g + 1) * outer, :inner]
            s_im = f_ref[g * outer : (g + 1) * outer, inner:]
            cross_re = cross_im = None
            for p in range(PAIRS):
                at = (g * PAIRS + p) * outer
                z = dot(stage[at : at + outer, :], second_ref[...])
                z_re, z_im = z[:, :inner], z[:, inner:]
                if backward:
                    k_re = k_ref[at : at + outer, :inner].astype(jnp.float32)
                    k_im = k_ref[at : at + outer, inner:].astype(jnp.float32)
                    part_re = k_re * z_re + k_im * z_im
                    part_im = k_re * z_im - k_im * z_re
                    cross_re = part_re if cross_re is None else cross_re + part_re
                    cross_im = part_im if cross_im is None else cross_im + part_im
                    o_re = s_re * z_re + s_im * z_im
                    o_im = s_re * z_im - s_im * z_re
                else:
                    z_ref[at : at + outer, :] = z
                    o_re = s_re * z_re - s_im * z_im
                    o_im = s_re * z_im + s_im * z_re
                stage[at : at + outer, :inner] = o_re.astype(jnp.bfloat16)
                stage[at : at + outer, inner:] = o_im.astype(jnp.bfloat16)
            if backward:
                cross_ref[g * outer : (g + 1) * outer, :inner] = cross_re.astype(jnp.bfloat16)
                cross_ref[g * outer : (g + 1) * outer, inner:] = cross_im.astype(jnp.bfloat16)
        for pair in range(groups * PAIRS):
            at = pair * outer
            h = dot(stage[at : at + outer, :], third_ref[...])
            h_re, h_im = h[:, :inner], h[:, inner:]
            lanes = slice(pair * inner, (pair + 1) * inner)
            turn[:outer, lanes] = (h_re * tr_ref[...] - h_im * ti_ref[...]).astype(jnp.bfloat16)
            turn[outer:, lanes] = (h_im * tr_ref[...] + h_re * ti_ref[...]).astype(jnp.bfloat16)
        for g in range(groups):
            span = PAIRS * inner
            y = dot(fourth_ref[...], turn[:, g * span : (g + 1) * span]) * (1.0 / padded)
            for p in range(PAIRS):
                for part in range(2):
                    c = (g * PAIRS + p) * 2 + part
                    for h in range(fold):
                        at = part * half + h * sources
                        rows = y[at : at + sources, p * inner : (p + 1) * inner]
                        put_spread(tall, rows, channels, c, height, (h * inner, (h + 1) * inner))
        for t in range(local // LANES):
            block = tall[t * height : (t + 1) * height, :].reshape(sources, channels, LANES)
            y_ref[:, :, t * LANES : (t + 1) * LANES] = block.astype(jnp.bfloat16)

    pairs = groups * PAIRS
    if backward:
        extra = jax.ShapeDtypeStruct((groups * outer, 2 * inner), jnp.bfloat16)
    else:
        extra = jax.ShapeDtypeStruct((pairs * outer, 2 * inner), jnp.float32)
    operands = [arrived, filters] + ([other] if backward else [])
    operands += [tables[n] for n in ("first", "second", "third", "fourth", "twist_re", "twist_im")]
    return pl.pallas_call(
        kernel,
        name="correlate" if backward else "convolve",
        out_shape=(jax.ShapeDtypeStruct(arrived.shape, jnp.bfloat16), extra),
        scratch_shapes=[
            pltpu.VMEM((sources * channels * local // LANES, LANES), jnp.float32),
            pltpu.VMEM((outer, pairs * inner), jnp.bfloat16),
            pltpu.VMEM((pairs * outer, 2 * inner), jnp.bfloat16),
            pltpu.VMEM((2 * outer, pairs * inner), jnp.bfloat16),
        ],
        compiler_params=pltpu.CompilerParams(vmem_limit_bytes=VMEM_LIMIT),
        cost_estimate=pl.CostEstimate(flops=2_000_000_000, bytes_accessed=5_000_000, transcendentals=0),
    )(*operands)


def filter_gradient(cross, tables, seq_len):
    padded, inner, outer = sizes_of(seq_len)
    half = outer // 2
    groups = cross.shape[0] // outer
    scale = seq_len ** -0.5 / padded

    def kernel(s_ref, third_ref, fourth_ref, tr_ref, ti_ref, out_ref, tall, turn):
        for g in range(groups):
            h = dot(s_ref[g * outer : (g + 1) * outer, :], third_ref[...])
            h_re, h_im = h[:, :inner], h[:, inner:]
            turn[:outer, g * inner : (g + 1) * inner] = (h_re * tr_ref[...] - h_im * ti_ref[...]).astype(jnp.bfloat16)
            turn[outer:, g * inner : (g + 1) * inner] = (h_im * tr_ref[...] + h_re * ti_ref[...]).astype(jnp.bfloat16)
        for g in range(groups):
            y = dot(fourth_ref[...], turn[:, g * inner : (g + 1) * inner]) * scale
            put_spread(tall, y, groups, g, half * groups, (0, inner))
        for b in range(half):
            for t in range(inner // LANES):
                at = (t * half + b) * groups
                out_ref[:, b * inner + t * LANES : b * inner + (t + 1) * LANES] = tall[at : at + groups, :]

    return pl.pallas_call(
        kernel,
        name="filter_gradient",
        out_shape=jax.ShapeDtypeStruct((groups, seq_len), jnp.float32),
        scratch_shapes=[
            pltpu.VMEM((half * groups * inner // LANES, LANES), jnp.float32),
            pltpu.VMEM((2 * outer, groups * inner), jnp.bfloat16),
        ],
        compiler_params=pltpu.CompilerParams(vmem_limit_bytes=VMEM_LIMIT),
        cost_estimate=pl.CostEstimate(flops=200_000_000, bytes_accessed=2_000_000, transcendentals=0),
    )(cross, tables["third"], tables["fourth_real"], tables["twist_re"], tables["twist_im"])


RIM = 8


def seven_taps(tall, value, rim, weights, forward):
    count = value.shape[0]
    if forward:
        tall[:RIM, :] = rim
        tall[RIM : RIM + count, :] = value
    else:
        tall[:count, :] = value
        tall[count : count + RIM, :] = rim
    total = value * weights[:1]
    for lag in range(1, TAPS):
        first = RIM - lag if forward else lag
        total = total + tall[first : first + count, :] * weights[lag : lag + 1]
    return total


def lane_block(i, offset=0):
    return pl.ds(pl.multiple_of(i * LANES + offset, LANES), LANES)


def whole_call(kernel, name, out_shape, operands, scratch=(), flops=10_000_000, **kwargs):
    return pl.pallas_call(
        kernel,
        name=name,
        out_shape=out_shape,
        scratch_shapes=list(scratch),
        compiler_params=pltpu.CompilerParams(vmem_limit_bytes=VMEM_LIMIT),
        cost_estimate=pl.CostEstimate(flops=flops, bytes_accessed=4_000_000, transcendentals=0),
        **kwargs,
    )(*operands)


def narrow_shape(*shape):
    return jax.ShapeDtypeStruct(shape, jnp.bfloat16)


def features_of(turned, rim, short_filter, cotangent):
    local, width = cotangent.shape

    def kernel(x_ref, rim_ref, w_ref, og_ref, f_ref, kv_ref, dconv_ref, tall):
        @pl.loop(0, width // LANES)
        def _(i):
            made = []
            for part in range(3):
                lanes = lane_block(i, part * width)
                total = seven_taps(
                    tall.at[part],
                    x_ref[:, lanes].astype(jnp.float32),
                    rim_ref[:, lanes].astype(jnp.float32),
                    w_ref[:, lanes].astype(jnp.float32),
                    True,
                ).astype(jnp.bfloat16)
                f_ref[:, lanes] = total
                made.append(total.astype(jnp.float32))
            rows = lane_block(i)
            kv_ref[rows, :] = (made[1] * made[2]).astype(jnp.bfloat16).T
            og = og_ref[:, rows].astype(jnp.float32)
            dconv_ref[rows, :] = (og * made[0]).astype(jnp.bfloat16).T

    return whole_call(
        kernel,
        "features",
        (narrow_shape(local, 3 * width), narrow_shape(width, local), narrow_shape(width, local)),
        (turned, rim, short_filter, cotangent),
        [pltpu.VMEM((3, local + RIM, LANES), jnp.float32)],
    )


def query_products(feats, conv, cotangent):
    width, local = conv.shape

    def kernel(f_ref, conv_ref, og_ref, mixed_ref, dq_ref, rim_ref):
        @pl.loop(0, width // LANES)
        def _(i):
            lanes = lane_block(i)
            here = conv_ref[lanes, :].T.astype(jnp.float32)
            mixed_ref[lanes, :] = (f_ref[:, lanes].astype(jnp.float32) * here).astype(jnp.bfloat16).T
            dq = (og_ref[:, lanes].astype(jnp.float32) * here).astype(jnp.bfloat16)
            dq_ref[:, lanes] = dq
            rim_ref[:, lanes] = dq[:RIM]

    return whole_call(
        kernel,
        "query_products",
        (narrow_shape(width, local), narrow_shape(local, width), narrow_shape(RIM, width)),
        (feats, conv, cotangent),
    )


def key_value_products(feats, back):
    width, local = back.shape

    def kernel(f_ref, back_ref, d_ref, rim_ref):
        @pl.loop(0, width // LANES)
        def _(i):
            here = back_ref[lane_block(i), :].T.astype(jnp.float32)
            for part in range(2):
                other = f_ref[:, lane_block(i, (2 - part) * width)].astype(jnp.float32)
                grad = (here * other).astype(jnp.bfloat16)
                d_ref[:, lane_block(i, part * width)] = grad
                rim_ref[:, lane_block(i, part * width)] = grad[:RIM]

    return whole_call(
        kernel,
        "key_value_products",
        (narrow_shape(local, 2 * width), narrow_shape(RIM, 2 * width)),
        (feats, back),
    )


def query_gradient(grad, rim, short_filter):
    local, width = grad.shape
    steps = width // GRAD_ROWS

    def kernel(d_ref, rim_ref, w_ref, out_ref, tall):
        gradient_block(d_ref, rim_ref, w_ref, out_ref, tall)

    return gradient_call(kernel, "query_gradient", (), grad, rim, short_filter, 1, 0)


def key_value_gradient(whole, grad, rim, short_filter):
    def kernel(_, d_ref, rim_ref, w_ref, out_ref, tall):
        gradient_block(d_ref, rim_ref, w_ref, out_ref, tall)

    return gradient_call(kernel, "key_value_gradient", (whole,), grad, rim, short_filter, 2, 1)


GRAD_ROWS = 512


def gradient_block(d_ref, rim_ref, w_ref, out_ref, tall):
    for c in range(GRAD_ROWS // LANES):
        lanes = slice(c * LANES, (c + 1) * LANES)
        total = seven_taps(
            tall.at[c],
            d_ref[:, lanes].astype(jnp.float32),
            rim_ref[:, lanes].astype(jnp.float32),
            w_ref[:, lanes].astype(jnp.float32),
            False,
        )
        out_ref[lanes, :] = total.astype(jnp.bfloat16).T


def gradient_call(kernel, name, whole, grad, rim, short_filter, parts, first):
    local, lanes = grad.shape
    width = lanes // parts
    steps = width // GRAD_ROWS
    return pl.pallas_call(
        kernel,
        name=name,
        grid=(parts * steps,),
        in_specs=[pl.BlockSpec(memory_space=pl.ANY)] * len(whole)
        + [
            pl.BlockSpec((local, GRAD_ROWS), lambda i: (0, i)),
            pl.BlockSpec((RIM, GRAD_ROWS), lambda i: (0, i)),
            pl.BlockSpec((TAPS, GRAD_ROWS), lambda i: (0, first * steps + i)),
        ],
        out_specs=pl.BlockSpec((GRAD_ROWS, local), lambda i: (first * steps + i, 0)),
        out_shape=narrow_shape(3 * width, local),
        scratch_shapes=[pltpu.VMEM((GRAD_ROWS // LANES, local + RIM, LANES), jnp.float32)],
        input_output_aliases={0: 0} if whole else {},
        cost_estimate=pl.CostEstimate(flops=20_000_000, bytes_accessed=4_000_000, transcendentals=0),
    )(*whole, grad, rim, short_filter)


def shards(projections, short_filter, long_filter, out_grad):
    width, local_len = out_grad.shape
    devices = lax.axis_size(EVERYONE)
    seq_len = local_len * devices
    owned = width // devices
    tables = make_tables(seq_len, devices)

    turned = projections.T
    cotangent = out_grad.T
    rim = shifted(turned[local_len - RIM :], EVERYONE, 1)
    feats, product, conv_grad = features_of(turned, rim, short_filter, cotangent)

    def exchange(block):
        pieces = block.reshape(devices, owned, local_len)
        return lax.all_to_all(pieces, EVERYONE, split_axis=0, concat_axis=0, tiled=True)

    filters = transform_filters(long_filter, tables, seq_len)
    prod_chan = exchange(product)
    conv_grad, prod_chan = lax.optimization_barrier((conv_grad, prod_chan))
    grad_chan = exchange(conv_grad)
    conv_chan, prod_spec = filtered(prod_chan, filters, tables, seq_len)
    conv_chan, grad_chan = lax.optimization_barrier((conv_chan, grad_chan))
    conv_tok = exchange(conv_chan)
    back_chan, cross = filtered(grad_chan, filters, tables, seq_len, prod_spec)
    back_chan, conv_tok = lax.optimization_barrier((back_chan, conv_tok))
    back_tok = exchange(back_chan)

    filter_grad = filter_gradient(cross, tables, seq_len)
    mixed, grad_q, rim_q = query_products(feats, conv_tok.reshape(width, local_len), cotangent)
    grad = query_gradient(grad_q, shifted(rim_q, EVERYONE, -1), short_filter)
    filter_grad, mixed, grad, back_tok = lax.optimization_barrier((filter_grad, mixed, grad, back_tok))

    grad_kv, rim_kv = key_value_products(feats, back_tok.reshape(width, local_len))
    grad = key_value_gradient(grad, grad_kv, shifted(rim_kv, EVERYONE, -1), short_filter)
    return (mixed, grad, filter_grad)


def solution(mesh):
    placed = (P(None, EVERYONE), P(), P(EVERYONE, None), P(None, EVERYONE))
    return jax.shard_map(
        shards,
        mesh=mesh,
        in_specs=placed,
        out_specs=(P(None, EVERYONE), P(None, EVERYONE), P(EVERYONE, None)),
        check_vma=False,
    )
```

```python
import math

import jax
import jax.numpy as jnp
import numpy as np
from jax import lax
from jax.experimental import pallas as pl
from jax.experimental.pallas import tpu as pltpu
from jax.sharding import PartitionSpec as P

CPG = 4
TAPS = 7
PAIRS = CPG // 2
EVERYONE = ("dp", "ctx")
VMEM_LIMIT = 20 * 1024 * 1024


def shifted(value, axis, steps):
    count = lax.axis_size(axis)
    first, last = (max(0, -steps), min(count, count - steps))
    return lax.ppermute(value, axis, [(source, source + steps) for source in range(first, last)])


def sizes_of(seq_len):
    padded = 2 * seq_len
    inner = max(d for d in range(1, seq_len + 1) if seq_len % d == 0 and d * d <= padded)
    return padded, inner, padded // inner


def table(count_out, count_in, period):
    turns = np.arange(count_out, dtype=np.int64)[:, None] * np.arange(count_in, dtype=np.int64)
    angle = (turns % period).astype(np.float64) * (2.0 * math.pi / period)
    return np.cos(angle), np.sin(angle)


def make_tables(seq_len, sources):
    padded, inner, outer = sizes_of(seq_len)
    half = outer // 2
    fold = half // sources
    order = np.arange(half).reshape(sources, fold).T.reshape(-1)
    cos_o, sin_o = table(outer, half, outer)
    cos_i, sin_i = table(inner, inner, inner)
    cos_p, sin_p = cos_o[:, order], sin_o[:, order]
    narrow = lambda blocks: jnp.asarray(np.block(blocks).astype(np.float32)).astype(jnp.bfloat16)
    twist = [jnp.asarray(t.astype(np.float32)) for t in table(outer, inner, padded)]
    return {
        "first": narrow([[cos_p, sin_p], [-sin_p, cos_p]]),
        "second": narrow([[cos_i, -sin_i], [sin_i, cos_i]]),
        "third": narrow([[cos_i, sin_i], [-sin_i, cos_i]]),
        "fourth": narrow([[cos_p.T, -sin_p.T], [sin_p.T, cos_p.T]]),
        "first_real": narrow([[cos_o], [-sin_o]]),
        "fourth_real": narrow([[cos_o.T, -sin_o.T]]),
        "twist_re": twist[0],
        "twist_im": twist[1],
    }


LANES = 128


def spread(tall, count, stride, first, height, width):
    tiles = [tall[pl.ds(t * height + first, count, stride=stride), :] for t in range(width[0] // LANES, width[1] // LANES)]
    return tiles[0] if len(tiles) == 1 else jnp.concatenate(tiles, axis=1)


def put_spread(tall, values, stride, first, height, width):
    for i, t in enumerate(range(width[0] // LANES, width[1] // LANES)):
        tall[pl.ds(t * height + first, values.shape[0], stride=stride), :] = values[:, i * LANES : (i + 1) * LANES]


def dot(left, right):
    return jnp.dot(left, right, preferred_element_type=jnp.float32)


def transform_filters(long_filter, tables, seq_len):
    padded, inner, outer = sizes_of(seq_len)
    half = outer // 2
    groups = long_filter.shape[0]
    scale = seq_len ** -0.5

    def kernel(x_ref, first_ref, second_ref, tr_ref, ti_ref, out_ref, tall):
        height = half * groups
        for b in range(half):
            for t in range(inner // LANES):
                at = t * height + b * groups
                lanes = slice(b * inner + t * LANES, b * inner + (t + 1) * LANES)
                tall[at : at + groups, :] = x_ref[:, lanes].astype(jnp.float32)
        for g in range(groups):
            x = spread(tall, half, groups, g, height, (0, inner)).astype(jnp.bfloat16)
            f = dot(first_ref[...], x)
            f_re, f_im = f[:outer], f[outer:]
            g_re = (f_re * tr_ref[...] + f_im * ti_ref[...]).astype(jnp.bfloat16)
            g_im = (f_im * tr_ref[...] - f_re * ti_ref[...]).astype(jnp.bfloat16)
            spec = dot(g_re, second_ref[:inner]) + dot(g_im, second_ref[inner:])
            out_ref[g * outer : (g + 1) * outer, :] = spec * scale

    return pl.pallas_call(
        kernel,
        name="filter_dft",
        out_shape=jax.ShapeDtypeStruct((groups * outer, 2 * inner), jnp.float32),
        scratch_shapes=[pltpu.VMEM((half * groups * inner // LANES, LANES), jnp.float32)],
        compiler_params=pltpu.CompilerParams(vmem_limit_bytes=VMEM_LIMIT),
        cost_estimate=pl.CostEstimate(flops=200_000_000, bytes_accessed=2_000_000, transcendentals=0),
    )(long_filter, tables["first_real"], tables["second"], tables["twist_re"], tables["twist_im"])


def filtered(arrived, channels, first_row, filters, tables, seq_len, other=None, edges=False):
    padded, inner, outer = sizes_of(seq_len)
    half = outer // 2
    sources, _, local = arrived.shape
    fold = local // inner
    groups = channels // CPG
    backward = other is not None

    def kernel(*refs):
        if backward:
            (x_ref, f_ref, k_ref, first_ref, second_ref, third_ref, fourth_ref, tr_ref, ti_ref,
             y_ref, cross_ref, tall, wide, stage, turn) = refs
        else:
            (x_ref, f_ref, first_ref, second_ref, third_ref, fourth_ref, tr_ref, ti_ref,
             y_ref, z_ref, tall, wide, stage, turn) = refs
        height = sources * channels
        for t in range(local // LANES):
            block = x_ref[:, first_row : first_row + channels, t * LANES : (t + 1) * LANES].astype(jnp.float32)
            tall[t * height : (t + 1) * height, :] = block.reshape(height, LANES)
        for c in range(channels):
            pair, part = divmod(c, 2)
            for h in range(fold):
                rows = spread(tall, sources, channels, c, height, (h * inner, (h + 1) * inner))
                at = part * half + h * sources
                wide[at : at + sources, pair * inner : (pair + 1) * inner] = rows.astype(jnp.bfloat16)
        for g in range(groups):
            span = PAIRS * inner
            f = dot(first_ref[...], wide[:, g * span : (g + 1) * span])
            for p in range(PAIRS):
                f_re = f[:outer, p * inner : (p + 1) * inner]
                f_im = f[outer:, p * inner : (p + 1) * inner]
                at = (g * PAIRS + p) * outer
                stage[at : at + outer, :inner] = (f_re * tr_ref[...] + f_im * ti_ref[...]).astype(jnp.bfloat16)
                stage[at : at + outer, inner:] = (f_im * tr_ref[...] - f_re * ti_ref[...]).astype(jnp.bfloat16)
        for g in range(groups):
            s_re = f_ref[g * outer : (g + 1) * outer, :inner]
            s_im = f_ref[g * outer : (g + 1) * outer, inner:]
            cross_re = cross_im = None
            for p in range(PAIRS):
                at = (g * PAIRS + p) * outer
                z = dot(stage[at : at + outer, :], second_ref[...])
                z_re, z_im = z[:, :inner], z[:, inner:]
                if backward:
                    k_re = k_ref[at : at + outer, :inner].astype(jnp.float32)
                    k_im = k_ref[at : at + outer, inner:].astype(jnp.float32)
                    part_re = k_re * z_re + k_im * z_im
                    part_im = k_re * z_im - k_im * z_re
                    cross_re = part_re if cross_re is None else cross_re + part_re
                    cross_im = part_im if cross_im is None else cross_im + part_im
                    o_re = s_re * z_re + s_im * z_im
                    o_im = s_re * z_im - s_im * z_re
                else:
                    z_ref[at : at + outer, :] = z
                    o_re = s_re * z_re - s_im * z_im
                    o_im = s_re * z_im + s_im * z_re
                stage[at : at + outer, :inner] = o_re.astype(jnp.bfloat16)
                stage[at : at + outer, inner:] = o_im.astype(jnp.bfloat16)
            if backward:
                cross_ref[g * outer : (g + 1) * outer, :inner] = cross_re.astype(jnp.bfloat16)
                cross_ref[g * outer : (g + 1) * outer, inner:] = cross_im.astype(jnp.bfloat16)
        for pair in range(groups * PAIRS):
            at = pair * outer
            h = dot(stage[at : at + outer, :], third_ref[...])
            h_re, h_im = h[:, :inner], h[:, inner:]
            lanes = slice(pair * inner, (pair + 1) * inner)
            turn[:outer, lanes] = (h_re * tr_ref[...] - h_im * ti_ref[...]).astype(jnp.bfloat16)
            turn[outer:, lanes] = (h_im * tr_ref[...] + h_re * ti_ref[...]).astype(jnp.bfloat16)
        for g in range(groups):
            span = PAIRS * inner
            y = dot(fourth_ref[...], turn[:, g * span : (g + 1) * span]) * (1.0 / padded)
            for p in range(PAIRS):
                for part in range(2):
                    c = (g * PAIRS + p) * 2 + part
                    for h in range(fold):
                        at = part * half + h * sources
                        rows = y[at : at + sources, p * inner : (p + 1) * inner]
                        put_spread(tall, rows, channels, c, height, (h * inner, (h + 1) * inner))
        for t in range(local // LANES):
            block = tall[t * height : (t + 1) * height, :].reshape(sources, channels, LANES).astype(jnp.bfloat16)
            if edges:
                y_ref[:, t * channels : (t + 1) * channels, :] = block
            else:
                y_ref[:, :, t * LANES : (t + 1) * LANES] = block
        if edges:
            spot = lax.broadcasted_iota(jnp.int32, (RIM, LANES), 0)
            lane = lax.broadcasted_iota(jnp.int32, (RIM, LANES), 1)
            pick = jnp.where(spot == lane, 1.0, 0.0).astype(jnp.bfloat16)
            first = tall[:height, :].astype(jnp.bfloat16)
            rim = lax.dot_general(pick, first, (((1,), (1,)), ((), ())), preferred_element_type=jnp.float32)
            at = local // LANES * channels
            for d in range(sources):
                tile, lanes = divmod((d + 1) % sources * channels, LANES)
                piece = rim[:, tile * LANES : (tile + 1) * LANES]
                if lanes:
                    piece = pltpu.roll(piece, LANES - lanes, 1)
                if d == sources - 1:
                    piece = jnp.zeros_like(piece)
                y_ref[d, at : at + RIM, :] = piece.astype(jnp.bfloat16)

    pairs = groups * PAIRS
    sent = (local // LANES * channels + RIM, LANES) if edges else (channels, local)
    if backward:
        extra = jax.ShapeDtypeStruct((groups * outer, 2 * inner), jnp.bfloat16)
    else:
        extra = jax.ShapeDtypeStruct((pairs * outer, 2 * inner), jnp.float32)
    operands = [arrived, filters] + ([other] if backward else [])
    operands += [tables[n] for n in ("first", "second", "third", "fourth", "twist_re", "twist_im")]
    return pl.pallas_call(
        kernel,
        name="correlate" if backward else "convolve",
        out_shape=(narrow_shape(sources, *sent), extra),
        scratch_shapes=[
            pltpu.VMEM((sources * channels * local // LANES, LANES), jnp.float32),
            pltpu.VMEM((outer, pairs * inner), jnp.bfloat16),
            pltpu.VMEM((pairs * outer, 2 * inner), jnp.bfloat16),
            pltpu.VMEM((2 * outer, pairs * inner), jnp.bfloat16),
        ],
        compiler_params=pltpu.CompilerParams(vmem_limit_bytes=VMEM_LIMIT),
        cost_estimate=pl.CostEstimate(flops=2_000_000_000, bytes_accessed=5_000_000, transcendentals=0),
    )(*operands)


def filter_gradient(cross, tables, seq_len):
    padded, inner, outer = sizes_of(seq_len)
    half = outer // 2
    groups = cross.shape[0] // outer
    scale = seq_len ** -0.5 / padded

    def kernel(s_ref, third_ref, fourth_ref, tr_ref, ti_ref, out_ref, tall, turn):
        for g in range(groups):
            h = dot(s_ref[g * outer : (g + 1) * outer, :], third_ref[...])
            h_re, h_im = h[:, :inner], h[:, inner:]
            turn[:outer, g * inner : (g + 1) * inner] = (h_re * tr_ref[...] - h_im * ti_ref[...]).astype(jnp.bfloat16)
            turn[outer:, g * inner : (g + 1) * inner] = (h_im * tr_ref[...] + h_re * ti_ref[...]).astype(jnp.bfloat16)
        for g in range(groups):
            y = dot(fourth_ref[...], turn[:, g * inner : (g + 1) * inner]) * scale
            put_spread(tall, y, groups, g, half * groups, (0, inner))
        for b in range(half):
            for t in range(inner // LANES):
                at = (t * half + b) * groups
                out_ref[:, b * inner + t * LANES : b * inner + (t + 1) * LANES] = tall[at : at + groups, :]

    return pl.pallas_call(
        kernel,
        name="filter_gradient",
        out_shape=jax.ShapeDtypeStruct((groups, seq_len), jnp.float32),
        scratch_shapes=[
            pltpu.VMEM((half * groups * inner // LANES, LANES), jnp.float32),
            pltpu.VMEM((2 * outer, groups * inner), jnp.bfloat16),
        ],
        compiler_params=pltpu.CompilerParams(vmem_limit_bytes=VMEM_LIMIT),
        cost_estimate=pl.CostEstimate(flops=200_000_000, bytes_accessed=2_000_000, transcendentals=0),
    )(cross, tables["third"], tables["fourth_real"], tables["twist_re"], tables["twist_im"])


RIM = 8
JOINED = True


def seven_taps(tall, value, rim, weights, forward):
    count = value.shape[0]
    if forward:
        tall[:RIM, :] = rim
        tall[RIM : RIM + count, :] = value
    else:
        tall[:count, :] = value
        tall[count : count + RIM, :] = rim
    total = value * weights[:1]
    for lag in range(1, TAPS):
        first = RIM - lag if forward else lag
        total = total + tall[first : first + count, :] * weights[lag : lag + 1]
    return total


def lane_block(i, offset=0):
    return pl.ds(pl.multiple_of(i * LANES + offset, LANES), LANES)


def whole_call(kernel, name, out_shape, operands, scratch=(), flops=10_000_000, **kwargs):
    return pl.pallas_call(
        kernel,
        name=name,
        out_shape=out_shape,
        scratch_shapes=list(scratch),
        compiler_params=pltpu.CompilerParams(vmem_limit_bytes=VMEM_LIMIT),
        cost_estimate=pl.CostEstimate(flops=flops, bytes_accessed=4_000_000, transcendentals=0),
        **kwargs,
    )(*operands)


def narrow_shape(*shape):
    return jax.ShapeDtypeStruct(shape, jnp.bfloat16)


def features_of(turned, rim, short_filter, cotangent, owned, joined):
    local, width = cotangent.shape
    near = LANES // owned

    def kernel(x_ref, rim_ref, w_ref, og_ref, f_ref, edge_ref, *rest):
        tall = rest[-1]

        @pl.loop(0, width // LANES)
        def _(i):
            made = []
            for part in range(3):
                lanes = lane_block(i, part * width)
                total = seven_taps(
                    tall.at[part],
                    x_ref[:, lanes].astype(jnp.float32),
                    rim_ref[:, lanes].astype(jnp.float32),
                    w_ref[:, lanes].astype(jnp.float32),
                    True,
                ).astype(jnp.bfloat16)
                f_ref[:, lanes] = total
                edge_ref[:, lanes] = total[:RIM]
                made.append(total.astype(jnp.float32))
            rows = lane_block(i)
            kv = (made[1] * made[2]).astype(jnp.bfloat16).T
            og = og_ref[:, rows].astype(jnp.float32)
            dconv = (og * made[0]).astype(jnp.bfloat16).T
            if joined:
                to = pl.ds(i * near, near)
                rest[0][to, :owned, :] = kv.reshape(near, owned, local)
                rest[0][to, owned:, :] = dconv.reshape(near, owned, local)
            else:
                rest[0][rows, :] = kv
                rest[1][rows, :] = dconv

    if joined:
        products = (narrow_shape(width // owned, 2 * owned, local),)
    else:
        products = (narrow_shape(width, local), narrow_shape(width, local))
    return whole_call(
        kernel,
        "features",
        (narrow_shape(local, 3 * width), narrow_shape(RIM, 3 * width)) + products,
        (turned, rim, short_filter, cotangent),
        [pltpu.VMEM((3, local + RIM, LANES), jnp.float32)],
    )


def query_products(feats, conv, cotangent):
    width, local = conv.shape

    def kernel(f_ref, conv_ref, og_ref, mixed_ref, dq_ref, rim_ref):
        @pl.loop(0, width // LANES)
        def _(i):
            lanes = lane_block(i)
            here = conv_ref[lanes, :].T.astype(jnp.float32)
            mixed_ref[lanes, :] = (f_ref[:, lanes].astype(jnp.float32) * here).astype(jnp.bfloat16).T
            dq = (og_ref[:, lanes].astype(jnp.float32) * here).astype(jnp.bfloat16)
            dq_ref[:, lanes] = dq
            rim_ref[:, lanes] = dq[:RIM]

    return whole_call(
        kernel,
        "query_products",
        (narrow_shape(width, local), narrow_shape(local, width), narrow_shape(RIM, width)),
        (feats, conv, cotangent),
    )


def key_value_products(feats, back):
    width, local = back.shape

    def kernel(f_ref, back_ref, d_ref, rim_ref):
        @pl.loop(0, width // LANES)
        def _(i):
            here = back_ref[lane_block(i), :].T.astype(jnp.float32)
            for part in range(2):
                other = f_ref[:, lane_block(i, (2 - part) * width)].astype(jnp.float32)
                grad = (here * other).astype(jnp.bfloat16)
                d_ref[:, lane_block(i, part * width)] = grad
                rim_ref[:, lane_block(i, part * width)] = grad[:RIM]

    return whole_call(
        kernel,
        "key_value_products",
        (narrow_shape(local, 2 * width), narrow_shape(RIM, 2 * width)),
        (feats, back),
    )


def query_gradient(grad, rim, short_filter):
    local, width = grad.shape
    steps = width // GRAD_ROWS

    def kernel(d_ref, rim_ref, w_ref, out_ref, tall):
        gradient_block(d_ref, rim_ref, w_ref, out_ref, tall)

    return gradient_call(kernel, "query_gradient", (), grad, rim, short_filter, 1, 0)


def key_value_gradient(whole, grad, rim, short_filter):
    def kernel(_, d_ref, rim_ref, w_ref, out_ref, tall):
        gradient_block(d_ref, rim_ref, w_ref, out_ref, tall)

    return gradient_call(kernel, "key_value_gradient", (whole,), grad, rim, short_filter, 2, 1)


GRAD_ROWS = 512


def gradient_block(d_ref, rim_ref, w_ref, out_ref, tall):
    for c in range(GRAD_ROWS // LANES):
        lanes = slice(c * LANES, (c + 1) * LANES)
        total = seven_taps(
            tall.at[c],
            d_ref[:, lanes].astype(jnp.float32),
            rim_ref[:, lanes].astype(jnp.float32),
            w_ref[:, lanes].astype(jnp.float32),
            False,
        )
        out_ref[lanes, :] = total.astype(jnp.bfloat16).T


def gradient_call(kernel, name, whole, grad, rim, short_filter, parts, first):
    local, lanes = grad.shape
    width = lanes // parts
    steps = width // GRAD_ROWS
    return pl.pallas_call(
        kernel,
        name=name,
        grid=(parts * steps,),
        in_specs=[pl.BlockSpec(memory_space=pl.ANY)] * len(whole)
        + [
            pl.BlockSpec((local, GRAD_ROWS), lambda i: (0, i)),
            pl.BlockSpec((RIM, GRAD_ROWS), lambda i: (0, i)),
            pl.BlockSpec((TAPS, GRAD_ROWS), lambda i: (0, first * steps + i)),
        ],
        out_specs=pl.BlockSpec((GRAD_ROWS, local), lambda i: (first * steps + i, 0)),
        out_shape=narrow_shape(3 * width, local),
        scratch_shapes=[pltpu.VMEM((GRAD_ROWS // LANES, local + RIM, LANES), jnp.float32)],
        input_output_aliases={0: 0} if whole else {},
        cost_estimate=pl.CostEstimate(flops=20_000_000, bytes_accessed=4_000_000, transcendentals=0),
    )(*whole, grad, rim, short_filter)


def key_value_side(whole, feats, edges, back, short_filter, owned):
    local = feats.shape[0]
    width = feats.shape[1] // 3
    near = LANES // owned
    blocks = width // LANES

    def kernel(_, f_ref, edge_ref, back_ref, w_ref, out_ref, tall, made, sent):
        lane = lax.broadcasted_iota(jnp.int32, (RIM, LANES), 1)

        def copy(at):
            rows = pl.ds(pl.multiple_of(width + at * LANES, LANES), LANES)
            return pltpu.make_async_copy(made.at[at], out_ref.at[rows, :], sent.at[at])

        @pl.loop(0, blocks)
        def _(i):
            held = pl.ds(i * near, near)
            tiles = [
                back_ref[held, t * owned : (t + 1) * owned, :].reshape(LANES, LANES).T for t in range(local // LANES)
            ]
            here = jnp.concatenate(tiles, axis=0).astype(jnp.float32)
            at = local // LANES * owned
            rim = back_ref[i * near, at : at + RIM, :].astype(jnp.float32)
            for k in range(1, near):
                piece = back_ref[i * near + k, at : at + RIM, :].astype(jnp.float32)
                rim = jnp.where(lane >= k * owned, pltpu.roll(piece, k * owned, 1), rim)
            for part in range(2):
                lanes = lane_block(i, (2 - part) * width)
                grad = (here * f_ref[:, lanes].astype(jnp.float32)).astype(jnp.bfloat16)
                edge = (rim * edge_ref[:, lanes].astype(jnp.float32)).astype(jnp.bfloat16)
                total = seven_taps(
                    tall.at[part],
                    grad.astype(jnp.float32),
                    edge.astype(jnp.float32),
                    w_ref[:, lane_block(i, (1 + part) * width)].astype(jnp.float32),
                    False,
                )
                made[part * blocks + i] = total.astype(jnp.bfloat16).T
                copy(part * blocks + i).start()

        @pl.loop(0, 2 * blocks)
        def _(at):
            copy(at).wait()

    vmem = pl.BlockSpec(memory_space=pltpu.VMEM)
    return whole_call(
        kernel,
        "key_value_side",
        narrow_shape(3 * width, local),
        (whole, feats, edges, back, short_filter),
        [
            pltpu.VMEM((2, local + RIM, LANES), jnp.float32),
            pltpu.VMEM((2 * blocks, LANES, local), jnp.bfloat16),
            pltpu.SemaphoreType.DMA((2 * blocks,)),
        ],
        in_specs=[pl.BlockSpec(memory_space=pl.ANY), vmem, vmem, vmem, vmem],
        out_specs=pl.BlockSpec(memory_space=pl.ANY),
        input_output_aliases={0: 0},
    )


def shards(projections, short_filter, long_filter, out_grad):
    width, local_len = out_grad.shape
    devices = lax.axis_size(EVERYONE)
    seq_len = local_len * devices
    owned = width // devices
    tables = make_tables(seq_len, devices)
    roomy = owned % 16 == 0 and LANES % owned == 0

    turned = projections.T
    cotangent = out_grad.T
    rim = shifted(turned[local_len - RIM :], EVERYONE, 1)
    feats, edges, *products = features_of(turned, rim, short_filter, cotangent, owned, JOINED and roomy)

    def exchange(pieces):
        return lax.all_to_all(pieces, EVERYONE, split_axis=0, concat_axis=0, tiled=True)

    filters = transform_filters(long_filter, tables, seq_len)
    if JOINED and roomy:
        prod_chan = grad_chan = exchange(products[0])
    else:
        prod_chan = exchange(products[0].reshape(devices, owned, local_len))
        conv_grad, prod_chan = lax.optimization_barrier((products[1], prod_chan))
        grad_chan = exchange(conv_grad.reshape(devices, owned, local_len))
    first_row = owned if JOINED and roomy else 0
    conv_chan, prod_spec = filtered(prod_chan, owned, 0, filters, tables, seq_len)
    conv_chan, grad_chan = lax.optimization_barrier((conv_chan, grad_chan))
    conv_tok = exchange(conv_chan)
    back_chan, cross = filtered(grad_chan, owned, first_row, filters, tables, seq_len, prod_spec, roomy)
    back_chan, conv_tok = lax.optimization_barrier((back_chan, conv_tok))
    back_tok = exchange(back_chan)

    filter_grad = filter_gradient(cross, tables, seq_len)
    mixed, grad_q, rim_q = query_products(feats, conv_tok.reshape(width, local_len), cotangent)
    grad = query_gradient(grad_q, shifted(rim_q, EVERYONE, -1), short_filter)
    if roomy:
        edges = shifted(edges, EVERYONE, -1)
        filter_grad, mixed, grad, edges, back_tok = lax.optimization_barrier(
            (filter_grad, mixed, grad, edges, back_tok)
        )
        grad = key_value_side(grad, feats, edges, back_tok, short_filter, owned)
    else:
        filter_grad, mixed, grad, back_tok = lax.optimization_barrier((filter_grad, mixed, grad, back_tok))
        grad_kv, rim_kv = key_value_products(feats, back_tok.reshape(width, local_len))
        grad = key_value_gradient(grad, grad_kv, shifted(rim_kv, EVERYONE, -1), short_filter)
    return (mixed, grad, filter_grad)


def solution(mesh):
    placed = (P(None, EVERYONE), P(), P(EVERYONE, None), P(None, EVERYONE))
    return jax.shard_map(
        shards,
        mesh=mesh,
        in_specs=placed,
        out_specs=(P(None, EVERYONE), P(None, EVERYONE), P(EVERYONE, None)),
        check_vma=False,
    )
```

```python
import math

import jax
import jax.numpy as jnp
import numpy as np
from jax import lax
from jax.experimental import pallas as pl
from jax.experimental.pallas import tpu as pltpu
from jax.sharding import PartitionSpec as P

CPG = 4
TAPS = 7
PAIRS = CPG // 2
EVERYONE = ("dp", "ctx")
VMEM_LIMIT = 24 * 1024 * 1024


def shifted(value, axis, steps):
    count = lax.axis_size(axis)
    first, last = (max(0, -steps), min(count, count - steps))
    return lax.ppermute(value, axis, [(source, source + steps) for source in range(first, last)])


def sizes_of(seq_len):
    padded = 2 * seq_len
    inner = max(d for d in range(1, seq_len + 1) if seq_len % d == 0 and d * d <= padded)
    return padded, inner, padded // inner


def table(count_out, count_in, period):
    turns = np.arange(count_out, dtype=np.int64)[:, None] * np.arange(count_in, dtype=np.int64)
    angle = (turns % period).astype(np.float64) * (2.0 * math.pi / period)
    return np.cos(angle), np.sin(angle)


def make_tables(seq_len, sources):
    padded, inner, outer = sizes_of(seq_len)
    half = outer // 2
    fold = half // sources
    order = np.arange(half).reshape(sources, fold).T.reshape(-1)
    cos_o, sin_o = table(outer, half, outer)
    cos_i, sin_i = table(inner, inner, inner)
    cos_p, sin_p = cos_o[:, order], sin_o[:, order]
    narrow = lambda blocks: jnp.asarray(np.block(blocks).astype(np.float32)).astype(jnp.bfloat16)
    twist = [jnp.asarray(t.astype(np.float32)) for t in table(outer, inner, padded)]
    return {
        "first": narrow([[cos_p, sin_p], [-sin_p, cos_p]]),
        "second": narrow([[cos_i, -sin_i], [sin_i, cos_i]]),
        "third": narrow([[cos_i, sin_i], [-sin_i, cos_i]]),
        "fourth": narrow([[cos_p.T, -sin_p.T], [sin_p.T, cos_p.T]]),
        "first_real": narrow([[cos_o], [-sin_o]]),
        "fourth_real": narrow([[cos_o.T, -sin_o.T]]),
        "twist_re": twist[0],
        "twist_im": twist[1],
    }


LANES = 128


def spread(tall, count, stride, first, height, width):
    tiles = [tall[pl.ds(t * height + first, count, stride=stride), :] for t in range(width[0] // LANES, width[1] // LANES)]
    return tiles[0] if len(tiles) == 1 else jnp.concatenate(tiles, axis=1)


def put_spread(tall, values, stride, first, height, width):
    for i, t in enumerate(range(width[0] // LANES, width[1] // LANES)):
        tall[pl.ds(t * height + first, values.shape[0], stride=stride), :] = values[:, i * LANES : (i + 1) * LANES]


def dot(left, right):
    return jnp.dot(left, right, preferred_element_type=jnp.float32)


def transform_filters(long_filter, tables, seq_len):
    padded, inner, outer = sizes_of(seq_len)
    half = outer // 2
    groups = long_filter.shape[0]
    scale = seq_len ** -0.5

    def kernel(x_ref, first_ref, second_ref, tr_ref, ti_ref, out_ref, tall):
        height = half * groups
        for b in range(half):
            for t in range(inner // LANES):
                at = t * height + b * groups
                lanes = slice(b * inner + t * LANES, b * inner + (t + 1) * LANES)
                tall[at : at + groups, :] = x_ref[:, lanes].astype(jnp.float32)
        for g in range(groups):
            x = spread(tall, half, groups, g, height, (0, inner)).astype(jnp.bfloat16)
            f = dot(first_ref[...], x)
            f_re, f_im = f[:outer], f[outer:]
            g_re = (f_re * tr_ref[...] + f_im * ti_ref[...]).astype(jnp.bfloat16)
            g_im = (f_im * tr_ref[...] - f_re * ti_ref[...]).astype(jnp.bfloat16)
            spec = dot(g_re, second_ref[:inner]) + dot(g_im, second_ref[inner:])
            out_ref[g * outer : (g + 1) * outer, :] = spec * scale

    return pl.pallas_call(
        kernel,
        name="filter_dft",
        out_shape=jax.ShapeDtypeStruct((groups * outer, 2 * inner), jnp.float32),
        scratch_shapes=[pltpu.VMEM((half * groups * inner // LANES, LANES), jnp.float32)],
        compiler_params=pltpu.CompilerParams(vmem_limit_bytes=VMEM_LIMIT),
        cost_estimate=pl.CostEstimate(flops=200_000_000, bytes_accessed=2_000_000, transcendentals=0),
    )(long_filter, tables["first_real"], tables["second"], tables["twist_re"], tables["twist_im"])


def filtered(arrived, filters, tables, seq_len, other=None):
    padded, inner, outer = sizes_of(seq_len)
    half = outer // 2
    sources, channels, local = arrived.shape
    fold = local // inner
    groups = channels // CPG
    backward = other is not None

    def kernel(*refs):
        if backward:
            (x_ref, f_ref, k_ref, first_ref, second_ref, third_ref, fourth_ref, tr_ref, ti_ref,
             y_ref, cross_ref, tall, wide, stage, turn) = refs
        else:
            (x_ref, f_ref, first_ref, second_ref, third_ref, fourth_ref, tr_ref, ti_ref,
             y_ref, z_ref, tall, wide, stage, turn) = refs
        height = sources * channels
        for t in range(local // LANES):
            block = x_ref[:, :, t * LANES : (t + 1) * LANES].astype(jnp.float32)
            tall[t * height : (t + 1) * height, :] = block.reshape(height, LANES)
        for c in range(channels):
            pair, part = divmod(c, 2)
            for h in range(fold):
                rows = spread(tall, sources, channels, c, height, (h * inner, (h + 1) * inner))
                at = part * half + h * sources
                wide[at : at + sources, pair * inner : (pair + 1) * inner] = rows.astype(jnp.bfloat16)
        for g in range(groups):
            span = PAIRS * inner
            f = dot(first_ref[...], wide[:, g * span : (g + 1) * span])
            for p in range(PAIRS):
                f_re = f[:outer, p * inner : (p + 1) * inner]
                f_im = f[outer:, p * inner : (p + 1) * inner]
                at = (g * PAIRS + p) * outer
                stage[at : at + outer, :inner] = (f_re * tr_ref[...] + f_im * ti_ref[...]).astype(jnp.bfloat16)
                stage[at : at + outer, inner:] = (f_im * tr_ref[...] - f_re * ti_ref[...]).astype(jnp.bfloat16)
        for g in range(groups):
            s_re = f_ref[g * outer : (g + 1) * outer, :inner]
            s_im = f_ref[g * outer : (g + 1) * outer, inner:]
            cross_re = cross_im = None
            for p in range(PAIRS):
                at = (g * PAIRS + p) * outer
                z = dot(stage[at : at + outer, :], second_ref[...])
                z_re, z_im = z[:, :inner], z[:, inner:]
                if backward:
                    k_re = k_ref[at : at + outer, :inner].astype(jnp.float32)
                    k_im = k_ref[at : at + outer, inner:].astype(jnp.float32)
                    part_re = k_re * z_re + k_im * z_im
                    part_im = k_re * z_im - k_im * z_re
                    cross_re = part_re if cross_re is None else cross_re + part_re
                    cross_im = part_im if cross_im is None else cross_im + part_im
                    o_re = s_re * z_re + s_im * z_im
                    o_im = s_re * z_im - s_im * z_re
                else:
                    z_ref[at : at + outer, :] = z
                    o_re = s_re * z_re - s_im * z_im
                    o_im = s_re * z_im + s_im * z_re
                stage[at : at + outer, :inner] = o_re.astype(jnp.bfloat16)
                stage[at : at + outer, inner:] = o_im.astype(jnp.bfloat16)
            if backward:
                cross_ref[g * outer : (g + 1) * outer, :inner] = cross_re.astype(jnp.bfloat16)
                cross_ref[g * outer : (g + 1) * outer, inner:] = cross_im.astype(jnp.bfloat16)
        for pair in range(groups * PAIRS):
            at = pair * outer
            h = dot(stage[at : at + outer, :], third_ref[...])
            h_re, h_im = h[:, :inner], h[:, inner:]
            lanes = slice(pair * inner, (pair + 1) * inner)
            turn[:outer, lanes] = (h_re * tr_ref[...] - h_im * ti_ref[...]).astype(jnp.bfloat16)
            turn[outer:, lanes] = (h_im * tr_ref[...] + h_re * ti_ref[...]).astype(jnp.bfloat16)
        for g in range(groups):
            span = PAIRS * inner
            y = dot(fourth_ref[...], turn[:, g * span : (g + 1) * span]) * (1.0 / padded)
            for p in range(PAIRS):
                for part in range(2):
                    c = (g * PAIRS + p) * 2 + part
                    for h in range(fold):
                        at = part * half + h * sources
                        rows = y[at : at + sources, p * inner : (p + 1) * inner]
                        put_spread(tall, rows, channels, c, height, (h * inner, (h + 1) * inner))
        for t in range(local // LANES):
            block = tall[t * height : (t + 1) * height, :].reshape(sources, channels, LANES)
            y_ref[:, :, t * LANES : (t + 1) * LANES] = block.astype(jnp.bfloat16)

    pairs = groups * PAIRS
    if backward:
        extra = jax.ShapeDtypeStruct((groups * outer, 2 * inner), jnp.bfloat16)
    else:
        extra = jax.ShapeDtypeStruct((pairs * outer, 2 * inner), jnp.float32)
    operands = [arrived, filters] + ([other] if backward else [])
    operands += [tables[n] for n in ("first", "second", "third", "fourth", "twist_re", "twist_im")]
    return pl.pallas_call(
        kernel,
        name="correlate" if backward else "convolve",
        out_shape=(jax.ShapeDtypeStruct(arrived.shape, jnp.bfloat16), extra),
        scratch_shapes=[
            pltpu.VMEM((sources * channels * local // LANES, LANES), jnp.float32),
            pltpu.VMEM((outer, pairs * inner), jnp.bfloat16),
            pltpu.VMEM((pairs * outer, 2 * inner), jnp.bfloat16),
            pltpu.VMEM((2 * outer, pairs * inner), jnp.bfloat16),
        ],
        compiler_params=pltpu.CompilerParams(vmem_limit_bytes=VMEM_LIMIT),
        cost_estimate=pl.CostEstimate(flops=2_000_000_000, bytes_accessed=5_000_000, transcendentals=0),
    )(*operands)


def filter_gradient(cross, tables, seq_len):
    padded, inner, outer = sizes_of(seq_len)
    half = outer // 2
    groups = cross.shape[0] // outer
    scale = seq_len ** -0.5 / padded

    def kernel(s_ref, third_ref, fourth_ref, tr_ref, ti_ref, out_ref, tall, turn):
        for g in range(groups):
            h = dot(s_ref[g * outer : (g + 1) * outer, :], third_ref[...])
            h_re, h_im = h[:, :inner], h[:, inner:]
            turn[:outer, g * inner : (g + 1) * inner] = (h_re * tr_ref[...] - h_im * ti_ref[...]).astype(jnp.bfloat16)
            turn[outer:, g * inner : (g + 1) * inner] = (h_im * tr_ref[...] + h_re * ti_ref[...]).astype(jnp.bfloat16)
        for g in range(groups):
            y = dot(fourth_ref[...], turn[:, g * inner : (g + 1) * inner]) * scale
            put_spread(tall, y, groups, g, half * groups, (0, inner))
        for b in range(half):
            for t in range(inner // LANES):
                at = (t * half + b) * groups
                out_ref[:, b * inner + t * LANES : b * inner + (t + 1) * LANES] = tall[at : at + groups, :]

    return pl.pallas_call(
        kernel,
        name="filter_gradient",
        out_shape=jax.ShapeDtypeStruct((groups, seq_len), jnp.float32),
        scratch_shapes=[
            pltpu.VMEM((half * groups * inner // LANES, LANES), jnp.float32),
            pltpu.VMEM((2 * outer, groups * inner), jnp.bfloat16),
        ],
        compiler_params=pltpu.CompilerParams(vmem_limit_bytes=VMEM_LIMIT),
        cost_estimate=pl.CostEstimate(flops=200_000_000, bytes_accessed=2_000_000, transcendentals=0),
    )(cross, tables["third"], tables["fourth_real"], tables["twist_re"], tables["twist_im"])


RIM = 8


def seven_taps(tall, value, rim, weights, forward):
    count = value.shape[0]
    if forward:
        tall[:RIM, :] = rim
        tall[RIM : RIM + count, :] = value
    else:
        tall[:count, :] = value
        tall[count : count + RIM, :] = rim
    total = value * weights[:1]
    for lag in range(1, TAPS):
        first = RIM - lag if forward else lag
        total = total + tall[first : first + count, :] * weights[lag : lag + 1]
    return total


def lane_block(i, offset=0):
    return pl.ds(pl.multiple_of(i * LANES + offset, LANES), LANES)


def whole_call(kernel, name, out_shape, operands, scratch=(), flops=10_000_000, **kwargs):
    return pl.pallas_call(
        kernel,
        name=name,
        out_shape=out_shape,
        scratch_shapes=list(scratch),
        compiler_params=pltpu.CompilerParams(vmem_limit_bytes=VMEM_LIMIT),
        cost_estimate=pl.CostEstimate(flops=flops, bytes_accessed=4_000_000, transcendentals=0),
        **kwargs,
    )(*operands)


def narrow_shape(*shape):
    return jax.ShapeDtypeStruct(shape, jnp.bfloat16)


def features_of(turned, rim, short_filter, cotangent):
    local, width = cotangent.shape

    def kernel(x_ref, rim_ref, w_ref, og_ref, f_ref, kv_ref, dconv_ref, tall):
        @pl.loop(0, width // LANES)
        def _(i):
            made = []
            for part in range(3):
                lanes = lane_block(i, part * width)
                total = seven_taps(
                    tall.at[part],
                    x_ref[:, lanes].astype(jnp.float32),
                    rim_ref[:, lanes].astype(jnp.float32),
                    w_ref[:, lanes].astype(jnp.float32),
                    True,
                ).astype(jnp.bfloat16)
                f_ref[:, lanes] = total
                made.append(total.astype(jnp.float32))
            rows = lane_block(i)
            kv_ref[rows, :] = (made[1] * made[2]).astype(jnp.bfloat16).T
            og = og_ref[:, rows].astype(jnp.float32)
            dconv_ref[rows, :] = (og * made[0]).astype(jnp.bfloat16).T

    return whole_call(
        kernel,
        "features",
        (narrow_shape(local, 3 * width), narrow_shape(width, local), narrow_shape(width, local)),
        (turned, rim, short_filter, cotangent),
        [pltpu.VMEM((3, local + RIM, LANES), jnp.float32)],
    )


def query_products(feats, conv, cotangent):
    width, local = conv.shape

    def kernel(f_ref, conv_ref, og_ref, mixed_ref, dq_ref, rim_ref):
        @pl.loop(0, width // LANES)
        def _(i):
            lanes = lane_block(i)
            here = conv_ref[lanes, :].T.astype(jnp.float32)
            mixed_ref[lanes, :] = (f_ref[:, lanes].astype(jnp.float32) * here).astype(jnp.bfloat16).T
            dq = (og_ref[:, lanes].astype(jnp.float32) * here).astype(jnp.bfloat16)
            dq_ref[:, lanes] = dq
            rim_ref[:, lanes] = dq[:RIM]

    return whole_call(
        kernel,
        "query_products",
        (narrow_shape(width, local), narrow_shape(local, width), narrow_shape(RIM, width)),
        (feats, conv, cotangent),
    )


def key_value_products(feats, back):
    width, local = back.shape

    def kernel(f_ref, back_ref, d_ref, rim_ref):
        @pl.loop(0, width // LANES)
        def _(i):
            here = back_ref[lane_block(i), :].T.astype(jnp.float32)
            for part in range(2):
                other = f_ref[:, lane_block(i, (2 - part) * width)].astype(jnp.float32)
                grad = (here * other).astype(jnp.bfloat16)
                d_ref[:, lane_block(i, part * width)] = grad
                rim_ref[:, lane_block(i, part * width)] = grad[:RIM]

    return whole_call(
        kernel,
        "key_value_products",
        (narrow_shape(local, 2 * width), narrow_shape(RIM, 2 * width)),
        (feats, back),
    )


def joined_features(turned, rim, short_filter, out_grad, owned):
    width, local = out_grad.shape
    near = LANES // owned
    blocks = width // LANES

    def kernel(x_ref, rim_ref, w_ref, og_ref, f_ref, msg_ref, edge_ref, tall, made, edge, sent):
        def copy(i):
            to = pl.ds(i * near, near)
            return pltpu.make_async_copy(made.at[to], msg_ref.at[to], sent.at[i])

        @pl.loop(0, blocks)
        def _(i):
            parts = []
            for part in range(3):
                lanes = lane_block(i, part * width)
                total = seven_taps(
                    tall.at[part],
                    x_ref[:, lanes].astype(jnp.float32),
                    rim_ref[:, lanes].astype(jnp.float32),
                    w_ref[:, lanes].astype(jnp.float32),
                    True,
                ).astype(jnp.bfloat16)
                f_ref[:, lanes] = total
                if part:
                    edge[:, lanes] = total[:RIM]
                parts.append(total.astype(jnp.float32))
            og = og_ref[lane_block(i), :].T
            edge[:, lane_block(i)] = og[:RIM]
            kv = (parts[1] * parts[2]).astype(jnp.bfloat16).T
            dconv = (og.astype(jnp.float32) * parts[0]).astype(jnp.bfloat16).T
            to = pl.ds(i * near, near)
            made[to, :owned, :] = kv.reshape(near, owned, local)
            made[to, owned:, :] = dconv.reshape(near, owned, local)
            copy(i).start()

        last = pltpu.make_async_copy(edge, edge_ref, sent.at[blocks])
        last.start()

        @pl.loop(0, blocks)
        def _(i):
            copy(i).wait()

        last.wait()

    vmem = pl.BlockSpec(memory_space=pltpu.VMEM)
    hbm = pl.BlockSpec(memory_space=pltpu.HBM)
    devices = width // owned
    return whole_call(
        kernel,
        "joined_features",
        (narrow_shape(local, 3 * width), narrow_shape(devices, 2 * owned, local), narrow_shape(RIM, 3 * width)),
        (turned, rim, short_filter, out_grad),
        [
            pltpu.VMEM((3, local + RIM, LANES), jnp.float32),
            pltpu.VMEM((devices, 2 * owned, local), jnp.bfloat16),
            pltpu.VMEM((RIM, 3 * width), jnp.bfloat16),
            pltpu.SemaphoreType.DMA((blocks + 1,)),
        ],
        in_specs=[vmem] * 4,
        out_specs=(vmem, hbm, hbm),
    )


def joined_filtering(arrived, filters, tables, seq_len):
    padded, inner, outer = sizes_of(seq_len)
    half = outer // 2
    sources, rows, local = arrived.shape
    channels = rows // 2
    tiles = local // LANES
    fold = local // inner
    groups = channels // CPG
    pairs = groups * PAIRS
    height = sources * channels
    chunk = sources // 4

    def kernel(x_ref, f_hbm, first_ref, second_ref, third_ref, fourth_ref, tr_ref, ti_ref,
               y_hbm, cross_ref, f_ref, y_ref, talls, wides, stages, turns, sems):
        fetch = pltpu.make_async_copy(f_hbm, f_ref, sems.at[0])
        fetch.start()
        tr, ti = tr_ref[...], ti_ref[...]
        for s in range(2):
            tall, wide, stage = talls.at[s], wides.at[s], stages.at[s]
            for t in range(tiles):
                block = x_ref[:, s * channels : (s + 1) * channels, t * LANES : (t + 1) * LANES]
                tall[t * height : (t + 1) * height, :] = block.astype(jnp.float32).reshape(height, LANES)
            for c in range(channels):
                pair, part = divmod(c, 2)
                for h in range(fold):
                    line = spread(tall, sources, channels, c, height, (h * inner, (h + 1) * inner))
                    at = part * half + h * sources
                    wide[at : at + sources, pair * inner : (pair + 1) * inner] = line.astype(jnp.bfloat16)
            for g in range(groups):
                span = PAIRS * inner
                f = dot(first_ref[...], wide[:, g * span : (g + 1) * span])
                for p in range(PAIRS):
                    f_re = f[:outer, p * inner : (p + 1) * inner]
                    f_im = f[outer:, p * inner : (p + 1) * inner]
                    at = (g * PAIRS + p) * outer
                    stage[at : at + outer, :inner] = (f_re * tr + f_im * ti).astype(jnp.bfloat16)
                    stage[at : at + outer, inner:] = (f_im * tr - f_re * ti).astype(jnp.bfloat16)
        fetch.wait()
        for g in range(groups):
            s_re = f_ref[g * outer : (g + 1) * outer, :inner]
            s_im = f_ref[g * outer : (g + 1) * outer, inner:]
            cross_re = cross_im = 0.0
            for p in range(PAIRS):
                at = (g * PAIRS + p) * outer
                k = dot(stages[0, at : at + outer, :], second_ref[...])
                d = dot(stages[1, at : at + outer, :], second_ref[...])
                k_re, k_im = k[:, :inner], k[:, inner:]
                d_re, d_im = d[:, :inner], d[:, inner:]
                cross_re = cross_re + (k_re * d_re + k_im * d_im)
                cross_im = cross_im + (k_re * d_im - k_im * d_re)
                stages[0, at : at + outer, :inner] = (s_re * k_re - s_im * k_im).astype(jnp.bfloat16)
                stages[0, at : at + outer, inner:] = (s_re * k_im + s_im * k_re).astype(jnp.bfloat16)
                stages[1, at : at + outer, :inner] = (s_re * d_re + s_im * d_im).astype(jnp.bfloat16)
                stages[1, at : at + outer, inner:] = (s_re * d_im - s_im * d_re).astype(jnp.bfloat16)
            cross_ref[g * outer : (g + 1) * outer, :inner] = cross_re.astype(jnp.bfloat16)
            cross_ref[g * outer : (g + 1) * outer, inner:] = cross_im.astype(jnp.bfloat16)
        spot = lax.broadcasted_iota(jnp.int32, (RIM, LANES), 0)
        lane = lax.broadcasted_iota(jnp.int32, (RIM, LANES), 1)
        pick = jnp.where(spot == lane, 1.0, 0.0).astype(jnp.bfloat16)
        rims = []
        for s in range(2):
            tall, stage, turn = talls.at[s], stages.at[s], turns.at[s]
            for pair in range(pairs):
                at = pair * outer
                h = dot(stage[at : at + outer, :], third_ref[...])
                h_re, h_im = h[:, :inner], h[:, inner:]
                lanes = slice(pair * inner, (pair + 1) * inner)
                turn[:outer, lanes] = (h_re * tr - h_im * ti).astype(jnp.bfloat16)
                turn[outer:, lanes] = (h_im * tr + h_re * ti).astype(jnp.bfloat16)
            for g in range(groups):
                span = PAIRS * inner
                y = dot(fourth_ref[...], turn[:, g * span : (g + 1) * span]) * (1.0 / padded)
                for p in range(PAIRS):
                    for part in range(2):
                        c = (g * PAIRS + p) * 2 + part
                        for h in range(fold):
                            at = part * half + h * sources
                            line = y[at : at + sources, p * inner : (p + 1) * inner]
                            put_spread(tall, line, channels, c, height, (h * inner, (h + 1) * inner))
            first = tall[:height, :].astype(jnp.bfloat16)
            rims.append(
                lax.dot_general(pick, first, (((1,), (1,)), ((), ())), preferred_element_type=jnp.float32)
            )
        copies = []
        for q in range(4):
            to = slice(q * chunk, (q + 1) * chunk)
            for s in range(2):
                for t in range(tiles):
                    at = t * height + q * chunk * channels
                    block = talls[s, at : at + chunk * channels, :].reshape(chunk, channels, LANES)
                    row = (s * tiles + t) * channels
                    y_ref[to, row : row + channels, :] = block.astype(jnp.bfloat16)
            for d in range(q * chunk, (q + 1) * chunk):
                tile, lanes = divmod((d + 1) % sources * channels, LANES)
                edge = jnp.zeros((RIM, LANES), jnp.float32)
                if d < sources - 1:
                    for s in range(2):
                        piece = rims[s][:, tile * LANES : (tile + 1) * LANES]
                        turn_by = (s * channels - lanes) % LANES
                        if turn_by:
                            piece = pltpu.roll(piece, turn_by, 1)
                        edge = piece if s == 0 else jnp.where(lane < channels, edge, piece)
                y_ref[d, 2 * tiles * channels :, :] = edge.astype(jnp.bfloat16)
            copies.append(pltpu.make_async_copy(y_ref.at[to], y_hbm.at[to], sems.at[1 + q]))
            copies[-1].start()
        for copy in copies:
            copy.wait()

    sent = (sources, 2 * tiles * channels + RIM, LANES)
    vmem = pl.BlockSpec(memory_space=pltpu.VMEM)
    hbm = pl.BlockSpec(memory_space=pltpu.HBM)
    names = ("first", "second", "third", "fourth", "twist_re", "twist_im")
    return whole_call(
        kernel,
        "joined_filtering",
        (narrow_shape(*sent), narrow_shape(groups * outer, 2 * inner)),
        [arrived, filters] + [tables[n] for n in names],
        [
            pltpu.VMEM((groups * outer, 2 * inner), jnp.float32),
            pltpu.VMEM(sent, jnp.bfloat16),
            pltpu.VMEM((2, tiles * height, LANES), jnp.float32),
            pltpu.VMEM((2, outer, pairs * inner), jnp.bfloat16),
            pltpu.VMEM((2, pairs * outer, 2 * inner), jnp.bfloat16),
            pltpu.VMEM((2, 2 * outer, pairs * inner), jnp.bfloat16),
            pltpu.SemaphoreType.DMA((5,)),
        ],
        flops=4_000_000_000,
        in_specs=[vmem, hbm] + [vmem] * 6,
        out_specs=(hbm, vmem),
    )


def joined_gradients(feats, edges, returned, out_grad, short_filter, owned):
    width, local = out_grad.shape
    tiles = local // LANES
    near = LANES // owned
    blocks = width // LANES

    def kernel(f_ref, edge_ref, back_ref, og_ref, w_ref, mixed_ref, out_ref, tall, made, sent):
        lane = lax.broadcasted_iota(jnp.int32, (RIM, LANES), 1)

        def copy(part, i):
            at = part * blocks + i
            if part < 3:
                to = out_ref.at[pl.ds(pl.multiple_of(at * LANES, LANES), LANES), :]
            else:
                to = mixed_ref.at[lane_block(i), :]
            return pltpu.make_async_copy(made.at[at], to, sent.at[at])

        @pl.loop(0, blocks)
        def _(i):
            held = pl.ds(i * near, near)
            sums = []
            for s in range(2):
                turned = [
                    back_ref[held, (s * tiles + t) * owned : (s * tiles + t + 1) * owned, :].reshape(LANES, LANES).T
                    for t in range(tiles)
                ]
                here = jnp.concatenate(turned, axis=0).astype(jnp.float32)
                rim = jnp.zeros((RIM, LANES), jnp.float32)
                for n in range(near):
                    piece = back_ref[i * near + n, 2 * tiles * owned :, :].astype(jnp.float32)
                    turn_by = (n - s) * owned % LANES
                    if turn_by:
                        piece = pltpu.roll(piece, turn_by, 1)
                    rim = jnp.where(lane >= n * owned, piece, rim) if n else piece
                sums.append((here, rim))
            query = f_ref[:, lane_block(i)].astype(jnp.float32)
            made[3 * blocks + i] = (query * sums[0][0]).astype(jnp.bfloat16).T
            copy(3, i).start()
            for part in range(3):
                here, rim = sums[min(part, 1)]
                if part == 0:
                    other = og_ref[lane_block(i), :].T
                else:
                    other = f_ref[:, lane_block(i, (3 - part) * width)]
                edge = edge_ref[:, lane_block(i, (3 - part) % 3 * width)].astype(jnp.float32)
                grad = (here * other.astype(jnp.float32)).astype(jnp.bfloat16)
                total = seven_taps(
                    tall.at[part],
                    grad.astype(jnp.float32),
                    (rim * edge).astype(jnp.bfloat16).astype(jnp.float32),
                    w_ref[:, lane_block(i, part * width)].astype(jnp.float32),
                    False,
                )
                made[part * blocks + i] = total.astype(jnp.bfloat16).T
                copy(part, i).start()

        @pl.loop(0, blocks)
        def _(i):
            for part in range(4):
                copy(part, i).wait()

    vmem = pl.BlockSpec(memory_space=pltpu.VMEM)
    hbm = pl.BlockSpec(memory_space=pltpu.HBM)
    return whole_call(
        kernel,
        "joined_gradients",
        (narrow_shape(width, local), narrow_shape(3 * width, local)),
        (feats, edges, returned, out_grad, short_filter),
        [
            pltpu.VMEM((3, local + RIM, LANES), jnp.float32),
            pltpu.VMEM((4 * blocks, LANES, local), jnp.bfloat16),
            pltpu.SemaphoreType.DMA((4 * blocks,)),
        ],
        in_specs=[vmem] * 5,
        out_specs=(hbm, hbm),
    )


def query_gradient(grad, rim, short_filter):
    local, width = grad.shape
    steps = width // GRAD_ROWS

    def kernel(d_ref, rim_ref, w_ref, out_ref, tall):
        gradient_block(d_ref, rim_ref, w_ref, out_ref, tall)

    return gradient_call(kernel, "query_gradient", (), grad, rim, short_filter, 1, 0)


def key_value_gradient(whole, grad, rim, short_filter):
    def kernel(_, d_ref, rim_ref, w_ref, out_ref, tall):
        gradient_block(d_ref, rim_ref, w_ref, out_ref, tall)

    return gradient_call(kernel, "key_value_gradient", (whole,), grad, rim, short_filter, 2, 1)


GRAD_ROWS = 512


def gradient_block(d_ref, rim_ref, w_ref, out_ref, tall):
    for c in range(GRAD_ROWS // LANES):
        lanes = slice(c * LANES, (c + 1) * LANES)
        total = seven_taps(
            tall.at[c],
            d_ref[:, lanes].astype(jnp.float32),
            rim_ref[:, lanes].astype(jnp.float32),
            w_ref[:, lanes].astype(jnp.float32),
            False,
        )
        out_ref[lanes, :] = total.astype(jnp.bfloat16).T


def gradient_call(kernel, name, whole, grad, rim, short_filter, parts, first):
    local, lanes = grad.shape
    width = lanes // parts
    steps = width // GRAD_ROWS
    return pl.pallas_call(
        kernel,
        name=name,
        grid=(parts * steps,),
        in_specs=[pl.BlockSpec(memory_space=pl.ANY)] * len(whole)
        + [
            pl.BlockSpec((local, GRAD_ROWS), lambda i: (0, i)),
            pl.BlockSpec((RIM, GRAD_ROWS), lambda i: (0, i)),
            pl.BlockSpec((TAPS, GRAD_ROWS), lambda i: (0, first * steps + i)),
        ],
        out_specs=pl.BlockSpec((GRAD_ROWS, local), lambda i: (first * steps + i, 0)),
        out_shape=narrow_shape(3 * width, local),
        scratch_shapes=[pltpu.VMEM((GRAD_ROWS // LANES, local + RIM, LANES), jnp.float32)],
        input_output_aliases={0: 0} if whole else {},
        cost_estimate=pl.CostEstimate(flops=20_000_000, bytes_accessed=4_000_000, transcendentals=0),
    )(*whole, grad, rim, short_filter)


def shards(projections, short_filter, long_filter, out_grad):
    width, local_len = out_grad.shape
    devices = lax.axis_size(EVERYONE)
    seq_len = local_len * devices
    owned = width // devices
    tables = make_tables(seq_len, devices)

    turned = projections.T
    rim = shifted(turned[local_len - RIM :], EVERYONE, 1)

    if owned % 16 == 0 and LANES % (2 * owned) == 0 and devices % 4 == 0:
        feats, message, edges = joined_features(turned, rim, short_filter, out_grad, owned)
        filters = transform_filters(long_filter, tables, seq_len)
        arrived = lax.all_to_all(message, EVERYONE, split_axis=0, concat_axis=0, tiled=True)
        edges, filters, arrived = lax.optimization_barrier((shifted(edges, EVERYONE, -1), filters, arrived))
        answer, cross = joined_filtering(arrived, filters, tables, seq_len)
        returned = lax.all_to_all(answer, EVERYONE, split_axis=0, concat_axis=0, tiled=True)
        filter_grad = filter_gradient(cross, tables, seq_len)
        filter_grad, returned = lax.optimization_barrier((filter_grad, returned))
        mixed, grad = joined_gradients(feats, edges, returned, out_grad, short_filter, owned)
        return (mixed, grad, filter_grad)

    cotangent = out_grad.T
    feats, product, conv_grad = features_of(turned, rim, short_filter, cotangent)

    def exchange(block):
        pieces = block.reshape(devices, owned, local_len)
        return lax.all_to_all(pieces, EVERYONE, split_axis=0, concat_axis=0, tiled=True)

    filters = transform_filters(long_filter, tables, seq_len)
    prod_chan = exchange(product)
    conv_grad, prod_chan = lax.optimization_barrier((conv_grad, prod_chan))
    grad_chan = exchange(conv_grad)
    conv_chan, prod_spec = filtered(prod_chan, filters, tables, seq_len)
    conv_chan, grad_chan = lax.optimization_barrier((conv_chan, grad_chan))
    conv_tok = exchange(conv_chan)
    back_chan, cross = filtered(grad_chan, filters, tables, seq_len, prod_spec)
    back_chan, conv_tok = lax.optimization_barrier((back_chan, conv_tok))
    back_tok = exchange(back_chan)

    filter_grad = filter_gradient(cross, tables, seq_len)
    mixed, grad_q, rim_q = query_products(feats, conv_tok.reshape(width, local_len), cotangent)
    grad = query_gradient(grad_q, shifted(rim_q, EVERYONE, -1), short_filter)
    filter_grad, mixed, grad, back_tok = lax.optimization_barrier((filter_grad, mixed, grad, back_tok))

    grad_kv, rim_kv = key_value_products(feats, back_tok.reshape(width, local_len))
    grad = key_value_gradient(grad, grad_kv, shifted(rim_kv, EVERYONE, -1), short_filter)
    return (mixed, grad, filter_grad)


def solution(mesh):
    placed = (P(None, EVERYONE), P(), P(EVERYONE, None), P(None, EVERYONE))
    return jax.shard_map(
        shards,
        mesh=mesh,
        in_specs=placed,
        out_specs=(P(None, EVERYONE), P(None, EVERYONE), P(EVERYONE, None)),
        check_vma=False,
    )
```

```python
import math

import jax
import jax.numpy as jnp
import numpy as np
from jax import lax
from jax.experimental import pallas as pl
from jax.experimental.pallas import tpu as pltpu
from jax.sharding import PartitionSpec as P

CPG = 4
TAPS = 7
PAIRS = CPG // 2
EVERYONE = ("dp", "ctx")
VMEM_LIMIT = 24 * 1024 * 1024


def shifted(value, axis, steps):
    count = lax.axis_size(axis)
    first, last = (max(0, -steps), min(count, count - steps))
    return lax.ppermute(value, axis, [(source, source + steps) for source in range(first, last)])


def sizes_of(seq_len):
    padded = 2 * seq_len
    inner = max(d for d in range(1, seq_len + 1) if seq_len % d == 0 and d * d <= padded)
    return padded, inner, padded // inner


def table(count_out, count_in, period):
    turns = np.arange(count_out, dtype=np.int64)[:, None] * np.arange(count_in, dtype=np.int64)
    angle = (turns % period).astype(np.float64) * (2.0 * math.pi / period)
    return np.cos(angle), np.sin(angle)


def make_tables(seq_len, sources):
    padded, inner, outer = sizes_of(seq_len)
    half = outer // 2
    fold = half // sources
    order = np.arange(half).reshape(sources, fold).T.reshape(-1)
    cos_o, sin_o = table(outer, half, outer)
    cos_i, sin_i = table(inner, inner, inner)
    cos_p, sin_p = cos_o[:, order], sin_o[:, order]
    narrow = lambda blocks: jnp.asarray(np.block(blocks).astype(np.float32)).astype(jnp.bfloat16)
    twist = [jnp.asarray(t.astype(np.float32)) for t in table(outer, inner, padded)]
    return {
        "first": narrow([[cos_p, sin_p], [-sin_p, cos_p]]),
        "second": narrow([[cos_i, -sin_i], [sin_i, cos_i]]),
        "third": narrow([[cos_i, sin_i], [-sin_i, cos_i]]),
        "fourth": narrow([[cos_p.T, -sin_p.T], [sin_p.T, cos_p.T]]),
        "fourth_scaled": narrow([[cos_p.T / padded, -sin_p.T / padded], [sin_p.T / padded, cos_p.T / padded]]),
        "first_real": narrow([[cos_o], [-sin_o]]),
        "fourth_real": narrow([[cos_o.T, -sin_o.T]]),
        "twist_re": twist[0],
        "twist_im": twist[1],
    }


LANES = 128


def spread(tall, count, stride, first, height, width):
    tiles = [tall[pl.ds(t * height + first, count, stride=stride), :] for t in range(width[0] // LANES, width[1] // LANES)]
    return tiles[0] if len(tiles) == 1 else jnp.concatenate(tiles, axis=1)


def put_spread(tall, values, stride, first, height, width):
    for i, t in enumerate(range(width[0] // LANES, width[1] // LANES)):
        tall[pl.ds(t * height + first, values.shape[0], stride=stride), :] = values[:, i * LANES : (i + 1) * LANES]


def dot(left, right):
    return jnp.dot(left, right, preferred_element_type=jnp.float32)


def transform_filters(long_filter, tables, seq_len):
    padded, inner, outer = sizes_of(seq_len)
    half = outer // 2
    groups = long_filter.shape[0]
    scale = seq_len ** -0.5

    def kernel(x_ref, first_ref, second_ref, tr_ref, ti_ref, out_ref, tall):
        height = half * groups
        for b in range(half):
            for t in range(inner // LANES):
                at = t * height + b * groups
                lanes = slice(b * inner + t * LANES, b * inner + (t + 1) * LANES)
                tall[at : at + groups, :] = x_ref[:, lanes].astype(jnp.float32)
        for g in range(groups):
            x = spread(tall, half, groups, g, height, (0, inner)).astype(jnp.bfloat16)
            f = dot(first_ref[...], x)
            f_re, f_im = f[:outer], f[outer:]
            g_re = (f_re * tr_ref[...] + f_im * ti_ref[...]).astype(jnp.bfloat16)
            g_im = (f_im * tr_ref[...] - f_re * ti_ref[...]).astype(jnp.bfloat16)
            spec = dot(g_re, second_ref[:inner]) + dot(g_im, second_ref[inner:])
            out_ref[g * outer : (g + 1) * outer, :] = spec * scale

    return pl.pallas_call(
        kernel,
        name="filter_dft",
        out_shape=jax.ShapeDtypeStruct((groups * outer, 2 * inner), jnp.float32),
        scratch_shapes=[pltpu.VMEM((half * groups * inner // LANES, LANES), jnp.float32)],
        compiler_params=pltpu.CompilerParams(vmem_limit_bytes=VMEM_LIMIT),
        cost_estimate=pl.CostEstimate(flops=200_000_000, bytes_accessed=2_000_000, transcendentals=0),
    )(long_filter, tables["first_real"], tables["second"], tables["twist_re"], tables["twist_im"])


def filtered(arrived, filters, tables, seq_len, other=None):
    padded, inner, outer = sizes_of(seq_len)
    half = outer // 2
    sources, channels, local = arrived.shape
    fold = local // inner
    groups = channels // CPG
    backward = other is not None

    def kernel(*refs):
        if backward:
            (x_ref, f_ref, k_ref, first_ref, second_ref, third_ref, fourth_ref, tr_ref, ti_ref,
             y_ref, cross_ref, tall, wide, stage, turn) = refs
        else:
            (x_ref, f_ref, first_ref, second_ref, third_ref, fourth_ref, tr_ref, ti_ref,
             y_ref, z_ref, tall, wide, stage, turn) = refs
        height = sources * channels
        for t in range(local // LANES):
            block = x_ref[:, :, t * LANES : (t + 1) * LANES].astype(jnp.float32)
            tall[t * height : (t + 1) * height, :] = block.reshape(height, LANES)
        for c in range(channels):
            pair, part = divmod(c, 2)
            for h in range(fold):
                rows = spread(tall, sources, channels, c, height, (h * inner, (h + 1) * inner))
                at = part * half + h * sources
                wide[at : at + sources, pair * inner : (pair + 1) * inner] = rows.astype(jnp.bfloat16)
        for g in range(groups):
            span = PAIRS * inner
            f = dot(first_ref[...], wide[:, g * span : (g + 1) * span])
            for p in range(PAIRS):
                f_re = f[:outer, p * inner : (p + 1) * inner]
                f_im = f[outer:, p * inner : (p + 1) * inner]
                at = (g * PAIRS + p) * outer
                stage[at : at + outer, :inner] = (f_re * tr_ref[...] + f_im * ti_ref[...]).astype(jnp.bfloat16)
                stage[at : at + outer, inner:] = (f_im * tr_ref[...] - f_re * ti_ref[...]).astype(jnp.bfloat16)
        for g in range(groups):
            s_re = f_ref[g * outer : (g + 1) * outer, :inner]
            s_im = f_ref[g * outer : (g + 1) * outer, inner:]
            cross_re = cross_im = None
            for p in range(PAIRS):
                at = (g * PAIRS + p) * outer
                z = dot(stage[at : at + outer, :], second_ref[...])
                z_re, z_im = z[:, :inner], z[:, inner:]
                if backward:
                    k_re = k_ref[at : at + outer, :inner].astype(jnp.float32)
                    k_im = k_ref[at : at + outer, inner:].astype(jnp.float32)
                    part_re = k_re * z_re + k_im * z_im
                    part_im = k_re * z_im - k_im * z_re
                    cross_re = part_re if cross_re is None else cross_re + part_re
                    cross_im = part_im if cross_im is None else cross_im + part_im
                    o_re = s_re * z_re + s_im * z_im
                    o_im = s_re * z_im - s_im * z_re
                else:
                    z_ref[at : at + outer, :] = z
                    o_re = s_re * z_re - s_im * z_im
                    o_im = s_re * z_im + s_im * z_re
                stage[at : at + outer, :inner] = o_re.astype(jnp.bfloat16)
                stage[at : at + outer, inner:] = o_im.astype(jnp.bfloat16)
            if backward:
                cross_ref[g * outer : (g + 1) * outer, :inner] = cross_re.astype(jnp.bfloat16)
                cross_ref[g * outer : (g + 1) * outer, inner:] = cross_im.astype(jnp.bfloat16)
        for pair in range(groups * PAIRS):
            at = pair * outer
            h = dot(stage[at : at + outer, :], third_ref[...])
            h_re, h_im = h[:, :inner], h[:, inner:]
            lanes = slice(pair * inner, (pair + 1) * inner)
            turn[:outer, lanes] = (h_re * tr_ref[...] - h_im * ti_ref[...]).astype(jnp.bfloat16)
            turn[outer:, lanes] = (h_im * tr_ref[...] + h_re * ti_ref[...]).astype(jnp.bfloat16)
        for g in range(groups):
            span = PAIRS * inner
            y = dot(fourth_ref[...], turn[:, g * span : (g + 1) * span]) * (1.0 / padded)
            for p in range(PAIRS):
                for part in range(2):
                    c = (g * PAIRS + p) * 2 + part
                    for h in range(fold):
                        at = part * half + h * sources
                        rows = y[at : at + sources, p * inner : (p + 1) * inner]
                        put_spread(tall, rows, channels, c, height, (h * inner, (h + 1) * inner))
        for t in range(local // LANES):
            block = tall[t * height : (t + 1) * height, :].reshape(sources, channels, LANES)
            y_ref[:, :, t * LANES : (t + 1) * LANES] = block.astype(jnp.bfloat16)

    pairs = groups * PAIRS
    if backward:
        extra = jax.ShapeDtypeStruct((groups * outer, 2 * inner), jnp.bfloat16)
    else:
        extra = jax.ShapeDtypeStruct((pairs * outer, 2 * inner), jnp.float32)
    operands = [arrived, filters] + ([other] if backward else [])
    operands += [tables[n] for n in ("first", "second", "third", "fourth", "twist_re", "twist_im")]
    return pl.pallas_call(
        kernel,
        name="correlate" if backward else "convolve",
        out_shape=(jax.ShapeDtypeStruct(arrived.shape, jnp.bfloat16), extra),
        scratch_shapes=[
            pltpu.VMEM((sources * channels * local // LANES, LANES), jnp.float32),
            pltpu.VMEM((outer, pairs * inner), jnp.bfloat16),
            pltpu.VMEM((pairs * outer, 2 * inner), jnp.bfloat16),
            pltpu.VMEM((2 * outer, pairs * inner), jnp.bfloat16),
        ],
        compiler_params=pltpu.CompilerParams(vmem_limit_bytes=VMEM_LIMIT),
        cost_estimate=pl.CostEstimate(flops=2_000_000_000, bytes_accessed=5_000_000, transcendentals=0),
    )(*operands)


def filter_gradient(cross, tables, seq_len):
    padded, inner, outer = sizes_of(seq_len)
    half = outer // 2
    groups = cross.shape[0] // outer
    scale = seq_len ** -0.5 / padded

    def kernel(s_ref, third_ref, fourth_ref, tr_ref, ti_ref, out_ref, tall, turn):
        for g in range(groups):
            h = dot(s_ref[g * outer : (g + 1) * outer, :], third_ref[...])
            h_re, h_im = h[:, :inner], h[:, inner:]
            turn[:outer, g * inner : (g + 1) * inner] = (h_re * tr_ref[...] - h_im * ti_ref[...]).astype(jnp.bfloat16)
            turn[outer:, g * inner : (g + 1) * inner] = (h_im * tr_ref[...] + h_re * ti_ref[...]).astype(jnp.bfloat16)
        for g in range(groups):
            y = dot(fourth_ref[...], turn[:, g * inner : (g + 1) * inner]) * scale
            put_spread(tall, y, groups, g, half * groups, (0, inner))
        for b in range(half):
            for t in range(inner // LANES):
                at = (t * half + b) * groups
                out_ref[:, b * inner + t * LANES : b * inner + (t + 1) * LANES] = tall[at : at + groups, :]

    return pl.pallas_call(
        kernel,
        name="filter_gradient",
        out_shape=jax.ShapeDtypeStruct((groups, seq_len), jnp.float32),
        scratch_shapes=[
            pltpu.VMEM((half * groups * inner // LANES, LANES), jnp.float32),
            pltpu.VMEM((2 * outer, groups * inner), jnp.bfloat16),
        ],
        compiler_params=pltpu.CompilerParams(vmem_limit_bytes=VMEM_LIMIT),
        cost_estimate=pl.CostEstimate(flops=200_000_000, bytes_accessed=2_000_000, transcendentals=0),
    )(cross, tables["third"], tables["fourth_real"], tables["twist_re"], tables["twist_im"])


RIM = 8


def seven_taps(tall, value, rim, weights, forward):
    count = value.shape[0]
    if forward:
        tall[:RIM, :] = rim
        tall[RIM : RIM + count, :] = value
    else:
        tall[:count, :] = value
        tall[count : count + RIM, :] = rim
    total = value * weights[:1]
    for lag in range(1, TAPS):
        first = RIM - lag if forward else lag
        total = total + tall[first : first + count, :] * weights[lag : lag + 1]
    return total


def lane_block(i, offset=0):
    return pl.ds(pl.multiple_of(i * LANES + offset, LANES), LANES)


def whole_call(kernel, name, out_shape, operands, scratch=(), flops=10_000_000, **kwargs):
    return pl.pallas_call(
        kernel,
        name=name,
        out_shape=out_shape,
        scratch_shapes=list(scratch),
        compiler_params=pltpu.CompilerParams(vmem_limit_bytes=VMEM_LIMIT),
        cost_estimate=pl.CostEstimate(flops=flops, bytes_accessed=4_000_000, transcendentals=0),
        **kwargs,
    )(*operands)


def narrow_shape(*shape):
    return jax.ShapeDtypeStruct(shape, jnp.bfloat16)


def features_of(turned, rim, short_filter, cotangent):
    local, width = cotangent.shape

    def kernel(x_ref, rim_ref, w_ref, og_ref, f_ref, kv_ref, dconv_ref, tall):
        @pl.loop(0, width // LANES)
        def _(i):
            made = []
            for part in range(3):
                lanes = lane_block(i, part * width)
                total = seven_taps(
                    tall.at[part],
                    x_ref[:, lanes].astype(jnp.float32),
                    rim_ref[:, lanes].astype(jnp.float32),
                    w_ref[:, lanes].astype(jnp.float32),
                    True,
                ).astype(jnp.bfloat16)
                f_ref[:, lanes] = total
                made.append(total.astype(jnp.float32))
            rows = lane_block(i)
            kv_ref[rows, :] = (made[1] * made[2]).astype(jnp.bfloat16).T
            og = og_ref[:, rows].astype(jnp.float32)
            dconv_ref[rows, :] = (og * made[0]).astype(jnp.bfloat16).T

    return whole_call(
        kernel,
        "features",
        (narrow_shape(local, 3 * width), narrow_shape(width, local), narrow_shape(width, local)),
        (turned, rim, short_filter, cotangent),
        [pltpu.VMEM((3, local + RIM, LANES), jnp.float32)],
    )


def query_products(feats, conv, cotangent):
    width, local = conv.shape

    def kernel(f_ref, conv_ref, og_ref, mixed_ref, dq_ref, rim_ref):
        @pl.loop(0, width // LANES)
        def _(i):
            lanes = lane_block(i)
            here = conv_ref[lanes, :].T.astype(jnp.float32)
            mixed_ref[lanes, :] = (f_ref[:, lanes].astype(jnp.float32) * here).astype(jnp.bfloat16).T
            dq = (og_ref[:, lanes].astype(jnp.float32) * here).astype(jnp.bfloat16)
            dq_ref[:, lanes] = dq
            rim_ref[:, lanes] = dq[:RIM]

    return whole_call(
        kernel,
        "query_products",
        (narrow_shape(width, local), narrow_shape(local, width), narrow_shape(RIM, width)),
        (feats, conv, cotangent),
    )


def key_value_products(feats, back):
    width, local = back.shape

    def kernel(f_ref, back_ref, d_ref, rim_ref):
        @pl.loop(0, width // LANES)
        def _(i):
            here = back_ref[lane_block(i), :].T.astype(jnp.float32)
            for part in range(2):
                other = f_ref[:, lane_block(i, (2 - part) * width)].astype(jnp.float32)
                grad = (here * other).astype(jnp.bfloat16)
                d_ref[:, lane_block(i, part * width)] = grad
                rim_ref[:, lane_block(i, part * width)] = grad[:RIM]

    return whole_call(
        kernel,
        "key_value_products",
        (narrow_shape(local, 2 * width), narrow_shape(RIM, 2 * width)),
        (feats, back),
    )


def joined_features(turned, rim, short_filter, out_grad, owned):
    width, local = out_grad.shape
    near = LANES // owned
    blocks = width // LANES

    def kernel(x_ref, rim_ref, w_ref, og_ref, f_hbm, msg_ref, edge_ref, tall, made, f_ref, edge, sent):
        def copy(i):
            to = pl.ds(i * near, near)
            return pltpu.make_async_copy(made.at[to], msg_ref.at[to], sent.at[i])

        def keep(i):
            to = pl.ds(3 * i, 3)
            return pltpu.make_async_copy(f_ref.at[to], f_hbm.at[to], sent.at[blocks + i])

        @pl.loop(0, blocks)
        def _(i):
            parts = []
            for part in range(3):
                lanes = lane_block(i, part * width)
                total = seven_taps(
                    tall.at[part],
                    x_ref[:, lanes].astype(jnp.float32),
                    rim_ref[:, lanes].astype(jnp.float32),
                    w_ref[:, lanes].astype(jnp.float32),
                    True,
                ).astype(jnp.bfloat16)
                f_ref[3 * i + part] = total
                if part:
                    edge[:, lanes] = total[:RIM]
                parts.append(total.astype(jnp.float32))
            og = og_ref[lane_block(i), :].T
            edge[:, lane_block(i)] = og[:RIM]
            kv = (parts[1] * parts[2]).astype(jnp.bfloat16).T
            dconv = (og.astype(jnp.float32) * parts[0]).astype(jnp.bfloat16).T
            to = pl.ds(i * near, near)
            made[to, :owned, :] = kv.reshape(near, owned, local)
            made[to, owned:, :] = dconv.reshape(near, owned, local)
            copy(i).start()
            keep(i).start()

        last = pltpu.make_async_copy(edge, edge_ref, sent.at[2 * blocks])
        last.start()

        @pl.loop(0, blocks)
        def _(i):
            copy(i).wait()
            keep(i).wait()

        last.wait()

    vmem = pl.BlockSpec(memory_space=pltpu.VMEM)
    hbm = pl.BlockSpec(memory_space=pltpu.HBM)
    devices = width // owned
    return whole_call(
        kernel,
        "joined_features",
        (
            narrow_shape(3 * blocks, local, LANES),
            narrow_shape(devices, 2 * owned, local),
            narrow_shape(RIM, 3 * width),
        ),
        (turned, rim, short_filter, out_grad),
        [
            pltpu.VMEM((3, local + RIM, LANES), jnp.float32),
            pltpu.VMEM((devices, 2 * owned, local), jnp.bfloat16),
            pltpu.VMEM((3 * blocks, local, LANES), jnp.bfloat16),
            pltpu.VMEM((RIM, 3 * width), jnp.bfloat16),
            pltpu.SemaphoreType.DMA((2 * blocks + 1,)),
        ],
        in_specs=[vmem] * 4,
        out_specs=(hbm, hbm, hbm),
    )


def joined_filtering(arrived, filters, tables, seq_len):
    padded, inner, outer = sizes_of(seq_len)
    half = outer // 2
    sources, rows, local = arrived.shape
    channels = rows // 2
    tiles = local // LANES
    fold = local // inner
    groups = channels // CPG
    pairs = groups * PAIRS
    height = sources * channels
    chunk = sources // 4

    def kernel(x_ref, *refs):
        sources_hbm, (y_hbm, cross_hbm), held = refs[:7], refs[7:9], refs[9:16]
        y_ref, cross_ref, talls, wides, stages, turns, sems, fetched = refs[16:]
        first_ref, tr_ref, ti_ref, second_ref, f_ref, third_ref, fourth_ref = held
        fetches = [pltpu.make_async_copy(a, b, fetched.at[n]) for n, (a, b) in enumerate(zip(sources_hbm, held))]
        for fetch in fetches:
            fetch.start()
        for s in range(2):
            tall, wide, stage = talls.at[s], wides.at[s], stages.at[s]
            for t in range(tiles):
                block = x_ref[:, s * channels : (s + 1) * channels, t * LANES : (t + 1) * LANES]
                tall[t * height : (t + 1) * height, :] = block.astype(jnp.float32).reshape(height, LANES)
            for c in range(channels):
                pair, part = divmod(c, 2)
                for h in range(fold):
                    line = spread(tall, sources, channels, c, height, (h * inner, (h + 1) * inner))
                    at = part * half + h * sources
                    wide[at : at + sources, pair * inner : (pair + 1) * inner] = line.astype(jnp.bfloat16)
            if s == 0:
                for fetch in fetches[:3]:
                    fetch.wait()
                tr, ti = tr_ref[...], ti_ref[...]
            for g in range(groups):
                span = PAIRS * inner
                f = dot(first_ref[...], wide[:, g * span : (g + 1) * span])
                for p in range(PAIRS):
                    f_re = f[:outer, p * inner : (p + 1) * inner]
                    f_im = f[outer:, p * inner : (p + 1) * inner]
                    at = (g * PAIRS + p) * outer
                    stage[at : at + outer, :inner] = (f_re * tr + f_im * ti).astype(jnp.bfloat16)
                    stage[at : at + outer, inner:] = (f_im * tr - f_re * ti).astype(jnp.bfloat16)
        for fetch in fetches[3:]:
            fetch.wait()
        for g in range(groups):
            s_re = f_ref[g * outer : (g + 1) * outer, :inner]
            s_im = f_ref[g * outer : (g + 1) * outer, inner:]
            cross_re = cross_im = 0.0
            for p in range(PAIRS):
                at = (g * PAIRS + p) * outer
                k = dot(stages[0, at : at + outer, :], second_ref[...])
                d = dot(stages[1, at : at + outer, :], second_ref[...])
                k_re, k_im = k[:, :inner], k[:, inner:]
                d_re, d_im = d[:, :inner], d[:, inner:]
                cross_re = cross_re + (k_re * d_re + k_im * d_im)
                cross_im = cross_im + (k_re * d_im - k_im * d_re)
                stages[0, at : at + outer, :inner] = (s_re * k_re - s_im * k_im).astype(jnp.bfloat16)
                stages[0, at : at + outer, inner:] = (s_re * k_im + s_im * k_re).astype(jnp.bfloat16)
                stages[1, at : at + outer, :inner] = (s_re * d_re + s_im * d_im).astype(jnp.bfloat16)
                stages[1, at : at + outer, inner:] = (s_re * d_im - s_im * d_re).astype(jnp.bfloat16)
            cross_ref[g * outer : (g + 1) * outer, :inner] = cross_re.astype(jnp.bfloat16)
            cross_ref[g * outer : (g + 1) * outer, inner:] = cross_im.astype(jnp.bfloat16)
        copies = [pltpu.make_async_copy(cross_ref, cross_hbm, sems.at[4])]
        copies[0].start()
        spot = lax.broadcasted_iota(jnp.int32, (RIM, LANES), 0)
        lane = lax.broadcasted_iota(jnp.int32, (RIM, LANES), 1)
        pick = jnp.where(spot == lane, 1.0, 0.0).astype(jnp.bfloat16)
        rims = []
        for s in range(2):
            tall, stage, turn = talls.at[s], stages.at[s], turns.at[s]
            for pair in range(pairs):
                at = pair * outer
                h = dot(stage[at : at + outer, :], third_ref[...])
                h_re, h_im = h[:, :inner], h[:, inner:]
                lanes = slice(pair * inner, (pair + 1) * inner)
                turn[:outer, lanes] = (h_re * tr - h_im * ti).astype(jnp.bfloat16)
                turn[outer:, lanes] = (h_im * tr + h_re * ti).astype(jnp.bfloat16)
            for g in range(groups):
                span = PAIRS * inner
                y = dot(fourth_ref[...], turn[:, g * span : (g + 1) * span])
                for p in range(PAIRS):
                    for part in range(2):
                        c = (g * PAIRS + p) * 2 + part
                        for h in range(fold):
                            at = part * half + h * sources
                            line = y[at : at + sources, p * inner : (p + 1) * inner]
                            put_spread(tall, line, channels, c, height, (h * inner, (h + 1) * inner))
            first = tall[:height, :].astype(jnp.bfloat16)
            rims.append(
                lax.dot_general(pick, first, (((1,), (1,)), ((), ())), preferred_element_type=jnp.float32)
            )
        for q in range(4):
            to = slice(q * chunk, (q + 1) * chunk)
            for s in range(2):
                for t in range(tiles):
                    at = t * height + q * chunk * channels
                    block = talls[s, at : at + chunk * channels, :].reshape(chunk, channels, LANES)
                    row = (s * tiles + t) * channels
                    y_ref[to, row : row + channels, :] = block.astype(jnp.bfloat16)
            for d in range(q * chunk, (q + 1) * chunk):
                tile, lanes = divmod((d + 1) % sources * channels, LANES)
                edge = jnp.zeros((RIM, LANES), jnp.float32)
                if d < sources - 1:
                    for s in range(2):
                        piece = rims[s][:, tile * LANES : (tile + 1) * LANES]
                        turn_by = (s * channels - lanes) % LANES
                        if turn_by:
                            piece = pltpu.roll(piece, turn_by, 1)
                        edge = piece if s == 0 else jnp.where(lane < channels, edge, piece)
                y_ref[d, 2 * tiles * channels :, :] = edge.astype(jnp.bfloat16)
            copies.append(pltpu.make_async_copy(y_ref.at[to], y_hbm.at[to], sems.at[q]))
            copies[-1].start()
        for copy in copies:
            copy.wait()

    sent = (sources, 2 * tiles * channels + RIM, LANES)
    vmem = pl.BlockSpec(memory_space=pltpu.VMEM)
    hbm = pl.BlockSpec(memory_space=pltpu.HBM)
    fetched = [tables[n] for n in ("first", "twist_re", "twist_im", "second")] + [filters]
    fetched += [tables[n] for n in ("third", "fourth_scaled")]
    return whole_call(
        kernel,
        "joined_filtering",
        (narrow_shape(*sent), narrow_shape(groups * outer, 2 * inner)),
        [arrived] + fetched,
        [pltpu.VMEM(array.shape, array.dtype) for array in fetched]
        + [
            pltpu.VMEM(sent, jnp.bfloat16),
            pltpu.VMEM((groups * outer, 2 * inner), jnp.bfloat16),
            pltpu.VMEM((2, tiles * height, LANES), jnp.float32),
            pltpu.VMEM((2, outer, pairs * inner), jnp.bfloat16),
            pltpu.VMEM((2, pairs * outer, 2 * inner), jnp.bfloat16),
            pltpu.VMEM((2, 2 * outer, pairs * inner), jnp.bfloat16),
            pltpu.SemaphoreType.DMA((5,)),
            pltpu.SemaphoreType.DMA((7,)),
        ],
        flops=4_000_000_000,
        in_specs=[vmem] + [hbm] * 7,
        out_specs=(hbm, hbm),
    )


def joined_gradients(feats, edges, returned, out_grad, short_filter, owned):
    width, local = out_grad.shape
    tiles = local // LANES
    near = LANES // owned
    blocks = width // LANES

    def kernel(f_hbm, edge_ref, back_ref, og_hbm, w_ref, mixed_ref, out_ref, tall, made, f_ref, og_ref, sent, fetched):
        def fetch(i):
            to = pl.ds(3 * i, 3)
            rows = lane_block(i)
            return (
                pltpu.make_async_copy(f_hbm.at[to], f_ref.at[to], fetched.at[i]),
                pltpu.make_async_copy(og_hbm.at[rows, :], og_ref.at[rows, :], fetched.at[blocks + i]),
            )

        @pl.loop(0, blocks)
        def _(i):
            for one in fetch(i):
                one.start()

        lane = lax.broadcasted_iota(jnp.int32, (RIM, LANES), 1)

        def copy(part, i):
            at = part * blocks + i
            if part < 3:
                to = out_ref.at[pl.ds(pl.multiple_of(at * LANES, LANES), LANES), :]
            else:
                to = mixed_ref.at[lane_block(i), :]
            return pltpu.make_async_copy(made.at[at], to, sent.at[at])

        @pl.loop(0, blocks)
        def _(i):
            held = pl.ds(i * near, near)
            sums = []
            for s in range(2):
                turned = [
                    back_ref[held, (s * tiles + t) * owned : (s * tiles + t + 1) * owned, :].reshape(LANES, LANES).T
                    for t in range(tiles)
                ]
                here = jnp.concatenate(turned, axis=0).astype(jnp.float32)
                rim = jnp.zeros((RIM, LANES), jnp.float32)
                for n in range(near):
                    piece = back_ref[i * near + n, 2 * tiles * owned :, :].astype(jnp.float32)
                    turn_by = (n - s) * owned % LANES
                    if turn_by:
                        piece = pltpu.roll(piece, turn_by, 1)
                    rim = jnp.where(lane >= n * owned, piece, rim) if n else piece
                sums.append((here, rim))
            for one in fetch(i):
                one.wait()
            query = f_ref[3 * i].astype(jnp.float32)
            made[3 * blocks + i] = (query * sums[0][0]).astype(jnp.bfloat16).T
            copy(3, i).start()
            for part in range(3):
                here, rim = sums[min(part, 1)]
                if part == 0:
                    other = og_ref[lane_block(i), :].T
                else:
                    other = f_ref[3 * i + 3 - part]
                edge = edge_ref[:, lane_block(i, (3 - part) % 3 * width)].astype(jnp.float32)
                grad = (here * other.astype(jnp.float32)).astype(jnp.bfloat16)
                total = seven_taps(
                    tall.at[part],
                    grad.astype(jnp.float32),
                    (rim * edge).astype(jnp.bfloat16).astype(jnp.float32),
                    w_ref[:, lane_block(i, part * width)].astype(jnp.float32),
                    False,
                )
                made[part * blocks + i] = total.astype(jnp.bfloat16).T
                copy(part, i).start()

        @pl.loop(0, blocks)
        def _(i):
            for part in range(4):
                copy(part, i).wait()

    vmem = pl.BlockSpec(memory_space=pltpu.VMEM)
    hbm = pl.BlockSpec(memory_space=pltpu.HBM)
    return whole_call(
        kernel,
        "joined_gradients",
        (narrow_shape(width, local), narrow_shape(3 * width, local)),
        (feats, edges, returned, out_grad, short_filter),
        [
            pltpu.VMEM((3, local + RIM, LANES), jnp.float32),
            pltpu.VMEM((4 * blocks, LANES, local), jnp.bfloat16),
            pltpu.VMEM((3 * blocks, local, LANES), jnp.bfloat16),
            pltpu.VMEM((width, local), jnp.bfloat16),
            pltpu.SemaphoreType.DMA((4 * blocks,)),
            pltpu.SemaphoreType.DMA((2 * blocks,)),
        ],
        in_specs=[hbm, vmem, vmem, hbm, vmem],
        out_specs=(hbm, hbm),
    )


def query_gradient(grad, rim, short_filter):
    local, width = grad.shape
    steps = width // GRAD_ROWS

    def kernel(d_ref, rim_ref, w_ref, out_ref, tall):
        gradient_block(d_ref, rim_ref, w_ref, out_ref, tall)

    return gradient_call(kernel, "query_gradient", (), grad, rim, short_filter, 1, 0)


def key_value_gradient(whole, grad, rim, short_filter):
    def kernel(_, d_ref, rim_ref, w_ref, out_ref, tall):
        gradient_block(d_ref, rim_ref, w_ref, out_ref, tall)

    return gradient_call(kernel, "key_value_gradient", (whole,), grad, rim, short_filter, 2, 1)


GRAD_ROWS = 512


def gradient_block(d_ref, rim_ref, w_ref, out_ref, tall):
    for c in range(GRAD_ROWS // LANES):
        lanes = slice(c * LANES, (c + 1) * LANES)
        total = seven_taps(
            tall.at[c],
            d_ref[:, lanes].astype(jnp.float32),
            rim_ref[:, lanes].astype(jnp.float32),
            w_ref[:, lanes].astype(jnp.float32),
            False,
        )
        out_ref[lanes, :] = total.astype(jnp.bfloat16).T


def gradient_call(kernel, name, whole, grad, rim, short_filter, parts, first):
    local, lanes = grad.shape
    width = lanes // parts
    steps = width // GRAD_ROWS
    return pl.pallas_call(
        kernel,
        name=name,
        grid=(parts * steps,),
        in_specs=[pl.BlockSpec(memory_space=pl.ANY)] * len(whole)
        + [
            pl.BlockSpec((local, GRAD_ROWS), lambda i: (0, i)),
            pl.BlockSpec((RIM, GRAD_ROWS), lambda i: (0, i)),
            pl.BlockSpec((TAPS, GRAD_ROWS), lambda i: (0, first * steps + i)),
        ],
        out_specs=pl.BlockSpec((GRAD_ROWS, local), lambda i: (first * steps + i, 0)),
        out_shape=narrow_shape(3 * width, local),
        scratch_shapes=[pltpu.VMEM((GRAD_ROWS // LANES, local + RIM, LANES), jnp.float32)],
        input_output_aliases={0: 0} if whole else {},
        cost_estimate=pl.CostEstimate(flops=20_000_000, bytes_accessed=4_000_000, transcendentals=0),
    )(*whole, grad, rim, short_filter)


def shards(projections, short_filter, long_filter, out_grad):
    width, local_len = out_grad.shape
    devices = lax.axis_size(EVERYONE)
    seq_len = local_len * devices
    owned = width // devices
    tables = make_tables(seq_len, devices)

    turned = projections.T
    rim = shifted(turned[local_len - RIM :], EVERYONE, 1)

    if owned % 16 == 0 and LANES % (2 * owned) == 0 and devices % 4 == 0:
        feats, message, edges = joined_features(turned, rim, short_filter, out_grad, owned)
        filters = transform_filters(long_filter, tables, seq_len)
        arrived = lax.all_to_all(message, EVERYONE, split_axis=0, concat_axis=0, tiled=True)
        edges, filters, arrived = lax.optimization_barrier((shifted(edges, EVERYONE, -1), filters, arrived))
        answer, cross = joined_filtering(arrived, filters, tables, seq_len)
        returned = lax.all_to_all(answer, EVERYONE, split_axis=0, concat_axis=0, tiled=True)
        filter_grad = filter_gradient(cross, tables, seq_len)
        filter_grad, returned = lax.optimization_barrier((filter_grad, returned))
        mixed, grad = joined_gradients(feats, edges, returned, out_grad, short_filter, owned)
        return (mixed, grad, filter_grad)

    cotangent = out_grad.T
    feats, product, conv_grad = features_of(turned, rim, short_filter, cotangent)

    def exchange(block):
        pieces = block.reshape(devices, owned, local_len)
        return lax.all_to_all(pieces, EVERYONE, split_axis=0, concat_axis=0, tiled=True)

    filters = transform_filters(long_filter, tables, seq_len)
    prod_chan = exchange(product)
    conv_grad, prod_chan = lax.optimization_barrier((conv_grad, prod_chan))
    grad_chan = exchange(conv_grad)
    conv_chan, prod_spec = filtered(prod_chan, filters, tables, seq_len)
    conv_chan, grad_chan = lax.optimization_barrier((conv_chan, grad_chan))
    conv_tok = exchange(conv_chan)
    back_chan, cross = filtered(grad_chan, filters, tables, seq_len, prod_spec)
    back_chan, conv_tok = lax.optimization_barrier((back_chan, conv_tok))
    back_tok = exchange(back_chan)

    filter_grad = filter_gradient(cross, tables, seq_len)
    mixed, grad_q, rim_q = query_products(feats, conv_tok.reshape(width, local_len), cotangent)
    grad = query_gradient(grad_q, shifted(rim_q, EVERYONE, -1), short_filter)
    filter_grad, mixed, grad, back_tok = lax.optimization_barrier((filter_grad, mixed, grad, back_tok))

    grad_kv, rim_kv = key_value_products(feats, back_tok.reshape(width, local_len))
    grad = key_value_gradient(grad, grad_kv, shifted(rim_kv, EVERYONE, -1), short_filter)
    return (mixed, grad, filter_grad)


def solution(mesh):
    placed = (P(None, EVERYONE), P(), P(EVERYONE, None), P(None, EVERYONE))
    return jax.shard_map(
        shards,
        mesh=mesh,
        in_specs=placed,
        out_specs=(P(None, EVERYONE), P(None, EVERYONE), P(EVERYONE, None)),
        check_vma=False,
    )
```

```python
import math

import jax
import jax.numpy as jnp
import numpy as np
from jax import lax
from jax.experimental import pallas as pl
from jax.experimental.pallas import tpu as pltpu
from jax.sharding import PartitionSpec as P

CPG = 4
TAPS = 7
PAIRS = CPG // 2
EVERYONE = ("dp", "ctx")
VMEM_LIMIT = 24 * 1024 * 1024
VMEM_MOST = 62 * 1024 * 1024


def shifted(value, axis, steps):
    count = lax.axis_size(axis)
    first, last = (max(0, -steps), min(count, count - steps))
    return lax.ppermute(value, axis, [(source, source + steps) for source in range(first, last)])


def sizes_of(seq_len):
    padded = 2 * seq_len
    inner = max(d for d in range(1, seq_len + 1) if seq_len % d == 0 and d * d <= padded)
    return padded, inner, padded // inner


def table(count_out, count_in, period):
    turns = np.arange(count_out, dtype=np.int64)[:, None] * np.arange(count_in, dtype=np.int64)
    angle = (turns % period).astype(np.float64) * (2.0 * math.pi / period)
    return np.cos(angle), np.sin(angle)


def make_tables(seq_len, sources):
    padded, inner, outer = sizes_of(seq_len)
    half = outer // 2
    fold = half // sources
    order = np.arange(half).reshape(sources, fold).T.reshape(-1)
    cos_o, sin_o = table(outer, half, outer)
    cos_i, sin_i = table(inner, inner, inner)
    cos_p, sin_p = cos_o[:, order], sin_o[:, order]
    narrow = lambda blocks: jnp.asarray(np.block(blocks).astype(np.float32)).astype(jnp.bfloat16)
    twist = [jnp.asarray(t.astype(np.float32)) for t in table(outer, inner, padded)]
    return {
        "first": narrow([[cos_p, sin_p], [-sin_p, cos_p]]),
        "second": narrow([[cos_i, -sin_i], [sin_i, cos_i]]),
        "third": narrow([[cos_i, sin_i], [-sin_i, cos_i]]),
        "fourth": narrow([[cos_p.T, -sin_p.T], [sin_p.T, cos_p.T]]),
        "fourth_scaled": narrow([[cos_p.T / padded, -sin_p.T / padded], [sin_p.T / padded, cos_p.T / padded]]),
        "first_real": narrow([[cos_o], [-sin_o]]),
        "fourth_real": narrow([[cos_o.T, -sin_o.T]]),
        "twist_re": twist[0],
        "twist_im": twist[1],
    }


LANES = 128


def spread(tall, count, stride, first, height, width):
    tiles = [tall[pl.ds(t * height + first, count, stride=stride), :] for t in range(width[0] // LANES, width[1] // LANES)]
    return tiles[0] if len(tiles) == 1 else jnp.concatenate(tiles, axis=1)


def put_spread(tall, values, stride, first, height, width):
    for i, t in enumerate(range(width[0] // LANES, width[1] // LANES)):
        tall[pl.ds(t * height + first, values.shape[0], stride=stride), :] = values[:, i * LANES : (i + 1) * LANES]


def dot(left, right):
    return jnp.dot(left, right, preferred_element_type=jnp.float32)


def transform_filters(long_filter, tables, seq_len):
    padded, inner, outer = sizes_of(seq_len)
    half = outer // 2
    groups = long_filter.shape[0]
    scale = seq_len ** -0.5

    def kernel(x_ref, first_ref, second_ref, tr_ref, ti_ref, out_ref, tall):
        height = half * groups
        for b in range(half):
            for t in range(inner // LANES):
                at = t * height + b * groups
                lanes = slice(b * inner + t * LANES, b * inner + (t + 1) * LANES)
                tall[at : at + groups, :] = x_ref[:, lanes].astype(jnp.float32)
        for g in range(groups):
            x = spread(tall, half, groups, g, height, (0, inner)).astype(jnp.bfloat16)
            f = dot(first_ref[...], x)
            f_re, f_im = f[:outer], f[outer:]
            g_re = (f_re * tr_ref[...] + f_im * ti_ref[...]).astype(jnp.bfloat16)
            g_im = (f_im * tr_ref[...] - f_re * ti_ref[...]).astype(jnp.bfloat16)
            spec = dot(g_re, second_ref[:inner]) + dot(g_im, second_ref[inner:])
            out_ref[g * outer : (g + 1) * outer, :] = spec * scale

    return pl.pallas_call(
        kernel,
        name="filter_dft",
        out_shape=jax.ShapeDtypeStruct((groups * outer, 2 * inner), jnp.float32),
        scratch_shapes=[pltpu.VMEM((half * groups * inner // LANES, LANES), jnp.float32)],
        compiler_params=pltpu.CompilerParams(vmem_limit_bytes=VMEM_LIMIT),
        cost_estimate=pl.CostEstimate(flops=200_000_000, bytes_accessed=2_000_000, transcendentals=0),
    )(long_filter, tables["first_real"], tables["second"], tables["twist_re"], tables["twist_im"])


def filtered(arrived, filters, tables, seq_len, other=None):
    padded, inner, outer = sizes_of(seq_len)
    half = outer // 2
    sources, channels, local = arrived.shape
    fold = local // inner
    groups = channels // CPG
    backward = other is not None

    def kernel(*refs):
        if backward:
            (x_ref, f_ref, k_ref, first_ref, second_ref, third_ref, fourth_ref, tr_ref, ti_ref,
             y_ref, cross_ref, tall, wide, stage, turn) = refs
        else:
            (x_ref, f_ref, first_ref, second_ref, third_ref, fourth_ref, tr_ref, ti_ref,
             y_ref, z_ref, tall, wide, stage, turn) = refs
        height = sources * channels
        for t in range(local // LANES):
            block = x_ref[:, :, t * LANES : (t + 1) * LANES].astype(jnp.float32)
            tall[t * height : (t + 1) * height, :] = block.reshape(height, LANES)
        for c in range(channels):
            pair, part = divmod(c, 2)
            for h in range(fold):
                rows = spread(tall, sources, channels, c, height, (h * inner, (h + 1) * inner))
                at = part * half + h * sources
                wide[at : at + sources, pair * inner : (pair + 1) * inner] = rows.astype(jnp.bfloat16)
        for g in range(groups):
            span = PAIRS * inner
            f = dot(first_ref[...], wide[:, g * span : (g + 1) * span])
            for p in range(PAIRS):
                f_re = f[:outer, p * inner : (p + 1) * inner]
                f_im = f[outer:, p * inner : (p + 1) * inner]
                at = (g * PAIRS + p) * outer
                stage[at : at + outer, :inner] = (f_re * tr_ref[...] + f_im * ti_ref[...]).astype(jnp.bfloat16)
                stage[at : at + outer, inner:] = (f_im * tr_ref[...] - f_re * ti_ref[...]).astype(jnp.bfloat16)
        for g in range(groups):
            s_re = f_ref[g * outer : (g + 1) * outer, :inner]
            s_im = f_ref[g * outer : (g + 1) * outer, inner:]
            cross_re = cross_im = None
            for p in range(PAIRS):
                at = (g * PAIRS + p) * outer
                z = dot(stage[at : at + outer, :], second_ref[...])
                z_re, z_im = z[:, :inner], z[:, inner:]
                if backward:
                    k_re = k_ref[at : at + outer, :inner].astype(jnp.float32)
                    k_im = k_ref[at : at + outer, inner:].astype(jnp.float32)
                    part_re = k_re * z_re + k_im * z_im
                    part_im = k_re * z_im - k_im * z_re
                    cross_re = part_re if cross_re is None else cross_re + part_re
                    cross_im = part_im if cross_im is None else cross_im + part_im
                    o_re = s_re * z_re + s_im * z_im
                    o_im = s_re * z_im - s_im * z_re
                else:
                    z_ref[at : at + outer, :] = z
                    o_re = s_re * z_re - s_im * z_im
                    o_im = s_re * z_im + s_im * z_re
                stage[at : at + outer, :inner] = o_re.astype(jnp.bfloat16)
                stage[at : at + outer, inner:] = o_im.astype(jnp.bfloat16)
            if backward:
                cross_ref[g * outer : (g + 1) * outer, :inner] = cross_re.astype(jnp.bfloat16)
                cross_ref[g * outer : (g + 1) * outer, inner:] = cross_im.astype(jnp.bfloat16)
        for pair in range(groups * PAIRS):
            at = pair * outer
            h = dot(stage[at : at + outer, :], third_ref[...])
            h_re, h_im = h[:, :inner], h[:, inner:]
            lanes = slice(pair * inner, (pair + 1) * inner)
            turn[:outer, lanes] = (h_re * tr_ref[...] - h_im * ti_ref[...]).astype(jnp.bfloat16)
            turn[outer:, lanes] = (h_im * tr_ref[...] + h_re * ti_ref[...]).astype(jnp.bfloat16)
        for g in range(groups):
            span = PAIRS * inner
            y = dot(fourth_ref[...], turn[:, g * span : (g + 1) * span]) * (1.0 / padded)
            for p in range(PAIRS):
                for part in range(2):
                    c = (g * PAIRS + p) * 2 + part
                    for h in range(fold):
                        at = part * half + h * sources
                        rows = y[at : at + sources, p * inner : (p + 1) * inner]
                        put_spread(tall, rows, channels, c, height, (h * inner, (h + 1) * inner))
        for t in range(local // LANES):
            block = tall[t * height : (t + 1) * height, :].reshape(sources, channels, LANES)
            y_ref[:, :, t * LANES : (t + 1) * LANES] = block.astype(jnp.bfloat16)

    pairs = groups * PAIRS
    if backward:
        extra = jax.ShapeDtypeStruct((groups * outer, 2 * inner), jnp.bfloat16)
    else:
        extra = jax.ShapeDtypeStruct((pairs * outer, 2 * inner), jnp.float32)
    operands = [arrived, filters] + ([other] if backward else [])
    operands += [tables[n] for n in ("first", "second", "third", "fourth", "twist_re", "twist_im")]
    return pl.pallas_call(
        kernel,
        name="correlate" if backward else "convolve",
        out_shape=(jax.ShapeDtypeStruct(arrived.shape, jnp.bfloat16), extra),
        scratch_shapes=[
            pltpu.VMEM((sources * channels * local // LANES, LANES), jnp.float32),
            pltpu.VMEM((outer, pairs * inner), jnp.bfloat16),
            pltpu.VMEM((pairs * outer, 2 * inner), jnp.bfloat16),
            pltpu.VMEM((2 * outer, pairs * inner), jnp.bfloat16),
        ],
        compiler_params=pltpu.CompilerParams(vmem_limit_bytes=VMEM_LIMIT),
        cost_estimate=pl.CostEstimate(flops=2_000_000_000, bytes_accessed=5_000_000, transcendentals=0),
    )(*operands)


def filter_gradient(cross, tables, seq_len):
    padded, inner, outer = sizes_of(seq_len)
    half = outer // 2
    groups = cross.shape[0] // outer
    scale = seq_len ** -0.5 / padded

    def kernel(s_ref, third_ref, fourth_ref, tr_ref, ti_ref, out_ref, tall, turn):
        for g in range(groups):
            h = dot(s_ref[g * outer : (g + 1) * outer, :], third_ref[...])
            h_re, h_im = h[:, :inner], h[:, inner:]
            turn[:outer, g * inner : (g + 1) * inner] = (h_re * tr_ref[...] - h_im * ti_ref[...]).astype(jnp.bfloat16)
            turn[outer:, g * inner : (g + 1) * inner] = (h_im * tr_ref[...] + h_re * ti_ref[...]).astype(jnp.bfloat16)
        for g in range(groups):
            y = dot(fourth_ref[...], turn[:, g * inner : (g + 1) * inner]) * scale
            put_spread(tall, y, groups, g, half * groups, (0, inner))
        for b in range(half):
            for t in range(inner // LANES):
                at = (t * half + b) * groups
                out_ref[:, b * inner + t * LANES : b * inner + (t + 1) * LANES] = tall[at : at + groups, :]

    return pl.pallas_call(
        kernel,
        name="filter_gradient",
        out_shape=jax.ShapeDtypeStruct((groups, seq_len), jnp.float32),
        scratch_shapes=[
            pltpu.VMEM((half * groups * inner // LANES, LANES), jnp.float32),
            pltpu.VMEM((2 * outer, groups * inner), jnp.bfloat16),
        ],
        compiler_params=pltpu.CompilerParams(vmem_limit_bytes=VMEM_LIMIT),
        cost_estimate=pl.CostEstimate(flops=200_000_000, bytes_accessed=2_000_000, transcendentals=0),
    )(cross, tables["third"], tables["fourth_real"], tables["twist_re"], tables["twist_im"])


RIM = 8


def seven_taps(tall, value, rim, weights, forward):
    count = value.shape[0]
    if forward:
        tall[:RIM, :] = rim
        tall[RIM : RIM + count, :] = value
    else:
        tall[:count, :] = value
        tall[count : count + RIM, :] = rim
    total = value * weights[:1]
    for lag in range(1, TAPS):
        first = RIM - lag if forward else lag
        total = total + tall[first : first + count, :] * weights[lag : lag + 1]
    return total


def lane_block(i, offset=0):
    return pl.ds(pl.multiple_of(i * LANES + offset, LANES), LANES)


def whole_call(kernel, name, out_shape, operands, scratch=(), flops=10_000_000, limit=VMEM_LIMIT, **kwargs):
    return pl.pallas_call(
        kernel,
        name=name,
        out_shape=out_shape,
        scratch_shapes=list(scratch),
        compiler_params=pltpu.CompilerParams(vmem_limit_bytes=limit),
        cost_estimate=pl.CostEstimate(flops=flops, bytes_accessed=4_000_000, transcendentals=0),
        **kwargs,
    )(*operands)


def narrow_shape(*shape):
    return jax.ShapeDtypeStruct(shape, jnp.bfloat16)


def features_of(turned, rim, short_filter, cotangent):
    local, width = cotangent.shape

    def kernel(x_ref, rim_ref, w_ref, og_ref, f_ref, kv_ref, dconv_ref, tall):
        @pl.loop(0, width // LANES)
        def _(i):
            made = []
            for part in range(3):
                lanes = lane_block(i, part * width)
                total = seven_taps(
                    tall.at[part],
                    x_ref[:, lanes].astype(jnp.float32),
                    rim_ref[:, lanes].astype(jnp.float32),
                    w_ref[:, lanes].astype(jnp.float32),
                    True,
                ).astype(jnp.bfloat16)
                f_ref[:, lanes] = total
                made.append(total.astype(jnp.float32))
            rows = lane_block(i)
            kv_ref[rows, :] = (made[1] * made[2]).astype(jnp.bfloat16).T
            og = og_ref[:, rows].astype(jnp.float32)
            dconv_ref[rows, :] = (og * made[0]).astype(jnp.bfloat16).T

    return whole_call(
        kernel,
        "features",
        (narrow_shape(local, 3 * width), narrow_shape(width, local), narrow_shape(width, local)),
        (turned, rim, short_filter, cotangent),
        [pltpu.VMEM((3, local + RIM, LANES), jnp.float32)],
    )


def query_products(feats, conv, cotangent):
    width, local = conv.shape

    def kernel(f_ref, conv_ref, og_ref, mixed_ref, dq_ref, rim_ref):
        @pl.loop(0, width // LANES)
        def _(i):
            lanes = lane_block(i)
            here = conv_ref[lanes, :].T.astype(jnp.float32)
            mixed_ref[lanes, :] = (f_ref[:, lanes].astype(jnp.float32) * here).astype(jnp.bfloat16).T
            dq = (og_ref[:, lanes].astype(jnp.float32) * here).astype(jnp.bfloat16)
            dq_ref[:, lanes] = dq
            rim_ref[:, lanes] = dq[:RIM]

    return whole_call(
        kernel,
        "query_products",
        (narrow_shape(width, local), narrow_shape(local, width), narrow_shape(RIM, width)),
        (feats, conv, cotangent),
    )


def key_value_products(feats, back):
    width, local = back.shape

    def kernel(f_ref, back_ref, d_ref, rim_ref):
        @pl.loop(0, width // LANES)
        def _(i):
            here = back_ref[lane_block(i), :].T.astype(jnp.float32)
            for part in range(2):
                other = f_ref[:, lane_block(i, (2 - part) * width)].astype(jnp.float32)
                grad = (here * other).astype(jnp.bfloat16)
                d_ref[:, lane_block(i, part * width)] = grad
                rim_ref[:, lane_block(i, part * width)] = grad[:RIM]

    return whole_call(
        kernel,
        "key_value_products",
        (narrow_shape(local, 2 * width), narrow_shape(RIM, 2 * width)),
        (feats, back),
    )


def joined_features(turned, rim, short_filter, out_grad, owned):
    width, local = out_grad.shape
    near = LANES // owned
    blocks = width // LANES

    def kernel(x_ref, rim_ref, w_ref, og_ref, f_ref, msg_ref, edge_ref, tall, made, edge, sent):
        def copy(i):
            to = pl.ds(i * near, near)
            return pltpu.make_async_copy(made.at[to], msg_ref.at[to], sent.at[i])

        @pl.loop(0, blocks)
        def _(i):
            parts = []
            for part in range(3):
                lanes = lane_block(i, part * width)
                total = seven_taps(
                    tall.at[part],
                    x_ref[:, lanes].astype(jnp.float32),
                    rim_ref[:, lanes].astype(jnp.float32),
                    w_ref[:, lanes].astype(jnp.float32),
                    True,
                ).astype(jnp.bfloat16)
                f_ref[3 * i + part] = total
                if part:
                    edge[:, lanes] = total[:RIM]
                parts.append(total.astype(jnp.float32))
            og = og_ref[lane_block(i), :].T
            edge[:, lane_block(i)] = og[:RIM]
            kv = (parts[1] * parts[2]).astype(jnp.bfloat16).T
            dconv = (og.astype(jnp.float32) * parts[0]).astype(jnp.bfloat16).T
            to = pl.ds(i * near, near)
            made[to, :owned, :] = kv.reshape(near, owned, local)
            made[to, owned:, :] = dconv.reshape(near, owned, local)
            copy(i).start()

        last = pltpu.make_async_copy(edge, edge_ref, sent.at[blocks])
        last.start()

        @pl.loop(0, blocks)
        def _(i):
            copy(i).wait()

        last.wait()

    vmem = pl.BlockSpec(memory_space=pltpu.VMEM)
    hbm = pl.BlockSpec(memory_space=pltpu.HBM)
    devices = width // owned
    return whole_call(
        kernel,
        "joined_features",
        (
            narrow_shape(3 * blocks, local, LANES),
            narrow_shape(devices, 2 * owned, local),
            narrow_shape(RIM, 3 * width),
        ),
        (turned, rim, short_filter, out_grad),
        [
            pltpu.VMEM((3, local + RIM, LANES), jnp.float32),
            pltpu.VMEM((devices, 2 * owned, local), jnp.bfloat16),
            pltpu.VMEM((RIM, 3 * width), jnp.bfloat16),
            pltpu.SemaphoreType.DMA((blocks + 1,)),
        ],
        in_specs=[vmem] * 4,
        out_specs=(vmem, hbm, hbm),
    )


def joined_filtering(arrived, filters, tables, seq_len):
    padded, inner, outer = sizes_of(seq_len)
    half = outer // 2
    sources, rows, local = arrived.shape
    channels = rows // 2
    tiles = local // LANES
    fold = local // inner
    groups = channels // CPG
    pairs = groups * PAIRS
    height = sources * channels
    chunk = sources // 4

    def kernel(x_hbm, *refs):
        sources_hbm, (y_hbm, cross_hbm), held = refs[:7], refs[7:9], refs[9:16]
        y_ref, cross_ref, x_ref, talls, wides, stages, turns, sems, fetched = refs[16:]
        arrivals = []
        for s in range(2):
            rows = slice(s * channels, (s + 1) * channels)
            for half_sources in range(2):
                to = slice(half_sources * sources // 2, (half_sources + 1) * sources // 2)
                arrivals.append(
                    pltpu.make_async_copy(x_hbm.at[to, rows, :], x_ref.at[to, rows, :], fetched.at[7 + len(arrivals)])
                )
        for arrival in arrivals[:2]:
            arrival.start()
        first_ref, tr_ref, ti_ref, second_ref, f_ref, third_ref, fourth_ref = held
        fetches = [pltpu.make_async_copy(a, b, fetched.at[n]) for n, (a, b) in enumerate(zip(sources_hbm, held))]
        for fetch in fetches[:3] + arrivals[2:] + fetches[3:]:
            fetch.start()
        for s in range(2):
            tall, wide, stage = talls.at[s], wides.at[s], stages.at[s]
            arrivals[2 * s].wait()
            arrivals[2 * s + 1].wait()
            for t in range(tiles):
                block = x_ref[:, s * channels : (s + 1) * channels, t * LANES : (t + 1) * LANES]
                tall[t * height : (t + 1) * height, :] = block.astype(jnp.float32).reshape(height, LANES)
            for c in range(channels):
                pair, part = divmod(c, 2)
                for h in range(fold):
                    line = spread(tall, sources, channels, c, height, (h * inner, (h + 1) * inner))
                    at = part * half + h * sources
                    wide[at : at + sources, pair * inner : (pair + 1) * inner] = line.astype(jnp.bfloat16)
            if s == 0:
                for fetch in fetches[:3]:
                    fetch.wait()
                tr, ti = tr_ref[...], ti_ref[...]
            for g in range(groups):
                span = PAIRS * inner
                f = dot(first_ref[...], wide[:, g * span : (g + 1) * span])
                for p in range(PAIRS):
                    f_re = f[:outer, p * inner : (p + 1) * inner]
                    f_im = f[outer:, p * inner : (p + 1) * inner]
                    at = (g * PAIRS + p) * outer
                    stage[at : at + outer, :inner] = (f_re * tr + f_im * ti).astype(jnp.bfloat16)
                    stage[at : at + outer, inner:] = (f_im * tr - f_re * ti).astype(jnp.bfloat16)
        for fetch in fetches[3:]:
            fetch.wait()
        for g in range(groups):
            s_re = f_ref[g * outer : (g + 1) * outer, :inner]
            s_im = f_ref[g * outer : (g + 1) * outer, inner:]
            cross_re = cross_im = 0.0
            for p in range(PAIRS):
                at = (g * PAIRS + p) * outer
                k = dot(stages[0, at : at + outer, :], second_ref[...])
                d = dot(stages[1, at : at + outer, :], second_ref[...])
                k_re, k_im = k[:, :inner], k[:, inner:]
                d_re, d_im = d[:, :inner], d[:, inner:]
                cross_re = cross_re + (k_re * d_re + k_im * d_im)
                cross_im = cross_im + (k_re * d_im - k_im * d_re)
                stages[0, at : at + outer, :inner] = (s_re * k_re - s_im * k_im).astype(jnp.bfloat16)
                stages[0, at : at + outer, inner:] = (s_re * k_im + s_im * k_re).astype(jnp.bfloat16)
                stages[1, at : at + outer, :inner] = (s_re * d_re + s_im * d_im).astype(jnp.bfloat16)
                stages[1, at : at + outer, inner:] = (s_re * d_im - s_im * d_re).astype(jnp.bfloat16)
            cross_ref[g * outer : (g + 1) * outer, :inner] = cross_re.astype(jnp.bfloat16)
            cross_ref[g * outer : (g + 1) * outer, inner:] = cross_im.astype(jnp.bfloat16)
        copies = [pltpu.make_async_copy(cross_ref, cross_hbm, sems.at[4])]
        copies[0].start()
        spot = lax.broadcasted_iota(jnp.int32, (RIM, LANES), 0)
        lane = lax.broadcasted_iota(jnp.int32, (RIM, LANES), 1)
        pick = jnp.where(spot == lane, 1.0, 0.0).astype(jnp.bfloat16)
        rims = []
        for s in range(2):
            tall, stage, turn = talls.at[s], stages.at[s], turns.at[s]
            for pair in range(pairs):
                at = pair * outer
                h = dot(stage[at : at + outer, :], third_ref[...])
                h_re, h_im = h[:, :inner], h[:, inner:]
                lanes = slice(pair * inner, (pair + 1) * inner)
                turn[:outer, lanes] = (h_re * tr - h_im * ti).astype(jnp.bfloat16)
                turn[outer:, lanes] = (h_im * tr + h_re * ti).astype(jnp.bfloat16)
            for g in range(groups):
                span = PAIRS * inner
                y = dot(fourth_ref[...], turn[:, g * span : (g + 1) * span])
                for p in range(PAIRS):
                    for part in range(2):
                        c = (g * PAIRS + p) * 2 + part
                        for h in range(fold):
                            at = part * half + h * sources
                            line = y[at : at + sources, p * inner : (p + 1) * inner]
                            put_spread(tall, line, channels, c, height, (h * inner, (h + 1) * inner))
            first = tall[:height, :].astype(jnp.bfloat16)
            rims.append(
                lax.dot_general(pick, first, (((1,), (1,)), ((), ())), preferred_element_type=jnp.float32)
            )
        for q in range(4):
            to = slice(q * chunk, (q + 1) * chunk)
            for s in range(2):
                for t in range(tiles):
                    at = t * height + q * chunk * channels
                    block = talls[s, at : at + chunk * channels, :].reshape(chunk, channels, LANES)
                    row = (s * tiles + t) * channels
                    y_ref[to, row : row + channels, :] = block.astype(jnp.bfloat16)
            for d in range(q * chunk, (q + 1) * chunk):
                tile, lanes = divmod((d + 1) % sources * channels, LANES)
                edge = jnp.zeros((RIM, LANES), jnp.float32)
                if d < sources - 1:
                    for s in range(2):
                        piece = rims[s][:, tile * LANES : (tile + 1) * LANES]
                        turn_by = (s * channels - lanes) % LANES
                        if turn_by:
                            piece = pltpu.roll(piece, turn_by, 1)
                        edge = piece if s == 0 else jnp.where(lane < channels, edge, piece)
                y_ref[d, 2 * tiles * channels :, :] = edge.astype(jnp.bfloat16)
            copies.append(pltpu.make_async_copy(y_ref.at[to], y_hbm.at[to], sems.at[q]))
            copies[-1].start()
        for copy in copies:
            copy.wait()

    sent = (sources, 2 * tiles * channels + RIM, LANES)
    hbm = pl.BlockSpec(memory_space=pltpu.HBM)
    fetched = [tables[n] for n in ("first", "twist_re", "twist_im", "second")] + [filters]
    fetched += [tables[n] for n in ("third", "fourth_scaled")]
    return whole_call(
        kernel,
        "joined_filtering",
        (narrow_shape(*sent), narrow_shape(groups * outer, 2 * inner)),
        [arrived] + fetched,
        [pltpu.VMEM(array.shape, array.dtype) for array in fetched]
        + [
            pltpu.VMEM(sent, jnp.bfloat16),
            pltpu.VMEM((groups * outer, 2 * inner), jnp.bfloat16),
            pltpu.VMEM(arrived.shape, jnp.bfloat16),
            pltpu.VMEM((2, tiles * height, LANES), jnp.float32),
            pltpu.VMEM((2, outer, pairs * inner), jnp.bfloat16),
            pltpu.VMEM((2, pairs * outer, 2 * inner), jnp.bfloat16),
            pltpu.VMEM((2, 2 * outer, pairs * inner), jnp.bfloat16),
            pltpu.SemaphoreType.DMA((5,)),
            pltpu.SemaphoreType.DMA((11,)),
        ],
        flops=4_000_000_000,
        limit=VMEM_MOST,
        in_specs=[hbm] * 8,
        out_specs=(hbm, hbm),
    )


def joined_gradients(feats, edges, returned, out_grad, short_filter, owned):
    width, local = out_grad.shape
    tiles = local // LANES
    near = LANES // owned
    blocks = width // LANES

    def kernel(f_hbm, edge_hbm, back_hbm, og_hbm, w_hbm, mixed_ref, out_ref,
               tall, made, f_ref, edge_ref, back_ref, og_ref, w_ref, sent, fetched):
        def fetch(i):
            to = pl.ds(3 * i, 3)
            rows = lane_block(i)
            held = pl.ds(i * near, near)
            return (
                pltpu.make_async_copy(back_hbm.at[held], back_ref.at[held], fetched.at[2 * blocks + i]),
                pltpu.make_async_copy(f_hbm.at[to], f_ref.at[to], fetched.at[i]),
                pltpu.make_async_copy(og_hbm.at[rows, :], og_ref.at[rows, :], fetched.at[blocks + i]),
            )

        small = [
            pltpu.make_async_copy(edge_hbm, edge_ref, fetched.at[3 * blocks]),
            pltpu.make_async_copy(w_hbm, w_ref, fetched.at[3 * blocks + 1]),
        ]
        for one in small:
            one.start()

        @pl.loop(0, blocks)
        def _(i):
            for one in fetch(i):
                one.start()

        lane = lax.broadcasted_iota(jnp.int32, (RIM, LANES), 1)
        for one in small:
            one.wait()

        def copy(part, i):
            at = part * blocks + i
            if part < 3:
                to = out_ref.at[pl.ds(pl.multiple_of(at * LANES, LANES), LANES), :]
            else:
                to = mixed_ref.at[lane_block(i), :]
            return pltpu.make_async_copy(made.at[at], to, sent.at[at])

        @pl.loop(0, blocks)
        def _(i):
            for one in fetch(i):
                one.wait()
            held = pl.ds(i * near, near)
            sums = []
            for s in range(2):
                turned = [
                    back_ref[held, (s * tiles + t) * owned : (s * tiles + t + 1) * owned, :].reshape(LANES, LANES).T
                    for t in range(tiles)
                ]
                here = jnp.concatenate(turned, axis=0).astype(jnp.float32)
                rim = jnp.zeros((RIM, LANES), jnp.float32)
                for n in range(near):
                    piece = back_ref[i * near + n, 2 * tiles * owned :, :].astype(jnp.float32)
                    turn_by = (n - s) * owned % LANES
                    if turn_by:
                        piece = pltpu.roll(piece, turn_by, 1)
                    rim = jnp.where(lane >= n * owned, piece, rim) if n else piece
                sums.append((here, rim))
            query = f_ref[3 * i].astype(jnp.float32)
            made[3 * blocks + i] = (query * sums[0][0]).astype(jnp.bfloat16).T
            copy(3, i).start()
            for part in range(3):
                here, rim = sums[min(part, 1)]
                if part == 0:
                    other = og_ref[lane_block(i), :].T
                else:
                    other = f_ref[3 * i + 3 - part]
                edge = edge_ref[:, lane_block(i, (3 - part) % 3 * width)].astype(jnp.float32)
                grad = (here * other.astype(jnp.float32)).astype(jnp.bfloat16)
                total = seven_taps(
                    tall.at[part],
                    grad.astype(jnp.float32),
                    (rim * edge).astype(jnp.bfloat16).astype(jnp.float32),
                    w_ref[:, lane_block(i, part * width)].astype(jnp.float32),
                    False,
                )
                made[part * blocks + i] = total.astype(jnp.bfloat16).T
                copy(part, i).start()

        @pl.loop(0, blocks)
        def _(i):
            for part in range(4):
                copy(part, i).wait()

    hbm = pl.BlockSpec(memory_space=pltpu.HBM)
    return whole_call(
        kernel,
        "joined_gradients",
        (narrow_shape(width, local), narrow_shape(3 * width, local)),
        (feats, edges, returned, out_grad, short_filter),
        [
            pltpu.VMEM((3, local + RIM, LANES), jnp.float32),
            pltpu.VMEM((4 * blocks, LANES, local), jnp.bfloat16),
            pltpu.VMEM((3 * blocks, local, LANES), jnp.bfloat16),
            pltpu.VMEM(edges.shape, jnp.bfloat16),
            pltpu.VMEM(returned.shape, jnp.bfloat16),
            pltpu.VMEM((width, local), jnp.bfloat16),
            pltpu.VMEM(short_filter.shape, jnp.bfloat16),
            pltpu.SemaphoreType.DMA((4 * blocks,)),
            pltpu.SemaphoreType.DMA((3 * blocks + 2,)),
        ],
        limit=VMEM_MOST,
        in_specs=[hbm] * 5,
        out_specs=(hbm, hbm),
    )


def query_gradient(grad, rim, short_filter):
    local, width = grad.shape
    steps = width // GRAD_ROWS

    def kernel(d_ref, rim_ref, w_ref, out_ref, tall):
        gradient_block(d_ref, rim_ref, w_ref, out_ref, tall)

    return gradient_call(kernel, "query_gradient", (), grad, rim, short_filter, 1, 0)


def key_value_gradient(whole, grad, rim, short_filter):
    def kernel(_, d_ref, rim_ref, w_ref, out_ref, tall):
        gradient_block(d_ref, rim_ref, w_ref, out_ref, tall)

    return gradient_call(kernel, "key_value_gradient", (whole,), grad, rim, short_filter, 2, 1)


GRAD_ROWS = 512


def gradient_block(d_ref, rim_ref, w_ref, out_ref, tall):
    for c in range(GRAD_ROWS // LANES):
        lanes = slice(c * LANES, (c + 1) * LANES)
        total = seven_taps(
            tall.at[c],
            d_ref[:, lanes].astype(jnp.float32),
            rim_ref[:, lanes].astype(jnp.float32),
            w_ref[:, lanes].astype(jnp.float32),
            False,
        )
        out_ref[lanes, :] = total.astype(jnp.bfloat16).T


def gradient_call(kernel, name, whole, grad, rim, short_filter, parts, first):
    local, lanes = grad.shape
    width = lanes // parts
    steps = width // GRAD_ROWS
    return pl.pallas_call(
        kernel,
        name=name,
        grid=(parts * steps,),
        in_specs=[pl.BlockSpec(memory_space=pl.ANY)] * len(whole)
        + [
            pl.BlockSpec((local, GRAD_ROWS), lambda i: (0, i)),
            pl.BlockSpec((RIM, GRAD_ROWS), lambda i: (0, i)),
            pl.BlockSpec((TAPS, GRAD_ROWS), lambda i: (0, first * steps + i)),
        ],
        out_specs=pl.BlockSpec((GRAD_ROWS, local), lambda i: (first * steps + i, 0)),
        out_shape=narrow_shape(3 * width, local),
        scratch_shapes=[pltpu.VMEM((GRAD_ROWS // LANES, local + RIM, LANES), jnp.float32)],
        input_output_aliases={0: 0} if whole else {},
        cost_estimate=pl.CostEstimate(flops=20_000_000, bytes_accessed=4_000_000, transcendentals=0),
    )(*whole, grad, rim, short_filter)


def shards(projections, short_filter, long_filter, out_grad):
    width, local_len = out_grad.shape
    devices = lax.axis_size(EVERYONE)
    seq_len = local_len * devices
    owned = width // devices
    tables = make_tables(seq_len, devices)

    turned = projections.T
    rim = shifted(turned[local_len - RIM :], EVERYONE, 1)

    if owned % 16 == 0 and LANES % (2 * owned) == 0 and devices % 4 == 0:
        feats, message, edges = joined_features(turned, rim, short_filter, out_grad, owned)
        filters = transform_filters(long_filter, tables, seq_len)
        arrived = lax.all_to_all(message, EVERYONE, split_axis=0, concat_axis=0, tiled=True)
        edges, filters, arrived = lax.optimization_barrier((shifted(edges, EVERYONE, -1), filters, arrived))
        answer, cross = joined_filtering(arrived, filters, tables, seq_len)
        returned = lax.all_to_all(answer, EVERYONE, split_axis=0, concat_axis=0, tiled=True)
        filter_grad = filter_gradient(cross, tables, seq_len)
        filter_grad, returned = lax.optimization_barrier((filter_grad, returned))
        mixed, grad = joined_gradients(feats, edges, returned, out_grad, short_filter, owned)
        return (mixed, grad, filter_grad)

    cotangent = out_grad.T
    feats, product, conv_grad = features_of(turned, rim, short_filter, cotangent)

    def exchange(block):
        pieces = block.reshape(devices, owned, local_len)
        return lax.all_to_all(pieces, EVERYONE, split_axis=0, concat_axis=0, tiled=True)

    filters = transform_filters(long_filter, tables, seq_len)
    prod_chan = exchange(product)
    conv_grad, prod_chan = lax.optimization_barrier((conv_grad, prod_chan))
    grad_chan = exchange(conv_grad)
    conv_chan, prod_spec = filtered(prod_chan, filters, tables, seq_len)
    conv_chan, grad_chan = lax.optimization_barrier((conv_chan, grad_chan))
    conv_tok = exchange(conv_chan)
    back_chan, cross = filtered(grad_chan, filters, tables, seq_len, prod_spec)
    back_chan, conv_tok = lax.optimization_barrier((back_chan, conv_tok))
    back_tok = exchange(back_chan)

    filter_grad = filter_gradient(cross, tables, seq_len)
    mixed, grad_q, rim_q = query_products(feats, conv_tok.reshape(width, local_len), cotangent)
    grad = query_gradient(grad_q, shifted(rim_q, EVERYONE, -1), short_filter)
    filter_grad, mixed, grad, back_tok = lax.optimization_barrier((filter_grad, mixed, grad, back_tok))

    grad_kv, rim_kv = key_value_products(feats, back_tok.reshape(width, local_len))
    grad = key_value_gradient(grad, grad_kv, shifted(rim_kv, EVERYONE, -1), short_filter)
    return (mixed, grad, filter_grad)


def solution(mesh):
    placed = (P(None, EVERYONE), P(), P(EVERYONE, None), P(None, EVERYONE))
    return jax.shard_map(
        shards,
        mesh=mesh,
        in_specs=placed,
        out_specs=(P(None, EVERYONE), P(None, EVERYONE), P(EVERYONE, None)),
        check_vma=False,
    )
```

```python
import math

import jax
import jax.numpy as jnp
import numpy as np
from jax import lax
from jax.experimental import pallas as pl
from jax.experimental.pallas import tpu as pltpu
from jax.sharding import PartitionSpec as P

CPG = 4
TAPS = 7
PAIRS = CPG // 2
EVERYONE = ("dp", "ctx")
VMEM_LIMIT = 24 * 1024 * 1024


def shifted(value, axis, steps):
    count = lax.axis_size(axis)
    first, last = (max(0, -steps), min(count, count - steps))
    return lax.ppermute(value, axis, [(source, source + steps) for source in range(first, last)])


def sizes_of(seq_len):
    padded = 2 * seq_len
    inner = max(d for d in range(1, seq_len + 1) if seq_len % d == 0 and d * d <= padded)
    return padded, inner, padded // inner


def table(count_out, count_in, period):
    turns = np.arange(count_out, dtype=np.int64)[:, None] * np.arange(count_in, dtype=np.int64)
    angle = (turns % period).astype(np.float64) * (2.0 * math.pi / period)
    return np.cos(angle), np.sin(angle)


def make_tables(seq_len, sources):
    padded, inner, outer = sizes_of(seq_len)
    half = outer // 2
    fold = half // sources
    order = np.arange(half).reshape(sources, fold).T.reshape(-1)
    cos_o, sin_o = table(outer, half, outer)
    cos_i, sin_i = table(inner, inner, inner)
    cos_p, sin_p = cos_o[:, order], sin_o[:, order]
    narrow = lambda blocks: jnp.asarray(np.block(blocks).astype(np.float32)).astype(jnp.bfloat16)
    twist = [jnp.asarray(t.astype(np.float32)) for t in table(outer, inner, padded)]
    return {
        "first": narrow([[cos_p, sin_p], [-sin_p, cos_p]]),
        "second": narrow([[cos_i, -sin_i], [sin_i, cos_i]]),
        "third": narrow([[cos_i, sin_i], [-sin_i, cos_i]]),
        "fourth": narrow([[cos_p.T, -sin_p.T], [sin_p.T, cos_p.T]]),
        "joined": narrow(
            [
                [cos_i, -sin_i],
                [sin_i, cos_i],
                [cos_i, sin_i],
                [-sin_i, cos_i],
                [cos_p.T / padded, -sin_p.T / padded],
                [sin_p.T / padded, cos_p.T / padded],
                [np.hstack([cos_p, sin_p]), np.hstack([-sin_p, cos_p])],
            ]
        )
        if inner == outer
        else None,
        "first_real": narrow([[cos_o], [-sin_o]]),
        "fourth_real": narrow([[cos_o.T, -sin_o.T]]),
        "twist_re": twist[0],
        "twist_im": twist[1],
    }


LANES = 128


def spread(tall, count, stride, first, height, width):
    tiles = [tall[pl.ds(t * height + first, count, stride=stride), :] for t in range(width[0] // LANES, width[1] // LANES)]
    return tiles[0] if len(tiles) == 1 else jnp.concatenate(tiles, axis=1)


def put_spread(tall, values, stride, first, height, width):
    for i, t in enumerate(range(width[0] // LANES, width[1] // LANES)):
        tall[pl.ds(t * height + first, values.shape[0], stride=stride), :] = values[:, i * LANES : (i + 1) * LANES]


def dot(left, right):
    return jnp.dot(left, right, preferred_element_type=jnp.float32)


def transform_filters(long_filter, tables, seq_len):
    padded, inner, outer = sizes_of(seq_len)
    half = outer // 2
    groups = long_filter.shape[0]
    scale = seq_len ** -0.5

    def kernel(x_ref, first_ref, second_ref, tr_ref, ti_ref, out_ref, tall):
        height = half * groups
        for b in range(half):
            for t in range(inner // LANES):
                at = t * height + b * groups
                lanes = slice(b * inner + t * LANES, b * inner + (t + 1) * LANES)
                tall[at : at + groups, :] = x_ref[:, lanes].astype(jnp.float32)
        for g in range(groups):
            x = spread(tall, half, groups, g, height, (0, inner)).astype(jnp.bfloat16)
            f = dot(first_ref[...], x)
            f_re, f_im = f[:outer], f[outer:]
            g_re = (f_re * tr_ref[...] + f_im * ti_ref[...]).astype(jnp.bfloat16)
            g_im = (f_im * tr_ref[...] - f_re * ti_ref[...]).astype(jnp.bfloat16)
            spec = dot(g_re, second_ref[:inner]) + dot(g_im, second_ref[inner:])
            out_ref[g * outer : (g + 1) * outer, :] = spec * scale

    return pl.pallas_call(
        kernel,
        name="filter_dft",
        out_shape=jax.ShapeDtypeStruct((groups * outer, 2 * inner), jnp.float32),
        scratch_shapes=[pltpu.VMEM((half * groups * inner // LANES, LANES), jnp.float32)],
        compiler_params=pltpu.CompilerParams(vmem_limit_bytes=VMEM_LIMIT),
        cost_estimate=pl.CostEstimate(flops=200_000_000, bytes_accessed=2_000_000, transcendentals=0),
    )(long_filter, tables["first_real"], tables["second"], tables["twist_re"], tables["twist_im"])


def filtered(arrived, filters, tables, seq_len, other=None):
    padded, inner, outer = sizes_of(seq_len)
    half = outer // 2
    sources, channels, local = arrived.shape
    fold = local // inner
    groups = channels // CPG
    backward = other is not None

    def kernel(*refs):
        if backward:
            (x_ref, f_ref, k_ref, first_ref, second_ref, third_ref, fourth_ref, tr_ref, ti_ref,
             y_ref, cross_ref, tall, wide, stage, turn) = refs
        else:
            (x_ref, f_ref, first_ref, second_ref, third_ref, fourth_ref, tr_ref, ti_ref,
             y_ref, z_ref, tall, wide, stage, turn) = refs
        height = sources * channels
        for t in range(local // LANES):
            block = x_ref[:, :, t * LANES : (t + 1) * LANES].astype(jnp.float32)
            tall[t * height : (t + 1) * height, :] = block.reshape(height, LANES)
        for c in range(channels):
            pair, part = divmod(c, 2)
            for h in range(fold):
                rows = spread(tall, sources, channels, c, height, (h * inner, (h + 1) * inner))
                at = part * half + h * sources
                wide[at : at + sources, pair * inner : (pair + 1) * inner] = rows.astype(jnp.bfloat16)
        for g in range(groups):
            span = PAIRS * inner
            f = dot(first_ref[...], wide[:, g * span : (g + 1) * span])
            for p in range(PAIRS):
                f_re = f[:outer, p * inner : (p + 1) * inner]
                f_im = f[outer:, p * inner : (p + 1) * inner]
                at = (g * PAIRS + p) * outer
                stage[at : at + outer, :inner] = (f_re * tr_ref[...] + f_im * ti_ref[...]).astype(jnp.bfloat16)
                stage[at : at + outer, inner:] = (f_im * tr_ref[...] - f_re * ti_ref[...]).astype(jnp.bfloat16)
        for g in range(groups):
            s_re = f_ref[g * outer : (g + 1) * outer, :inner]
            s_im = f_ref[g * outer : (g + 1) * outer, inner:]
            cross_re = cross_im = None
            for p in range(PAIRS):
                at = (g * PAIRS + p) * outer
                z = dot(stage[at : at + outer, :], second_ref[...])
                z_re, z_im = z[:, :inner], z[:, inner:]
                if backward:
                    k_re = k_ref[at : at + outer, :inner].astype(jnp.float32)
                    k_im = k_ref[at : at + outer, inner:].astype(jnp.float32)
                    part_re = k_re * z_re + k_im * z_im
                    part_im = k_re * z_im - k_im * z_re
                    cross_re = part_re if cross_re is None else cross_re + part_re
                    cross_im = part_im if cross_im is None else cross_im + part_im
                    o_re = s_re * z_re + s_im * z_im
                    o_im = s_re * z_im - s_im * z_re
                else:
                    z_ref[at : at + outer, :] = z
                    o_re = s_re * z_re - s_im * z_im
                    o_im = s_re * z_im + s_im * z_re
                stage[at : at + outer, :inner] = o_re.astype(jnp.bfloat16)
                stage[at : at + outer, inner:] = o_im.astype(jnp.bfloat16)
            if backward:
                cross_ref[g * outer : (g + 1) * outer, :inner] = cross_re.astype(jnp.bfloat16)
                cross_ref[g * outer : (g + 1) * outer, inner:] = cross_im.astype(jnp.bfloat16)
        for pair in range(groups * PAIRS):
            at = pair * outer
            h = dot(stage[at : at + outer, :], third_ref[...])
            h_re, h_im = h[:, :inner], h[:, inner:]
            lanes = slice(pair * inner, (pair + 1) * inner)
            turn[:outer, lanes] = (h_re * tr_ref[...] - h_im * ti_ref[...]).astype(jnp.bfloat16)
            turn[outer:, lanes] = (h_im * tr_ref[...] + h_re * ti_ref[...]).astype(jnp.bfloat16)
        for g in range(groups):
            span = PAIRS * inner
            y = dot(fourth_ref[...], turn[:, g * span : (g + 1) * span]) * (1.0 / padded)
            for p in range(PAIRS):
                for part in range(2):
                    c = (g * PAIRS + p) * 2 + part
                    for h in range(fold):
                        at = part * half + h * sources
                        rows = y[at : at + sources, p * inner : (p + 1) * inner]
                        put_spread(tall, rows, channels, c, height, (h * inner, (h + 1) * inner))
        for t in range(local // LANES):
            block = tall[t * height : (t + 1) * height, :].reshape(sources, channels, LANES)
            y_ref[:, :, t * LANES : (t + 1) * LANES] = block.astype(jnp.bfloat16)

    pairs = groups * PAIRS
    if backward:
        extra = jax.ShapeDtypeStruct((groups * outer, 2 * inner), jnp.bfloat16)
    else:
        extra = jax.ShapeDtypeStruct((pairs * outer, 2 * inner), jnp.float32)
    operands = [arrived, filters] + ([other] if backward else [])
    operands += [tables[n] for n in ("first", "second", "third", "fourth", "twist_re", "twist_im")]
    return pl.pallas_call(
        kernel,
        name="correlate" if backward else "convolve",
        out_shape=(jax.ShapeDtypeStruct(arrived.shape, jnp.bfloat16), extra),
        scratch_shapes=[
            pltpu.VMEM((sources * channels * local // LANES, LANES), jnp.float32),
            pltpu.VMEM((outer, pairs * inner), jnp.bfloat16),
            pltpu.VMEM((pairs * outer, 2 * inner), jnp.bfloat16),
            pltpu.VMEM((2 * outer, pairs * inner), jnp.bfloat16),
        ],
        compiler_params=pltpu.CompilerParams(vmem_limit_bytes=VMEM_LIMIT),
        cost_estimate=pl.CostEstimate(flops=2_000_000_000, bytes_accessed=5_000_000, transcendentals=0),
    )(*operands)


def filter_gradient(cross, tables, seq_len):
    padded, inner, outer = sizes_of(seq_len)
    half = outer // 2
    groups = cross.shape[0] // outer
    scale = seq_len ** -0.5 / padded

    def kernel(s_ref, third_ref, fourth_ref, tr_ref, ti_ref, out_ref, tall, turn):
        for g in range(groups):
            h = dot(s_ref[g * outer : (g + 1) * outer, :], third_ref[...])
            h_re, h_im = h[:, :inner], h[:, inner:]
            turn[:outer, g * inner : (g + 1) * inner] = (h_re * tr_ref[...] - h_im * ti_ref[...]).astype(jnp.bfloat16)
            turn[outer:, g * inner : (g + 1) * inner] = (h_im * tr_ref[...] + h_re * ti_ref[...]).astype(jnp.bfloat16)
        for g in range(groups):
            y = dot(fourth_ref[...], turn[:, g * inner : (g + 1) * inner]) * scale
            put_spread(tall, y, groups, g, half * groups, (0, inner))
        for b in range(half):
            for t in range(inner // LANES):
                at = (t * half + b) * groups
                out_ref[:, b * inner + t * LANES : b * inner + (t + 1) * LANES] = tall[at : at + groups, :]

    return pl.pallas_call(
        kernel,
        name="filter_gradient",
        out_shape=jax.ShapeDtypeStruct((groups, seq_len), jnp.float32),
        scratch_shapes=[
            pltpu.VMEM((half * groups * inner // LANES, LANES), jnp.float32),
            pltpu.VMEM((2 * outer, groups * inner), jnp.bfloat16),
        ],
        compiler_params=pltpu.CompilerParams(vmem_limit_bytes=VMEM_LIMIT),
        cost_estimate=pl.CostEstimate(flops=200_000_000, bytes_accessed=2_000_000, transcendentals=0),
    )(cross, tables["third"], tables["fourth_real"], tables["twist_re"], tables["twist_im"])


RIM = 8


def seven_taps(tall, value, rim, weights, forward):
    count = value.shape[0]
    if forward:
        tall[:RIM, :] = rim
        tall[RIM : RIM + count, :] = value
    else:
        tall[:count, :] = value
        tall[count : count + RIM, :] = rim
    total = value * weights[:1]
    for lag in range(1, TAPS):
        first = RIM - lag if forward else lag
        total = total + tall[first : first + count, :] * weights[lag : lag + 1]
    return total


def lane_block(i, offset=0):
    return pl.ds(pl.multiple_of(i * LANES + offset, LANES), LANES)


def whole_call(kernel, name, out_shape, operands, scratch=(), flops=10_000_000, **kwargs):
    return pl.pallas_call(
        kernel,
        name=name,
        out_shape=out_shape,
        scratch_shapes=list(scratch),
        compiler_params=pltpu.CompilerParams(vmem_limit_bytes=VMEM_LIMIT),
        cost_estimate=pl.CostEstimate(flops=flops, bytes_accessed=4_000_000, transcendentals=0),
        **kwargs,
    )(*operands)


def narrow_shape(*shape):
    return jax.ShapeDtypeStruct(shape, jnp.bfloat16)


def features_of(turned, rim, short_filter, cotangent):
    local, width = cotangent.shape

    def kernel(x_ref, rim_ref, w_ref, og_ref, f_ref, kv_ref, dconv_ref, tall):
        @pl.loop(0, width // LANES)
        def _(i):
            made = []
            for part in range(3):
                lanes = lane_block(i, part * width)
                total = seven_taps(
                    tall.at[part],
                    x_ref[:, lanes].astype(jnp.float32),
                    rim_ref[:, lanes].astype(jnp.float32),
                    w_ref[:, lanes].astype(jnp.float32),
                    True,
                ).astype(jnp.bfloat16)
                f_ref[:, lanes] = total
                made.append(total.astype(jnp.float32))
            rows = lane_block(i)
            kv_ref[rows, :] = (made[1] * made[2]).astype(jnp.bfloat16).T
            og = og_ref[:, rows].astype(jnp.float32)
            dconv_ref[rows, :] = (og * made[0]).astype(jnp.bfloat16).T

    return whole_call(
        kernel,
        "features",
        (narrow_shape(local, 3 * width), narrow_shape(width, local), narrow_shape(width, local)),
        (turned, rim, short_filter, cotangent),
        [pltpu.VMEM((3, local + RIM, LANES), jnp.float32)],
    )


def query_products(feats, conv, cotangent):
    width, local = conv.shape

    def kernel(f_ref, conv_ref, og_ref, mixed_ref, dq_ref, rim_ref):
        @pl.loop(0, width // LANES)
        def _(i):
            lanes = lane_block(i)
            here = conv_ref[lanes, :].T.astype(jnp.float32)
            mixed_ref[lanes, :] = (f_ref[:, lanes].astype(jnp.float32) * here).astype(jnp.bfloat16).T
            dq = (og_ref[:, lanes].astype(jnp.float32) * here).astype(jnp.bfloat16)
            dq_ref[:, lanes] = dq
            rim_ref[:, lanes] = dq[:RIM]

    return whole_call(
        kernel,
        "query_products",
        (narrow_shape(width, local), narrow_shape(local, width), narrow_shape(RIM, width)),
        (feats, conv, cotangent),
    )


def key_value_products(feats, back):
    width, local = back.shape

    def kernel(f_ref, back_ref, d_ref, rim_ref):
        @pl.loop(0, width // LANES)
        def _(i):
            here = back_ref[lane_block(i), :].T.astype(jnp.float32)
            for part in range(2):
                other = f_ref[:, lane_block(i, (2 - part) * width)].astype(jnp.float32)
                grad = (here * other).astype(jnp.bfloat16)
                d_ref[:, lane_block(i, part * width)] = grad
                rim_ref[:, lane_block(i, part * width)] = grad[:RIM]

    return whole_call(
        kernel,
        "key_value_products",
        (narrow_shape(local, 2 * width), narrow_shape(RIM, 2 * width)),
        (feats, back),
    )


def joined_features(turned, rim, short_filter, out_grad, owned):
    width, local = out_grad.shape
    near = LANES // owned
    blocks = width // LANES

    def kernel(x_ref, rim_ref, w_ref, og_ref, f_hbm, msg_ref, edge_ref, tall, made, f_ref, edge, sent):
        def copy(i):
            to = pl.ds(i * near, near)
            return pltpu.make_async_copy(made.at[to], msg_ref.at[to], sent.at[i])

        def keep(part, i):
            at = part * blocks + i
            to = pl.ds(pl.multiple_of(at * LANES, LANES), LANES)
            return pltpu.make_async_copy(f_ref.at[at], f_hbm.at[to, :], sent.at[blocks + at])

        @pl.loop(0, blocks)
        def _(i):
            parts = []
            for part in range(3):
                lanes = lane_block(i, part * width)
                total = seven_taps(
                    tall.at[part],
                    x_ref[:, lanes].astype(jnp.float32),
                    rim_ref[:, lanes].astype(jnp.float32),
                    w_ref[:, lanes].astype(jnp.float32),
                    True,
                ).astype(jnp.bfloat16)
                for t in range(local // LANES):
                    f_ref[part * blocks + i, :, t * LANES : (t + 1) * LANES] = total[t * LANES : (t + 1) * LANES]
                keep(part, i).start()
                if part:
                    edge[:, lanes] = total[:RIM]
                parts.append(total.astype(jnp.float32))
            og = og_ref[lane_block(i), :].T
            edge[:, lane_block(i)] = og[:RIM]
            kv = (parts[1] * parts[2]).astype(jnp.bfloat16).T
            dconv = (og.astype(jnp.float32) * parts[0]).astype(jnp.bfloat16).T
            to = pl.ds(i * near, near)
            made[to, :owned, :] = kv.reshape(near, owned, local)
            made[to, owned:, :] = dconv.reshape(near, owned, local)
            copy(i).start()

        last = pltpu.make_async_copy(edge, edge_ref, sent.at[4 * blocks])
        last.start()

        @pl.loop(0, blocks)
        def _(i):
            copy(i).wait()
            for part in range(3):
                keep(part, i).wait()

        last.wait()

    vmem = pl.BlockSpec(memory_space=pltpu.VMEM)
    hbm = pl.BlockSpec(memory_space=pltpu.HBM)
    devices = width // owned
    return whole_call(
        kernel,
        "joined_features",
        (narrow_shape(3 * width, local), narrow_shape(devices, 2 * owned, local), narrow_shape(RIM, 3 * width)),
        (turned, rim, short_filter, out_grad),
        [
            pltpu.VMEM((3, local + RIM, LANES), jnp.float32),
            pltpu.VMEM((devices, 2 * owned, local), jnp.bfloat16),
            pltpu.VMEM((3 * blocks, LANES, local), jnp.bfloat16),
            pltpu.VMEM((RIM, 3 * width), jnp.bfloat16),
            pltpu.SemaphoreType.DMA((4 * blocks + 1,)),
        ],
        in_specs=[vmem] * 4,
        out_specs=(hbm, hbm, hbm),
    )


def joined_filtering(arrived, filters, tables, seq_len):
    padded, inner, outer = sizes_of(seq_len)
    half = outer // 2
    sources, rows, local = arrived.shape
    channels = rows // 2
    tiles = local // LANES
    fold = local // inner
    groups = channels // CPG
    pairs = groups * PAIRS
    height = sources * channels
    chunk = sources // 4

    def kernel(x_ref, f_ref, table_ref, tr_ref, ti_ref, y_hbm, cross_hbm, y_ref, cross_ref, talls, wides, stages, turns, sems):
        second_ref, third_ref = table_ref.at[: 2 * inner], table_ref.at[2 * inner : 4 * inner]
        fourth_ref = table_ref.at[4 * inner : 4 * inner + 2 * half]
        firsts = table_ref[4 * inner + 2 * half :, :]
        first = jnp.concatenate([firsts[:, : 2 * half], firsts[:, 2 * half :]], axis=0)
        tr, ti = tr_ref[...], ti_ref[...]
        for s in range(2):
            tall, wide, stage = talls.at[s], wides.at[s], stages.at[s]
            for t in range(tiles):
                block = x_ref[:, s * channels : (s + 1) * channels, t * LANES : (t + 1) * LANES]
                tall[t * height : (t + 1) * height, :] = block.astype(jnp.float32).reshape(height, LANES)
            for c in range(channels):
                pair, part = divmod(c, 2)
                for h in range(fold):
                    line = spread(tall, sources, channels, c, height, (h * inner, (h + 1) * inner))
                    at = part * half + h * sources
                    wide[at : at + sources, pair * inner : (pair + 1) * inner] = line.astype(jnp.bfloat16)
            for g in range(groups):
                span = PAIRS * inner
                f = dot(first, wide[:, g * span : (g + 1) * span])
                for p in range(PAIRS):
                    f_re = f[:outer, p * inner : (p + 1) * inner]
                    f_im = f[outer:, p * inner : (p + 1) * inner]
                    at = (g * PAIRS + p) * outer
                    stage[at : at + outer, :inner] = (f_re * tr + f_im * ti).astype(jnp.bfloat16)
                    stage[at : at + outer, inner:] = (f_im * tr - f_re * ti).astype(jnp.bfloat16)
        for g in range(groups):
            s_re = f_ref[g * outer : (g + 1) * outer, :inner]
            s_im = f_ref[g * outer : (g + 1) * outer, inner:]
            cross_re = cross_im = 0.0
            for p in range(PAIRS):
                at = (g * PAIRS + p) * outer
                k = dot(stages[0, at : at + outer, :], second_ref[...])
                d = dot(stages[1, at : at + outer, :], second_ref[...])
                k_re, k_im = k[:, :inner], k[:, inner:]
                d_re, d_im = d[:, :inner], d[:, inner:]
                cross_re = cross_re + (k_re * d_re + k_im * d_im)
                cross_im = cross_im + (k_re * d_im - k_im * d_re)
                stages[0, at : at + outer, :inner] = (s_re * k_re - s_im * k_im).astype(jnp.bfloat16)
                stages[0, at : at + outer, inner:] = (s_re * k_im + s_im * k_re).astype(jnp.bfloat16)
                stages[1, at : at + outer, :inner] = (s_re * d_re + s_im * d_im).astype(jnp.bfloat16)
                stages[1, at : at + outer, inner:] = (s_re * d_im - s_im * d_re).astype(jnp.bfloat16)
            cross_ref[g * outer : (g + 1) * outer, :inner] = cross_re.astype(jnp.bfloat16)
            cross_ref[g * outer : (g + 1) * outer, inner:] = cross_im.astype(jnp.bfloat16)
        copies = [pltpu.make_async_copy(cross_ref, cross_hbm, sems.at[4])]
        copies[0].start()
        spot = lax.broadcasted_iota(jnp.int32, (RIM, LANES), 0)
        lane = lax.broadcasted_iota(jnp.int32, (RIM, LANES), 1)
        pick = jnp.where(spot == lane, 1.0, 0.0).astype(jnp.bfloat16)
        rims = []
        for s in range(2):
            tall, stage, turn = talls.at[s], stages.at[s], turns.at[s]
            for pair in range(pairs):
                at = pair * outer
                h = dot(stage[at : at + outer, :], third_ref[...])
                h_re, h_im = h[:, :inner], h[:, inner:]
                lanes = slice(pair * inner, (pair + 1) * inner)
                turn[:outer, lanes] = (h_re * tr - h_im * ti).astype(jnp.bfloat16)
                turn[outer:, lanes] = (h_im * tr + h_re * ti).astype(jnp.bfloat16)
            for g in range(groups):
                span = PAIRS * inner
                y = dot(fourth_ref[...], turn[:, g * span : (g + 1) * span])
                for p in range(PAIRS):
                    for part in range(2):
                        c = (g * PAIRS + p) * 2 + part
                        for h in range(fold):
                            at = part * half + h * sources
                            line = y[at : at + sources, p * inner : (p + 1) * inner]
                            put_spread(tall, line, channels, c, height, (h * inner, (h + 1) * inner))
            front = tall[:height, :].astype(jnp.bfloat16)
            rims.append(
                lax.dot_general(pick, front, (((1,), (1,)), ((), ())), preferred_element_type=jnp.float32)
            )
        for q in range(4):
            to = slice(q * chunk, (q + 1) * chunk)
            for s in range(2):
                for t in range(tiles):
                    at = t * height + q * chunk * channels
                    block = talls[s, at : at + chunk * channels, :].reshape(chunk, channels, LANES)
                    row = (s * tiles + t) * channels
                    y_ref[to, row : row + channels, :] = block.astype(jnp.bfloat16)
            for d in range(q * chunk, (q + 1) * chunk):
                tile, lanes = divmod((d + 1) % sources * channels, LANES)
                edge = jnp.zeros((RIM, LANES), jnp.float32)
                if d < sources - 1:
                    for s in range(2):
                        piece = rims[s][:, tile * LANES : (tile + 1) * LANES]
                        turn_by = (s * channels - lanes) % LANES
                        if turn_by:
                            piece = pltpu.roll(piece, turn_by, 1)
                        edge = piece if s == 0 else jnp.where(lane < channels, edge, piece)
                y_ref[d, 2 * tiles * channels :, :] = edge.astype(jnp.bfloat16)
            copies.append(pltpu.make_async_copy(y_ref.at[to], y_hbm.at[to], sems.at[q]))
            copies[-1].start()
        for copy in copies:
            copy.wait()

    sent = (sources, 2 * tiles * channels + RIM, LANES)
    vmem = pl.BlockSpec(memory_space=pltpu.VMEM)
    hbm = pl.BlockSpec(memory_space=pltpu.HBM)
    return whole_call(
        kernel,
        "joined_filtering",
        (narrow_shape(*sent), narrow_shape(groups * outer, 2 * inner)),
        [arrived, filters] + [tables[n] for n in ("joined", "twist_re", "twist_im")],
        [
            pltpu.VMEM(sent, jnp.bfloat16),
            pltpu.VMEM((groups * outer, 2 * inner), jnp.bfloat16),
            pltpu.VMEM((2, tiles * height, LANES), jnp.float32),
            pltpu.VMEM((2, outer, pairs * inner), jnp.bfloat16),
            pltpu.VMEM((2, pairs * outer, 2 * inner), jnp.bfloat16),
            pltpu.VMEM((2, 2 * outer, pairs * inner), jnp.bfloat16),
            pltpu.SemaphoreType.DMA((5,)),
        ],
        flops=4_000_000_000,
        in_specs=[vmem] * 5,
        out_specs=(hbm, hbm),
    )


def joined_gradients(cross, feats, edges, returned, out_grad, short_filter, owned):
    width, local = out_grad.shape
    tiles = local // LANES
    near = LANES // owned
    blocks = width // LANES

    def kernel(_, f_hbm, edge_ref, back_ref, og_ref, w_ref, mixed_ref, out_ref, tall, made, f_ref, sent, fetched):
        def fetch(part, i):
            at = part * blocks + i
            rows = pl.ds(pl.multiple_of(at * LANES, LANES), LANES)
            return pltpu.make_async_copy(f_hbm.at[rows, :], f_ref.at[at], fetched.at[at])

        @pl.loop(0, blocks)
        def _(i):
            for part in range(3):
                fetch(part, i).start()

        def features(part, i):
            fetch(part, i).wait()
            held = [f_ref[part * blocks + i, :, t * LANES : (t + 1) * LANES] for t in range(tiles)]
            return jnp.concatenate(held, axis=0).astype(jnp.float32)

        lane = lax.broadcasted_iota(jnp.int32, (RIM, LANES), 1)

        def copy(part, i):
            at = part * blocks + i
            if part < 3:
                to = out_ref.at[pl.ds(pl.multiple_of(at * LANES, LANES), LANES), :]
            else:
                to = mixed_ref.at[lane_block(i), :]
            return pltpu.make_async_copy(made.at[at], to, sent.at[at])

        @pl.loop(0, blocks)
        def _(i):
            held = pl.ds(i * near, near)
            sums = []
            for s in range(2):
                turned = [
                    back_ref[held, (s * tiles + t) * owned : (s * tiles + t + 1) * owned, :].reshape(LANES, LANES).T
                    for t in range(tiles)
                ]
                here = jnp.concatenate(turned, axis=0).astype(jnp.float32)
                rim = jnp.zeros((RIM, LANES), jnp.float32)
                for n in range(near):
                    piece = back_ref[i * near + n, 2 * tiles * owned :, :].astype(jnp.float32)
                    turn_by = (n - s) * owned % LANES
                    if turn_by:
                        piece = pltpu.roll(piece, turn_by, 1)
                    rim = jnp.where(lane >= n * owned, piece, rim) if n else piece
                sums.append((here, rim))
            query, key, value = [features(part, i) for part in range(3)]
            made[3 * blocks + i] = (query * sums[0][0]).astype(jnp.bfloat16).T
            copy(3, i).start()
            for part in range(3):
                here, rim = sums[min(part, 1)]
                other = (og_ref[lane_block(i), :].T.astype(jnp.float32), value, key)[part]
                edge = edge_ref[:, lane_block(i, (3 - part) % 3 * width)].astype(jnp.float32)
                grad = (here * other).astype(jnp.bfloat16)
                total = seven_taps(
                    tall.at[part],
                    grad.astype(jnp.float32),
                    (rim * edge).astype(jnp.bfloat16).astype(jnp.float32),
                    w_ref[:, lane_block(i, part * width)].astype(jnp.float32),
                    False,
                )
                made[part * blocks + i] = total.astype(jnp.bfloat16).T
                copy(part, i).start()

        @pl.loop(0, blocks)
        def _(i):
            for part in range(4):
                copy(part, i).wait()

    vmem = pl.BlockSpec(memory_space=pltpu.VMEM)
    hbm = pl.BlockSpec(memory_space=pltpu.HBM)
    return whole_call(
        kernel,
        "joined_gradients",
        (narrow_shape(width, local), narrow_shape(3 * width, local)),
        (cross, feats, edges, returned, out_grad, short_filter),
        [
            pltpu.VMEM((3, local + RIM, LANES), jnp.float32),
            pltpu.VMEM((4 * blocks, LANES, local), jnp.bfloat16),
            pltpu.VMEM((3 * blocks, LANES, local), jnp.bfloat16),
            pltpu.SemaphoreType.DMA((4 * blocks,)),
            pltpu.SemaphoreType.DMA((3 * blocks,)),
        ],
        in_specs=[hbm, hbm] + [vmem] * 4,
        out_specs=(hbm, hbm),
        input_output_aliases={0: 0, 1: 1},
    )


def query_gradient(grad, rim, short_filter):
    local, width = grad.shape
    steps = width // GRAD_ROWS

    def kernel(d_ref, rim_ref, w_ref, out_ref, tall):
        gradient_block(d_ref, rim_ref, w_ref, out_ref, tall)

    return gradient_call(kernel, "query_gradient", (), grad, rim, short_filter, 1, 0)


def key_value_gradient(whole, grad, rim, short_filter):
    def kernel(_, d_ref, rim_ref, w_ref, out_ref, tall):
        gradient_block(d_ref, rim_ref, w_ref, out_ref, tall)

    return gradient_call(kernel, "key_value_gradient", (whole,), grad, rim, short_filter, 2, 1)


GRAD_ROWS = 512


def gradient_block(d_ref, rim_ref, w_ref, out_ref, tall):
    for c in range(GRAD_ROWS // LANES):
        lanes = slice(c * LANES, (c + 1) * LANES)
        total = seven_taps(
            tall.at[c],
            d_ref[:, lanes].astype(jnp.float32),
            rim_ref[:, lanes].astype(jnp.float32),
            w_ref[:, lanes].astype(jnp.float32),
            False,
        )
        out_ref[lanes, :] = total.astype(jnp.bfloat16).T


def gradient_call(kernel, name, whole, grad, rim, short_filter, parts, first):
    local, lanes = grad.shape
    width = lanes // parts
    steps = width // GRAD_ROWS
    return pl.pallas_call(
        kernel,
        name=name,
        grid=(parts * steps,),
        in_specs=[pl.BlockSpec(memory_space=pl.ANY)] * len(whole)
        + [
            pl.BlockSpec((local, GRAD_ROWS), lambda i: (0, i)),
            pl.BlockSpec((RIM, GRAD_ROWS), lambda i: (0, i)),
            pl.BlockSpec((TAPS, GRAD_ROWS), lambda i: (0, first * steps + i)),
        ],
        out_specs=pl.BlockSpec((GRAD_ROWS, local), lambda i: (first * steps + i, 0)),
        out_shape=narrow_shape(3 * width, local),
        scratch_shapes=[pltpu.VMEM((GRAD_ROWS // LANES, local + RIM, LANES), jnp.float32)],
        input_output_aliases={0: 0} if whole else {},
        cost_estimate=pl.CostEstimate(flops=20_000_000, bytes_accessed=4_000_000, transcendentals=0),
    )(*whole, grad, rim, short_filter)


def shards(projections, short_filter, long_filter, out_grad):
    width, local_len = out_grad.shape
    devices = lax.axis_size(EVERYONE)
    seq_len = local_len * devices
    owned = width // devices
    tables = make_tables(seq_len, devices)

    turned = projections.T
    rim = shifted(turned[local_len - RIM :], EVERYONE, 1)

    _, inner, outer = sizes_of(seq_len)
    twin = owned // CPG * outer == width and 2 * inner == local_len and inner == outer
    if owned % 16 == 0 and LANES % (2 * owned) == 0 and devices % 4 == 0 and twin:
        feats, message, edges = joined_features(turned, rim, short_filter, out_grad, owned)
        filters = transform_filters(long_filter, tables, seq_len)
        arrived = lax.all_to_all(message, EVERYONE, split_axis=0, concat_axis=0, tiled=True)
        edges, filters, arrived = lax.optimization_barrier((shifted(edges, EVERYONE, -1), filters, arrived))
        answer, cross = joined_filtering(arrived, filters, tables, seq_len)
        returned = lax.all_to_all(answer, EVERYONE, split_axis=0, concat_axis=0, tiled=True)
        filter_grad = filter_gradient(cross, tables, seq_len)
        filter_grad, returned, cross = lax.optimization_barrier((filter_grad, returned, cross))
        mixed, grad = joined_gradients(cross, feats, edges, returned, out_grad, short_filter, owned)
        return (mixed, grad, filter_grad)

    cotangent = out_grad.T
    feats, product, conv_grad = features_of(turned, rim, short_filter, cotangent)

    def exchange(block):
        pieces = block.reshape(devices, owned, local_len)
        return lax.all_to_all(pieces, EVERYONE, split_axis=0, concat_axis=0, tiled=True)

    filters = transform_filters(long_filter, tables, seq_len)
    prod_chan = exchange(product)
    conv_grad, prod_chan = lax.optimization_barrier((conv_grad, prod_chan))
    grad_chan = exchange(conv_grad)
    conv_chan, prod_spec = filtered(prod_chan, filters, tables, seq_len)
    conv_chan, grad_chan = lax.optimization_barrier((conv_chan, grad_chan))
    conv_tok = exchange(conv_chan)
    back_chan, cross = filtered(grad_chan, filters, tables, seq_len, prod_spec)
    back_chan, conv_tok = lax.optimization_barrier((back_chan, conv_tok))
    back_tok = exchange(back_chan)

    filter_grad = filter_gradient(cross, tables, seq_len)
    mixed, grad_q, rim_q = query_products(feats, conv_tok.reshape(width, local_len), cotangent)
    grad = query_gradient(grad_q, shifted(rim_q, EVERYONE, -1), short_filter)
    filter_grad, mixed, grad, back_tok = lax.optimization_barrier((filter_grad, mixed, grad, back_tok))

    grad_kv, rim_kv = key_value_products(feats, back_tok.reshape(width, local_len))
    grad = key_value_gradient(grad, grad_kv, shifted(rim_kv, EVERYONE, -1), short_filter)
    return (mixed, grad, filter_grad)


def solution(mesh):
    placed = (P(None, EVERYONE), P(), P(EVERYONE, None), P(None, EVERYONE))
    return jax.shard_map(
        shards,
        mesh=mesh,
        in_specs=placed,
        out_specs=(P(None, EVERYONE), P(None, EVERYONE), P(EVERYONE, None)),
        check_vma=False,
    )
```

```python
import math

import jax
import jax.numpy as jnp
import numpy as np
from jax import lax
from jax.experimental import pallas as pl
from jax.experimental.pallas import tpu as pltpu
from jax.sharding import PartitionSpec as P

CPG = 4
TAPS = 7
PAIRS = CPG // 2
EVERYONE = ("dp", "ctx")
VMEM_LIMIT = 24 * 1024 * 1024


def shifted(value, axis, steps):
    count = lax.axis_size(axis)
    first, last = (max(0, -steps), min(count, count - steps))
    return lax.ppermute(value, axis, [(source, source + steps) for source in range(first, last)])


def sizes_of(seq_len):
    padded = 2 * seq_len
    inner = max(d for d in range(1, seq_len + 1) if seq_len % d == 0 and d * d <= padded)
    return padded, inner, padded // inner


def table(count_out, count_in, period):
    turns = np.arange(count_out, dtype=np.int64)[:, None] * np.arange(count_in, dtype=np.int64)
    angle = (turns % period).astype(np.float64) * (2.0 * math.pi / period)
    return np.cos(angle), np.sin(angle)


def make_tables(seq_len, sources):
    padded, inner, outer = sizes_of(seq_len)
    half = outer // 2
    fold = half // sources
    order = np.arange(half).reshape(sources, fold).T.reshape(-1)
    cos_o, sin_o = table(outer, half, outer)
    cos_i, sin_i = table(inner, inner, inner)
    cos_p, sin_p = cos_o[:, order], sin_o[:, order]
    narrow = lambda blocks: jnp.asarray(np.block(blocks).astype(np.float32)).astype(jnp.bfloat16)
    twist = [jnp.asarray(t.astype(np.float32)) for t in table(outer, inner, padded)]
    return {
        "first": narrow([[cos_p, sin_p], [-sin_p, cos_p]]),
        "second": narrow([[cos_i, -sin_i], [sin_i, cos_i]]),
        "third": narrow([[cos_i, sin_i], [-sin_i, cos_i]]),
        "fourth": narrow([[cos_p.T, -sin_p.T], [sin_p.T, cos_p.T]]),
        "joined": narrow(
            [
                [cos_i, -sin_i],
                [sin_i, cos_i],
                [cos_i, sin_i],
                [-sin_i, cos_i],
                [cos_p.T / padded, -sin_p.T / padded],
                [sin_p.T / padded, cos_p.T / padded],
                [np.hstack([cos_p, sin_p]), np.hstack([-sin_p, cos_p])],
            ]
        )
        if inner == outer
        else None,
        "first_real": narrow([[cos_o], [-sin_o]]),
        "fourth_real": narrow([[cos_o.T, -sin_o.T]]),
        "twist_re": twist[0],
        "twist_im": twist[1],
    }


LANES = 128


def spread(tall, count, stride, first, height, width):
    tiles = [tall[pl.ds(t * height + first, count, stride=stride), :] for t in range(width[0] // LANES, width[1] // LANES)]
    return tiles[0] if len(tiles) == 1 else jnp.concatenate(tiles, axis=1)


def put_spread(tall, values, stride, first, height, width):
    for i, t in enumerate(range(width[0] // LANES, width[1] // LANES)):
        tall[pl.ds(t * height + first, values.shape[0], stride=stride), :] = values[:, i * LANES : (i + 1) * LANES]


def dot(left, right):
    return jnp.dot(left, right, preferred_element_type=jnp.float32)


def transform_filters(long_filter, tables, seq_len, handed=()):
    padded, inner, outer = sizes_of(seq_len)
    half = outer // 2
    groups = long_filter.shape[0]
    scale = seq_len ** -0.5

    def kernel(x_ref, first_ref, second_ref, tr_ref, ti_ref, *refs):
        count = len(handed)
        out_ref, tall = refs[count], refs[-1]
        for n in range(count):
            refs[count + 1 + n][...] = refs[n][...]
        height = half * groups
        for b in range(half):
            for t in range(inner // LANES):
                at = t * height + b * groups
                lanes = slice(b * inner + t * LANES, b * inner + (t + 1) * LANES)
                tall[at : at + groups, :] = x_ref[:, lanes].astype(jnp.float32)
        for g in range(groups):
            x = spread(tall, half, groups, g, height, (0, inner)).astype(jnp.bfloat16)
            f = dot(first_ref[...], x)
            f_re, f_im = f[:outer], f[outer:]
            g_re = (f_re * tr_ref[...] + f_im * ti_ref[...]).astype(jnp.bfloat16)
            g_im = (f_im * tr_ref[...] - f_re * ti_ref[...]).astype(jnp.bfloat16)
            spec = dot(g_re, second_ref[:inner]) + dot(g_im, second_ref[inner:])
            out_ref[g * outer : (g + 1) * outer, :] = spec * scale

    return pl.pallas_call(
        kernel,
        name="filter_dft",
        out_shape=[jax.ShapeDtypeStruct((groups * outer, 2 * inner), jnp.float32)]
        + [jax.ShapeDtypeStruct(array.shape, array.dtype) for array in handed],
        scratch_shapes=[pltpu.VMEM((half * groups * inner // LANES, LANES), jnp.float32)],
        compiler_params=pltpu.CompilerParams(vmem_limit_bytes=VMEM_LIMIT),
        cost_estimate=pl.CostEstimate(flops=200_000_000, bytes_accessed=2_000_000, transcendentals=0),
    )(long_filter, tables["first_real"], tables["second"], tables["twist_re"], tables["twist_im"], *handed)


def filtered(arrived, filters, tables, seq_len, other=None):
    padded, inner, outer = sizes_of(seq_len)
    half = outer // 2
    sources, channels, local = arrived.shape
    fold = local // inner
    groups = channels // CPG
    backward = other is not None

    def kernel(*refs):
        if backward:
            (x_ref, f_ref, k_ref, first_ref, second_ref, third_ref, fourth_ref, tr_ref, ti_ref,
             y_ref, cross_ref, tall, wide, stage, turn) = refs
        else:
            (x_ref, f_ref, first_ref, second_ref, third_ref, fourth_ref, tr_ref, ti_ref,
             y_ref, z_ref, tall, wide, stage, turn) = refs
        height = sources * channels
        for t in range(local // LANES):
            block = x_ref[:, :, t * LANES : (t + 1) * LANES].astype(jnp.float32)
            tall[t * height : (t + 1) * height, :] = block.reshape(height, LANES)
        for c in range(channels):
            pair, part = divmod(c, 2)
            for h in range(fold):
                rows = spread(tall, sources, channels, c, height, (h * inner, (h + 1) * inner))
                at = part * half + h * sources
                wide[at : at + sources, pair * inner : (pair + 1) * inner] = rows.astype(jnp.bfloat16)
        for g in range(groups):
            span = PAIRS * inner
            f = dot(first_ref[...], wide[:, g * span : (g + 1) * span])
            for p in range(PAIRS):
                f_re = f[:outer, p * inner : (p + 1) * inner]
                f_im = f[outer:, p * inner : (p + 1) * inner]
                at = (g * PAIRS + p) * outer
                stage[at : at + outer, :inner] = (f_re * tr_ref[...] + f_im * ti_ref[...]).astype(jnp.bfloat16)
                stage[at : at + outer, inner:] = (f_im * tr_ref[...] - f_re * ti_ref[...]).astype(jnp.bfloat16)
        for g in range(groups):
            s_re = f_ref[g * outer : (g + 1) * outer, :inner]
            s_im = f_ref[g * outer : (g + 1) * outer, inner:]
            cross_re = cross_im = None
            for p in range(PAIRS):
                at = (g * PAIRS + p) * outer
                z = dot(stage[at : at + outer, :], second_ref[...])
                z_re, z_im = z[:, :inner], z[:, inner:]
                if backward:
                    k_re = k_ref[at : at + outer, :inner].astype(jnp.float32)
                    k_im = k_ref[at : at + outer, inner:].astype(jnp.float32)
                    part_re = k_re * z_re + k_im * z_im
                    part_im = k_re * z_im - k_im * z_re
                    cross_re = part_re if cross_re is None else cross_re + part_re
                    cross_im = part_im if cross_im is None else cross_im + part_im
                    o_re = s_re * z_re + s_im * z_im
                    o_im = s_re * z_im - s_im * z_re
                else:
                    z_ref[at : at + outer, :] = z
                    o_re = s_re * z_re - s_im * z_im
                    o_im = s_re * z_im + s_im * z_re
                stage[at : at + outer, :inner] = o_re.astype(jnp.bfloat16)
                stage[at : at + outer, inner:] = o_im.astype(jnp.bfloat16)
            if backward:
                cross_ref[g * outer : (g + 1) * outer, :inner] = cross_re.astype(jnp.bfloat16)
                cross_ref[g * outer : (g + 1) * outer, inner:] = cross_im.astype(jnp.bfloat16)
        for pair in range(groups * PAIRS):
            at = pair * outer
            h = dot(stage[at : at + outer, :], third_ref[...])
            h_re, h_im = h[:, :inner], h[:, inner:]
            lanes = slice(pair * inner, (pair + 1) * inner)
            turn[:outer, lanes] = (h_re * tr_ref[...] - h_im * ti_ref[...]).astype(jnp.bfloat16)
            turn[outer:, lanes] = (h_im * tr_ref[...] + h_re * ti_ref[...]).astype(jnp.bfloat16)
        for g in range(groups):
            span = PAIRS * inner
            y = dot(fourth_ref[...], turn[:, g * span : (g + 1) * span]) * (1.0 / padded)
            for p in range(PAIRS):
                for part in range(2):
                    c = (g * PAIRS + p) * 2 + part
                    for h in range(fold):
                        at = part * half + h * sources
                        rows = y[at : at + sources, p * inner : (p + 1) * inner]
                        put_spread(tall, rows, channels, c, height, (h * inner, (h + 1) * inner))
        for t in range(local // LANES):
            block = tall[t * height : (t + 1) * height, :].reshape(sources, channels, LANES)
            y_ref[:, :, t * LANES : (t + 1) * LANES] = block.astype(jnp.bfloat16)

    pairs = groups * PAIRS
    if backward:
        extra = jax.ShapeDtypeStruct((groups * outer, 2 * inner), jnp.bfloat16)
    else:
        extra = jax.ShapeDtypeStruct((pairs * outer, 2 * inner), jnp.float32)
    operands = [arrived, filters] + ([other] if backward else [])
    operands += [tables[n] for n in ("first", "second", "third", "fourth", "twist_re", "twist_im")]
    return pl.pallas_call(
        kernel,
        name="correlate" if backward else "convolve",
        out_shape=(jax.ShapeDtypeStruct(arrived.shape, jnp.bfloat16), extra),
        scratch_shapes=[
            pltpu.VMEM((sources * channels * local // LANES, LANES), jnp.float32),
            pltpu.VMEM((outer, pairs * inner), jnp.bfloat16),
            pltpu.VMEM((pairs * outer, 2 * inner), jnp.bfloat16),
            pltpu.VMEM((2 * outer, pairs * inner), jnp.bfloat16),
        ],
        compiler_params=pltpu.CompilerParams(vmem_limit_bytes=VMEM_LIMIT),
        cost_estimate=pl.CostEstimate(flops=2_000_000_000, bytes_accessed=5_000_000, transcendentals=0),
    )(*operands)


def filter_gradient(cross, tables, seq_len):
    padded, inner, outer = sizes_of(seq_len)
    half = outer // 2
    groups = cross.shape[0] // outer
    scale = seq_len ** -0.5 / padded

    def kernel(s_ref, third_ref, fourth_ref, tr_ref, ti_ref, out_ref, tall, turn):
        for g in range(groups):
            h = dot(s_ref[g * outer : (g + 1) * outer, :], third_ref[...])
            h_re, h_im = h[:, :inner], h[:, inner:]
            turn[:outer, g * inner : (g + 1) * inner] = (h_re * tr_ref[...] - h_im * ti_ref[...]).astype(jnp.bfloat16)
            turn[outer:, g * inner : (g + 1) * inner] = (h_im * tr_ref[...] + h_re * ti_ref[...]).astype(jnp.bfloat16)
        for g in range(groups):
            y = dot(fourth_ref[...], turn[:, g * inner : (g + 1) * inner]) * scale
            put_spread(tall, y, groups, g, half * groups, (0, inner))
        for b in range(half):
            for t in range(inner // LANES):
                at = (t * half + b) * groups
                out_ref[:, b * inner + t * LANES : b * inner + (t + 1) * LANES] = tall[at : at + groups, :]

    return pl.pallas_call(
        kernel,
        name="filter_gradient",
        out_shape=jax.ShapeDtypeStruct((groups, seq_len), jnp.float32),
        scratch_shapes=[
            pltpu.VMEM((half * groups * inner // LANES, LANES), jnp.float32),
            pltpu.VMEM((2 * outer, groups * inner), jnp.bfloat16),
        ],
        compiler_params=pltpu.CompilerParams(vmem_limit_bytes=VMEM_LIMIT),
        cost_estimate=pl.CostEstimate(flops=200_000_000, bytes_accessed=2_000_000, transcendentals=0),
    )(cross, tables["third"], tables["fourth_real"], tables["twist_re"], tables["twist_im"])


RIM = 8


def seven_taps(tall, value, rim, weights, forward):
    count = value.shape[0]
    if forward:
        tall[:RIM, :] = rim
        tall[RIM : RIM + count, :] = value
    else:
        tall[:count, :] = value
        tall[count : count + RIM, :] = rim
    total = value * weights[:1]
    for lag in range(1, TAPS):
        first = RIM - lag if forward else lag
        total = total + tall[first : first + count, :] * weights[lag : lag + 1]
    return total


def lane_block(i, offset=0):
    return pl.ds(pl.multiple_of(i * LANES + offset, LANES), LANES)


def whole_call(kernel, name, out_shape, operands, scratch=(), flops=10_000_000, **kwargs):
    return pl.pallas_call(
        kernel,
        name=name,
        out_shape=out_shape,
        scratch_shapes=list(scratch),
        compiler_params=pltpu.CompilerParams(vmem_limit_bytes=VMEM_LIMIT),
        cost_estimate=pl.CostEstimate(flops=flops, bytes_accessed=4_000_000, transcendentals=0),
        **kwargs,
    )(*operands)


def narrow_shape(*shape):
    return jax.ShapeDtypeStruct(shape, jnp.bfloat16)


def features_of(turned, rim, short_filter, cotangent):
    local, width = cotangent.shape

    def kernel(x_ref, rim_ref, w_ref, og_ref, f_ref, kv_ref, dconv_ref, tall):
        @pl.loop(0, width // LANES)
        def _(i):
            made = []
            for part in range(3):
                lanes = lane_block(i, part * width)
                total = seven_taps(
                    tall.at[part],
                    x_ref[:, lanes].astype(jnp.float32),
                    rim_ref[:, lanes].astype(jnp.float32),
                    w_ref[:, lanes].astype(jnp.float32),
                    True,
                ).astype(jnp.bfloat16)
                f_ref[:, lanes] = total
                made.append(total.astype(jnp.float32))
            rows = lane_block(i)
            kv_ref[rows, :] = (made[1] * made[2]).astype(jnp.bfloat16).T
            og = og_ref[:, rows].astype(jnp.float32)
            dconv_ref[rows, :] = (og * made[0]).astype(jnp.bfloat16).T

    return whole_call(
        kernel,
        "features",
        (narrow_shape(local, 3 * width), narrow_shape(width, local), narrow_shape(width, local)),
        (turned, rim, short_filter, cotangent),
        [pltpu.VMEM((3, local + RIM, LANES), jnp.float32)],
    )


def query_products(feats, conv, cotangent):
    width, local = conv.shape

    def kernel(f_ref, conv_ref, og_ref, mixed_ref, dq_ref, rim_ref):
        @pl.loop(0, width // LANES)
        def _(i):
            lanes = lane_block(i)
            here = conv_ref[lanes, :].T.astype(jnp.float32)
            mixed_ref[lanes, :] = (f_ref[:, lanes].astype(jnp.float32) * here).astype(jnp.bfloat16).T
            dq = (og_ref[:, lanes].astype(jnp.float32) * here).astype(jnp.bfloat16)
            dq_ref[:, lanes] = dq
            rim_ref[:, lanes] = dq[:RIM]

    return whole_call(
        kernel,
        "query_products",
        (narrow_shape(width, local), narrow_shape(local, width), narrow_shape(RIM, width)),
        (feats, conv, cotangent),
    )


def key_value_products(feats, back):
    width, local = back.shape

    def kernel(f_ref, back_ref, d_ref, rim_ref):
        @pl.loop(0, width // LANES)
        def _(i):
            here = back_ref[lane_block(i), :].T.astype(jnp.float32)
            for part in range(2):
                other = f_ref[:, lane_block(i, (2 - part) * width)].astype(jnp.float32)
                grad = (here * other).astype(jnp.bfloat16)
                d_ref[:, lane_block(i, part * width)] = grad
                rim_ref[:, lane_block(i, part * width)] = grad[:RIM]

    return whole_call(
        kernel,
        "key_value_products",
        (narrow_shape(local, 2 * width), narrow_shape(RIM, 2 * width)),
        (feats, back),
    )


def joined_features(turned, rim, short_filter, out_grad, owned):
    width, local = out_grad.shape
    near = LANES // owned
    blocks = width // LANES

    def kernel(x_ref, rim_ref, w_ref, og_ref, f_hbm, msg_ref, edge_ref, tall, made, f_ref, edge, sent):
        def copy(i):
            to = pl.ds(i * near, near)
            return pltpu.make_async_copy(made.at[to], msg_ref.at[to], sent.at[i])

        def keep(part, i):
            at = part * blocks + i
            to = pl.ds(pl.multiple_of(at * LANES, LANES), LANES)
            return pltpu.make_async_copy(f_ref.at[at], f_hbm.at[to, :], sent.at[blocks + at])

        @pl.loop(0, blocks)
        def _(i):
            parts = []
            for part in range(3):
                lanes = lane_block(i, part * width)
                total = seven_taps(
                    tall.at[part],
                    x_ref[:, lanes].astype(jnp.float32),
                    rim_ref[:, lanes].astype(jnp.float32),
                    w_ref[:, lanes].astype(jnp.float32),
                    True,
                ).astype(jnp.bfloat16)
                for t in range(local // LANES):
                    f_ref[part * blocks + i, :, t * LANES : (t + 1) * LANES] = total[t * LANES : (t + 1) * LANES]
                keep(part, i).start()
                if part:
                    edge[:, lanes] = total[:RIM]
                parts.append(total.astype(jnp.float32))
            og = og_ref[lane_block(i), :].T
            edge[:, lane_block(i)] = og[:RIM]
            kv = (parts[1] * parts[2]).astype(jnp.bfloat16).T
            dconv = (og.astype(jnp.float32) * parts[0]).astype(jnp.bfloat16).T
            to = pl.ds(i * near, near)
            made[to, :owned, :] = kv.reshape(near, owned, local)
            made[to, owned:, :] = dconv.reshape(near, owned, local)
            copy(i).start()

        last = pltpu.make_async_copy(edge, edge_ref, sent.at[4 * blocks])
        last.start()

        @pl.loop(0, blocks)
        def _(i):
            copy(i).wait()
            for part in range(3):
                keep(part, i).wait()

        last.wait()

    vmem = pl.BlockSpec(memory_space=pltpu.VMEM)
    hbm = pl.BlockSpec(memory_space=pltpu.HBM)
    devices = width // owned
    return whole_call(
        kernel,
        "joined_features",
        (narrow_shape(3 * width, local), narrow_shape(devices, 2 * owned, local), narrow_shape(RIM, 3 * width)),
        (turned, rim, short_filter, out_grad),
        [
            pltpu.VMEM((3, local + RIM, LANES), jnp.float32),
            pltpu.VMEM((devices, 2 * owned, local), jnp.bfloat16),
            pltpu.VMEM((3 * blocks, LANES, local), jnp.bfloat16),
            pltpu.VMEM((RIM, 3 * width), jnp.bfloat16),
            pltpu.SemaphoreType.DMA((4 * blocks + 1,)),
        ],
        in_specs=[vmem] * 4,
        out_specs=(hbm, hbm, hbm),
    )


def joined_filtering(arrived, filters, joined, tables, seq_len):
    padded, inner, outer = sizes_of(seq_len)
    half = outer // 2
    sources, rows, local = arrived.shape
    channels = rows // 2
    tiles = local // LANES
    fold = local // inner
    groups = channels // CPG
    pairs = groups * PAIRS
    height = sources * channels
    chunk = sources // 4

    def kernel(x_ref, f_ref, table_ref, tr_ref, ti_ref, y_hbm, cross_hbm, y_ref, cross_ref, talls, wides, stages, turns, sems):
        second_ref, third_ref = table_ref.at[: 2 * inner], table_ref.at[2 * inner : 4 * inner]
        fourth_ref = table_ref.at[4 * inner : 4 * inner + 2 * half]
        firsts = table_ref[4 * inner + 2 * half :, :]
        first = jnp.concatenate([firsts[:, : 2 * half], firsts[:, 2 * half :]], axis=0)
        tr, ti = tr_ref[...], ti_ref[...]
        for s in range(2):
            tall, wide, stage = talls.at[s], wides.at[s], stages.at[s]
            for t in range(tiles):
                block = x_ref[:, s * channels : (s + 1) * channels, t * LANES : (t + 1) * LANES]
                tall[t * height : (t + 1) * height, :] = block.astype(jnp.float32).reshape(height, LANES)
            for c in range(channels):
                pair, part = divmod(c, 2)
                for h in range(fold):
                    line = spread(tall, sources, channels, c, height, (h * inner, (h + 1) * inner))
                    at = part * half + h * sources
                    wide[at : at + sources, pair * inner : (pair + 1) * inner] = line.astype(jnp.bfloat16)
            for g in range(groups):
                span = PAIRS * inner
                f = dot(first, wide[:, g * span : (g + 1) * span])
                for p in range(PAIRS):
                    f_re = f[:outer, p * inner : (p + 1) * inner]
                    f_im = f[outer:, p * inner : (p + 1) * inner]
                    at = (g * PAIRS + p) * outer
                    stage[at : at + outer, :inner] = (f_re * tr + f_im * ti).astype(jnp.bfloat16)
                    stage[at : at + outer, inner:] = (f_im * tr - f_re * ti).astype(jnp.bfloat16)
        for g in range(groups):
            s_re = f_ref[g * outer : (g + 1) * outer, :inner]
            s_im = f_ref[g * outer : (g + 1) * outer, inner:]
            cross_re = cross_im = 0.0
            for p in range(PAIRS):
                at = (g * PAIRS + p) * outer
                k = dot(stages[0, at : at + outer, :], second_ref[...])
                d = dot(stages[1, at : at + outer, :], second_ref[...])
                k_re, k_im = k[:, :inner], k[:, inner:]
                d_re, d_im = d[:, :inner], d[:, inner:]
                cross_re = cross_re + (k_re * d_re + k_im * d_im)
                cross_im = cross_im + (k_re * d_im - k_im * d_re)
                stages[0, at : at + outer, :inner] = (s_re * k_re - s_im * k_im).astype(jnp.bfloat16)
                stages[0, at : at + outer, inner:] = (s_re * k_im + s_im * k_re).astype(jnp.bfloat16)
                stages[1, at : at + outer, :inner] = (s_re * d_re + s_im * d_im).astype(jnp.bfloat16)
                stages[1, at : at + outer, inner:] = (s_re * d_im - s_im * d_re).astype(jnp.bfloat16)
            cross_ref[g * outer : (g + 1) * outer, :inner] = cross_re.astype(jnp.bfloat16)
            cross_ref[g * outer : (g + 1) * outer, inner:] = cross_im.astype(jnp.bfloat16)
        copies = [pltpu.make_async_copy(cross_ref, cross_hbm, sems.at[4])]
        copies[0].start()
        spot = lax.broadcasted_iota(jnp.int32, (RIM, LANES), 0)
        lane = lax.broadcasted_iota(jnp.int32, (RIM, LANES), 1)
        pick = jnp.where(spot == lane, 1.0, 0.0).astype(jnp.bfloat16)
        rims = []
        for s in range(2):
            tall, stage, turn = talls.at[s], stages.at[s], turns.at[s]
            for pair in range(pairs):
                at = pair * outer
                h = dot(stage[at : at + outer, :], third_ref[...])
                h_re, h_im = h[:, :inner], h[:, inner:]
                lanes = slice(pair * inner, (pair + 1) * inner)
                turn[:outer, lanes] = (h_re * tr - h_im * ti).astype(jnp.bfloat16)
                turn[outer:, lanes] = (h_im * tr + h_re * ti).astype(jnp.bfloat16)
            for g in range(groups):
                span = PAIRS * inner
                y = dot(fourth_ref[...], turn[:, g * span : (g + 1) * span])
                for p in range(PAIRS):
                    for part in range(2):
                        c = (g * PAIRS + p) * 2 + part
                        for h in range(fold):
                            at = part * half + h * sources
                            line = y[at : at + sources, p * inner : (p + 1) * inner]
                            put_spread(tall, line, channels, c, height, (h * inner, (h + 1) * inner))
            front = tall[:height, :].astype(jnp.bfloat16)
            rims.append(
                lax.dot_general(pick, front, (((1,), (1,)), ((), ())), preferred_element_type=jnp.float32)
            )
        for q in range(4):
            to = slice(q * chunk, (q + 1) * chunk)
            for s in range(2):
                for t in range(tiles):
                    at = t * height + q * chunk * channels
                    block = talls[s, at : at + chunk * channels, :].reshape(chunk, channels, LANES)
                    row = (s * tiles + t) * channels
                    y_ref[to, row : row + channels, :] = block.astype(jnp.bfloat16)
            for d in range(q * chunk, (q + 1) * chunk):
                tile, lanes = divmod((d + 1) % sources * channels, LANES)
                edge = jnp.zeros((RIM, LANES), jnp.float32)
                if d < sources - 1:
                    for s in range(2):
                        piece = rims[s][:, tile * LANES : (tile + 1) * LANES]
                        turn_by = (s * channels - lanes) % LANES
                        if turn_by:
                            piece = pltpu.roll(piece, turn_by, 1)
                        edge = piece if s == 0 else jnp.where(lane < channels, edge, piece)
                y_ref[d, 2 * tiles * channels :, :] = edge.astype(jnp.bfloat16)
            copies.append(pltpu.make_async_copy(y_ref.at[to], y_hbm.at[to], sems.at[q]))
            copies[-1].start()
        for copy in copies:
            copy.wait()

    sent = (sources, 2 * tiles * channels + RIM, LANES)
    vmem = pl.BlockSpec(memory_space=pltpu.VMEM)
    hbm = pl.BlockSpec(memory_space=pltpu.HBM)
    return whole_call(
        kernel,
        "joined_filtering",
        (narrow_shape(*sent), narrow_shape(groups * outer, 2 * inner)),
        [arrived, filters, joined, tables["twist_re"], tables["twist_im"]],
        [
            pltpu.VMEM(sent, jnp.bfloat16),
            pltpu.VMEM((groups * outer, 2 * inner), jnp.bfloat16),
            pltpu.VMEM((2, tiles * height, LANES), jnp.float32),
            pltpu.VMEM((2, outer, pairs * inner), jnp.bfloat16),
            pltpu.VMEM((2, pairs * outer, 2 * inner), jnp.bfloat16),
            pltpu.VMEM((2, 2 * outer, pairs * inner), jnp.bfloat16),
            pltpu.SemaphoreType.DMA((5,)),
        ],
        flops=4_000_000_000,
        in_specs=[vmem] * 5,
        out_specs=(hbm, hbm),
    )


def joined_gradients(cross, feats, edges, returned, out_grad, short_filter, owned):
    width, local = out_grad.shape
    tiles = local // LANES
    near = LANES // owned
    blocks = width // LANES

    def kernel(_, f_hbm, edge_ref, back_ref, og_ref, w_ref, mixed_ref, out_ref, tall, made, f_ref, sent, fetched):
        def fetch(part, i):
            at = part * blocks + i
            rows = pl.ds(pl.multiple_of(at * LANES, LANES), LANES)
            return pltpu.make_async_copy(f_hbm.at[rows, :], f_ref.at[at], fetched.at[at])

        @pl.loop(0, blocks)
        def _(i):
            for part in range(3):
                fetch(part, i).start()

        def features(part, i):
            held = [f_ref[part * blocks + i, :, t * LANES : (t + 1) * LANES] for t in range(tiles)]
            return jnp.concatenate(held, axis=0).astype(jnp.float32)

        lane = lax.broadcasted_iota(jnp.int32, (RIM, LANES), 1)

        def copy(part, i):
            at = part * blocks + i
            if part < 3:
                to = out_ref.at[pl.ds(pl.multiple_of(at * LANES, LANES), LANES), :]
            else:
                to = mixed_ref.at[lane_block(i), :]
            return pltpu.make_async_copy(made.at[at], to, sent.at[at])

        def turned(s, i):
            held = pl.ds(i * near, near)
            pieces = [
                back_ref[held, (s * tiles + t) * owned : (s * tiles + t + 1) * owned, :].reshape(LANES, LANES).T
                for t in range(tiles)
            ]
            return jnp.concatenate(pieces, axis=0).astype(jnp.float32)

        def rim_of(s, i):
            rim = None
            for n in range(near):
                piece = back_ref[i * near + n, 2 * tiles * owned :, :].astype(jnp.float32)
                turn_by = (n - s) * owned % LANES
                if turn_by:
                    piece = pltpu.roll(piece, turn_by, 1)
                rim = jnp.where(lane >= n * owned, piece, rim) if n else piece
            return rim

        def third(part, i, here, rim, other):
            edge = edge_ref[:, lane_block(i, (3 - part) % 3 * width)].astype(jnp.float32)
            total = seven_taps(
                tall.at[part],
                (here * other).astype(jnp.bfloat16).astype(jnp.float32),
                (rim * edge).astype(jnp.bfloat16).astype(jnp.float32),
                w_ref[:, lane_block(i, part * width)].astype(jnp.float32),
                False,
            )
            made[part * blocks + i] = total.astype(jnp.bfloat16).T
            if part == 0:
                fetch(0, i).wait()
            copy(part, i).start()

        @pl.loop(0, blocks)
        def _(i):
            third(0, i, turned(0, i), rim_of(0, i), og_ref[lane_block(i), :].T.astype(jnp.float32))

        @pl.loop(0, blocks)
        def _(i):
            fetch(1, i).wait()
            fetch(2, i).wait()
            query, key, value = [features(part, i) for part in range(3)]
            made[3 * blocks + i] = (query * turned(0, i)).astype(jnp.bfloat16).T
            copy(3, i).start()
            here, rim = turned(1, i), rim_of(1, i)
            third(1, i, here, rim, value)
            third(2, i, here, rim, key)

        @pl.loop(0, blocks)
        def _(i):
            for part in range(4):
                copy(part, i).wait()

    vmem = pl.BlockSpec(memory_space=pltpu.VMEM)
    hbm = pl.BlockSpec(memory_space=pltpu.HBM)
    return whole_call(
        kernel,
        "joined_gradients",
        (narrow_shape(width, local), narrow_shape(3 * width, local)),
        (cross, feats, edges, returned, out_grad, short_filter),
        [
            pltpu.VMEM((3, local + RIM, LANES), jnp.float32),
            pltpu.VMEM((4 * blocks, LANES, local), jnp.bfloat16),
            pltpu.VMEM((3 * blocks, LANES, local), jnp.bfloat16),
            pltpu.SemaphoreType.DMA((4 * blocks,)),
            pltpu.SemaphoreType.DMA((3 * blocks,)),
        ],
        in_specs=[hbm, hbm] + [vmem] * 4,
        out_specs=(hbm, hbm),
        input_output_aliases={0: 0, 1: 1},
    )


def query_gradient(grad, rim, short_filter):
    local, width = grad.shape
    steps = width // GRAD_ROWS

    def kernel(d_ref, rim_ref, w_ref, out_ref, tall):
        gradient_block(d_ref, rim_ref, w_ref, out_ref, tall)

    return gradient_call(kernel, "query_gradient", (), grad, rim, short_filter, 1, 0)


def key_value_gradient(whole, grad, rim, short_filter):
    def kernel(_, d_ref, rim_ref, w_ref, out_ref, tall):
        gradient_block(d_ref, rim_ref, w_ref, out_ref, tall)

    return gradient_call(kernel, "key_value_gradient", (whole,), grad, rim, short_filter, 2, 1)


GRAD_ROWS = 512


def gradient_block(d_ref, rim_ref, w_ref, out_ref, tall):
    for c in range(GRAD_ROWS // LANES):
        lanes = slice(c * LANES, (c + 1) * LANES)
        total = seven_taps(
            tall.at[c],
            d_ref[:, lanes].astype(jnp.float32),
            rim_ref[:, lanes].astype(jnp.float32),
            w_ref[:, lanes].astype(jnp.float32),
            False,
        )
        out_ref[lanes, :] = total.astype(jnp.bfloat16).T


def gradient_call(kernel, name, whole, grad, rim, short_filter, parts, first):
    local, lanes = grad.shape
    width = lanes // parts
    steps = width // GRAD_ROWS
    return pl.pallas_call(
        kernel,
        name=name,
        grid=(parts * steps,),
        in_specs=[pl.BlockSpec(memory_space=pl.ANY)] * len(whole)
        + [
            pl.BlockSpec((local, GRAD_ROWS), lambda i: (0, i)),
            pl.BlockSpec((RIM, GRAD_ROWS), lambda i: (0, i)),
            pl.BlockSpec((TAPS, GRAD_ROWS), lambda i: (0, first * steps + i)),
        ],
        out_specs=pl.BlockSpec((GRAD_ROWS, local), lambda i: (first * steps + i, 0)),
        out_shape=narrow_shape(3 * width, local),
        scratch_shapes=[pltpu.VMEM((GRAD_ROWS // LANES, local + RIM, LANES), jnp.float32)],
        input_output_aliases={0: 0} if whole else {},
        cost_estimate=pl.CostEstimate(flops=20_000_000, bytes_accessed=4_000_000, transcendentals=0),
    )(*whole, grad, rim, short_filter)


def shards(projections, short_filter, long_filter, out_grad):
    width, local_len = out_grad.shape
    devices = lax.axis_size(EVERYONE)
    seq_len = local_len * devices
    owned = width // devices
    tables = make_tables(seq_len, devices)

    turned = projections.T
    rim = shifted(turned[local_len - RIM :], EVERYONE, 1)

    _, inner, outer = sizes_of(seq_len)
    twin = owned // CPG * outer == width and 2 * inner == local_len and inner == outer
    if owned % 16 == 0 and LANES % (2 * owned) == 0 and devices % 4 == 0 and twin:
        feats, message, edges = joined_features(turned, rim, short_filter, out_grad, owned)
        filters, joined = transform_filters(long_filter, tables, seq_len, [tables["joined"]])
        arrived = lax.all_to_all(message, EVERYONE, split_axis=0, concat_axis=0, tiled=True)
        edges, filters, joined, arrived = lax.optimization_barrier(
            (shifted(edges, EVERYONE, -1), filters, joined, arrived)
        )
        answer, cross = joined_filtering(arrived, filters, joined, tables, seq_len)
        returned = lax.all_to_all(answer, EVERYONE, split_axis=0, concat_axis=0, tiled=True)
        filter_grad = filter_gradient(cross, tables, seq_len)
        filter_grad, returned, cross = lax.optimization_barrier((filter_grad, returned, cross))
        mixed, grad = joined_gradients(cross, feats, edges, returned, out_grad, short_filter, owned)
        return (mixed, grad, filter_grad)

    cotangent = out_grad.T
    feats, product, conv_grad = features_of(turned, rim, short_filter, cotangent)

    def exchange(block):
        pieces = block.reshape(devices, owned, local_len)
        return lax.all_to_all(pieces, EVERYONE, split_axis=0, concat_axis=0, tiled=True)

    (filters,) = transform_filters(long_filter, tables, seq_len)
    prod_chan = exchange(product)
    conv_grad, prod_chan = lax.optimization_barrier((conv_grad, prod_chan))
    grad_chan = exchange(conv_grad)
    conv_chan, prod_spec = filtered(prod_chan, filters, tables, seq_len)
    conv_chan, grad_chan = lax.optimization_barrier((conv_chan, grad_chan))
    conv_tok = exchange(conv_chan)
    back_chan, cross = filtered(grad_chan, filters, tables, seq_len, prod_spec)
    back_chan, conv_tok = lax.optimization_barrier((back_chan, conv_tok))
    back_tok = exchange(back_chan)

    filter_grad = filter_gradient(cross, tables, seq_len)
    mixed, grad_q, rim_q = query_products(feats, conv_tok.reshape(width, local_len), cotangent)
    grad = query_gradient(grad_q, shifted(rim_q, EVERYONE, -1), short_filter)
    filter_grad, mixed, grad, back_tok = lax.optimization_barrier((filter_grad, mixed, grad, back_tok))

    grad_kv, rim_kv = key_value_products(feats, back_tok.reshape(width, local_len))
    grad = key_value_gradient(grad, grad_kv, shifted(rim_kv, EVERYONE, -1), short_filter)
    return (mixed, grad, filter_grad)


def solution(mesh):
    placed = (P(None, EVERYONE), P(), P(EVERYONE, None), P(None, EVERYONE))
    return jax.shard_map(
        shards,
        mesh=mesh,
        in_specs=placed,
        out_specs=(P(None, EVERYONE), P(None, EVERYONE), P(EVERYONE, None)),
        check_vma=False,
    )
```

```python
import math

import jax
import jax.numpy as jnp
import numpy as np
from jax import lax
from jax.experimental import pallas as pl
from jax.experimental.pallas import tpu as pltpu
from jax.sharding import PartitionSpec as P

CPG = 4
TAPS = 7
PAIRS = CPG // 2
EVERYONE = ("dp", "ctx")
VMEM_LIMIT = 24 * 1024 * 1024


def shifted(value, axis, steps):
    count = lax.axis_size(axis)
    first, last = (max(0, -steps), min(count, count - steps))
    return lax.ppermute(value, axis, [(source, source + steps) for source in range(first, last)])


def sizes_of(seq_len):
    padded = 2 * seq_len
    inner = max(d for d in range(1, seq_len + 1) if seq_len % d == 0 and d * d <= padded)
    return padded, inner, padded // inner


def table(count_out, count_in, period):
    turns = np.arange(count_out, dtype=np.int64)[:, None] * np.arange(count_in, dtype=np.int64)
    angle = (turns % period).astype(np.float64) * (2.0 * math.pi / period)
    return np.cos(angle), np.sin(angle)


def make_tables(seq_len, sources):
    padded, inner, outer = sizes_of(seq_len)
    half = outer // 2
    fold = half // sources
    order = np.arange(half).reshape(sources, fold).T.reshape(-1)
    cos_o, sin_o = table(outer, half, outer)
    cos_i, sin_i = table(inner, inner, inner)
    cos_p, sin_p = cos_o[:, order], sin_o[:, order]
    narrow = lambda blocks: jnp.asarray(np.block(blocks).astype(np.float32)).astype(jnp.bfloat16)
    twist = [jnp.asarray(t.astype(np.float32)) for t in table(outer, inner, padded)]
    return {
        "first": narrow([[cos_p, sin_p], [-sin_p, cos_p]]),
        "second": narrow([[cos_i, -sin_i], [sin_i, cos_i]]),
        "third": narrow([[cos_i, sin_i], [-sin_i, cos_i]]),
        "fourth": narrow([[cos_p.T, -sin_p.T], [sin_p.T, cos_p.T]]),
        "joined": narrow(
            [
                [cos_i, -sin_i],
                [sin_i, cos_i],
                [cos_i, sin_i],
                [-sin_i, cos_i],
                [cos_p.T / padded, -sin_p.T / padded],
                [sin_p.T / padded, cos_p.T / padded],
                [np.hstack([cos_p, sin_p]), np.hstack([-sin_p, cos_p])],
            ]
        )
        if inner == outer
        else None,
        "first_real": narrow([[cos_o], [-sin_o]]),
        "fourth_real": narrow([[cos_o.T, -sin_o.T]]),
        "twist_re": twist[0],
        "twist_im": twist[1],
    }


LANES = 128


def spread(tall, count, stride, first, height, width):
    tiles = [tall[pl.ds(t * height + first, count, stride=stride), :] for t in range(width[0] // LANES, width[1] // LANES)]
    return tiles[0] if len(tiles) == 1 else jnp.concatenate(tiles, axis=1)


def put_spread(tall, values, stride, first, height, width):
    for i, t in enumerate(range(width[0] // LANES, width[1] // LANES)):
        tall[pl.ds(t * height + first, values.shape[0], stride=stride), :] = values[:, i * LANES : (i + 1) * LANES]


def dot(left, right):
    return jnp.dot(left, right, preferred_element_type=jnp.float32)


def transform_filters(long_filter, tables, seq_len, kind=jnp.float32, handed=()):
    padded, inner, outer = sizes_of(seq_len)
    half = outer // 2
    groups = long_filter.shape[0]
    scale = seq_len ** -0.5

    def kernel(x_ref, first_ref, second_ref, tr_ref, ti_ref, *refs):
        count = len(handed)
        out_ref, tall = refs[count], refs[-1]
        for n in range(count):
            refs[count + 1 + n][...] = refs[n][...]
        height = half * groups
        for b in range(half):
            for t in range(inner // LANES):
                at = t * height + b * groups
                lanes = slice(b * inner + t * LANES, b * inner + (t + 1) * LANES)
                tall[at : at + groups, :] = x_ref[:, lanes].astype(jnp.float32)
        for g in range(groups):
            x = spread(tall, half, groups, g, height, (0, inner)).astype(jnp.bfloat16)
            f = dot(first_ref[...], x)
            f_re, f_im = f[:outer], f[outer:]
            g_re = (f_re * tr_ref[...] + f_im * ti_ref[...]).astype(jnp.bfloat16)
            g_im = (f_im * tr_ref[...] - f_re * ti_ref[...]).astype(jnp.bfloat16)
            spec = dot(g_re, second_ref[:inner]) + dot(g_im, second_ref[inner:])
            out_ref[g * outer : (g + 1) * outer, :] = (spec * scale).astype(kind)

    return pl.pallas_call(
        kernel,
        name="filter_dft",
        out_shape=[jax.ShapeDtypeStruct((groups * outer, 2 * inner), kind)]
        + [jax.ShapeDtypeStruct(array.shape, array.dtype) for array in handed],
        scratch_shapes=[pltpu.VMEM((half * groups * inner // LANES, LANES), jnp.float32)],
        compiler_params=pltpu.CompilerParams(vmem_limit_bytes=VMEM_LIMIT),
        cost_estimate=pl.CostEstimate(flops=200_000_000, bytes_accessed=2_000_000, transcendentals=0),
    )(long_filter, tables["first_real"], tables["second"], tables["twist_re"], tables["twist_im"], *handed)


def filtered(arrived, filters, tables, seq_len, other=None):
    padded, inner, outer = sizes_of(seq_len)
    half = outer // 2
    sources, channels, local = arrived.shape
    fold = local // inner
    groups = channels // CPG
    backward = other is not None

    def kernel(*refs):
        if backward:
            (x_ref, f_ref, k_ref, first_ref, second_ref, third_ref, fourth_ref, tr_ref, ti_ref,
             y_ref, cross_ref, tall, wide, stage, turn) = refs
        else:
            (x_ref, f_ref, first_ref, second_ref, third_ref, fourth_ref, tr_ref, ti_ref,
             y_ref, z_ref, tall, wide, stage, turn) = refs
        height = sources * channels
        for t in range(local // LANES):
            block = x_ref[:, :, t * LANES : (t + 1) * LANES].astype(jnp.float32)
            tall[t * height : (t + 1) * height, :] = block.reshape(height, LANES)
        for c in range(channels):
            pair, part = divmod(c, 2)
            for h in range(fold):
                rows = spread(tall, sources, channels, c, height, (h * inner, (h + 1) * inner))
                at = part * half + h * sources
                wide[at : at + sources, pair * inner : (pair + 1) * inner] = rows.astype(jnp.bfloat16)
        for g in range(groups):
            span = PAIRS * inner
            f = dot(first_ref[...], wide[:, g * span : (g + 1) * span])
            for p in range(PAIRS):
                f_re = f[:outer, p * inner : (p + 1) * inner]
                f_im = f[outer:, p * inner : (p + 1) * inner]
                at = (g * PAIRS + p) * outer
                stage[at : at + outer, :inner] = (f_re * tr_ref[...] + f_im * ti_ref[...]).astype(jnp.bfloat16)
                stage[at : at + outer, inner:] = (f_im * tr_ref[...] - f_re * ti_ref[...]).astype(jnp.bfloat16)
        for g in range(groups):
            s_re = f_ref[g * outer : (g + 1) * outer, :inner]
            s_im = f_ref[g * outer : (g + 1) * outer, inner:]
            cross_re = cross_im = None
            for p in range(PAIRS):
                at = (g * PAIRS + p) * outer
                z = dot(stage[at : at + outer, :], second_ref[...])
                z_re, z_im = z[:, :inner], z[:, inner:]
                if backward:
                    k_re = k_ref[at : at + outer, :inner].astype(jnp.float32)
                    k_im = k_ref[at : at + outer, inner:].astype(jnp.float32)
                    part_re = k_re * z_re + k_im * z_im
                    part_im = k_re * z_im - k_im * z_re
                    cross_re = part_re if cross_re is None else cross_re + part_re
                    cross_im = part_im if cross_im is None else cross_im + part_im
                    o_re = s_re * z_re + s_im * z_im
                    o_im = s_re * z_im - s_im * z_re
                else:
                    z_ref[at : at + outer, :] = z
                    o_re = s_re * z_re - s_im * z_im
                    o_im = s_re * z_im + s_im * z_re
                stage[at : at + outer, :inner] = o_re.astype(jnp.bfloat16)
                stage[at : at + outer, inner:] = o_im.astype(jnp.bfloat16)
            if backward:
                cross_ref[g * outer : (g + 1) * outer, :inner] = cross_re.astype(jnp.bfloat16)
                cross_ref[g * outer : (g + 1) * outer, inner:] = cross_im.astype(jnp.bfloat16)
        for pair in range(groups * PAIRS):
            at = pair * outer
            h = dot(stage[at : at + outer, :], third_ref[...])
            h_re, h_im = h[:, :inner], h[:, inner:]
            lanes = slice(pair * inner, (pair + 1) * inner)
            turn[:outer, lanes] = (h_re * tr_ref[...] - h_im * ti_ref[...]).astype(jnp.bfloat16)
            turn[outer:, lanes] = (h_im * tr_ref[...] + h_re * ti_ref[...]).astype(jnp.bfloat16)
        for g in range(groups):
            span = PAIRS * inner
            y = dot(fourth_ref[...], turn[:, g * span : (g + 1) * span]) * (1.0 / padded)
            for p in range(PAIRS):
                for part in range(2):
                    c = (g * PAIRS + p) * 2 + part
                    for h in range(fold):
                        at = part * half + h * sources
                        rows = y[at : at + sources, p * inner : (p + 1) * inner]
                        put_spread(tall, rows, channels, c, height, (h * inner, (h + 1) * inner))
        for t in range(local // LANES):
            block = tall[t * height : (t + 1) * height, :].reshape(sources, channels, LANES)
            y_ref[:, :, t * LANES : (t + 1) * LANES] = block.astype(jnp.bfloat16)

    pairs = groups * PAIRS
    if backward:
        extra = jax.ShapeDtypeStruct((groups * outer, 2 * inner), jnp.bfloat16)
    else:
        extra = jax.ShapeDtypeStruct((pairs * outer, 2 * inner), jnp.float32)
    operands = [arrived, filters] + ([other] if backward else [])
    operands += [tables[n] for n in ("first", "second", "third", "fourth", "twist_re", "twist_im")]
    return pl.pallas_call(
        kernel,
        name="correlate" if backward else "convolve",
        out_shape=(jax.ShapeDtypeStruct(arrived.shape, jnp.bfloat16), extra),
        scratch_shapes=[
            pltpu.VMEM((sources * channels * local // LANES, LANES), jnp.float32),
            pltpu.VMEM((outer, pairs * inner), jnp.bfloat16),
            pltpu.VMEM((pairs * outer, 2 * inner), jnp.bfloat16),
            pltpu.VMEM((2 * outer, pairs * inner), jnp.bfloat16),
        ],
        compiler_params=pltpu.CompilerParams(vmem_limit_bytes=VMEM_LIMIT),
        cost_estimate=pl.CostEstimate(flops=2_000_000_000, bytes_accessed=5_000_000, transcendentals=0),
    )(*operands)


def filter_gradient(cross, tables, seq_len):
    padded, inner, outer = sizes_of(seq_len)
    half = outer // 2
    groups = cross.shape[0] // outer
    scale = seq_len ** -0.5 / padded

    def kernel(s_ref, third_ref, fourth_ref, tr_ref, ti_ref, out_ref, tall, turn):
        for g in range(groups):
            h = dot(s_ref[g * outer : (g + 1) * outer, :], third_ref[...])
            h_re, h_im = h[:, :inner], h[:, inner:]
            turn[:outer, g * inner : (g + 1) * inner] = (h_re * tr_ref[...] - h_im * ti_ref[...]).astype(jnp.bfloat16)
            turn[outer:, g * inner : (g + 1) * inner] = (h_im * tr_ref[...] + h_re * ti_ref[...]).astype(jnp.bfloat16)
        for g in range(groups):
            y = dot(fourth_ref[...], turn[:, g * inner : (g + 1) * inner]) * scale
            put_spread(tall, y, groups, g, half * groups, (0, inner))
        for b in range(half):
            for t in range(inner // LANES):
                at = (t * half + b) * groups
                out_ref[:, b * inner + t * LANES : b * inner + (t + 1) * LANES] = tall[at : at + groups, :]

    return pl.pallas_call(
        kernel,
        name="filter_gradient",
        out_shape=jax.ShapeDtypeStruct((groups, seq_len), jnp.float32),
        scratch_shapes=[
            pltpu.VMEM((half * groups * inner // LANES, LANES), jnp.float32),
            pltpu.VMEM((2 * outer, groups * inner), jnp.bfloat16),
        ],
        compiler_params=pltpu.CompilerParams(vmem_limit_bytes=VMEM_LIMIT),
        cost_estimate=pl.CostEstimate(flops=200_000_000, bytes_accessed=2_000_000, transcendentals=0),
    )(cross, tables["third"], tables["fourth_real"], tables["twist_re"], tables["twist_im"])


RIM = 8
STEP = 2


def seven_taps(tall, value, rim, weights, forward):
    count = value.shape[0]
    if forward:
        tall[:RIM, :] = rim
        tall[RIM : RIM + count, :] = value
    else:
        tall[:count, :] = value
        tall[count : count + RIM, :] = rim
    total = value * weights[:1]
    for lag in range(1, TAPS):
        first = RIM - lag if forward else lag
        total = total + tall[first : first + count, :] * weights[lag : lag + 1]
    return total


def lane_block(i, offset=0):
    return pl.ds(pl.multiple_of(i * LANES + offset, LANES), LANES)


def whole_call(kernel, name, out_shape, operands, scratch=(), flops=10_000_000, **kwargs):
    return pl.pallas_call(
        kernel,
        name=name,
        out_shape=out_shape,
        scratch_shapes=list(scratch),
        compiler_params=pltpu.CompilerParams(vmem_limit_bytes=VMEM_LIMIT),
        cost_estimate=pl.CostEstimate(flops=flops, bytes_accessed=4_000_000, transcendentals=0),
        **kwargs,
    )(*operands)


def narrow_shape(*shape):
    return jax.ShapeDtypeStruct(shape, jnp.bfloat16)


def features_of(turned, rim, short_filter, cotangent):
    local, width = cotangent.shape

    def kernel(x_ref, rim_ref, w_ref, og_ref, f_ref, kv_ref, dconv_ref, tall):
        @pl.loop(0, width // LANES)
        def _(i):
            made = []
            for part in range(3):
                lanes = lane_block(i, part * width)
                total = seven_taps(
                    tall.at[part],
                    x_ref[:, lanes].astype(jnp.float32),
                    rim_ref[:, lanes].astype(jnp.float32),
                    w_ref[:, lanes].astype(jnp.float32),
                    True,
                ).astype(jnp.bfloat16)
                f_ref[:, lanes] = total
                made.append(total.astype(jnp.float32))
            rows = lane_block(i)
            kv_ref[rows, :] = (made[1] * made[2]).astype(jnp.bfloat16).T
            og = og_ref[:, rows].astype(jnp.float32)
            dconv_ref[rows, :] = (og * made[0]).astype(jnp.bfloat16).T

    return whole_call(
        kernel,
        "features",
        (narrow_shape(local, 3 * width), narrow_shape(width, local), narrow_shape(width, local)),
        (turned, rim, short_filter, cotangent),
        [pltpu.VMEM((3, local + RIM, LANES), jnp.float32)],
    )


def query_products(feats, conv, cotangent):
    width, local = conv.shape

    def kernel(f_ref, conv_ref, og_ref, mixed_ref, dq_ref, rim_ref):
        @pl.loop(0, width // LANES)
        def _(i):
            lanes = lane_block(i)
            here = conv_ref[lanes, :].T.astype(jnp.float32)
            mixed_ref[lanes, :] = (f_ref[:, lanes].astype(jnp.float32) * here).astype(jnp.bfloat16).T
            dq = (og_ref[:, lanes].astype(jnp.float32) * here).astype(jnp.bfloat16)
            dq_ref[:, lanes] = dq
            rim_ref[:, lanes] = dq[:RIM]

    return whole_call(
        kernel,
        "query_products",
        (narrow_shape(width, local), narrow_shape(local, width), narrow_shape(RIM, width)),
        (feats, conv, cotangent),
    )


def key_value_products(feats, back):
    width, local = back.shape

    def kernel(f_ref, back_ref, d_ref, rim_ref):
        @pl.loop(0, width // LANES)
        def _(i):
            here = back_ref[lane_block(i), :].T.astype(jnp.float32)
            for part in range(2):
                other = f_ref[:, lane_block(i, (2 - part) * width)].astype(jnp.float32)
                grad = (here * other).astype(jnp.bfloat16)
                d_ref[:, lane_block(i, part * width)] = grad
                rim_ref[:, lane_block(i, part * width)] = grad[:RIM]

    return whole_call(
        kernel,
        "key_value_products",
        (narrow_shape(local, 2 * width), narrow_shape(RIM, 2 * width)),
        (feats, back),
    )


def joined_features(turned, rim, short_filter, out_grad, owned):
    width, local = out_grad.shape
    near = LANES // owned
    blocks = width // LANES

    def kernel(x_ref, rim_ref, w_ref, og_ref, f_hbm, msg_ref, edge_ref, tall, made, f_ref, edge, sent):
        def copy(i):
            to = pl.ds(i * near, near)
            return pltpu.make_async_copy(made.at[to], msg_ref.at[to], sent.at[i])

        def keep(part, i):
            at = part * blocks + i
            to = pl.ds(pl.multiple_of(at * LANES, LANES), LANES)
            return pltpu.make_async_copy(f_ref.at[at], f_hbm.at[to, :], sent.at[blocks + at])

        @pl.loop(0, blocks // STEP)
        def _(step):
            for slot in range(STEP):
                i = step * STEP + slot
                parts = []
                for part in range(3):
                    lanes = lane_block(i, part * width)
                    total = seven_taps(
                        tall.at[3 * slot + part],
                        x_ref[:, lanes].astype(jnp.float32),
                        rim_ref[:, lanes].astype(jnp.float32),
                        w_ref[:, lanes].astype(jnp.float32),
                        True,
                    ).astype(jnp.bfloat16)
                    for t in range(local // LANES):
                        f_ref[part * blocks + i, :, t * LANES : (t + 1) * LANES] = total[t * LANES : (t + 1) * LANES]
                    if part:
                        edge[:, lanes] = total[:RIM]
                    parts.append(total.astype(jnp.float32))
                og = og_ref[lane_block(i), :].T
                edge[:, lane_block(i)] = og[:RIM]
                kv = (parts[1] * parts[2]).astype(jnp.bfloat16).T
                dconv = (og.astype(jnp.float32) * parts[0]).astype(jnp.bfloat16).T
                to = pl.ds(i * near, near)
                made[to, :owned, :] = kv.reshape(near, owned, local)
                made[to, owned:, :] = dconv.reshape(near, owned, local)
            for slot in range(STEP):
                copy(step * STEP + slot).start()
                for part in range(3):
                    keep(part, step * STEP + slot).start()

        last = pltpu.make_async_copy(edge, edge_ref, sent.at[4 * blocks])
        last.start()

        @pl.loop(0, blocks)
        def _(i):
            copy(i).wait()
            for part in range(3):
                keep(part, i).wait()

        last.wait()

    vmem = pl.BlockSpec(memory_space=pltpu.VMEM)
    hbm = pl.BlockSpec(memory_space=pltpu.HBM)
    devices = width // owned
    return whole_call(
        kernel,
        "joined_features",
        (narrow_shape(3 * width, local), narrow_shape(devices, 2 * owned, local), narrow_shape(RIM, 3 * width)),
        (turned, rim, short_filter, out_grad),
        [
            pltpu.VMEM((3 * STEP, local + RIM, LANES), jnp.float32),
            pltpu.VMEM((devices, 2 * owned, local), jnp.bfloat16),
            pltpu.VMEM((3 * blocks, LANES, local), jnp.bfloat16),
            pltpu.VMEM((RIM, 3 * width), jnp.bfloat16),
            pltpu.SemaphoreType.DMA((4 * blocks + 1,)),
        ],
        in_specs=[vmem] * 4,
        out_specs=(hbm, hbm, hbm),
    )


def joined_filtering(arrived, filters, joined, tables, seq_len):
    padded, inner, outer = sizes_of(seq_len)
    half = outer // 2
    sources, rows, local = arrived.shape
    channels = rows // 2
    tiles = local // LANES
    fold = local // inner
    groups = channels // CPG
    pairs = groups * PAIRS
    height = sources * channels
    chunk = sources // 4

    def kernel(x_ref, f_ref, table_ref, tr_ref, ti_ref, y_hbm, cross_hbm, y_ref, cross_ref, talls, wides, stages, turns, sems):
        second_ref, third_ref = table_ref.at[: 2 * inner], table_ref.at[2 * inner : 4 * inner]
        fourth_ref = table_ref.at[4 * inner : 4 * inner + 2 * half]
        firsts = table_ref[4 * inner + 2 * half :, :]
        first = jnp.concatenate([firsts[:, : 2 * half], firsts[:, 2 * half :]], axis=0)
        tr, ti = tr_ref[...], ti_ref[...]
        for s in range(2):
            tall, wide, stage = talls.at[s], wides.at[s], stages.at[s]
            for t in range(tiles):
                block = x_ref[:, s * channels : (s + 1) * channels, t * LANES : (t + 1) * LANES]
                tall[t * height : (t + 1) * height, :] = block.astype(jnp.float32).reshape(height, LANES)
            for c in range(channels):
                pair, part = divmod(c, 2)
                for h in range(fold):
                    line = spread(tall, sources, channels, c, height, (h * inner, (h + 1) * inner))
                    at = part * half + h * sources
                    wide[at : at + sources, pair * inner : (pair + 1) * inner] = line.astype(jnp.bfloat16)
            for g in range(groups):
                span = PAIRS * inner
                f = dot(first, wide[:, g * span : (g + 1) * span])
                for p in range(PAIRS):
                    f_re = f[:outer, p * inner : (p + 1) * inner]
                    f_im = f[outer:, p * inner : (p + 1) * inner]
                    at = (g * PAIRS + p) * outer
                    stage[at : at + outer, :inner] = (f_re * tr + f_im * ti).astype(jnp.bfloat16)
                    stage[at : at + outer, inner:] = (f_im * tr - f_re * ti).astype(jnp.bfloat16)
        for g in range(groups):
            s_re = f_ref[g * outer : (g + 1) * outer, :inner].astype(jnp.float32)
            s_im = f_ref[g * outer : (g + 1) * outer, inner:].astype(jnp.float32)
            cross_re = cross_im = 0.0
            for p in range(PAIRS):
                at = (g * PAIRS + p) * outer
                k = dot(stages[0, at : at + outer, :], second_ref[...])
                d = dot(stages[1, at : at + outer, :], second_ref[...])
                k_re, k_im = k[:, :inner], k[:, inner:]
                d_re, d_im = d[:, :inner], d[:, inner:]
                cross_re = cross_re + (k_re * d_re + k_im * d_im)
                cross_im = cross_im + (k_re * d_im - k_im * d_re)
                stages[0, at : at + outer, :inner] = (s_re * k_re - s_im * k_im).astype(jnp.bfloat16)
                stages[0, at : at + outer, inner:] = (s_re * k_im + s_im * k_re).astype(jnp.bfloat16)
                stages[1, at : at + outer, :inner] = (s_re * d_re + s_im * d_im).astype(jnp.bfloat16)
                stages[1, at : at + outer, inner:] = (s_re * d_im - s_im * d_re).astype(jnp.bfloat16)
            cross_ref[g * outer : (g + 1) * outer, :inner] = cross_re.astype(jnp.bfloat16)
            cross_ref[g * outer : (g + 1) * outer, inner:] = cross_im.astype(jnp.bfloat16)
        copies = [pltpu.make_async_copy(cross_ref, cross_hbm, sems.at[4])]
        copies[0].start()
        spot = lax.broadcasted_iota(jnp.int32, (RIM, LANES), 0)
        lane = lax.broadcasted_iota(jnp.int32, (RIM, LANES), 1)
        pick = jnp.where(spot == lane, 1.0, 0.0).astype(jnp.bfloat16)
        rims = []
        for s in range(2):
            tall, stage, turn = talls.at[s], stages.at[s], turns.at[s]
            for pair in range(pairs):
                at = pair * outer
                h = dot(stage[at : at + outer, :], third_ref[...])
                h_re, h_im = h[:, :inner], h[:, inner:]
                lanes = slice(pair * inner, (pair + 1) * inner)
                turn[:outer, lanes] = (h_re * tr - h_im * ti).astype(jnp.bfloat16)
                turn[outer:, lanes] = (h_im * tr + h_re * ti).astype(jnp.bfloat16)
            for g in range(groups):
                span = PAIRS * inner
                y = dot(fourth_ref[...], turn[:, g * span : (g + 1) * span])
                for p in range(PAIRS):
                    for part in range(2):
                        c = (g * PAIRS + p) * 2 + part
                        for h in range(fold):
                            at = part * half + h * sources
                            line = y[at : at + sources, p * inner : (p + 1) * inner]
                            put_spread(tall, line, channels, c, height, (h * inner, (h + 1) * inner))
            front = tall[:height, :].astype(jnp.bfloat16)
            rims.append(
                lax.dot_general(pick, front, (((1,), (1,)), ((), ())), preferred_element_type=jnp.float32)
            )
        for q in range(4):
            to = slice(q * chunk, (q + 1) * chunk)
            for s in range(2):
                for t in range(tiles):
                    at = t * height + q * chunk * channels
                    block = talls[s, at : at + chunk * channels, :].reshape(chunk, channels, LANES)
                    row = (s * tiles + t) * channels
                    y_ref[to, row : row + channels, :] = block.astype(jnp.bfloat16)
            for d in range(q * chunk, (q + 1) * chunk):
                tile, lanes = divmod((d + 1) % sources * channels, LANES)
                edge = jnp.zeros((RIM, LANES), jnp.float32)
                if d < sources - 1:
                    for s in range(2):
                        piece = rims[s][:, tile * LANES : (tile + 1) * LANES]
                        turn_by = (s * channels - lanes) % LANES
                        if turn_by:
                            piece = pltpu.roll(piece, turn_by, 1)
                        edge = piece if s == 0 else jnp.where(lane < channels, edge, piece)
                y_ref[d, 2 * tiles * channels :, :] = edge.astype(jnp.bfloat16)
            copies.append(pltpu.make_async_copy(y_ref.at[to], y_hbm.at[to], sems.at[q]))
            copies[-1].start()
        for copy in copies:
            copy.wait()

    sent = (sources, 2 * tiles * channels + RIM, LANES)
    vmem = pl.BlockSpec(memory_space=pltpu.VMEM)
    hbm = pl.BlockSpec(memory_space=pltpu.HBM)
    return whole_call(
        kernel,
        "joined_filtering",
        (narrow_shape(*sent), narrow_shape(groups * outer, 2 * inner)),
        [arrived, filters, joined, tables["twist_re"], tables["twist_im"]],
        [
            pltpu.VMEM(sent, jnp.bfloat16),
            pltpu.VMEM((groups * outer, 2 * inner), jnp.bfloat16),
            pltpu.VMEM((2, tiles * height, LANES), jnp.float32),
            pltpu.VMEM((2, outer, pairs * inner), jnp.bfloat16),
            pltpu.VMEM((2, pairs * outer, 2 * inner), jnp.bfloat16),
            pltpu.VMEM((2, 2 * outer, pairs * inner), jnp.bfloat16),
            pltpu.SemaphoreType.DMA((5,)),
        ],
        flops=4_000_000_000,
        in_specs=[vmem] * 5,
        out_specs=(hbm, hbm),
    )


def joined_gradients(cross, feats, edges, returned, out_grad, short_filter, owned):
    width, local = out_grad.shape
    tiles = local // LANES
    near = LANES // owned
    blocks = width // LANES

    def kernel(_, f_hbm, edge_ref, back_ref, og_ref, w_ref, mixed_ref, out_ref, tall, made, f_ref, sent, fetched):
        def fetch(part, i):
            at = part * blocks + i
            rows = pl.ds(pl.multiple_of(at * LANES, LANES), LANES)
            return pltpu.make_async_copy(f_hbm.at[rows, :], f_ref.at[at], fetched.at[at])

        @pl.loop(0, blocks)
        def _(i):
            for part in range(3):
                fetch(part, i).start()

        def features(part, i):
            held = [f_ref[part * blocks + i, :, t * LANES : (t + 1) * LANES] for t in range(tiles)]
            return jnp.concatenate(held, axis=0).astype(jnp.float32)

        lane = lax.broadcasted_iota(jnp.int32, (RIM, LANES), 1)

        def copy(part, i):
            at = part * blocks + i
            if part < 3:
                to = out_ref.at[pl.ds(pl.multiple_of(at * LANES, LANES), LANES), :]
            else:
                to = mixed_ref.at[lane_block(i), :]
            return pltpu.make_async_copy(made.at[at], to, sent.at[at])

        def turned(s, i):
            held = pl.ds(i * near, near)
            pieces = [
                back_ref[held, (s * tiles + t) * owned : (s * tiles + t + 1) * owned, :].reshape(LANES, LANES).T
                for t in range(tiles)
            ]
            return jnp.concatenate(pieces, axis=0).astype(jnp.float32)

        def rim_of(s, i):
            rim = None
            for n in range(near):
                piece = back_ref[i * near + n, 2 * tiles * owned :, :].astype(jnp.float32)
                turn_by = (n - s) * owned % LANES
                if turn_by:
                    piece = pltpu.roll(piece, turn_by, 1)
                rim = jnp.where(lane >= n * owned, piece, rim) if n else piece
            return rim

        def third(part, slot, i, here, rim, other):
            edge = edge_ref[:, lane_block(i, (3 - part) % 3 * width)].astype(jnp.float32)
            total = seven_taps(
                tall.at[3 * slot + part],
                (here * other).astype(jnp.bfloat16).astype(jnp.float32),
                (rim * edge).astype(jnp.bfloat16).astype(jnp.float32),
                w_ref[:, lane_block(i, part * width)].astype(jnp.float32),
                False,
            )
            made[part * blocks + i] = total.astype(jnp.bfloat16).T

        @pl.loop(0, blocks // STEP)
        def _(step):
            for slot in range(STEP):
                for part in range(3):
                    fetch(part, step * STEP + slot).wait()
            for slot in range(STEP):
                i = step * STEP + slot
                query, key, value = [features(part, i) for part in range(3)]
                conv = turned(0, i)
                made[3 * blocks + i] = (query * conv).astype(jnp.bfloat16).T
                third(0, slot, i, conv, rim_of(0, i), og_ref[lane_block(i), :].T.astype(jnp.float32))
                back, rim = turned(1, i), rim_of(1, i)
                third(1, slot, i, back, rim, value)
                third(2, slot, i, back, rim, key)
            for slot in range(STEP):
                for part in range(4):
                    copy(part, step * STEP + slot).start()

        @pl.loop(0, blocks)
        def _(i):
            for part in range(4):
                copy(part, i).wait()

    vmem = pl.BlockSpec(memory_space=pltpu.VMEM)
    hbm = pl.BlockSpec(memory_space=pltpu.HBM)
    return whole_call(
        kernel,
        "joined_gradients",
        (narrow_shape(width, local), narrow_shape(3 * width, local)),
        (cross, feats, edges, returned, out_grad, short_filter),
        [
            pltpu.VMEM((3 * STEP, local + RIM, LANES), jnp.float32),
            pltpu.VMEM((4 * blocks, LANES, local), jnp.bfloat16),
            pltpu.VMEM((3 * blocks, LANES, local), jnp.bfloat16),
            pltpu.SemaphoreType.DMA((4 * blocks,)),
            pltpu.SemaphoreType.DMA((3 * blocks,)),
        ],
        in_specs=[hbm, hbm] + [vmem] * 4,
        out_specs=(hbm, hbm),
        input_output_aliases={0: 0, 1: 1},
    )


def query_gradient(grad, rim, short_filter):
    local, width = grad.shape
    steps = width // GRAD_ROWS

    def kernel(d_ref, rim_ref, w_ref, out_ref, tall):
        gradient_block(d_ref, rim_ref, w_ref, out_ref, tall)

    return gradient_call(kernel, "query_gradient", (), grad, rim, short_filter, 1, 0)


def key_value_gradient(whole, grad, rim, short_filter):
    def kernel(_, d_ref, rim_ref, w_ref, out_ref, tall):
        gradient_block(d_ref, rim_ref, w_ref, out_ref, tall)

    return gradient_call(kernel, "key_value_gradient", (whole,), grad, rim, short_filter, 2, 1)


GRAD_ROWS = 512


def gradient_block(d_ref, rim_ref, w_ref, out_ref, tall):
    for c in range(GRAD_ROWS // LANES):
        lanes = slice(c * LANES, (c + 1) * LANES)
        total = seven_taps(
            tall.at[c],
            d_ref[:, lanes].astype(jnp.float32),
            rim_ref[:, lanes].astype(jnp.float32),
            w_ref[:, lanes].astype(jnp.float32),
            False,
        )
        out_ref[lanes, :] = total.astype(jnp.bfloat16).T


def gradient_call(kernel, name, whole, grad, rim, short_filter, parts, first):
    local, lanes = grad.shape
    width = lanes // parts
    steps = width // GRAD_ROWS
    return pl.pallas_call(
        kernel,
        name=name,
        grid=(parts * steps,),
        in_specs=[pl.BlockSpec(memory_space=pl.ANY)] * len(whole)
        + [
            pl.BlockSpec((local, GRAD_ROWS), lambda i: (0, i)),
            pl.BlockSpec((RIM, GRAD_ROWS), lambda i: (0, i)),
            pl.BlockSpec((TAPS, GRAD_ROWS), lambda i: (0, first * steps + i)),
        ],
        out_specs=pl.BlockSpec((GRAD_ROWS, local), lambda i: (first * steps + i, 0)),
        out_shape=narrow_shape(3 * width, local),
        scratch_shapes=[pltpu.VMEM((GRAD_ROWS // LANES, local + RIM, LANES), jnp.float32)],
        input_output_aliases={0: 0} if whole else {},
        cost_estimate=pl.CostEstimate(flops=20_000_000, bytes_accessed=4_000_000, transcendentals=0),
    )(*whole, grad, rim, short_filter)


def shards(projections, short_filter, long_filter, out_grad):
    width, local_len = out_grad.shape
    devices = lax.axis_size(EVERYONE)
    seq_len = local_len * devices
    owned = width // devices
    tables = make_tables(seq_len, devices)

    turned = projections.T
    rim = shifted(turned[local_len - RIM :], EVERYONE, 1)

    _, inner, outer = sizes_of(seq_len)
    twin = owned // CPG * outer == width and 2 * inner == local_len and inner == outer
    if owned % 16 == 0 and LANES % (2 * owned) == 0 and devices % 4 == 0 and twin and width % (STEP * LANES) == 0:
        feats, message, edges = joined_features(turned, rim, short_filter, out_grad, owned)
        filters, joined = transform_filters(long_filter, tables, seq_len, jnp.bfloat16, [tables["joined"]])
        arrived = lax.all_to_all(message, EVERYONE, split_axis=0, concat_axis=0, tiled=True)
        edges, filters, joined, arrived = lax.optimization_barrier(
            (shifted(edges, EVERYONE, -1), filters, joined, arrived)
        )
        answer, cross = joined_filtering(arrived, filters, joined, tables, seq_len)
        returned = lax.all_to_all(answer, EVERYONE, split_axis=0, concat_axis=0, tiled=True)
        filter_grad = filter_gradient(cross, tables, seq_len)
        filter_grad, returned, cross = lax.optimization_barrier((filter_grad, returned, cross))
        mixed, grad = joined_gradients(cross, feats, edges, returned, out_grad, short_filter, owned)
        return (mixed, grad, filter_grad)

    cotangent = out_grad.T
    feats, product, conv_grad = features_of(turned, rim, short_filter, cotangent)

    def exchange(block):
        pieces = block.reshape(devices, owned, local_len)
        return lax.all_to_all(pieces, EVERYONE, split_axis=0, concat_axis=0, tiled=True)

    (filters,) = transform_filters(long_filter, tables, seq_len)
    prod_chan = exchange(product)
    conv_grad, prod_chan = lax.optimization_barrier((conv_grad, prod_chan))
    grad_chan = exchange(conv_grad)
    conv_chan, prod_spec = filtered(prod_chan, filters, tables, seq_len)
    conv_chan, grad_chan = lax.optimization_barrier((conv_chan, grad_chan))
    conv_tok = exchange(conv_chan)
    back_chan, cross = filtered(grad_chan, filters, tables, seq_len, prod_spec)
    back_chan, conv_tok = lax.optimization_barrier((back_chan, conv_tok))
    back_tok = exchange(back_chan)

    filter_grad = filter_gradient(cross, tables, seq_len)
    mixed, grad_q, rim_q = query_products(feats, conv_tok.reshape(width, local_len), cotangent)
    grad = query_gradient(grad_q, shifted(rim_q, EVERYONE, -1), short_filter)
    filter_grad, mixed, grad, back_tok = lax.optimization_barrier((filter_grad, mixed, grad, back_tok))

    grad_kv, rim_kv = key_value_products(feats, back_tok.reshape(width, local_len))
    grad = key_value_gradient(grad, grad_kv, shifted(rim_kv, EVERYONE, -1), short_filter)
    return (mixed, grad, filter_grad)


def solution(mesh):
    placed = (P(None, EVERYONE), P(), P(EVERYONE, None), P(None, EVERYONE))
    return jax.shard_map(
        shards,
        mesh=mesh,
        in_specs=placed,
        out_specs=(P(None, EVERYONE), P(None, EVERYONE), P(EVERYONE, None)),
        check_vma=False,
    )
```

```python
import math

import jax
import jax.numpy as jnp
import numpy as np
from jax import lax
from jax.experimental import pallas as pl
from jax.experimental.pallas import tpu as pltpu
from jax.sharding import PartitionSpec as P

CPG = 4
TAPS = 7
PAIRS = CPG // 2
EVERYONE = ("dp", "ctx")
VMEM_LIMIT = 24 * 1024 * 1024


def shifted(value, axis, steps):
    count = lax.axis_size(axis)
    first, last = (max(0, -steps), min(count, count - steps))
    return lax.ppermute(value, axis, [(source, source + steps) for source in range(first, last)])


def sizes_of(seq_len):
    padded = 2 * seq_len
    inner = max(d for d in range(1, seq_len + 1) if seq_len % d == 0 and d * d <= padded)
    return padded, inner, padded // inner


def table(count_out, count_in, period):
    turns = np.arange(count_out, dtype=np.int64)[:, None] * np.arange(count_in, dtype=np.int64)
    angle = (turns % period).astype(np.float64) * (2.0 * math.pi / period)
    return np.cos(angle), np.sin(angle)


def make_tables(seq_len, sources):
    padded, inner, outer = sizes_of(seq_len)
    half = outer // 2
    fold = half // sources
    order = np.arange(half).reshape(sources, fold).T.reshape(-1)
    cos_o, sin_o = table(outer, half, outer)
    cos_i, sin_i = table(inner, inner, inner)
    cos_p, sin_p = cos_o[:, order], sin_o[:, order]
    narrow = lambda blocks: jnp.asarray(np.block(blocks).astype(np.float32)).astype(jnp.bfloat16)
    twist = [jnp.asarray(t.astype(np.float32)) for t in table(outer, inner, padded)]
    return {
        "first": narrow([[cos_p, sin_p], [-sin_p, cos_p]]),
        "second": narrow([[cos_i, -sin_i], [sin_i, cos_i]]),
        "third": narrow([[cos_i, sin_i], [-sin_i, cos_i]]),
        "fourth": narrow([[cos_p.T, -sin_p.T], [sin_p.T, cos_p.T]]),
        "joined": narrow(
            [
                [cos_i, -sin_i],
                [sin_i, cos_i],
                [cos_i, sin_i],
                [-sin_i, cos_i],
                [cos_p.T / padded, -sin_p.T / padded],
                [sin_p.T / padded, cos_p.T / padded],
                [np.hstack([cos_p, sin_p]), np.hstack([-sin_p, cos_p])],
            ]
        )
        if inner == outer
        else None,
        "first_real": narrow([[cos_o], [-sin_o]]),
        "fourth_real": narrow([[cos_o.T, -sin_o.T]]),
        "twist_re": twist[0],
        "twist_im": twist[1],
    }


LANES = 128


def spread(tall, count, stride, first, height, width):
    tiles = [tall[pl.ds(t * height + first, count, stride=stride), :] for t in range(width[0] // LANES, width[1] // LANES)]
    return tiles[0] if len(tiles) == 1 else jnp.concatenate(tiles, axis=1)


def put_spread(tall, values, stride, first, height, width):
    for i, t in enumerate(range(width[0] // LANES, width[1] // LANES)):
        tall[pl.ds(t * height + first, values.shape[0], stride=stride), :] = values[:, i * LANES : (i + 1) * LANES]


def dot(left, right):
    return jnp.dot(left, right, preferred_element_type=jnp.float32)


def transform_filters(long_filter, tables, seq_len, kind=jnp.float32, handed=()):
    padded, inner, outer = sizes_of(seq_len)
    half = outer // 2
    groups = long_filter.shape[0]
    scale = seq_len ** -0.5

    def kernel(x_ref, first_ref, second_ref, tr_ref, ti_ref, *refs):
        count = len(handed)
        out_ref, tall = refs[count], refs[-1]
        for n in range(count):
            refs[count + 1 + n][...] = refs[n][...]
        height = half * groups
        for b in range(half):
            for t in range(inner // LANES):
                at = t * height + b * groups
                lanes = slice(b * inner + t * LANES, b * inner + (t + 1) * LANES)
                tall[at : at + groups, :] = x_ref[:, lanes].astype(jnp.float32)
        for g in range(groups):
            x = spread(tall, half, groups, g, height, (0, inner)).astype(jnp.bfloat16)
            f = dot(first_ref[...], x)
            f_re, f_im = f[:outer], f[outer:]
            g_re = (f_re * tr_ref[...] + f_im * ti_ref[...]).astype(jnp.bfloat16)
            g_im = (f_im * tr_ref[...] - f_re * ti_ref[...]).astype(jnp.bfloat16)
            spec = dot(g_re, second_ref[:inner]) + dot(g_im, second_ref[inner:])
            out_ref[g * outer : (g + 1) * outer, :] = (spec * scale).astype(kind)

    return pl.pallas_call(
        kernel,
        name="filter_dft",
        out_shape=[jax.ShapeDtypeStruct((groups * outer, 2 * inner), kind)]
        + [jax.ShapeDtypeStruct(array.shape, array.dtype) for array in handed],
        scratch_shapes=[pltpu.VMEM((half * groups * inner // LANES, LANES), jnp.float32)],
        compiler_params=pltpu.CompilerParams(vmem_limit_bytes=VMEM_LIMIT),
        cost_estimate=pl.CostEstimate(flops=200_000_000, bytes_accessed=2_000_000, transcendentals=0),
    )(long_filter, tables["first_real"], tables["second"], tables["twist_re"], tables["twist_im"], *handed)


def filtered(arrived, filters, tables, seq_len, other=None):
    padded, inner, outer = sizes_of(seq_len)
    half = outer // 2
    sources, channels, local = arrived.shape
    fold = local // inner
    groups = channels // CPG
    backward = other is not None

    def kernel(*refs):
        if backward:
            (x_ref, f_ref, k_ref, first_ref, second_ref, third_ref, fourth_ref, tr_ref, ti_ref,
             y_ref, cross_ref, tall, wide, stage, turn) = refs
        else:
            (x_ref, f_ref, first_ref, second_ref, third_ref, fourth_ref, tr_ref, ti_ref,
             y_ref, z_ref, tall, wide, stage, turn) = refs
        height = sources * channels
        for t in range(local // LANES):
            block = x_ref[:, :, t * LANES : (t + 1) * LANES].astype(jnp.float32)
            tall[t * height : (t + 1) * height, :] = block.reshape(height, LANES)
        for c in range(channels):
            pair, part = divmod(c, 2)
            for h in range(fold):
                rows = spread(tall, sources, channels, c, height, (h * inner, (h + 1) * inner))
                at = part * half + h * sources
                wide[at : at + sources, pair * inner : (pair + 1) * inner] = rows.astype(jnp.bfloat16)
        for g in range(groups):
            span = PAIRS * inner
            f = dot(first_ref[...], wide[:, g * span : (g + 1) * span])
            for p in range(PAIRS):
                f_re = f[:outer, p * inner : (p + 1) * inner]
                f_im = f[outer:, p * inner : (p + 1) * inner]
                at = (g * PAIRS + p) * outer
                stage[at : at + outer, :inner] = (f_re * tr_ref[...] + f_im * ti_ref[...]).astype(jnp.bfloat16)
                stage[at : at + outer, inner:] = (f_im * tr_ref[...] - f_re * ti_ref[...]).astype(jnp.bfloat16)
        for g in range(groups):
            s_re = f_ref[g * outer : (g + 1) * outer, :inner]
            s_im = f_ref[g * outer : (g + 1) * outer, inner:]
            cross_re = cross_im = None
            for p in range(PAIRS):
                at = (g * PAIRS + p) * outer
                z = dot(stage[at : at + outer, :], second_ref[...])
                z_re, z_im = z[:, :inner], z[:, inner:]
                if backward:
                    k_re = k_ref[at : at + outer, :inner].astype(jnp.float32)
                    k_im = k_ref[at : at + outer, inner:].astype(jnp.float32)
                    part_re = k_re * z_re + k_im * z_im
                    part_im = k_re * z_im - k_im * z_re
                    cross_re = part_re if cross_re is None else cross_re + part_re
                    cross_im = part_im if cross_im is None else cross_im + part_im
                    o_re = s_re * z_re + s_im * z_im
                    o_im = s_re * z_im - s_im * z_re
                else:
                    z_ref[at : at + outer, :] = z
                    o_re = s_re * z_re - s_im * z_im
                    o_im = s_re * z_im + s_im * z_re
                stage[at : at + outer, :inner] = o_re.astype(jnp.bfloat16)
                stage[at : at + outer, inner:] = o_im.astype(jnp.bfloat16)
            if backward:
                cross_ref[g * outer : (g + 1) * outer, :inner] = cross_re.astype(jnp.bfloat16)
                cross_ref[g * outer : (g + 1) * outer, inner:] = cross_im.astype(jnp.bfloat16)
        for pair in range(groups * PAIRS):
            at = pair * outer
            h = dot(stage[at : at + outer, :], third_ref[...])
            h_re, h_im = h[:, :inner], h[:, inner:]
            lanes = slice(pair * inner, (pair + 1) * inner)
            turn[:outer, lanes] = (h_re * tr_ref[...] - h_im * ti_ref[...]).astype(jnp.bfloat16)
            turn[outer:, lanes] = (h_im * tr_ref[...] + h_re * ti_ref[...]).astype(jnp.bfloat16)
        for g in range(groups):
            span = PAIRS * inner
            y = dot(fourth_ref[...], turn[:, g * span : (g + 1) * span]) * (1.0 / padded)
            for p in range(PAIRS):
                for part in range(2):
                    c = (g * PAIRS + p) * 2 + part
                    for h in range(fold):
                        at = part * half + h * sources
                        rows = y[at : at + sources, p * inner : (p + 1) * inner]
                        put_spread(tall, rows, channels, c, height, (h * inner, (h + 1) * inner))
        for t in range(local // LANES):
            block = tall[t * height : (t + 1) * height, :].reshape(sources, channels, LANES)
            y_ref[:, :, t * LANES : (t + 1) * LANES] = block.astype(jnp.bfloat16)

    pairs = groups * PAIRS
    if backward:
        extra = jax.ShapeDtypeStruct((groups * outer, 2 * inner), jnp.bfloat16)
    else:
        extra = jax.ShapeDtypeStruct((pairs * outer, 2 * inner), jnp.float32)
    operands = [arrived, filters] + ([other] if backward else [])
    operands += [tables[n] for n in ("first", "second", "third", "fourth", "twist_re", "twist_im")]
    return pl.pallas_call(
        kernel,
        name="correlate" if backward else "convolve",
        out_shape=(jax.ShapeDtypeStruct(arrived.shape, jnp.bfloat16), extra),
        scratch_shapes=[
            pltpu.VMEM((sources * channels * local // LANES, LANES), jnp.float32),
            pltpu.VMEM((outer, pairs * inner), jnp.bfloat16),
            pltpu.VMEM((pairs * outer, 2 * inner), jnp.bfloat16),
            pltpu.VMEM((2 * outer, pairs * inner), jnp.bfloat16),
        ],
        compiler_params=pltpu.CompilerParams(vmem_limit_bytes=VMEM_LIMIT),
        cost_estimate=pl.CostEstimate(flops=2_000_000_000, bytes_accessed=5_000_000, transcendentals=0),
    )(*operands)


def filter_gradient(cross, tables, seq_len):
    padded, inner, outer = sizes_of(seq_len)
    half = outer // 2
    groups = cross.shape[0] // outer
    scale = seq_len ** -0.5 / padded

    def kernel(s_ref, third_ref, fourth_ref, tr_ref, ti_ref, out_ref, tall, turn):
        for g in range(groups):
            h = dot(s_ref[g * outer : (g + 1) * outer, :], third_ref[...])
            h_re, h_im = h[:, :inner], h[:, inner:]
            turn[:outer, g * inner : (g + 1) * inner] = (h_re * tr_ref[...] - h_im * ti_ref[...]).astype(jnp.bfloat16)
            turn[outer:, g * inner : (g + 1) * inner] = (h_im * tr_ref[...] + h_re * ti_ref[...]).astype(jnp.bfloat16)
        for g in range(groups):
            y = dot(fourth_ref[...], turn[:, g * inner : (g + 1) * inner]) * scale
            put_spread(tall, y, groups, g, half * groups, (0, inner))
        for b in range(half):
            for t in range(inner // LANES):
                at = (t * half + b) * groups
                out_ref[:, b * inner + t * LANES : b * inner + (t + 1) * LANES] = tall[at : at + groups, :]

    return pl.pallas_call(
        kernel,
        name="filter_gradient",
        out_shape=jax.ShapeDtypeStruct((groups, seq_len), jnp.float32),
        scratch_shapes=[
            pltpu.VMEM((half * groups * inner // LANES, LANES), jnp.float32),
            pltpu.VMEM((2 * outer, groups * inner), jnp.bfloat16),
        ],
        compiler_params=pltpu.CompilerParams(vmem_limit_bytes=VMEM_LIMIT),
        cost_estimate=pl.CostEstimate(flops=200_000_000, bytes_accessed=2_000_000, transcendentals=0),
    )(cross, tables["third"], tables["fourth_real"], tables["twist_re"], tables["twist_im"])


RIM = 8
STEP = 2
BATCH = 2


def seven_taps(tall, value, rim, weights, forward):
    count = value.shape[0]
    if forward:
        tall[:RIM, :] = rim
        tall[RIM : RIM + count, :] = value
    else:
        tall[:count, :] = value
        tall[count : count + RIM, :] = rim
    total = value * weights[:1]
    for lag in range(1, TAPS):
        first = RIM - lag if forward else lag
        total = total + tall[first : first + count, :] * weights[lag : lag + 1]
    return total


def lane_block(i, offset=0):
    return pl.ds(pl.multiple_of(i * LANES + offset, LANES), LANES)


def whole_call(kernel, name, out_shape, operands, scratch=(), flops=10_000_000, **kwargs):
    return pl.pallas_call(
        kernel,
        name=name,
        out_shape=out_shape,
        scratch_shapes=list(scratch),
        compiler_params=pltpu.CompilerParams(vmem_limit_bytes=VMEM_LIMIT),
        cost_estimate=pl.CostEstimate(flops=flops, bytes_accessed=4_000_000, transcendentals=0),
        **kwargs,
    )(*operands)


def narrow_shape(*shape):
    return jax.ShapeDtypeStruct(shape, jnp.bfloat16)


def features_of(turned, rim, short_filter, cotangent):
    local, width = cotangent.shape

    def kernel(x_ref, rim_ref, w_ref, og_ref, f_ref, kv_ref, dconv_ref, tall):
        @pl.loop(0, width // LANES)
        def _(i):
            made = []
            for part in range(3):
                lanes = lane_block(i, part * width)
                total = seven_taps(
                    tall.at[part],
                    x_ref[:, lanes].astype(jnp.float32),
                    rim_ref[:, lanes].astype(jnp.float32),
                    w_ref[:, lanes].astype(jnp.float32),
                    True,
                ).astype(jnp.bfloat16)
                f_ref[:, lanes] = total
                made.append(total.astype(jnp.float32))
            rows = lane_block(i)
            kv_ref[rows, :] = (made[1] * made[2]).astype(jnp.bfloat16).T
            og = og_ref[:, rows].astype(jnp.float32)
            dconv_ref[rows, :] = (og * made[0]).astype(jnp.bfloat16).T

    return whole_call(
        kernel,
        "features",
        (narrow_shape(local, 3 * width), narrow_shape(width, local), narrow_shape(width, local)),
        (turned, rim, short_filter, cotangent),
        [pltpu.VMEM((3, local + RIM, LANES), jnp.float32)],
    )


def query_products(feats, conv, cotangent):
    width, local = conv.shape

    def kernel(f_ref, conv_ref, og_ref, mixed_ref, dq_ref, rim_ref):
        @pl.loop(0, width // LANES)
        def _(i):
            lanes = lane_block(i)
            here = conv_ref[lanes, :].T.astype(jnp.float32)
            mixed_ref[lanes, :] = (f_ref[:, lanes].astype(jnp.float32) * here).astype(jnp.bfloat16).T
            dq = (og_ref[:, lanes].astype(jnp.float32) * here).astype(jnp.bfloat16)
            dq_ref[:, lanes] = dq
            rim_ref[:, lanes] = dq[:RIM]

    return whole_call(
        kernel,
        "query_products",
        (narrow_shape(width, local), narrow_shape(local, width), narrow_shape(RIM, width)),
        (feats, conv, cotangent),
    )


def key_value_products(feats, back):
    width, local = back.shape

    def kernel(f_ref, back_ref, d_ref, rim_ref):
        @pl.loop(0, width // LANES)
        def _(i):
            here = back_ref[lane_block(i), :].T.astype(jnp.float32)
            for part in range(2):
                other = f_ref[:, lane_block(i, (2 - part) * width)].astype(jnp.float32)
                grad = (here * other).astype(jnp.bfloat16)
                d_ref[:, lane_block(i, part * width)] = grad
                rim_ref[:, lane_block(i, part * width)] = grad[:RIM]

    return whole_call(
        kernel,
        "key_value_products",
        (narrow_shape(local, 2 * width), narrow_shape(RIM, 2 * width)),
        (feats, back),
    )


def joined_features(turned, rim, short_filter, out_grad, owned):
    width, local = out_grad.shape
    near = LANES // owned
    blocks = width // LANES

    def kernel(x_ref, rim_ref, w_ref, og_ref, f_hbm, msg_ref, edge_ref, tall, made, f_ref, edge, sent):
        def copy(i):
            to = pl.ds(i * near, near)
            return pltpu.make_async_copy(made.at[to], msg_ref.at[to], sent.at[i])

        def keep(part, i):
            at = part * blocks + i
            to = pl.ds(pl.multiple_of(at * LANES, LANES), LANES)
            return pltpu.make_async_copy(f_ref.at[at], f_hbm.at[to, :], sent.at[blocks + at])

        @pl.loop(0, blocks // STEP)
        def _(step):
            for slot in range(STEP):
                i = step * STEP + slot
                parts = []
                for part in range(3):
                    lanes = lane_block(i, part * width)
                    total = seven_taps(
                        tall.at[3 * slot + part],
                        x_ref[:, lanes].astype(jnp.float32),
                        rim_ref[:, lanes].astype(jnp.float32),
                        w_ref[:, lanes].astype(jnp.float32),
                        True,
                    ).astype(jnp.bfloat16)
                    for t in range(local // LANES):
                        f_ref[part * blocks + i, :, t * LANES : (t + 1) * LANES] = total[t * LANES : (t + 1) * LANES]
                    if part:
                        edge[:, lanes] = total[:RIM]
                    parts.append(total.astype(jnp.float32))
                og = og_ref[lane_block(i), :].T
                edge[:, lane_block(i)] = og[:RIM]
                kv = (parts[1] * parts[2]).astype(jnp.bfloat16).T
                dconv = (og.astype(jnp.float32) * parts[0]).astype(jnp.bfloat16).T
                to = pl.ds(i * near, near)
                made[to, :owned, :] = kv.reshape(near, owned, local)
                made[to, owned:, :] = dconv.reshape(near, owned, local)
            for slot in range(STEP):
                copy(step * STEP + slot).start()
                for part in range(3):
                    keep(part, step * STEP + slot).start()

        last = pltpu.make_async_copy(edge, edge_ref, sent.at[4 * blocks])
        last.start()

        @pl.loop(0, blocks)
        def _(i):
            copy(i).wait()
            for part in range(3):
                keep(part, i).wait()

        last.wait()

    vmem = pl.BlockSpec(memory_space=pltpu.VMEM)
    hbm = pl.BlockSpec(memory_space=pltpu.HBM)
    devices = width // owned
    return whole_call(
        kernel,
        "joined_features",
        (narrow_shape(3 * width, local), narrow_shape(devices, 2 * owned, local), narrow_shape(RIM, 3 * width)),
        (turned, rim, short_filter, out_grad),
        [
            pltpu.VMEM((3 * STEP, local + RIM, LANES), jnp.float32),
            pltpu.VMEM((devices, 2 * owned, local), jnp.bfloat16),
            pltpu.VMEM((3 * blocks, LANES, local), jnp.bfloat16),
            pltpu.VMEM((RIM, 3 * width), jnp.bfloat16),
            pltpu.SemaphoreType.DMA((4 * blocks + 1,)),
        ],
        in_specs=[vmem] * 4,
        out_specs=(hbm, hbm, hbm),
    )


def joined_filtering(arrived, filters, joined, tables, seq_len):
    padded, inner, outer = sizes_of(seq_len)
    half = outer // 2
    sources, rows, local = arrived.shape
    channels = rows // 2
    tiles = local // LANES
    fold = local // inner
    groups = channels // CPG
    pairs = groups * PAIRS
    height = sources * channels
    chunk = sources // 4

    def kernel(x_ref, f_ref, table_ref, tr_ref, ti_ref, y_hbm, cross_hbm, y_ref, cross_ref, talls, wides, stages, turns, sems):
        second_ref, third_ref = table_ref.at[: 2 * inner], table_ref.at[2 * inner : 4 * inner]
        fourth_ref = table_ref.at[4 * inner : 4 * inner + 2 * half]
        firsts = table_ref[4 * inner + 2 * half :, :]
        first = jnp.concatenate([firsts[:, : 2 * half], firsts[:, 2 * half :]], axis=0)
        tr, ti = tr_ref[...], ti_ref[...]
        for s in range(2):
            tall, wide, stage = talls.at[s], wides.at[s], stages.at[s]
            for t in range(tiles):
                block = x_ref[:, s * channels : (s + 1) * channels, t * LANES : (t + 1) * LANES]
                tall[t * height : (t + 1) * height, :] = block.astype(jnp.float32).reshape(height, LANES)
            for c in range(channels):
                pair, part = divmod(c, 2)
                for h in range(fold):
                    line = spread(tall, sources, channels, c, height, (h * inner, (h + 1) * inner))
                    at = part * half + h * sources
                    wide[at : at + sources, pair * inner : (pair + 1) * inner] = line.astype(jnp.bfloat16)
            for g in range(groups):
                span = PAIRS * inner
                f = dot(first, wide[:, g * span : (g + 1) * span])
                for p in range(PAIRS):
                    f_re = f[:outer, p * inner : (p + 1) * inner]
                    f_im = f[outer:, p * inner : (p + 1) * inner]
                    at = (g * PAIRS + p) * outer
                    stage[at : at + outer, :inner] = (f_re * tr + f_im * ti).astype(jnp.bfloat16)
                    stage[at : at + outer, inner:] = (f_im * tr - f_re * ti).astype(jnp.bfloat16)
        batch = PAIRS * outer
        for g in range(groups):
            if g % BATCH == 0:
                rows = slice(g * batch, min(g + BATCH, groups) * batch)
                k_many = dot(stages[0, rows, :], second_ref[...])
                d_many = dot(stages[1, rows, :], second_ref[...])
            s_re = f_ref[g * outer : (g + 1) * outer, :inner].astype(jnp.float32)
            s_im = f_ref[g * outer : (g + 1) * outer, inner:].astype(jnp.float32)
            cross_re = cross_im = 0.0
            for p in range(PAIRS):
                at = (g * PAIRS + p) * outer
                here = slice((g % BATCH * PAIRS + p) * outer, (g % BATCH * PAIRS + p + 1) * outer)
                k, d = k_many[here], d_many[here]
                k_re, k_im = k[:, :inner], k[:, inner:]
                d_re, d_im = d[:, :inner], d[:, inner:]
                cross_re = cross_re + (k_re * d_re + k_im * d_im)
                cross_im = cross_im + (k_re * d_im - k_im * d_re)
                stages[0, at : at + outer, :inner] = (s_re * k_re - s_im * k_im).astype(jnp.bfloat16)
                stages[0, at : at + outer, inner:] = (s_re * k_im + s_im * k_re).astype(jnp.bfloat16)
                stages[1, at : at + outer, :inner] = (s_re * d_re + s_im * d_im).astype(jnp.bfloat16)
                stages[1, at : at + outer, inner:] = (s_re * d_im - s_im * d_re).astype(jnp.bfloat16)
            cross_ref[g * outer : (g + 1) * outer, :inner] = cross_re.astype(jnp.bfloat16)
            cross_ref[g * outer : (g + 1) * outer, inner:] = cross_im.astype(jnp.bfloat16)
        copies = [pltpu.make_async_copy(cross_ref, cross_hbm, sems.at[4])]
        copies[0].start()
        spot = lax.broadcasted_iota(jnp.int32, (RIM, LANES), 0)
        lane = lax.broadcasted_iota(jnp.int32, (RIM, LANES), 1)
        pick = jnp.where(spot == lane, 1.0, 0.0).astype(jnp.bfloat16)
        rims = []
        for s in range(2):
            tall, stage, turn = talls.at[s], stages.at[s], turns.at[s]
            for pair in range(pairs):
                if pair % (BATCH * PAIRS) == 0:
                    h_many = dot(stage[pair * outer : min(pair + BATCH * PAIRS, pairs) * outer, :], third_ref[...])
                h = h_many[pair % (BATCH * PAIRS) * outer : (pair % (BATCH * PAIRS) + 1) * outer]
                h_re, h_im = h[:, :inner], h[:, inner:]
                lanes = slice(pair * inner, (pair + 1) * inner)
                turn[:outer, lanes] = (h_re * tr - h_im * ti).astype(jnp.bfloat16)
                turn[outer:, lanes] = (h_im * tr + h_re * ti).astype(jnp.bfloat16)
            for g in range(groups):
                span = PAIRS * inner
                y = dot(fourth_ref[...], turn[:, g * span : (g + 1) * span])
                for p in range(PAIRS):
                    for part in range(2):
                        c = (g * PAIRS + p) * 2 + part
                        for h in range(fold):
                            at = part * half + h * sources
                            line = y[at : at + sources, p * inner : (p + 1) * inner]
                            put_spread(tall, line, channels, c, height, (h * inner, (h + 1) * inner))
            front = tall[:height, :].astype(jnp.bfloat16)
            rims.append(
                lax.dot_general(pick, front, (((1,), (1,)), ((), ())), preferred_element_type=jnp.float32)
            )
        for q in range(4):
            to = slice(q * chunk, (q + 1) * chunk)
            for s in range(2):
                for t in range(tiles):
                    at = t * height + q * chunk * channels
                    block = talls[s, at : at + chunk * channels, :].reshape(chunk, channels, LANES)
                    row = (s * tiles + t) * channels
                    y_ref[to, row : row + channels, :] = block.astype(jnp.bfloat16)
            for d in range(q * chunk, (q + 1) * chunk):
                tile, lanes = divmod((d + 1) % sources * channels, LANES)
                edge = jnp.zeros((RIM, LANES), jnp.float32)
                if d < sources - 1:
                    for s in range(2):
                        piece = rims[s][:, tile * LANES : (tile + 1) * LANES]
                        turn_by = (s * channels - lanes) % LANES
                        if turn_by:
                            piece = pltpu.roll(piece, turn_by, 1)
                        edge = piece if s == 0 else jnp.where(lane < channels, edge, piece)
                y_ref[d, 2 * tiles * channels :, :] = edge.astype(jnp.bfloat16)
            copies.append(pltpu.make_async_copy(y_ref.at[to], y_hbm.at[to], sems.at[q]))
            copies[-1].start()
        for copy in copies:
            copy.wait()

    sent = (sources, 2 * tiles * channels + RIM, LANES)
    vmem = pl.BlockSpec(memory_space=pltpu.VMEM)
    hbm = pl.BlockSpec(memory_space=pltpu.HBM)
    return whole_call(
        kernel,
        "joined_filtering",
        (narrow_shape(*sent), narrow_shape(groups * outer, 2 * inner)),
        [arrived, filters, joined, tables["twist_re"], tables["twist_im"]],
        [
            pltpu.VMEM(sent, jnp.bfloat16),
            pltpu.VMEM((groups * outer, 2 * inner), jnp.bfloat16),
            pltpu.VMEM((2, tiles * height, LANES), jnp.float32),
            pltpu.VMEM((2, outer, pairs * inner), jnp.bfloat16),
            pltpu.VMEM((2, pairs * outer, 2 * inner), jnp.bfloat16),
            pltpu.VMEM((2, 2 * outer, pairs * inner), jnp.bfloat16),
            pltpu.SemaphoreType.DMA((5,)),
        ],
        flops=4_000_000_000,
        in_specs=[vmem] * 5,
        out_specs=(hbm, hbm),
    )


def joined_gradients(cross, feats, edges, returned, out_grad, short_filter, owned):
    width, local = out_grad.shape
    tiles = local // LANES
    near = LANES // owned
    blocks = width // LANES

    def kernel(_, f_hbm, edge_ref, back_ref, og_ref, w_ref, mixed_ref, out_ref, tall, made, f_ref, sent, fetched):
        def fetch(part, i):
            at = part * blocks + i
            rows = pl.ds(pl.multiple_of(at * LANES, LANES), LANES)
            return pltpu.make_async_copy(f_hbm.at[rows, :], f_ref.at[at], fetched.at[at])

        @pl.loop(0, blocks)
        def _(i):
            for part in range(3):
                fetch(part, i).start()

        def features(part, i):
            held = [f_ref[part * blocks + i, :, t * LANES : (t + 1) * LANES] for t in range(tiles)]
            return jnp.concatenate(held, axis=0).astype(jnp.float32)

        lane = lax.broadcasted_iota(jnp.int32, (RIM, LANES), 1)

        def copy(part, i):
            at = part * blocks + i
            if part < 3:
                to = out_ref.at[pl.ds(pl.multiple_of(at * LANES, LANES), LANES), :]
            else:
                to = mixed_ref.at[lane_block(i), :]
            return pltpu.make_async_copy(made.at[at], to, sent.at[at])

        def turned(s, i):
            held = pl.ds(i * near, near)
            pieces = [
                back_ref[held, (s * tiles + t) * owned : (s * tiles + t + 1) * owned, :].reshape(LANES, LANES).T
                for t in range(tiles)
            ]
            return jnp.concatenate(pieces, axis=0).astype(jnp.float32)

        def rim_of(s, i):
            rim = None
            for n in range(near):
                piece = back_ref[i * near + n, 2 * tiles * owned :, :].astype(jnp.float32)
                turn_by = (n - s) * owned % LANES
                if turn_by:
                    piece = pltpu.roll(piece, turn_by, 1)
                rim = jnp.where(lane >= n * owned, piece, rim) if n else piece
            return rim

        def third(part, slot, i, here, rim, other):
            edge = edge_ref[:, lane_block(i, (3 - part) % 3 * width)].astype(jnp.float32)
            total = seven_taps(
                tall.at[3 * slot + part],
                (here * other).astype(jnp.bfloat16).astype(jnp.float32),
                (rim * edge).astype(jnp.bfloat16).astype(jnp.float32),
                w_ref[:, lane_block(i, part * width)].astype(jnp.float32),
                False,
            )
            made[part * blocks + i] = total.astype(jnp.bfloat16).T

        @pl.loop(0, blocks // STEP)
        def _(step):
            for slot in range(STEP):
                for part in range(3):
                    fetch(part, step * STEP + slot).wait()
            for slot in range(STEP):
                i = step * STEP + slot
                query, key, value = [features(part, i) for part in range(3)]
                conv = turned(0, i)
                made[3 * blocks + i] = (query * conv).astype(jnp.bfloat16).T
                third(0, slot, i, conv, rim_of(0, i), og_ref[lane_block(i), :].T.astype(jnp.float32))
                back, rim = turned(1, i), rim_of(1, i)
                third(1, slot, i, back, rim, value)
                third(2, slot, i, back, rim, key)
            for slot in range(STEP):
                for part in range(4):
                    copy(part, step * STEP + slot).start()

        @pl.loop(0, blocks)
        def _(i):
            for part in range(4):
                copy(part, i).wait()

    vmem = pl.BlockSpec(memory_space=pltpu.VMEM)
    hbm = pl.BlockSpec(memory_space=pltpu.HBM)
    return whole_call(
        kernel,
        "joined_gradients",
        (narrow_shape(width, local), narrow_shape(3 * width, local)),
        (cross, feats, edges, returned, out_grad, short_filter),
        [
            pltpu.VMEM((3 * STEP, local + RIM, LANES), jnp.float32),
            pltpu.VMEM((4 * blocks, LANES, local), jnp.bfloat16),
            pltpu.VMEM((3 * blocks, LANES, local), jnp.bfloat16),
            pltpu.SemaphoreType.DMA((4 * blocks,)),
            pltpu.SemaphoreType.DMA((3 * blocks,)),
        ],
        in_specs=[hbm, hbm] + [vmem] * 4,
        out_specs=(hbm, hbm),
        input_output_aliases={0: 0, 1: 1},
    )


def query_gradient(grad, rim, short_filter):
    local, width = grad.shape
    steps = width // GRAD_ROWS

    def kernel(d_ref, rim_ref, w_ref, out_ref, tall):
        gradient_block(d_ref, rim_ref, w_ref, out_ref, tall)

    return gradient_call(kernel, "query_gradient", (), grad, rim, short_filter, 1, 0)


def key_value_gradient(whole, grad, rim, short_filter):
    def kernel(_, d_ref, rim_ref, w_ref, out_ref, tall):
        gradient_block(d_ref, rim_ref, w_ref, out_ref, tall)

    return gradient_call(kernel, "key_value_gradient", (whole,), grad, rim, short_filter, 2, 1)


GRAD_ROWS = 512


def gradient_block(d_ref, rim_ref, w_ref, out_ref, tall):
    for c in range(GRAD_ROWS // LANES):
        lanes = slice(c * LANES, (c + 1) * LANES)
        total = seven_taps(
            tall.at[c],
            d_ref[:, lanes].astype(jnp.float32),
            rim_ref[:, lanes].astype(jnp.float32),
            w_ref[:, lanes].astype(jnp.float32),
            False,
        )
        out_ref[lanes, :] = total.astype(jnp.bfloat16).T


def gradient_call(kernel, name, whole, grad, rim, short_filter, parts, first):
    local, lanes = grad.shape
    width = lanes // parts
    steps = width // GRAD_ROWS
    return pl.pallas_call(
        kernel,
        name=name,
        grid=(parts * steps,),
        in_specs=[pl.BlockSpec(memory_space=pl.ANY)] * len(whole)
        + [
            pl.BlockSpec((local, GRAD_ROWS), lambda i: (0, i)),
            pl.BlockSpec((RIM, GRAD_ROWS), lambda i: (0, i)),
            pl.BlockSpec((TAPS, GRAD_ROWS), lambda i: (0, first * steps + i)),
        ],
        out_specs=pl.BlockSpec((GRAD_ROWS, local), lambda i: (first * steps + i, 0)),
        out_shape=narrow_shape(3 * width, local),
        scratch_shapes=[pltpu.VMEM((GRAD_ROWS // LANES, local + RIM, LANES), jnp.float32)],
        input_output_aliases={0: 0} if whole else {},
        cost_estimate=pl.CostEstimate(flops=20_000_000, bytes_accessed=4_000_000, transcendentals=0),
    )(*whole, grad, rim, short_filter)


def shards(projections, short_filter, long_filter, out_grad):
    width, local_len = out_grad.shape
    devices = lax.axis_size(EVERYONE)
    seq_len = local_len * devices
    owned = width // devices
    tables = make_tables(seq_len, devices)

    turned = projections.T
    rim = shifted(turned[local_len - RIM :], EVERYONE, 1)

    _, inner, outer = sizes_of(seq_len)
    twin = owned // CPG * outer == width and 2 * inner == local_len and inner == outer
    if owned % 16 == 0 and LANES % (2 * owned) == 0 and devices % 4 == 0 and twin and width % (STEP * LANES) == 0:
        feats, message, edges = joined_features(turned, rim, short_filter, out_grad, owned)
        filters, joined = transform_filters(long_filter, tables, seq_len, jnp.bfloat16, [tables["joined"]])
        arrived = lax.all_to_all(message, EVERYONE, split_axis=0, concat_axis=0, tiled=True)
        edges, filters, joined, arrived = lax.optimization_barrier(
            (shifted(edges, EVERYONE, -1), filters, joined, arrived)
        )
        answer, cross = joined_filtering(arrived, filters, joined, tables, seq_len)
        returned = lax.all_to_all(answer, EVERYONE, split_axis=0, concat_axis=0, tiled=True)
        filter_grad = filter_gradient(cross, tables, seq_len)
        filter_grad, returned, cross = lax.optimization_barrier((filter_grad, returned, cross))
        mixed, grad = joined_gradients(cross, feats, edges, returned, out_grad, short_filter, owned)
        return (mixed, grad, filter_grad)

    cotangent = out_grad.T
    feats, product, conv_grad = features_of(turned, rim, short_filter, cotangent)

    def exchange(block):
        pieces = block.reshape(devices, owned, local_len)
        return lax.all_to_all(pieces, EVERYONE, split_axis=0, concat_axis=0, tiled=True)

    (filters,) = transform_filters(long_filter, tables, seq_len)
    prod_chan = exchange(product)
    conv_grad, prod_chan = lax.optimization_barrier((conv_grad, prod_chan))
    grad_chan = exchange(conv_grad)
    conv_chan, prod_spec = filtered(prod_chan, filters, tables, seq_len)
    conv_chan, grad_chan = lax.optimization_barrier((conv_chan, grad_chan))
    conv_tok = exchange(conv_chan)
    back_chan, cross = filtered(grad_chan, filters, tables, seq_len, prod_spec)
    back_chan, conv_tok = lax.optimization_barrier((back_chan, conv_tok))
    back_tok = exchange(back_chan)

    filter_grad = filter_gradient(cross, tables, seq_len)
    mixed, grad_q, rim_q = query_products(feats, conv_tok.reshape(width, local_len), cotangent)
    grad = query_gradient(grad_q, shifted(rim_q, EVERYONE, -1), short_filter)
    filter_grad, mixed, grad, back_tok = lax.optimization_barrier((filter_grad, mixed, grad, back_tok))

    grad_kv, rim_kv = key_value_products(feats, back_tok.reshape(width, local_len))
    grad = key_value_gradient(grad, grad_kv, shifted(rim_kv, EVERYONE, -1), short_filter)
    return (mixed, grad, filter_grad)


def solution(mesh):
    placed = (P(None, EVERYONE), P(), P(EVERYONE, None), P(None, EVERYONE))
    return jax.shard_map(
        shards,
        mesh=mesh,
        in_specs=placed,
        out_specs=(P(None, EVERYONE), P(None, EVERYONE), P(EVERYONE, None)),
        check_vma=False,
    )
```

```python
import math

import jax
import jax.numpy as jnp
import numpy as np
from jax import lax
from jax.experimental import pallas as pl
from jax.experimental.pallas import tpu as pltpu
from jax.sharding import PartitionSpec as P

CPG = 4
TAPS = 7
PAIRS = CPG // 2
EVERYONE = ("dp", "ctx")
VMEM_LIMIT = 24 * 1024 * 1024


def shifted(value, axis, steps):
    count = lax.axis_size(axis)
    first, last = (max(0, -steps), min(count, count - steps))
    return lax.ppermute(value, axis, [(source, source + steps) for source in range(first, last)])


def sizes_of(seq_len):
    padded = 2 * seq_len
    inner = max(d for d in range(1, seq_len + 1) if seq_len % d == 0 and d * d <= padded)
    return padded, inner, padded // inner


def table(count_out, count_in, period):
    turns = np.arange(count_out, dtype=np.int64)[:, None] * np.arange(count_in, dtype=np.int64)
    angle = (turns % period).astype(np.float64) * (2.0 * math.pi / period)
    return np.cos(angle), np.sin(angle)


def make_tables(seq_len, sources):
    padded, inner, outer = sizes_of(seq_len)
    half = outer // 2
    fold = half // sources
    order = np.arange(half).reshape(sources, fold).T.reshape(-1)
    cos_o, sin_o = table(outer, half, outer)
    cos_i, sin_i = table(inner, inner, inner)
    cos_p, sin_p = cos_o[:, order], sin_o[:, order]
    narrow = lambda blocks: jnp.asarray(np.block(blocks).astype(np.float32)).astype(jnp.bfloat16)
    twist = [jnp.asarray(t.astype(np.float32)) for t in table(outer, inner, padded)]
    return {
        "first": narrow([[cos_p, sin_p], [-sin_p, cos_p]]),
        "second": narrow([[cos_i, -sin_i], [sin_i, cos_i]]),
        "third": narrow([[cos_i, sin_i], [-sin_i, cos_i]]),
        "fourth": narrow([[cos_p.T, -sin_p.T], [sin_p.T, cos_p.T]]),
        "joined": narrow(
            [
                [cos_i, -sin_i],
                [sin_i, cos_i],
                [cos_i, sin_i],
                [-sin_i, cos_i],
                [cos_p.T / padded, -sin_p.T / padded],
                [sin_p.T / padded, cos_p.T / padded],
                [np.hstack([cos_p, sin_p]), np.hstack([-sin_p, cos_p])],
            ]
        )
        if inner == outer
        else None,
        "first_real": narrow([[cos_o], [-sin_o]]),
        "fourth_real": narrow([[cos_o.T, -sin_o.T]]),
        "twist_re": twist[0],
        "twist_im": twist[1],
    }


LANES = 128


def spread(tall, count, stride, first, height, width):
    tiles = [tall[pl.ds(t * height + first, count, stride=stride), :] for t in range(width[0] // LANES, width[1] // LANES)]
    return tiles[0] if len(tiles) == 1 else jnp.concatenate(tiles, axis=1)


def put_spread(tall, values, stride, first, height, width):
    for i, t in enumerate(range(width[0] // LANES, width[1] // LANES)):
        tall[pl.ds(t * height + first, values.shape[0], stride=stride), :] = values[:, i * LANES : (i + 1) * LANES]


def dot(left, right):
    return jnp.dot(left, right, preferred_element_type=jnp.float32)


def transform_filters(long_filter, tables, seq_len, kind=jnp.float32, handed=()):
    padded, inner, outer = sizes_of(seq_len)
    half = outer // 2
    groups = long_filter.shape[0]
    scale = seq_len ** -0.5

    def kernel(x_ref, first_ref, second_ref, tr_ref, ti_ref, *refs):
        count = len(handed)
        out_ref, tall = refs[count], refs[-1]
        for n in range(count):
            refs[count + 1 + n][...] = refs[n][...]
        height = half * groups
        for b in range(half):
            for t in range(inner // LANES):
                at = t * height + b * groups
                lanes = slice(b * inner + t * LANES, b * inner + (t + 1) * LANES)
                tall[at : at + groups, :] = x_ref[:, lanes].astype(jnp.float32)
        for g in range(groups):
            x = spread(tall, half, groups, g, height, (0, inner)).astype(jnp.bfloat16)
            f = dot(first_ref[...], x)
            f_re, f_im = f[:outer], f[outer:]
            g_re = (f_re * tr_ref[...] + f_im * ti_ref[...]).astype(jnp.bfloat16)
            g_im = (f_im * tr_ref[...] - f_re * ti_ref[...]).astype(jnp.bfloat16)
            spec = dot(g_re, second_ref[:inner]) + dot(g_im, second_ref[inner:])
            out_ref[g * outer : (g + 1) * outer, :] = (spec * scale).astype(kind)

    return pl.pallas_call(
        kernel,
        name="filter_dft",
        out_shape=[jax.ShapeDtypeStruct((groups * outer, 2 * inner), kind)]
        + [jax.ShapeDtypeStruct(array.shape, array.dtype) for array in handed],
        scratch_shapes=[pltpu.VMEM((half * groups * inner // LANES, LANES), jnp.float32)],
        compiler_params=pltpu.CompilerParams(vmem_limit_bytes=VMEM_LIMIT),
        cost_estimate=pl.CostEstimate(flops=200_000_000, bytes_accessed=2_000_000, transcendentals=0),
    )(long_filter, tables["first_real"], tables["second"], tables["twist_re"], tables["twist_im"], *handed)


def filtered(arrived, filters, tables, seq_len, other=None):
    padded, inner, outer = sizes_of(seq_len)
    half = outer // 2
    sources, channels, local = arrived.shape
    fold = local // inner
    groups = channels // CPG
    backward = other is not None

    def kernel(*refs):
        if backward:
            (x_ref, f_ref, k_ref, first_ref, second_ref, third_ref, fourth_ref, tr_ref, ti_ref,
             y_ref, cross_ref, tall, wide, stage, turn) = refs
        else:
            (x_ref, f_ref, first_ref, second_ref, third_ref, fourth_ref, tr_ref, ti_ref,
             y_ref, z_ref, tall, wide, stage, turn) = refs
        height = sources * channels
        for t in range(local // LANES):
            block = x_ref[:, :, t * LANES : (t + 1) * LANES].astype(jnp.float32)
            tall[t * height : (t + 1) * height, :] = block.reshape(height, LANES)
        for c in range(channels):
            pair, part = divmod(c, 2)
            for h in range(fold):
                rows = spread(tall, sources, channels, c, height, (h * inner, (h + 1) * inner))
                at = part * half + h * sources
                wide[at : at + sources, pair * inner : (pair + 1) * inner] = rows.astype(jnp.bfloat16)
        for g in range(groups):
            span = PAIRS * inner
            f = dot(first_ref[...], wide[:, g * span : (g + 1) * span])
            for p in range(PAIRS):
                f_re = f[:outer, p * inner : (p + 1) * inner]
                f_im = f[outer:, p * inner : (p + 1) * inner]
                at = (g * PAIRS + p) * outer
                stage[at : at + outer, :inner] = (f_re * tr_ref[...] + f_im * ti_ref[...]).astype(jnp.bfloat16)
                stage[at : at + outer, inner:] = (f_im * tr_ref[...] - f_re * ti_ref[...]).astype(jnp.bfloat16)
        for g in range(groups):
            s_re = f_ref[g * outer : (g + 1) * outer, :inner]
            s_im = f_ref[g * outer : (g + 1) * outer, inner:]
            cross_re = cross_im = None
            for p in range(PAIRS):
                at = (g * PAIRS + p) * outer
                z = dot(stage[at : at + outer, :], second_ref[...])
                z_re, z_im = z[:, :inner], z[:, inner:]
                if backward:
                    k_re = k_ref[at : at + outer, :inner].astype(jnp.float32)
                    k_im = k_ref[at : at + outer, inner:].astype(jnp.float32)
                    part_re = k_re * z_re + k_im * z_im
                    part_im = k_re * z_im - k_im * z_re
                    cross_re = part_re if cross_re is None else cross_re + part_re
                    cross_im = part_im if cross_im is None else cross_im + part_im
                    o_re = s_re * z_re + s_im * z_im
                    o_im = s_re * z_im - s_im * z_re
                else:
                    z_ref[at : at + outer, :] = z
                    o_re = s_re * z_re - s_im * z_im
                    o_im = s_re * z_im + s_im * z_re
                stage[at : at + outer, :inner] = o_re.astype(jnp.bfloat16)
                stage[at : at + outer, inner:] = o_im.astype(jnp.bfloat16)
            if backward:
                cross_ref[g * outer : (g + 1) * outer, :inner] = cross_re.astype(jnp.bfloat16)
                cross_ref[g * outer : (g + 1) * outer, inner:] = cross_im.astype(jnp.bfloat16)
        for pair in range(groups * PAIRS):
            at = pair * outer
            h = dot(stage[at : at + outer, :], third_ref[...])
            h_re, h_im = h[:, :inner], h[:, inner:]
            lanes = slice(pair * inner, (pair + 1) * inner)
            turn[:outer, lanes] = (h_re * tr_ref[...] - h_im * ti_ref[...]).astype(jnp.bfloat16)
            turn[outer:, lanes] = (h_im * tr_ref[...] + h_re * ti_ref[...]).astype(jnp.bfloat16)
        for g in range(groups):
            span = PAIRS * inner
            y = dot(fourth_ref[...], turn[:, g * span : (g + 1) * span]) * (1.0 / padded)
            for p in range(PAIRS):
                for part in range(2):
                    c = (g * PAIRS + p) * 2 + part
                    for h in range(fold):
                        at = part * half + h * sources
                        rows = y[at : at + sources, p * inner : (p + 1) * inner]
                        put_spread(tall, rows, channels, c, height, (h * inner, (h + 1) * inner))
        for t in range(local // LANES):
            block = tall[t * height : (t + 1) * height, :].reshape(sources, channels, LANES)
            y_ref[:, :, t * LANES : (t + 1) * LANES] = block.astype(jnp.bfloat16)

    pairs = groups * PAIRS
    if backward:
        extra = jax.ShapeDtypeStruct((groups * outer, 2 * inner), jnp.bfloat16)
    else:
        extra = jax.ShapeDtypeStruct((pairs * outer, 2 * inner), jnp.float32)
    operands = [arrived, filters] + ([other] if backward else [])
    operands += [tables[n] for n in ("first", "second", "third", "fourth", "twist_re", "twist_im")]
    return pl.pallas_call(
        kernel,
        name="correlate" if backward else "convolve",
        out_shape=(jax.ShapeDtypeStruct(arrived.shape, jnp.bfloat16), extra),
        scratch_shapes=[
            pltpu.VMEM((sources * channels * local // LANES, LANES), jnp.float32),
            pltpu.VMEM((outer, pairs * inner), jnp.bfloat16),
            pltpu.VMEM((pairs * outer, 2 * inner), jnp.bfloat16),
            pltpu.VMEM((2 * outer, pairs * inner), jnp.bfloat16),
        ],
        compiler_params=pltpu.CompilerParams(vmem_limit_bytes=VMEM_LIMIT),
        cost_estimate=pl.CostEstimate(flops=2_000_000_000, bytes_accessed=5_000_000, transcendentals=0),
    )(*operands)


def filter_gradient(cross, tables, seq_len):
    padded, inner, outer = sizes_of(seq_len)
    half = outer // 2
    groups = cross.shape[0] // outer
    scale = seq_len ** -0.5 / padded

    def kernel(s_ref, third_ref, fourth_ref, tr_ref, ti_ref, out_ref, tall, turn):
        for g in range(groups):
            h = dot(s_ref[g * outer : (g + 1) * outer, :], third_ref[...])
            h_re, h_im = h[:, :inner], h[:, inner:]
            turn[:outer, g * inner : (g + 1) * inner] = (h_re * tr_ref[...] - h_im * ti_ref[...]).astype(jnp.bfloat16)
            turn[outer:, g * inner : (g + 1) * inner] = (h_im * tr_ref[...] + h_re * ti_ref[...]).astype(jnp.bfloat16)
        for g in range(groups):
            y = dot(fourth_ref[...], turn[:, g * inner : (g + 1) * inner]) * scale
            put_spread(tall, y, groups, g, half * groups, (0, inner))
        for b in range(half):
            for t in range(inner // LANES):
                at = (t * half + b) * groups
                out_ref[:, b * inner + t * LANES : b * inner + (t + 1) * LANES] = tall[at : at + groups, :]

    return pl.pallas_call(
        kernel,
        name="filter_gradient",
        out_shape=jax.ShapeDtypeStruct((groups, seq_len), jnp.float32),
        scratch_shapes=[
            pltpu.VMEM((half * groups * inner // LANES, LANES), jnp.float32),
            pltpu.VMEM((2 * outer, groups * inner), jnp.bfloat16),
        ],
        compiler_params=pltpu.CompilerParams(vmem_limit_bytes=VMEM_LIMIT),
        cost_estimate=pl.CostEstimate(flops=200_000_000, bytes_accessed=2_000_000, transcendentals=0),
    )(cross, tables["third"], tables["fourth_real"], tables["twist_re"], tables["twist_im"])


RIM = 8
STEP = 2


def seven_taps(tall, value, rim, weights, forward):
    count = value.shape[0]
    if forward:
        tall[:RIM, :] = rim
        tall[RIM : RIM + count, :] = value
    else:
        tall[:count, :] = value
        tall[count : count + RIM, :] = rim
    total = value * weights[:1]
    for lag in range(1, TAPS):
        first = RIM - lag if forward else lag
        total = total + tall[first : first + count, :] * weights[lag : lag + 1]
    return total


def lane_block(i, offset=0):
    return pl.ds(pl.multiple_of(i * LANES + offset, LANES), LANES)


def whole_call(kernel, name, out_shape, operands, scratch=(), flops=10_000_000, **kwargs):
    return pl.pallas_call(
        kernel,
        name=name,
        out_shape=out_shape,
        scratch_shapes=list(scratch),
        compiler_params=pltpu.CompilerParams(vmem_limit_bytes=VMEM_LIMIT),
        cost_estimate=pl.CostEstimate(flops=flops, bytes_accessed=4_000_000, transcendentals=0),
        **kwargs,
    )(*operands)


def narrow_shape(*shape):
    return jax.ShapeDtypeStruct(shape, jnp.bfloat16)


def features_of(turned, rim, short_filter, cotangent):
    local, width = cotangent.shape

    def kernel(x_ref, rim_ref, w_ref, og_ref, f_ref, kv_ref, dconv_ref, tall):
        @pl.loop(0, width // LANES)
        def _(i):
            made = []
            for part in range(3):
                lanes = lane_block(i, part * width)
                total = seven_taps(
                    tall.at[part],
                    x_ref[:, lanes].astype(jnp.float32),
                    rim_ref[:, lanes].astype(jnp.float32),
                    w_ref[:, lanes].astype(jnp.float32),
                    True,
                ).astype(jnp.bfloat16)
                f_ref[:, lanes] = total
                made.append(total.astype(jnp.float32))
            rows = lane_block(i)
            kv_ref[rows, :] = (made[1] * made[2]).astype(jnp.bfloat16).T
            og = og_ref[:, rows].astype(jnp.float32)
            dconv_ref[rows, :] = (og * made[0]).astype(jnp.bfloat16).T

    return whole_call(
        kernel,
        "features",
        (narrow_shape(local, 3 * width), narrow_shape(width, local), narrow_shape(width, local)),
        (turned, rim, short_filter, cotangent),
        [pltpu.VMEM((3, local + RIM, LANES), jnp.float32)],
    )


def query_products(feats, conv, cotangent):
    width, local = conv.shape

    def kernel(f_ref, conv_ref, og_ref, mixed_ref, dq_ref, rim_ref):
        @pl.loop(0, width // LANES)
        def _(i):
            lanes = lane_block(i)
            here = conv_ref[lanes, :].T.astype(jnp.float32)
            mixed_ref[lanes, :] = (f_ref[:, lanes].astype(jnp.float32) * here).astype(jnp.bfloat16).T
            dq = (og_ref[:, lanes].astype(jnp.float32) * here).astype(jnp.bfloat16)
            dq_ref[:, lanes] = dq
            rim_ref[:, lanes] = dq[:RIM]

    return whole_call(
        kernel,
        "query_products",
        (narrow_shape(width, local), narrow_shape(local, width), narrow_shape(RIM, width)),
        (feats, conv, cotangent),
    )


def key_value_products(feats, back):
    width, local = back.shape

    def kernel(f_ref, back_ref, d_ref, rim_ref):
        @pl.loop(0, width // LANES)
        def _(i):
            here = back_ref[lane_block(i), :].T.astype(jnp.float32)
            for part in range(2):
                other = f_ref[:, lane_block(i, (2 - part) * width)].astype(jnp.float32)
                grad = (here * other).astype(jnp.bfloat16)
                d_ref[:, lane_block(i, part * width)] = grad
                rim_ref[:, lane_block(i, part * width)] = grad[:RIM]

    return whole_call(
        kernel,
        "key_value_products",
        (narrow_shape(local, 2 * width), narrow_shape(RIM, 2 * width)),
        (feats, back),
    )


def joined_features(turned, rim, short_filter, out_grad, owned):
    width, local = out_grad.shape
    near = LANES // owned
    steps = width // LANES // STEP

    def kernel(x_ref, rim_ref, w_ref, og_ref, f_hbm, msg_ref, edge_ref, tall, made, f_ref, edge, sent):
        def copy(step):
            to = pl.ds(step * STEP * near, STEP * near)
            return pltpu.make_async_copy(made.at[to], msg_ref.at[to], sent.at[step])

        def keep(part, step):
            to = pl.ds(pl.multiple_of(part * width + step * STEP * LANES, STEP * LANES), STEP * LANES)
            return pltpu.make_async_copy(f_ref.at[to, :], f_hbm.at[to, :], sent.at[(1 + part) * steps + step])

        @pl.loop(0, steps)
        def _(step):
            for slot in range(STEP):
                i = step * STEP + slot
                parts = []
                for part in range(3):
                    lanes = lane_block(i, part * width)
                    total = seven_taps(
                        tall.at[3 * slot + part],
                        x_ref[:, lanes].astype(jnp.float32),
                        rim_ref[:, lanes].astype(jnp.float32),
                        w_ref[:, lanes].astype(jnp.float32),
                        True,
                    ).astype(jnp.bfloat16)
                    for t in range(local // LANES):
                        f_ref[lanes, t * LANES : (t + 1) * LANES] = total[t * LANES : (t + 1) * LANES]
                    if part:
                        edge[:, lanes] = total[:RIM]
                    parts.append(total.astype(jnp.float32))
                og = og_ref[lane_block(i), :].T
                edge[:, lane_block(i)] = og[:RIM]
                kv = (parts[1] * parts[2]).astype(jnp.bfloat16).T
                dconv = (og.astype(jnp.float32) * parts[0]).astype(jnp.bfloat16).T
                to = pl.ds(i * near, near)
                made[to, :owned, :] = kv.reshape(near, owned, local)
                made[to, owned:, :] = dconv.reshape(near, owned, local)
            copy(step).start()
            for part in range(3):
                keep(part, step).start()

        last = pltpu.make_async_copy(edge, edge_ref, sent.at[4 * steps])
        last.start()

        @pl.loop(0, steps)
        def _(step):
            copy(step).wait()
            for part in range(3):
                keep(part, step).wait()

        last.wait()

    vmem = pl.BlockSpec(memory_space=pltpu.VMEM)
    hbm = pl.BlockSpec(memory_space=pltpu.HBM)
    devices = width // owned
    return whole_call(
        kernel,
        "joined_features",
        (narrow_shape(3 * width, local), narrow_shape(devices, 2 * owned, local), narrow_shape(RIM, 3 * width)),
        (turned, rim, short_filter, out_grad),
        [
            pltpu.VMEM((3 * STEP, local + RIM, LANES), jnp.float32),
            pltpu.VMEM((devices, 2 * owned, local), jnp.bfloat16),
            pltpu.VMEM((3 * width, local), jnp.bfloat16),
            pltpu.VMEM((RIM, 3 * width), jnp.bfloat16),
            pltpu.SemaphoreType.DMA((4 * steps + 1,)),
        ],
        in_specs=[vmem] * 4,
        out_specs=(hbm, hbm, hbm),
    )


def joined_filtering(arrived, filters, joined, tables, seq_len):
    padded, inner, outer = sizes_of(seq_len)
    half = outer // 2
    sources, rows, local = arrived.shape
    channels = rows // 2
    tiles = local // LANES
    fold = local // inner
    groups = channels // CPG
    pairs = groups * PAIRS
    height = sources * channels
    chunk = sources // 4

    def kernel(x_ref, f_ref, table_ref, tr_ref, ti_ref, y_hbm, cross_hbm, y_ref, cross_ref, talls, wides, stages, turns, sems):
        second_ref, third_ref = table_ref.at[: 2 * inner], table_ref.at[2 * inner : 4 * inner]
        fourth_ref = table_ref.at[4 * inner : 4 * inner + 2 * half]
        firsts = table_ref[4 * inner + 2 * half :, :]
        first = jnp.concatenate([firsts[:, : 2 * half], firsts[:, 2 * half :]], axis=0)
        tr, ti = tr_ref[...], ti_ref[...]
        for s in range(2):
            tall, wide, stage = talls.at[s], wides.at[s], stages.at[s]
            for t in range(tiles):
                block = x_ref[:, s * channels : (s + 1) * channels, t * LANES : (t + 1) * LANES]
                tall[t * height : (t + 1) * height, :] = block.astype(jnp.float32).reshape(height, LANES)
            for c in range(channels):
                pair, part = divmod(c, 2)
                for h in range(fold):
                    line = spread(tall, sources, channels, c, height, (h * inner, (h + 1) * inner))
                    at = part * half + h * sources
                    wide[at : at + sources, pair * inner : (pair + 1) * inner] = line.astype(jnp.bfloat16)
            for g in range(groups):
                span = PAIRS * inner
                f = dot(first, wide[:, g * span : (g + 1) * span])
                for p in range(PAIRS):
                    f_re = f[:outer, p * inner : (p + 1) * inner]
                    f_im = f[outer:, p * inner : (p + 1) * inner]
                    at = (g * PAIRS + p) * outer
                    stage[at : at + outer, :inner] = (f_re * tr + f_im * ti).astype(jnp.bfloat16)
                    stage[at : at + outer, inner:] = (f_im * tr - f_re * ti).astype(jnp.bfloat16)
        for g in range(groups):
            s_re = f_ref[g * outer : (g + 1) * outer, :inner].astype(jnp.float32)
            s_im = f_ref[g * outer : (g + 1) * outer, inner:].astype(jnp.float32)
            cross_re = cross_im = 0.0
            for p in range(PAIRS):
                at = (g * PAIRS + p) * outer
                k = dot(stages[0, at : at + outer, :], second_ref[...])
                d = dot(stages[1, at : at + outer, :], second_ref[...])
                k_re, k_im = k[:, :inner], k[:, inner:]
                d_re, d_im = d[:, :inner], d[:, inner:]
                cross_re = cross_re + (k_re * d_re + k_im * d_im)
                cross_im = cross_im + (k_re * d_im - k_im * d_re)
                stages[0, at : at + outer, :inner] = (s_re * k_re - s_im * k_im).astype(jnp.bfloat16)
                stages[0, at : at + outer, inner:] = (s_re * k_im + s_im * k_re).astype(jnp.bfloat16)
                stages[1, at : at + outer, :inner] = (s_re * d_re + s_im * d_im).astype(jnp.bfloat16)
                stages[1, at : at + outer, inner:] = (s_re * d_im - s_im * d_re).astype(jnp.bfloat16)
            cross_ref[g * outer : (g + 1) * outer, :inner] = cross_re.astype(jnp.bfloat16)
            cross_ref[g * outer : (g + 1) * outer, inner:] = cross_im.astype(jnp.bfloat16)
        copies = [pltpu.make_async_copy(cross_ref, cross_hbm, sems.at[4])]
        copies[0].start()
        spot = lax.broadcasted_iota(jnp.int32, (RIM, LANES), 0)
        lane = lax.broadcasted_iota(jnp.int32, (RIM, LANES), 1)
        pick = jnp.where(spot == lane, 1.0, 0.0).astype(jnp.bfloat16)
        rims = []
        for s in range(2):
            tall, stage, turn = talls.at[s], stages.at[s], turns.at[s]
            for pair in range(pairs):
                at = pair * outer
                h = dot(stage[at : at + outer, :], third_ref[...])
                h_re, h_im = h[:, :inner], h[:, inner:]
                lanes = slice(pair * inner, (pair + 1) * inner)
                turn[:outer, lanes] = (h_re * tr - h_im * ti).astype(jnp.bfloat16)
                turn[outer:, lanes] = (h_im * tr + h_re * ti).astype(jnp.bfloat16)
            for g in range(groups):
                span = PAIRS * inner
                y = dot(fourth_ref[...], turn[:, g * span : (g + 1) * span])
                for p in range(PAIRS):
                    for part in range(2):
                        c = (g * PAIRS + p) * 2 + part
                        for h in range(fold):
                            at = part * half + h * sources
                            line = y[at : at + sources, p * inner : (p + 1) * inner]
                            put_spread(tall, line, channels, c, height, (h * inner, (h + 1) * inner))
            front = tall[:height, :].astype(jnp.bfloat16)
            rims.append(
                lax.dot_general(pick, front, (((1,), (1,)), ((), ())), preferred_element_type=jnp.float32)
            )
        for q in range(4):
            to = slice(q * chunk, (q + 1) * chunk)
            for s in range(2):
                for t in range(tiles):
                    at = t * height + q * chunk * channels
                    block = talls[s, at : at + chunk * channels, :].reshape(chunk, channels, LANES)
                    row = (s * tiles + t) * channels
                    y_ref[to, row : row + channels, :] = block.astype(jnp.bfloat16)
            for d in range(q * chunk, (q + 1) * chunk):
                tile, lanes = divmod((d + 1) % sources * channels, LANES)
                edge = jnp.zeros((RIM, LANES), jnp.float32)
                if d < sources - 1:
                    for s in range(2):
                        piece = rims[s][:, tile * LANES : (tile + 1) * LANES]
                        turn_by = (s * channels - lanes) % LANES
                        if turn_by:
                            piece = pltpu.roll(piece, turn_by, 1)
                        edge = piece if s == 0 else jnp.where(lane < channels, edge, piece)
                y_ref[d, 2 * tiles * channels :, :] = edge.astype(jnp.bfloat16)
            copies.append(pltpu.make_async_copy(y_ref.at[to], y_hbm.at[to], sems.at[q]))
            copies[-1].start()
        for copy in copies:
            copy.wait()

    sent = (sources, 2 * tiles * channels + RIM, LANES)
    vmem = pl.BlockSpec(memory_space=pltpu.VMEM)
    hbm = pl.BlockSpec(memory_space=pltpu.HBM)
    return whole_call(
        kernel,
        "joined_filtering",
        (narrow_shape(*sent), narrow_shape(groups * outer, 2 * inner)),
        [arrived, filters, joined, tables["twist_re"], tables["twist_im"]],
        [
            pltpu.VMEM(sent, jnp.bfloat16),
            pltpu.VMEM((groups * outer, 2 * inner), jnp.bfloat16),
            pltpu.VMEM((2, tiles * height, LANES), jnp.float32),
            pltpu.VMEM((2, outer, pairs * inner), jnp.bfloat16),
            pltpu.VMEM((2, pairs * outer, 2 * inner), jnp.bfloat16),
            pltpu.VMEM((2, 2 * outer, pairs * inner), jnp.bfloat16),
            pltpu.SemaphoreType.DMA((5,)),
        ],
        flops=4_000_000_000,
        in_specs=[vmem] * 5,
        out_specs=(hbm, hbm),
    )


def joined_gradients(cross, feats, edges, returned, out_grad, short_filter, owned):
    width, local = out_grad.shape
    tiles = local // LANES
    near = LANES // owned
    steps = width // LANES // STEP

    def kernel(_, f_hbm, edge_ref, back_ref, og_ref, w_ref, mixed_ref, out_ref, tall, made, f_ref, sent, fetched):
        def step_rows(part, step):
            return pl.ds(pl.multiple_of(part * width + step * STEP * LANES, STEP * LANES), STEP * LANES)

        def fetch(part, step):
            rows = step_rows(part, step)
            return pltpu.make_async_copy(f_hbm.at[rows, :], f_ref.at[rows, :], fetched.at[part * steps + step])

        @pl.loop(0, steps)
        def _(step):
            for part in range(3):
                fetch(part, step).start()

        def features(part, i):
            rows = lane_block(i, part * width)
            held = [f_ref[rows, t * LANES : (t + 1) * LANES] for t in range(tiles)]
            return jnp.concatenate(held, axis=0).astype(jnp.float32)

        lane = lax.broadcasted_iota(jnp.int32, (RIM, LANES), 1)

        def copy(part, step):
            rows = step_rows(part, step)
            to = out_ref.at[rows, :] if part < 3 else mixed_ref.at[step_rows(0, step), :]
            return pltpu.make_async_copy(made.at[rows, :], to, sent.at[part * steps + step])

        def turned(s, i):
            held = pl.ds(i * near, near)
            pieces = [
                back_ref[held, (s * tiles + t) * owned : (s * tiles + t + 1) * owned, :].reshape(LANES, LANES).T
                for t in range(tiles)
            ]
            return jnp.concatenate(pieces, axis=0).astype(jnp.float32)

        def rim_of(s, i):
            rim = None
            for n in range(near):
                piece = back_ref[i * near + n, 2 * tiles * owned :, :].astype(jnp.float32)
                turn_by = (n - s) * owned % LANES
                if turn_by:
                    piece = pltpu.roll(piece, turn_by, 1)
                rim = jnp.where(lane >= n * owned, piece, rim) if n else piece
            return rim

        def third(part, slot, i, here, rim, other):
            edge = edge_ref[:, lane_block(i, (3 - part) % 3 * width)].astype(jnp.float32)
            total = seven_taps(
                tall.at[3 * slot + part],
                (here * other).astype(jnp.bfloat16).astype(jnp.float32),
                (rim * edge).astype(jnp.bfloat16).astype(jnp.float32),
                w_ref[:, lane_block(i, part * width)].astype(jnp.float32),
                False,
            )
            made[lane_block(i, part * width), :] = total.astype(jnp.bfloat16).T

        @pl.loop(0, steps)
        def _(step):
            for part in range(3):
                fetch(part, step).wait()
            for slot in range(STEP):
                i = step * STEP + slot
                query, key, value = [features(part, i) for part in range(3)]
                conv = turned(0, i)
                made[lane_block(i, 3 * width), :] = (query * conv).astype(jnp.bfloat16).T
                third(0, slot, i, conv, rim_of(0, i), og_ref[lane_block(i), :].T.astype(jnp.float32))
                back, rim = turned(1, i), rim_of(1, i)
                third(1, slot, i, back, rim, value)
                third(2, slot, i, back, rim, key)
            for part in range(4):
                copy(part, step).start()

        @pl.loop(0, steps)
        def _(step):
            for part in range(4):
                copy(part, step).wait()

    vmem = pl.BlockSpec(memory_space=pltpu.VMEM)
    hbm = pl.BlockSpec(memory_space=pltpu.HBM)
    return whole_call(
        kernel,
        "joined_gradients",
        (narrow_shape(width, local), narrow_shape(3 * width, local)),
        (cross, feats, edges, returned, out_grad, short_filter),
        [
            pltpu.VMEM((3 * STEP, local + RIM, LANES), jnp.float32),
            pltpu.VMEM((4 * width, local), jnp.bfloat16),
            pltpu.VMEM((3 * width, local), jnp.bfloat16),
            pltpu.SemaphoreType.DMA((4 * steps,)),
            pltpu.SemaphoreType.DMA((3 * steps,)),
        ],
        in_specs=[hbm, hbm] + [vmem] * 4,
        out_specs=(hbm, hbm),
        input_output_aliases={0: 0, 1: 1},
    )


def query_gradient(grad, rim, short_filter):
    local, width = grad.shape
    steps = width // GRAD_ROWS

    def kernel(d_ref, rim_ref, w_ref, out_ref, tall):
        gradient_block(d_ref, rim_ref, w_ref, out_ref, tall)

    return gradient_call(kernel, "query_gradient", (), grad, rim, short_filter, 1, 0)


def key_value_gradient(whole, grad, rim, short_filter):
    def kernel(_, d_ref, rim_ref, w_ref, out_ref, tall):
        gradient_block(d_ref, rim_ref, w_ref, out_ref, tall)

    return gradient_call(kernel, "key_value_gradient", (whole,), grad, rim, short_filter, 2, 1)


GRAD_ROWS = 512


def gradient_block(d_ref, rim_ref, w_ref, out_ref, tall):
    for c in range(GRAD_ROWS // LANES):
        lanes = slice(c * LANES, (c + 1) * LANES)
        total = seven_taps(
            tall.at[c],
            d_ref[:, lanes].astype(jnp.float32),
            rim_ref[:, lanes].astype(jnp.float32),
            w_ref[:, lanes].astype(jnp.float32),
            False,
        )
        out_ref[lanes, :] = total.astype(jnp.bfloat16).T


def gradient_call(kernel, name, whole, grad, rim, short_filter, parts, first):
    local, lanes = grad.shape
    width = lanes // parts
    steps = width // GRAD_ROWS
    return pl.pallas_call(
        kernel,
        name=name,
        grid=(parts * steps,),
        in_specs=[pl.BlockSpec(memory_space=pl.ANY)] * len(whole)
        + [
            pl.BlockSpec((local, GRAD_ROWS), lambda i: (0, i)),
            pl.BlockSpec((RIM, GRAD_ROWS), lambda i: (0, i)),
            pl.BlockSpec((TAPS, GRAD_ROWS), lambda i: (0, first * steps + i)),
        ],
        out_specs=pl.BlockSpec((GRAD_ROWS, local), lambda i: (first * steps + i, 0)),
        out_shape=narrow_shape(3 * width, local),
        scratch_shapes=[pltpu.VMEM((GRAD_ROWS // LANES, local + RIM, LANES), jnp.float32)],
        input_output_aliases={0: 0} if whole else {},
        cost_estimate=pl.CostEstimate(flops=20_000_000, bytes_accessed=4_000_000, transcendentals=0),
    )(*whole, grad, rim, short_filter)


def shards(projections, short_filter, long_filter, out_grad):
    width, local_len = out_grad.shape
    devices = lax.axis_size(EVERYONE)
    seq_len = local_len * devices
    owned = width // devices
    tables = make_tables(seq_len, devices)

    turned = projections.T
    rim = shifted(turned[local_len - RIM :], EVERYONE, 1)

    _, inner, outer = sizes_of(seq_len)
    twin = owned // CPG * outer == width and 2 * inner == local_len and inner == outer
    if owned % 16 == 0 and LANES % (2 * owned) == 0 and devices % 4 == 0 and twin and width % (STEP * LANES) == 0:
        feats, message, edges = joined_features(turned, rim, short_filter, out_grad, owned)
        filters, joined = transform_filters(long_filter, tables, seq_len, jnp.bfloat16, [tables["joined"]])
        arrived = lax.all_to_all(message, EVERYONE, split_axis=0, concat_axis=0, tiled=True)
        edges, filters, joined, arrived = lax.optimization_barrier(
            (shifted(edges, EVERYONE, -1), filters, joined, arrived)
        )
        answer, cross = joined_filtering(arrived, filters, joined, tables, seq_len)
        returned = lax.all_to_all(answer, EVERYONE, split_axis=0, concat_axis=0, tiled=True)
        filter_grad = filter_gradient(cross, tables, seq_len)
        filter_grad, returned, cross = lax.optimization_barrier((filter_grad, returned, cross))
        mixed, grad = joined_gradients(cross, feats, edges, returned, out_grad, short_filter, owned)
        return (mixed, grad, filter_grad)

    cotangent = out_grad.T
    feats, product, conv_grad = features_of(turned, rim, short_filter, cotangent)

    def exchange(block):
        pieces = block.reshape(devices, owned, local_len)
        return lax.all_to_all(pieces, EVERYONE, split_axis=0, concat_axis=0, tiled=True)

    (filters,) = transform_filters(long_filter, tables, seq_len)
    prod_chan = exchange(product)
    conv_grad, prod_chan = lax.optimization_barrier((conv_grad, prod_chan))
    grad_chan = exchange(conv_grad)
    conv_chan, prod_spec = filtered(prod_chan, filters, tables, seq_len)
    conv_chan, grad_chan = lax.optimization_barrier((conv_chan, grad_chan))
    conv_tok = exchange(conv_chan)
    back_chan, cross = filtered(grad_chan, filters, tables, seq_len, prod_spec)
    back_chan, conv_tok = lax.optimization_barrier((back_chan, conv_tok))
    back_tok = exchange(back_chan)

    filter_grad = filter_gradient(cross, tables, seq_len)
    mixed, grad_q, rim_q = query_products(feats, conv_tok.reshape(width, local_len), cotangent)
    grad = query_gradient(grad_q, shifted(rim_q, EVERYONE, -1), short_filter)
    filter_grad, mixed, grad, back_tok = lax.optimization_barrier((filter_grad, mixed, grad, back_tok))

    grad_kv, rim_kv = key_value_products(feats, back_tok.reshape(width, local_len))
    grad = key_value_gradient(grad, grad_kv, shifted(rim_kv, EVERYONE, -1), short_filter)
    return (mixed, grad, filter_grad)


def solution(mesh):
    placed = (P(None, EVERYONE), P(), P(EVERYONE, None), P(None, EVERYONE))
    return jax.shard_map(
        shards,
        mesh=mesh,
        in_specs=placed,
        out_specs=(P(None, EVERYONE), P(None, EVERYONE), P(EVERYONE, None)),
        check_vma=False,
    )
```

```python
import math

import jax
import jax.numpy as jnp
import numpy as np
from jax import lax
from jax.experimental import pallas as pl
from jax.experimental.pallas import tpu as pltpu
from jax.sharding import PartitionSpec as P

CPG = 4
TAPS = 7
PAIRS = CPG // 2
EVERYONE = ("dp", "ctx")
VMEM_LIMIT = 24 * 1024 * 1024


def shifted(value, axis, steps):
    count = lax.axis_size(axis)
    first, last = (max(0, -steps), min(count, count - steps))
    return lax.ppermute(value, axis, [(source, source + steps) for source in range(first, last)])


def sizes_of(seq_len):
    padded = 2 * seq_len
    inner = max(d for d in range(1, seq_len + 1) if seq_len % d == 0 and d * d <= padded)
    return padded, inner, padded // inner


def table(count_out, count_in, period):
    turns = np.arange(count_out, dtype=np.int64)[:, None] * np.arange(count_in, dtype=np.int64)
    angle = (turns % period).astype(np.float64) * (2.0 * math.pi / period)
    return np.cos(angle), np.sin(angle)


def make_tables(seq_len, sources):
    padded, inner, outer = sizes_of(seq_len)
    half = outer // 2
    fold = half // sources
    order = np.arange(half).reshape(sources, fold).T.reshape(-1)
    cos_o, sin_o = table(outer, half, outer)
    cos_i, sin_i = table(inner, inner, inner)
    cos_p, sin_p = cos_o[:, order], sin_o[:, order]
    narrow = lambda blocks: jnp.asarray(np.block(blocks).astype(np.float32)).astype(jnp.bfloat16)
    twist = [jnp.asarray(t.astype(np.float32)) for t in table(outer, inner, padded)]
    return {
        "first": narrow([[cos_p, sin_p], [-sin_p, cos_p]]),
        "second": narrow([[cos_i, -sin_i], [sin_i, cos_i]]),
        "third": narrow([[cos_i, sin_i], [-sin_i, cos_i]]),
        "fourth": narrow([[cos_p.T, -sin_p.T], [sin_p.T, cos_p.T]]),
        "joined": narrow(
            [
                [cos_i, -sin_i],
                [sin_i, cos_i],
                [cos_i, sin_i],
                [-sin_i, cos_i],
                [cos_p.T / padded, -sin_p.T / padded],
                [sin_p.T / padded, cos_p.T / padded],
                [np.hstack([cos_p, sin_p]), np.hstack([-sin_p, cos_p])],
            ]
        )
        if inner == outer
        else None,
        "first_real": narrow([[cos_o], [-sin_o]]),
        "fourth_real": narrow([[cos_o.T, -sin_o.T]]),
        "twist_re": twist[0],
        "twist_im": twist[1],
    }


LANES = 128


def spread(tall, count, stride, first, height, width):
    tiles = [tall[pl.ds(t * height + first, count, stride=stride), :] for t in range(width[0] // LANES, width[1] // LANES)]
    return tiles[0] if len(tiles) == 1 else jnp.concatenate(tiles, axis=1)


def put_spread(tall, values, stride, first, height, width):
    for i, t in enumerate(range(width[0] // LANES, width[1] // LANES)):
        tall[pl.ds(t * height + first, values.shape[0], stride=stride), :] = values[:, i * LANES : (i + 1) * LANES]


def dot(left, right):
    return jnp.dot(left, right, preferred_element_type=jnp.float32)


def transform_filters(long_filter, tables, seq_len, kind=jnp.float32, handed=()):
    padded, inner, outer = sizes_of(seq_len)
    half = outer // 2
    groups = long_filter.shape[0]
    scale = seq_len ** -0.5

    def kernel(x_ref, first_ref, second_ref, tr_ref, ti_ref, *refs):
        count = len(handed)
        out_ref, tall = refs[count], refs[-1]
        for n in range(count):
            refs[count + 1 + n][...] = refs[n][...]
        height = half * groups
        for b in range(half):
            for t in range(inner // LANES):
                at = t * height + b * groups
                lanes = slice(b * inner + t * LANES, b * inner + (t + 1) * LANES)
                tall[at : at + groups, :] = x_ref[:, lanes].astype(jnp.float32)
        for g in range(groups):
            x = spread(tall, half, groups, g, height, (0, inner)).astype(jnp.bfloat16)
            f = dot(first_ref[...], x)
            f_re, f_im = f[:outer], f[outer:]
            g_re = (f_re * tr_ref[...] + f_im * ti_ref[...]).astype(jnp.bfloat16)
            g_im = (f_im * tr_ref[...] - f_re * ti_ref[...]).astype(jnp.bfloat16)
            spec = dot(g_re, second_ref[:inner]) + dot(g_im, second_ref[inner:])
            out_ref[g * outer : (g + 1) * outer, :] = (spec * scale).astype(kind)

    return pl.pallas_call(
        kernel,
        name="filter_dft",
        out_shape=[jax.ShapeDtypeStruct((groups * outer, 2 * inner), kind)]
        + [jax.ShapeDtypeStruct(array.shape, array.dtype) for array in handed],
        scratch_shapes=[pltpu.VMEM((half * groups * inner // LANES, LANES), jnp.float32)],
        compiler_params=pltpu.CompilerParams(vmem_limit_bytes=VMEM_LIMIT),
        cost_estimate=pl.CostEstimate(flops=200_000_000, bytes_accessed=2_000_000, transcendentals=0),
    )(long_filter, tables["first_real"], tables["second"], tables["twist_re"], tables["twist_im"], *handed)


def filtered(arrived, filters, tables, seq_len, other=None):
    padded, inner, outer = sizes_of(seq_len)
    half = outer // 2
    sources, channels, local = arrived.shape
    fold = local // inner
    groups = channels // CPG
    backward = other is not None

    def kernel(*refs):
        if backward:
            (x_ref, f_ref, k_ref, first_ref, second_ref, third_ref, fourth_ref, tr_ref, ti_ref,
             y_ref, cross_ref, tall, wide, stage, turn) = refs
        else:
            (x_ref, f_ref, first_ref, second_ref, third_ref, fourth_ref, tr_ref, ti_ref,
             y_ref, z_ref, tall, wide, stage, turn) = refs
        height = sources * channels
        for t in range(local // LANES):
            block = x_ref[:, :, t * LANES : (t + 1) * LANES].astype(jnp.float32)
            tall[t * height : (t + 1) * height, :] = block.reshape(height, LANES)
        for c in range(channels):
            pair, part = divmod(c, 2)
            for h in range(fold):
                rows = spread(tall, sources, channels, c, height, (h * inner, (h + 1) * inner))
                at = part * half + h * sources
                wide[at : at + sources, pair * inner : (pair + 1) * inner] = rows.astype(jnp.bfloat16)
        for g in range(groups):
            span = PAIRS * inner
            f = dot(first_ref[...], wide[:, g * span : (g + 1) * span])
            for p in range(PAIRS):
                f_re = f[:outer, p * inner : (p + 1) * inner]
                f_im = f[outer:, p * inner : (p + 1) * inner]
                at = (g * PAIRS + p) * outer
                stage[at : at + outer, :inner] = (f_re * tr_ref[...] + f_im * ti_ref[...]).astype(jnp.bfloat16)
                stage[at : at + outer, inner:] = (f_im * tr_ref[...] - f_re * ti_ref[...]).astype(jnp.bfloat16)
        for g in range(groups):
            s_re = f_ref[g * outer : (g + 1) * outer, :inner]
            s_im = f_ref[g * outer : (g + 1) * outer, inner:]
            cross_re = cross_im = None
            for p in range(PAIRS):
                at = (g * PAIRS + p) * outer
                z = dot(stage[at : at + outer, :], second_ref[...])
                z_re, z_im = z[:, :inner], z[:, inner:]
                if backward:
                    k_re = k_ref[at : at + outer, :inner].astype(jnp.float32)
                    k_im = k_ref[at : at + outer, inner:].astype(jnp.float32)
                    part_re = k_re * z_re + k_im * z_im
                    part_im = k_re * z_im - k_im * z_re
                    cross_re = part_re if cross_re is None else cross_re + part_re
                    cross_im = part_im if cross_im is None else cross_im + part_im
                    o_re = s_re * z_re + s_im * z_im
                    o_im = s_re * z_im - s_im * z_re
                else:
                    z_ref[at : at + outer, :] = z
                    o_re = s_re * z_re - s_im * z_im
                    o_im = s_re * z_im + s_im * z_re
                stage[at : at + outer, :inner] = o_re.astype(jnp.bfloat16)
                stage[at : at + outer, inner:] = o_im.astype(jnp.bfloat16)
            if backward:
                cross_ref[g * outer : (g + 1) * outer, :inner] = cross_re.astype(jnp.bfloat16)
                cross_ref[g * outer : (g + 1) * outer, inner:] = cross_im.astype(jnp.bfloat16)
        for pair in range(groups * PAIRS):
            at = pair * outer
            h = dot(stage[at : at + outer, :], third_ref[...])
            h_re, h_im = h[:, :inner], h[:, inner:]
            lanes = slice(pair * inner, (pair + 1) * inner)
            turn[:outer, lanes] = (h_re * tr_ref[...] - h_im * ti_ref[...]).astype(jnp.bfloat16)
            turn[outer:, lanes] = (h_im * tr_ref[...] + h_re * ti_ref[...]).astype(jnp.bfloat16)
        for g in range(groups):
            span = PAIRS * inner
            y = dot(fourth_ref[...], turn[:, g * span : (g + 1) * span]) * (1.0 / padded)
            for p in range(PAIRS):
                for part in range(2):
                    c = (g * PAIRS + p) * 2 + part
                    for h in range(fold):
                        at = part * half + h * sources
                        rows = y[at : at + sources, p * inner : (p + 1) * inner]
                        put_spread(tall, rows, channels, c, height, (h * inner, (h + 1) * inner))
        for t in range(local // LANES):
            block = tall[t * height : (t + 1) * height, :].reshape(sources, channels, LANES)
            y_ref[:, :, t * LANES : (t + 1) * LANES] = block.astype(jnp.bfloat16)

    pairs = groups * PAIRS
    if backward:
        extra = jax.ShapeDtypeStruct((groups * outer, 2 * inner), jnp.bfloat16)
    else:
        extra = jax.ShapeDtypeStruct((pairs * outer, 2 * inner), jnp.float32)
    operands = [arrived, filters] + ([other] if backward else [])
    operands += [tables[n] for n in ("first", "second", "third", "fourth", "twist_re", "twist_im")]
    return pl.pallas_call(
        kernel,
        name="correlate" if backward else "convolve",
        out_shape=(jax.ShapeDtypeStruct(arrived.shape, jnp.bfloat16), extra),
        scratch_shapes=[
            pltpu.VMEM((sources * channels * local // LANES, LANES), jnp.float32),
            pltpu.VMEM((outer, pairs * inner), jnp.bfloat16),
            pltpu.VMEM((pairs * outer, 2 * inner), jnp.bfloat16),
            pltpu.VMEM((2 * outer, pairs * inner), jnp.bfloat16),
        ],
        compiler_params=pltpu.CompilerParams(vmem_limit_bytes=VMEM_LIMIT),
        cost_estimate=pl.CostEstimate(flops=2_000_000_000, bytes_accessed=5_000_000, transcendentals=0),
    )(*operands)


def filter_gradient(cross, tables, seq_len):
    padded, inner, outer = sizes_of(seq_len)
    half = outer // 2
    groups = cross.shape[0] // outer
    scale = seq_len ** -0.5 / padded

    def kernel(s_ref, third_ref, fourth_ref, tr_ref, ti_ref, out_ref, tall, turn):
        for g in range(groups):
            h = dot(s_ref[g * outer : (g + 1) * outer, :], third_ref[...])
            h_re, h_im = h[:, :inner], h[:, inner:]
            turn[:outer, g * inner : (g + 1) * inner] = (h_re * tr_ref[...] - h_im * ti_ref[...]).astype(jnp.bfloat16)
            turn[outer:, g * inner : (g + 1) * inner] = (h_im * tr_ref[...] + h_re * ti_ref[...]).astype(jnp.bfloat16)
        for g in range(groups):
            y = dot(fourth_ref[...], turn[:, g * inner : (g + 1) * inner]) * scale
            put_spread(tall, y, groups, g, half * groups, (0, inner))
        for b in range(half):
            for t in range(inner // LANES):
                at = (t * half + b) * groups
                out_ref[:, b * inner + t * LANES : b * inner + (t + 1) * LANES] = tall[at : at + groups, :]

    return pl.pallas_call(
        kernel,
        name="filter_gradient",
        out_shape=jax.ShapeDtypeStruct((groups, seq_len), jnp.float32),
        scratch_shapes=[
            pltpu.VMEM((half * groups * inner // LANES, LANES), jnp.float32),
            pltpu.VMEM((2 * outer, groups * inner), jnp.bfloat16),
        ],
        compiler_params=pltpu.CompilerParams(vmem_limit_bytes=VMEM_LIMIT),
        cost_estimate=pl.CostEstimate(flops=200_000_000, bytes_accessed=2_000_000, transcendentals=0),
    )(cross, tables["third"], tables["fourth_real"], tables["twist_re"], tables["twist_im"])


RIM = 8
STEP = 2


def seven_taps(tall, value, rim, weights, forward):
    count = value.shape[0]
    if forward:
        tall[:RIM, :] = rim
        tall[RIM : RIM + count, :] = value
    else:
        tall[:count, :] = value
        tall[count : count + RIM, :] = rim
    total = value * weights[:1]
    for lag in range(1, TAPS):
        first = RIM - lag if forward else lag
        total = total + tall[first : first + count, :] * weights[lag : lag + 1]
    return total


def lane_block(i, offset=0):
    return pl.ds(pl.multiple_of(i * LANES + offset, LANES), LANES)


def whole_call(kernel, name, out_shape, operands, scratch=(), flops=10_000_000, **kwargs):
    return pl.pallas_call(
        kernel,
        name=name,
        out_shape=out_shape,
        scratch_shapes=list(scratch),
        compiler_params=pltpu.CompilerParams(vmem_limit_bytes=VMEM_LIMIT),
        cost_estimate=pl.CostEstimate(flops=flops, bytes_accessed=4_000_000, transcendentals=0),
        **kwargs,
    )(*operands)


def narrow_shape(*shape):
    return jax.ShapeDtypeStruct(shape, jnp.bfloat16)


def features_of(turned, rim, short_filter, cotangent):
    local, width = cotangent.shape

    def kernel(x_ref, rim_ref, w_ref, og_ref, f_ref, kv_ref, dconv_ref, tall):
        @pl.loop(0, width // LANES)
        def _(i):
            made = []
            for part in range(3):
                lanes = lane_block(i, part * width)
                total = seven_taps(
                    tall.at[part],
                    x_ref[:, lanes].astype(jnp.float32),
                    rim_ref[:, lanes].astype(jnp.float32),
                    w_ref[:, lanes].astype(jnp.float32),
                    True,
                ).astype(jnp.bfloat16)
                f_ref[:, lanes] = total
                made.append(total.astype(jnp.float32))
            rows = lane_block(i)
            kv_ref[rows, :] = (made[1] * made[2]).astype(jnp.bfloat16).T
            og = og_ref[:, rows].astype(jnp.float32)
            dconv_ref[rows, :] = (og * made[0]).astype(jnp.bfloat16).T

    return whole_call(
        kernel,
        "features",
        (narrow_shape(local, 3 * width), narrow_shape(width, local), narrow_shape(width, local)),
        (turned, rim, short_filter, cotangent),
        [pltpu.VMEM((3, local + RIM, LANES), jnp.float32)],
    )


def query_products(feats, conv, cotangent):
    width, local = conv.shape

    def kernel(f_ref, conv_ref, og_ref, mixed_ref, dq_ref, rim_ref):
        @pl.loop(0, width // LANES)
        def _(i):
            lanes = lane_block(i)
            here = conv_ref[lanes, :].T.astype(jnp.float32)
            mixed_ref[lanes, :] = (f_ref[:, lanes].astype(jnp.float32) * here).astype(jnp.bfloat16).T
            dq = (og_ref[:, lanes].astype(jnp.float32) * here).astype(jnp.bfloat16)
            dq_ref[:, lanes] = dq
            rim_ref[:, lanes] = dq[:RIM]

    return whole_call(
        kernel,
        "query_products",
        (narrow_shape(width, local), narrow_shape(local, width), narrow_shape(RIM, width)),
        (feats, conv, cotangent),
    )


def key_value_products(feats, back):
    width, local = back.shape

    def kernel(f_ref, back_ref, d_ref, rim_ref):
        @pl.loop(0, width // LANES)
        def _(i):
            here = back_ref[lane_block(i), :].T.astype(jnp.float32)
            for part in range(2):
                other = f_ref[:, lane_block(i, (2 - part) * width)].astype(jnp.float32)
                grad = (here * other).astype(jnp.bfloat16)
                d_ref[:, lane_block(i, part * width)] = grad
                rim_ref[:, lane_block(i, part * width)] = grad[:RIM]

    return whole_call(
        kernel,
        "key_value_products",
        (narrow_shape(local, 2 * width), narrow_shape(RIM, 2 * width)),
        (feats, back),
    )


def joined_features(turned, rim, short_filter, out_grad, owned):
    width, local = out_grad.shape
    near = LANES // owned
    steps = width // LANES // STEP

    def kernel(x_ref, rim_ref, w_ref, og_ref, f_hbm, msg_ref, edge_ref, tall, made, f_ref, edge, sent):
        def copy(step):
            to = pl.ds(step * STEP * near, STEP * near)
            return pltpu.make_async_copy(made.at[to], msg_ref.at[to], sent.at[step])

        def keep(part, step):
            to = pl.ds(pl.multiple_of(part * width + step * STEP * LANES, STEP * LANES), STEP * LANES)
            return pltpu.make_async_copy(f_ref.at[to, :], f_hbm.at[to, :], sent.at[(1 + part) * steps + step])

        @pl.loop(0, steps)
        def _(step):
            for slot in range(STEP):
                i = step * STEP + slot
                parts = []
                for part in range(3):
                    lanes = lane_block(i, part * width)
                    total = seven_taps(
                        tall.at[3 * slot + part],
                        x_ref[:, lanes].astype(jnp.float32),
                        rim_ref[:, lanes].astype(jnp.float32),
                        w_ref[:, lanes].astype(jnp.float32),
                        True,
                    ).astype(jnp.bfloat16)
                    for t in range(local // LANES):
                        f_ref[lanes, t * LANES : (t + 1) * LANES] = total[t * LANES : (t + 1) * LANES]
                    if part:
                        edge[:, lanes] = total[:RIM]
                    parts.append(total.astype(jnp.float32))
                og = og_ref[lane_block(i), :].T
                edge[:, lane_block(i)] = og[:RIM]
                kv = (parts[1] * parts[2]).astype(jnp.bfloat16).T
                dconv = (og.astype(jnp.float32) * parts[0]).astype(jnp.bfloat16).T
                to = pl.ds(i * near, near)
                made[to, :owned, :] = kv.reshape(near, owned, local)
                made[to, owned:, :] = dconv.reshape(near, owned, local)
            copy(step).start()
            for part in range(3):
                keep(part, step).start()

        last = pltpu.make_async_copy(edge, edge_ref, sent.at[4 * steps])
        last.start()

        @pl.loop(0, steps)
        def _(step):
            copy(step).wait()
            for part in range(3):
                keep(part, step).wait()

        last.wait()

    vmem = pl.BlockSpec(memory_space=pltpu.VMEM)
    hbm = pl.BlockSpec(memory_space=pltpu.HBM)
    devices = width // owned
    return whole_call(
        kernel,
        "joined_features",
        (narrow_shape(3 * width, local), narrow_shape(devices, 2 * owned, local), narrow_shape(RIM, 3 * width)),
        (turned, rim, short_filter, out_grad),
        [
            pltpu.VMEM((3 * STEP, local + RIM, LANES), jnp.float32),
            pltpu.VMEM((devices, 2 * owned, local), jnp.bfloat16),
            pltpu.VMEM((3 * width, local), jnp.bfloat16),
            pltpu.VMEM((RIM, 3 * width), jnp.bfloat16),
            pltpu.SemaphoreType.DMA((4 * steps + 1,)),
        ],
        in_specs=[vmem] * 4,
        out_specs=(hbm, hbm, hbm),
    )


def joined_filtering(arrived, filters, joined, tables, seq_len):
    padded, inner, outer = sizes_of(seq_len)
    half = outer // 2
    sources, rows, local = arrived.shape
    channels = rows // 2
    tiles = local // LANES
    fold = local // inner
    groups = channels // CPG
    height = sources * channels
    chunk = sources // 4

    def kernel(x_ref, f_ref, table_ref, tr_ref, ti_ref, y_hbm, cross_hbm, y_ref, cross_ref, talls, sems):
        second_ref, third_ref = table_ref.at[: 2 * inner], table_ref.at[2 * inner : 4 * inner]
        fourth_ref = table_ref.at[4 * inner : 4 * inner + 2 * half]
        firsts = table_ref[4 * inner + 2 * half :, :]
        first = jnp.concatenate([firsts[:, : 2 * half], firsts[:, 2 * half :]], axis=0)
        tr, ti = tr_ref[...], ti_ref[...]
        for s in range(2):
            for t in range(tiles):
                block = x_ref[:, s * channels : (s + 1) * channels, t * LANES : (t + 1) * LANES]
                talls[s, t * height : (t + 1) * height, :] = block.astype(jnp.float32).reshape(height, LANES)

        def gathered(s, g):
            pieces = []
            for p in range(PAIRS):
                lines = [
                    spread(talls.at[s], sources, channels, g * CPG + 2 * p + part, height, (h * inner, (h + 1) * inner))
                    for part in range(2)
                    for h in range(fold)
                ]
                pieces.append(jnp.concatenate(lines, axis=0).astype(jnp.bfloat16))
            return jnp.concatenate(pieces, axis=1)

        def spectrum(s, g):
            f = dot(first, gathered(s, g))
            turned = []
            for p in range(PAIRS):
                f_re = f[:outer, p * inner : (p + 1) * inner]
                f_im = f[outer:, p * inner : (p + 1) * inner]
                parts = [f_re * tr + f_im * ti, f_im * tr - f_re * ti]
                turned.append(jnp.concatenate([part.astype(jnp.bfloat16) for part in parts], axis=1))
            return dot(jnp.concatenate(turned, axis=0), second_ref[...])

        def back(s, g, products):
            joined = [jnp.concatenate([part.astype(jnp.bfloat16) for part in pair], axis=1) for pair in products]
            h = dot(jnp.concatenate(joined, axis=0), third_ref[...])
            turned = []
            for p in range(PAIRS):
                h_re = h[p * outer : (p + 1) * outer, :inner]
                h_im = h[p * outer : (p + 1) * outer, inner:]
                parts = [h_re * tr - h_im * ti, h_im * tr + h_re * ti]
                turned.append(jnp.concatenate([part.astype(jnp.bfloat16) for part in parts], axis=0))
            y = dot(fourth_ref[...], jnp.concatenate(turned, axis=1))
            for p in range(PAIRS):
                for part in range(2):
                    for h in range(fold):
                        at = part * half + h * sources
                        line = y[at : at + sources, p * inner : (p + 1) * inner]
                        c = g * CPG + 2 * p + part
                        put_spread(talls.at[s], line, channels, c, height, (h * inner, (h + 1) * inner))

        @pl.loop(0, groups // STEP)
        def _(step):
            slots = [step * STEP + slot for slot in range(STEP)]
            spectra = [[spectrum(s, g) for s in range(2)] for g in slots]
            answers = []
            for g, (k, d) in zip(slots, spectra):
                lines = pl.ds(pl.multiple_of(g * outer, outer), outer)
                s_re = f_ref[lines, :inner].astype(jnp.float32)
                s_im = f_ref[lines, inner:].astype(jnp.float32)
                cross_re = cross_im = 0.0
                conv, dkv = [], []
                for p in range(PAIRS):
                    here = slice(p * outer, (p + 1) * outer)
                    k_re, k_im = k[here, :inner], k[here, inner:]
                    d_re, d_im = d[here, :inner], d[here, inner:]
                    cross_re = cross_re + (k_re * d_re + k_im * d_im)
                    cross_im = cross_im + (k_re * d_im - k_im * d_re)
                    conv.append((s_re * k_re - s_im * k_im, s_re * k_im + s_im * k_re))
                    dkv.append((s_re * d_re + s_im * d_im, s_re * d_im - s_im * d_re))
                cross_ref[lines, :inner] = cross_re.astype(jnp.bfloat16)
                cross_ref[lines, inner:] = cross_im.astype(jnp.bfloat16)
                answers.append((conv, dkv))
            for g, answer in zip(slots, answers):
                for s in range(2):
                    back(s, g, answer[s])

        copies = [pltpu.make_async_copy(cross_ref, cross_hbm, sems.at[4])]
        copies[0].start()
        spot = lax.broadcasted_iota(jnp.int32, (RIM, LANES), 0)
        lane = lax.broadcasted_iota(jnp.int32, (RIM, LANES), 1)
        pick = jnp.where(spot == lane, 1.0, 0.0).astype(jnp.bfloat16)
        rims = []
        for s in range(2):
            front = talls[s, :height, :].astype(jnp.bfloat16)
            rims.append(
                lax.dot_general(pick, front, (((1,), (1,)), ((), ())), preferred_element_type=jnp.float32)
            )
        for q in range(4):
            to = slice(q * chunk, (q + 1) * chunk)
            for s in range(2):
                for t in range(tiles):
                    at = t * height + q * chunk * channels
                    block = talls[s, at : at + chunk * channels, :].reshape(chunk, channels, LANES)
                    row = (s * tiles + t) * channels
                    y_ref[to, row : row + channels, :] = block.astype(jnp.bfloat16)
            for d in range(q * chunk, (q + 1) * chunk):
                tile, lanes = divmod((d + 1) % sources * channels, LANES)
                edge = jnp.zeros((RIM, LANES), jnp.float32)
                if d < sources - 1:
                    for s in range(2):
                        piece = rims[s][:, tile * LANES : (tile + 1) * LANES]
                        turn_by = (s * channels - lanes) % LANES
                        if turn_by:
                            piece = pltpu.roll(piece, turn_by, 1)
                        edge = piece if s == 0 else jnp.where(lane < channels, edge, piece)
                y_ref[d, 2 * tiles * channels :, :] = edge.astype(jnp.bfloat16)
            copies.append(pltpu.make_async_copy(y_ref.at[to], y_hbm.at[to], sems.at[q]))
            copies[-1].start()
        for copy in copies:
            copy.wait()

    sent = (sources, 2 * tiles * channels + RIM, LANES)
    vmem = pl.BlockSpec(memory_space=pltpu.VMEM)
    hbm = pl.BlockSpec(memory_space=pltpu.HBM)
    return whole_call(
        kernel,
        "joined_filtering",
        (narrow_shape(*sent), narrow_shape(groups * outer, 2 * inner)),
        [arrived, filters, joined, tables["twist_re"], tables["twist_im"]],
        [
            pltpu.VMEM(sent, jnp.bfloat16),
            pltpu.VMEM((groups * outer, 2 * inner), jnp.bfloat16),
            pltpu.VMEM((2, tiles * height, LANES), jnp.float32),
            pltpu.SemaphoreType.DMA((5,)),
        ],
        flops=4_000_000_000,
        in_specs=[vmem] * 5,
        out_specs=(hbm, hbm),
    )


def joined_gradients(cross, feats, edges, returned, out_grad, short_filter, owned):
    width, local = out_grad.shape
    tiles = local // LANES
    near = LANES // owned
    steps = width // LANES // STEP

    def kernel(_, f_hbm, edge_ref, back_ref, og_ref, w_ref, mixed_ref, out_ref, tall, made, f_ref, sent, fetched):
        def step_rows(part, step):
            return pl.ds(pl.multiple_of(part * width + step * STEP * LANES, STEP * LANES), STEP * LANES)

        def fetch(part, step):
            rows = step_rows(part, step)
            return pltpu.make_async_copy(f_hbm.at[rows, :], f_ref.at[rows, :], fetched.at[part * steps + step])

        @pl.loop(0, steps)
        def _(step):
            for part in range(3):
                fetch(part, step).start()

        def features(part, i):
            rows = lane_block(i, part * width)
            held = [f_ref[rows, t * LANES : (t + 1) * LANES] for t in range(tiles)]
            return jnp.concatenate(held, axis=0).astype(jnp.float32)

        lane = lax.broadcasted_iota(jnp.int32, (RIM, LANES), 1)

        def copy(part, step):
            rows = step_rows(part, step)
            to = out_ref.at[rows, :] if part < 3 else mixed_ref.at[step_rows(0, step), :]
            return pltpu.make_async_copy(made.at[rows, :], to, sent.at[part * steps + step])

        def turned(s, i):
            held = pl.ds(i * near, near)
            pieces = [
                back_ref[held, (s * tiles + t) * owned : (s * tiles + t + 1) * owned, :].reshape(LANES, LANES).T
                for t in range(tiles)
            ]
            return jnp.concatenate(pieces, axis=0).astype(jnp.float32)

        def rim_of(s, i):
            rim = None
            for n in range(near):
                piece = back_ref[i * near + n, 2 * tiles * owned :, :].astype(jnp.float32)
                turn_by = (n - s) * owned % LANES
                if turn_by:
                    piece = pltpu.roll(piece, turn_by, 1)
                rim = jnp.where(lane >= n * owned, piece, rim) if n else piece
            return rim

        def third(part, slot, i, here, rim, other):
            edge = edge_ref[:, lane_block(i, (3 - part) % 3 * width)].astype(jnp.float32)
            total = seven_taps(
                tall.at[3 * slot + part],
                (here * other).astype(jnp.bfloat16).astype(jnp.float32),
                (rim * edge).astype(jnp.bfloat16).astype(jnp.float32),
                w_ref[:, lane_block(i, part * width)].astype(jnp.float32),
                False,
            )
            made[lane_block(i, part * width), :] = total.astype(jnp.bfloat16).T

        @pl.loop(0, steps)
        def _(step):
            for part in range(3):
                fetch(part, step).wait()
            for slot in range(STEP):
                i = step * STEP + slot
                query, key, value = [features(part, i) for part in range(3)]
                conv = turned(0, i)
                made[lane_block(i, 3 * width), :] = (query * conv).astype(jnp.bfloat16).T
                third(0, slot, i, conv, rim_of(0, i), og_ref[lane_block(i), :].T.astype(jnp.float32))
                back, rim = turned(1, i), rim_of(1, i)
                third(1, slot, i, back, rim, value)
                third(2, slot, i, back, rim, key)
            for part in range(4):
                copy(part, step).start()

        @pl.loop(0, steps)
        def _(step):
            for part in range(4):
                copy(part, step).wait()

    vmem = pl.BlockSpec(memory_space=pltpu.VMEM)
    hbm = pl.BlockSpec(memory_space=pltpu.HBM)
    return whole_call(
        kernel,
        "joined_gradients",
        (narrow_shape(width, local), narrow_shape(3 * width, local)),
        (cross, feats, edges, returned, out_grad, short_filter),
        [
            pltpu.VMEM((3 * STEP, local + RIM, LANES), jnp.float32),
            pltpu.VMEM((4 * width, local), jnp.bfloat16),
            pltpu.VMEM((3 * width, local), jnp.bfloat16),
            pltpu.SemaphoreType.DMA((4 * steps,)),
            pltpu.SemaphoreType.DMA((3 * steps,)),
        ],
        in_specs=[hbm, hbm] + [vmem] * 4,
        out_specs=(hbm, hbm),
        input_output_aliases={0: 0, 1: 1},
    )


def query_gradient(grad, rim, short_filter):
    local, width = grad.shape
    steps = width // GRAD_ROWS

    def kernel(d_ref, rim_ref, w_ref, out_ref, tall):
        gradient_block(d_ref, rim_ref, w_ref, out_ref, tall)

    return gradient_call(kernel, "query_gradient", (), grad, rim, short_filter, 1, 0)


def key_value_gradient(whole, grad, rim, short_filter):
    def kernel(_, d_ref, rim_ref, w_ref, out_ref, tall):
        gradient_block(d_ref, rim_ref, w_ref, out_ref, tall)

    return gradient_call(kernel, "key_value_gradient", (whole,), grad, rim, short_filter, 2, 1)


GRAD_ROWS = 512


def gradient_block(d_ref, rim_ref, w_ref, out_ref, tall):
    for c in range(GRAD_ROWS // LANES):
        lanes = slice(c * LANES, (c + 1) * LANES)
        total = seven_taps(
            tall.at[c],
            d_ref[:, lanes].astype(jnp.float32),
            rim_ref[:, lanes].astype(jnp.float32),
            w_ref[:, lanes].astype(jnp.float32),
            False,
        )
        out_ref[lanes, :] = total.astype(jnp.bfloat16).T


def gradient_call(kernel, name, whole, grad, rim, short_filter, parts, first):
    local, lanes = grad.shape
    width = lanes // parts
    steps = width // GRAD_ROWS
    return pl.pallas_call(
        kernel,
        name=name,
        grid=(parts * steps,),
        in_specs=[pl.BlockSpec(memory_space=pl.ANY)] * len(whole)
        + [
            pl.BlockSpec((local, GRAD_ROWS), lambda i: (0, i)),
            pl.BlockSpec((RIM, GRAD_ROWS), lambda i: (0, i)),
            pl.BlockSpec((TAPS, GRAD_ROWS), lambda i: (0, first * steps + i)),
        ],
        out_specs=pl.BlockSpec((GRAD_ROWS, local), lambda i: (first * steps + i, 0)),
        out_shape=narrow_shape(3 * width, local),
        scratch_shapes=[pltpu.VMEM((GRAD_ROWS // LANES, local + RIM, LANES), jnp.float32)],
        input_output_aliases={0: 0} if whole else {},
        cost_estimate=pl.CostEstimate(flops=20_000_000, bytes_accessed=4_000_000, transcendentals=0),
    )(*whole, grad, rim, short_filter)


def shards(projections, short_filter, long_filter, out_grad):
    width, local_len = out_grad.shape
    devices = lax.axis_size(EVERYONE)
    seq_len = local_len * devices
    owned = width // devices
    tables = make_tables(seq_len, devices)

    turned = projections.T
    rim = shifted(turned[local_len - RIM :], EVERYONE, 1)

    _, inner, outer = sizes_of(seq_len)
    twin = owned // CPG * outer == width and 2 * inner == local_len and inner == outer
    if owned % 16 == 0 and LANES % (2 * owned) == 0 and devices % 4 == 0 and twin and width % (STEP * LANES) == owned // CPG % STEP == 0:
        feats, message, edges = joined_features(turned, rim, short_filter, out_grad, owned)
        filters, joined = transform_filters(long_filter, tables, seq_len, jnp.bfloat16, [tables["joined"]])
        arrived = lax.all_to_all(message, EVERYONE, split_axis=0, concat_axis=0, tiled=True)
        edges, filters, joined, arrived = lax.optimization_barrier(
            (shifted(edges, EVERYONE, -1), filters, joined, arrived)
        )
        answer, cross = joined_filtering(arrived, filters, joined, tables, seq_len)
        returned = lax.all_to_all(answer, EVERYONE, split_axis=0, concat_axis=0, tiled=True)
        filter_grad = filter_gradient(cross, tables, seq_len)
        filter_grad, returned, cross = lax.optimization_barrier((filter_grad, returned, cross))
        mixed, grad = joined_gradients(cross, feats, edges, returned, out_grad, short_filter, owned)
        return (mixed, grad, filter_grad)

    cotangent = out_grad.T
    feats, product, conv_grad = features_of(turned, rim, short_filter, cotangent)

    def exchange(block):
        pieces = block.reshape(devices, owned, local_len)
        return lax.all_to_all(pieces, EVERYONE, split_axis=0, concat_axis=0, tiled=True)

    (filters,) = transform_filters(long_filter, tables, seq_len)
    prod_chan = exchange(product)
    conv_grad, prod_chan = lax.optimization_barrier((conv_grad, prod_chan))
    grad_chan = exchange(conv_grad)
    conv_chan, prod_spec = filtered(prod_chan, filters, tables, seq_len)
    conv_chan, grad_chan = lax.optimization_barrier((conv_chan, grad_chan))
    conv_tok = exchange(conv_chan)
    back_chan, cross = filtered(grad_chan, filters, tables, seq_len, prod_spec)
    back_chan, conv_tok = lax.optimization_barrier((back_chan, conv_tok))
    back_tok = exchange(back_chan)

    filter_grad = filter_gradient(cross, tables, seq_len)
    mixed, grad_q, rim_q = query_products(feats, conv_tok.reshape(width, local_len), cotangent)
    grad = query_gradient(grad_q, shifted(rim_q, EVERYONE, -1), short_filter)
    filter_grad, mixed, grad, back_tok = lax.optimization_barrier((filter_grad, mixed, grad, back_tok))

    grad_kv, rim_kv = key_value_products(feats, back_tok.reshape(width, local_len))
    grad = key_value_gradient(grad, grad_kv, shifted(rim_kv, EVERYONE, -1), short_filter)
    return (mixed, grad, filter_grad)


def solution(mesh):
    placed = (P(None, EVERYONE), P(), P(EVERYONE, None), P(None, EVERYONE))
    return jax.shard_map(
        shards,
        mesh=mesh,
        in_specs=placed,
        out_specs=(P(None, EVERYONE), P(None, EVERYONE), P(EVERYONE, None)),
        check_vma=False,
    )
```

```python
import math

import jax
import jax.numpy as jnp
import numpy as np
from jax import lax
from jax.experimental import pallas as pl
from jax.experimental.pallas import tpu as pltpu
from jax.sharding import PartitionSpec as P

CPG = 4
TAPS = 7
PAIRS = CPG // 2
EVERYONE = ("dp", "ctx")
VMEM_LIMIT = 24 * 1024 * 1024


def shifted(value, axis, steps):
    count = lax.axis_size(axis)
    first, last = (max(0, -steps), min(count, count - steps))
    return lax.ppermute(value, axis, [(source, source + steps) for source in range(first, last)])


def sizes_of(seq_len):
    padded = 2 * seq_len
    inner = max(d for d in range(1, seq_len + 1) if seq_len % d == 0 and d * d <= padded)
    return padded, inner, padded // inner


def table(count_out, count_in, period):
    turns = np.arange(count_out, dtype=np.int64)[:, None] * np.arange(count_in, dtype=np.int64)
    angle = (turns % period).astype(np.float64) * (2.0 * math.pi / period)
    return np.cos(angle), np.sin(angle)


def make_tables(seq_len, sources):
    padded, inner, outer = sizes_of(seq_len)
    half = outer // 2
    fold = half // sources
    order = np.arange(half).reshape(sources, fold).T.reshape(-1)
    cos_o, sin_o = table(outer, half, outer)
    cos_i, sin_i = table(inner, inner, inner)
    cos_p, sin_p = cos_o[:, order], sin_o[:, order]
    narrow = lambda blocks: jnp.asarray(np.block(blocks).astype(np.float32)).astype(jnp.bfloat16)
    twist = [jnp.asarray(t.astype(np.float32)) for t in table(outer, inner, padded)]
    return {
        "first": narrow([[cos_p, sin_p], [-sin_p, cos_p]]),
        "second": narrow([[cos_i, -sin_i], [sin_i, cos_i]]),
        "third": narrow([[cos_i, sin_i], [-sin_i, cos_i]]),
        "fourth": narrow([[cos_p.T, -sin_p.T], [sin_p.T, cos_p.T]]),
        "joined": narrow(
            [
                [cos_i, -sin_i],
                [sin_i, cos_i],
                [cos_i, sin_i],
                [-sin_i, cos_i],
                [cos_p.T / padded, -sin_p.T / padded],
                [sin_p.T / padded, cos_p.T / padded],
                [np.hstack([cos_p, sin_p]), np.hstack([-sin_p, cos_p])],
            ]
        )
        if inner == outer
        else None,
        "first_real": narrow([[cos_o], [-sin_o]]),
        "fourth_real": narrow([[cos_o.T, -sin_o.T]]),
        "twist_re": twist[0],
        "twist_im": twist[1],
    }


LANES = 128


def spread(tall, count, stride, first, height, width):
    tiles = [tall[pl.ds(t * height + first, count, stride=stride), :] for t in range(width[0] // LANES, width[1] // LANES)]
    return tiles[0] if len(tiles) == 1 else jnp.concatenate(tiles, axis=1)


def put_spread(tall, values, stride, first, height, width):
    for i, t in enumerate(range(width[0] // LANES, width[1] // LANES)):
        tall[pl.ds(t * height + first, values.shape[0], stride=stride), :] = values[:, i * LANES : (i + 1) * LANES]


def dot(left, right):
    return jnp.dot(left, right, preferred_element_type=jnp.float32)


def transform_filters(long_filter, tables, seq_len, kind=jnp.float32, handed=()):
    padded, inner, outer = sizes_of(seq_len)
    half = outer // 2
    groups = long_filter.shape[0]
    scale = seq_len ** -0.5

    def kernel(x_ref, first_ref, second_ref, tr_ref, ti_ref, *refs):
        count = len(handed)
        out_ref, tall = refs[count], refs[-1]
        for n in range(count):
            refs[count + 1 + n][...] = refs[n][...]
        height = half * groups
        for b in range(half):
            for t in range(inner // LANES):
                at = t * height + b * groups
                lanes = slice(b * inner + t * LANES, b * inner + (t + 1) * LANES)
                tall[at : at + groups, :] = x_ref[:, lanes].astype(jnp.float32)
        for g in range(groups):
            x = spread(tall, half, groups, g, height, (0, inner)).astype(jnp.bfloat16)
            f = dot(first_ref[...], x)
            f_re, f_im = f[:outer], f[outer:]
            g_re = (f_re * tr_ref[...] + f_im * ti_ref[...]).astype(jnp.bfloat16)
            g_im = (f_im * tr_ref[...] - f_re * ti_ref[...]).astype(jnp.bfloat16)
            spec = dot(g_re, second_ref[:inner]) + dot(g_im, second_ref[inner:])
            out_ref[g * outer : (g + 1) * outer, :] = (spec * scale).astype(kind)

    return pl.pallas_call(
        kernel,
        name="filter_dft",
        out_shape=[jax.ShapeDtypeStruct((groups * outer, 2 * inner), kind)]
        + [jax.ShapeDtypeStruct(array.shape, array.dtype) for array in handed],
        scratch_shapes=[pltpu.VMEM((half * groups * inner // LANES, LANES), jnp.float32)],
        compiler_params=pltpu.CompilerParams(vmem_limit_bytes=VMEM_LIMIT),
        cost_estimate=pl.CostEstimate(flops=200_000_000, bytes_accessed=2_000_000, transcendentals=0),
    )(long_filter, tables["first_real"], tables["second"], tables["twist_re"], tables["twist_im"], *handed)


def filtered(arrived, filters, tables, seq_len, other=None):
    padded, inner, outer = sizes_of(seq_len)
    half = outer // 2
    sources, channels, local = arrived.shape
    fold = local // inner
    groups = channels // CPG
    backward = other is not None

    def kernel(*refs):
        if backward:
            (x_ref, f_ref, k_ref, first_ref, second_ref, third_ref, fourth_ref, tr_ref, ti_ref,
             y_ref, cross_ref, tall, wide, stage, turn) = refs
        else:
            (x_ref, f_ref, first_ref, second_ref, third_ref, fourth_ref, tr_ref, ti_ref,
             y_ref, z_ref, tall, wide, stage, turn) = refs
        height = sources * channels
        for t in range(local // LANES):
            block = x_ref[:, :, t * LANES : (t + 1) * LANES].astype(jnp.float32)
            tall[t * height : (t + 1) * height, :] = block.reshape(height, LANES)
        for c in range(channels):
            pair, part = divmod(c, 2)
            for h in range(fold):
                rows = spread(tall, sources, channels, c, height, (h * inner, (h + 1) * inner))
                at = part * half + h * sources
                wide[at : at + sources, pair * inner : (pair + 1) * inner] = rows.astype(jnp.bfloat16)
        for g in range(groups):
            span = PAIRS * inner
            f = dot(first_ref[...], wide[:, g * span : (g + 1) * span])
            for p in range(PAIRS):
                f_re = f[:outer, p * inner : (p + 1) * inner]
                f_im = f[outer:, p * inner : (p + 1) * inner]
                at = (g * PAIRS + p) * outer
                stage[at : at + outer, :inner] = (f_re * tr_ref[...] + f_im * ti_ref[...]).astype(jnp.bfloat16)
                stage[at : at + outer, inner:] = (f_im * tr_ref[...] - f_re * ti_ref[...]).astype(jnp.bfloat16)
        for g in range(groups):
            s_re = f_ref[g * outer : (g + 1) * outer, :inner]
            s_im = f_ref[g * outer : (g + 1) * outer, inner:]
            cross_re = cross_im = None
            for p in range(PAIRS):
                at = (g * PAIRS + p) * outer
                z = dot(stage[at : at + outer, :], second_ref[...])
                z_re, z_im = z[:, :inner], z[:, inner:]
                if backward:
                    k_re = k_ref[at : at + outer, :inner].astype(jnp.float32)
                    k_im = k_ref[at : at + outer, inner:].astype(jnp.float32)
                    part_re = k_re * z_re + k_im * z_im
                    part_im = k_re * z_im - k_im * z_re
                    cross_re = part_re if cross_re is None else cross_re + part_re
                    cross_im = part_im if cross_im is None else cross_im + part_im
                    o_re = s_re * z_re + s_im * z_im
                    o_im = s_re * z_im - s_im * z_re
                else:
                    z_ref[at : at + outer, :] = z
                    o_re = s_re * z_re - s_im * z_im
                    o_im = s_re * z_im + s_im * z_re
                stage[at : at + outer, :inner] = o_re.astype(jnp.bfloat16)
                stage[at : at + outer, inner:] = o_im.astype(jnp.bfloat16)
            if backward:
                cross_ref[g * outer : (g + 1) * outer, :inner] = cross_re.astype(jnp.bfloat16)
                cross_ref[g * outer : (g + 1) * outer, inner:] = cross_im.astype(jnp.bfloat16)
        for pair in range(groups * PAIRS):
            at = pair * outer
            h = dot(stage[at : at + outer, :], third_ref[...])
            h_re, h_im = h[:, :inner], h[:, inner:]
            lanes = slice(pair * inner, (pair + 1) * inner)
            turn[:outer, lanes] = (h_re * tr_ref[...] - h_im * ti_ref[...]).astype(jnp.bfloat16)
            turn[outer:, lanes] = (h_im * tr_ref[...] + h_re * ti_ref[...]).astype(jnp.bfloat16)
        for g in range(groups):
            span = PAIRS * inner
            y = dot(fourth_ref[...], turn[:, g * span : (g + 1) * span]) * (1.0 / padded)
            for p in range(PAIRS):
                for part in range(2):
                    c = (g * PAIRS + p) * 2 + part
                    for h in range(fold):
                        at = part * half + h * sources
                        rows = y[at : at + sources, p * inner : (p + 1) * inner]
                        put_spread(tall, rows, channels, c, height, (h * inner, (h + 1) * inner))
        for t in range(local // LANES):
            block = tall[t * height : (t + 1) * height, :].reshape(sources, channels, LANES)
            y_ref[:, :, t * LANES : (t + 1) * LANES] = block.astype(jnp.bfloat16)

    pairs = groups * PAIRS
    if backward:
        extra = jax.ShapeDtypeStruct((groups * outer, 2 * inner), jnp.bfloat16)
    else:
        extra = jax.ShapeDtypeStruct((pairs * outer, 2 * inner), jnp.float32)
    operands = [arrived, filters] + ([other] if backward else [])
    operands += [tables[n] for n in ("first", "second", "third", "fourth", "twist_re", "twist_im")]
    return pl.pallas_call(
        kernel,
        name="correlate" if backward else "convolve",
        out_shape=(jax.ShapeDtypeStruct(arrived.shape, jnp.bfloat16), extra),
        scratch_shapes=[
            pltpu.VMEM((sources * channels * local // LANES, LANES), jnp.float32),
            pltpu.VMEM((outer, pairs * inner), jnp.bfloat16),
            pltpu.VMEM((pairs * outer, 2 * inner), jnp.bfloat16),
            pltpu.VMEM((2 * outer, pairs * inner), jnp.bfloat16),
        ],
        compiler_params=pltpu.CompilerParams(vmem_limit_bytes=VMEM_LIMIT),
        cost_estimate=pl.CostEstimate(flops=2_000_000_000, bytes_accessed=5_000_000, transcendentals=0),
    )(*operands)


def filter_gradient(cross, tables, seq_len):
    padded, inner, outer = sizes_of(seq_len)
    half = outer // 2
    groups = cross.shape[0] // outer
    scale = seq_len ** -0.5 / padded

    def kernel(s_ref, third_ref, fourth_ref, tr_ref, ti_ref, out_ref, tall, turn):
        for g in range(groups):
            h = dot(s_ref[g * outer : (g + 1) * outer, :], third_ref[...])
            h_re, h_im = h[:, :inner], h[:, inner:]
            turn[:outer, g * inner : (g + 1) * inner] = (h_re * tr_ref[...] - h_im * ti_ref[...]).astype(jnp.bfloat16)
            turn[outer:, g * inner : (g + 1) * inner] = (h_im * tr_ref[...] + h_re * ti_ref[...]).astype(jnp.bfloat16)
        for g in range(groups):
            y = dot(fourth_ref[...], turn[:, g * inner : (g + 1) * inner]) * scale
            put_spread(tall, y, groups, g, half * groups, (0, inner))
        for b in range(half):
            for t in range(inner // LANES):
                at = (t * half + b) * groups
                out_ref[:, b * inner + t * LANES : b * inner + (t + 1) * LANES] = tall[at : at + groups, :]

    return pl.pallas_call(
        kernel,
        name="filter_gradient",
        out_shape=jax.ShapeDtypeStruct((groups, seq_len), jnp.float32),
        scratch_shapes=[
            pltpu.VMEM((half * groups * inner // LANES, LANES), jnp.float32),
            pltpu.VMEM((2 * outer, groups * inner), jnp.bfloat16),
        ],
        compiler_params=pltpu.CompilerParams(vmem_limit_bytes=VMEM_LIMIT),
        cost_estimate=pl.CostEstimate(flops=200_000_000, bytes_accessed=2_000_000, transcendentals=0),
    )(cross, tables["third"], tables["fourth_real"], tables["twist_re"], tables["twist_im"])


RIM = 8
STEP = 2


def seven_taps(tall, value, rim, weights, forward):
    count = value.shape[0]
    if forward:
        tall[:RIM, :] = rim
        tall[RIM : RIM + count, :] = value
    else:
        tall[:count, :] = value
        tall[count : count + RIM, :] = rim
    total = value * weights[:1]
    for lag in range(1, TAPS):
        first = RIM - lag if forward else lag
        total = total + tall[first : first + count, :] * weights[lag : lag + 1]
    return total


def lane_block(i, offset=0):
    return pl.ds(pl.multiple_of(i * LANES + offset, LANES), LANES)


def whole_call(kernel, name, out_shape, operands, scratch=(), flops=10_000_000, **kwargs):
    return pl.pallas_call(
        kernel,
        name=name,
        out_shape=out_shape,
        scratch_shapes=list(scratch),
        compiler_params=pltpu.CompilerParams(vmem_limit_bytes=VMEM_LIMIT),
        cost_estimate=pl.CostEstimate(flops=flops, bytes_accessed=4_000_000, transcendentals=0),
        **kwargs,
    )(*operands)


def narrow_shape(*shape):
    return jax.ShapeDtypeStruct(shape, jnp.bfloat16)


def features_of(turned, rim, short_filter, cotangent):
    local, width = cotangent.shape

    def kernel(x_ref, rim_ref, w_ref, og_ref, f_ref, kv_ref, dconv_ref, tall):
        @pl.loop(0, width // LANES)
        def _(i):
            made = []
            for part in range(3):
                lanes = lane_block(i, part * width)
                total = seven_taps(
                    tall.at[part],
                    x_ref[:, lanes].astype(jnp.float32),
                    rim_ref[:, lanes].astype(jnp.float32),
                    w_ref[:, lanes].astype(jnp.float32),
                    True,
                ).astype(jnp.bfloat16)
                f_ref[:, lanes] = total
                made.append(total.astype(jnp.float32))
            rows = lane_block(i)
            kv_ref[rows, :] = (made[1] * made[2]).astype(jnp.bfloat16).T
            og = og_ref[:, rows].astype(jnp.float32)
            dconv_ref[rows, :] = (og * made[0]).astype(jnp.bfloat16).T

    return whole_call(
        kernel,
        "features",
        (narrow_shape(local, 3 * width), narrow_shape(width, local), narrow_shape(width, local)),
        (turned, rim, short_filter, cotangent),
        [pltpu.VMEM((3, local + RIM, LANES), jnp.float32)],
    )


def query_products(feats, conv, cotangent):
    width, local = conv.shape

    def kernel(f_ref, conv_ref, og_ref, mixed_ref, dq_ref, rim_ref):
        @pl.loop(0, width // LANES)
        def _(i):
            lanes = lane_block(i)
            here = conv_ref[lanes, :].T.astype(jnp.float32)
            mixed_ref[lanes, :] = (f_ref[:, lanes].astype(jnp.float32) * here).astype(jnp.bfloat16).T
            dq = (og_ref[:, lanes].astype(jnp.float32) * here).astype(jnp.bfloat16)
            dq_ref[:, lanes] = dq
            rim_ref[:, lanes] = dq[:RIM]

    return whole_call(
        kernel,
        "query_products",
        (narrow_shape(width, local), narrow_shape(local, width), narrow_shape(RIM, width)),
        (feats, conv, cotangent),
    )


def key_value_products(feats, back):
    width, local = back.shape

    def kernel(f_ref, back_ref, d_ref, rim_ref):
        @pl.loop(0, width // LANES)
        def _(i):
            here = back_ref[lane_block(i), :].T.astype(jnp.float32)
            for part in range(2):
                other = f_ref[:, lane_block(i, (2 - part) * width)].astype(jnp.float32)
                grad = (here * other).astype(jnp.bfloat16)
                d_ref[:, lane_block(i, part * width)] = grad
                rim_ref[:, lane_block(i, part * width)] = grad[:RIM]

    return whole_call(
        kernel,
        "key_value_products",
        (narrow_shape(local, 2 * width), narrow_shape(RIM, 2 * width)),
        (feats, back),
    )


def joined_features(turned, rim, short_filter, out_grad, owned):
    width, local = out_grad.shape
    near = LANES // owned
    blocks = width // LANES

    def kernel(x_ref, rim_ref, w_ref, og_ref, f_hbm, msg_ref, edge_ref, tall, made, f_ref, edge, sent):
        def copy(i):
            to = pl.ds(i * near, near)
            return pltpu.make_async_copy(made.at[to], msg_ref.at[to], sent.at[i])

        def keep(part, i):
            at = part * blocks + i
            to = pl.ds(pl.multiple_of(at * LANES, LANES), LANES)
            return pltpu.make_async_copy(f_ref.at[at], f_hbm.at[to, :], sent.at[blocks + at])

        @pl.loop(0, blocks // STEP)
        def _(step):
            for slot in range(STEP):
                i = step * STEP + slot
                parts = []
                for part in range(3):
                    lanes = lane_block(i, part * width)
                    total = seven_taps(
                        tall.at[3 * slot + part],
                        x_ref[:, lanes].astype(jnp.float32),
                        rim_ref[:, lanes].astype(jnp.float32),
                        w_ref[:, lanes].astype(jnp.float32),
                        True,
                    ).astype(jnp.bfloat16)
                    for t in range(local // LANES):
                        f_ref[part * blocks + i, :, t * LANES : (t + 1) * LANES] = total[t * LANES : (t + 1) * LANES]
                    if part:
                        edge[:, lanes] = total[:RIM]
                    parts.append(total.astype(jnp.float32))
                og = og_ref[lane_block(i), :].T
                edge[:, lane_block(i)] = og[:RIM]
                kv = (parts[1] * parts[2]).astype(jnp.bfloat16).T
                dconv = (og.astype(jnp.float32) * parts[0]).astype(jnp.bfloat16).T
                to = pl.ds(i * near, near)
                made[to, :owned, :] = kv.reshape(near, owned, local)
                made[to, owned:, :] = dconv.reshape(near, owned, local)
            for slot in range(STEP):
                copy(step * STEP + slot).start()
                for part in range(3):
                    keep(part, step * STEP + slot).start()

        last = pltpu.make_async_copy(edge, edge_ref, sent.at[4 * blocks])
        last.start()

        @pl.loop(0, blocks)
        def _(i):
            copy(i).wait()
            for part in range(3):
                keep(part, i).wait()

        last.wait()

    vmem = pl.BlockSpec(memory_space=pltpu.VMEM)
    hbm = pl.BlockSpec(memory_space=pltpu.HBM)
    devices = width // owned
    return whole_call(
        kernel,
        "joined_features",
        (narrow_shape(3 * width, local), narrow_shape(devices, 2 * owned, local), narrow_shape(RIM, 3 * width)),
        (turned, rim, short_filter, out_grad),
        [
            pltpu.VMEM((3 * STEP, local + RIM, LANES), jnp.float32),
            pltpu.VMEM((devices, 2 * owned, local), jnp.bfloat16),
            pltpu.VMEM((3 * blocks, LANES, local), jnp.bfloat16),
            pltpu.VMEM((RIM, 3 * width), jnp.bfloat16),
            pltpu.SemaphoreType.DMA((4 * blocks + 1,)),
        ],
        in_specs=[vmem] * 4,
        out_specs=(hbm, hbm, hbm),
    )


def joined_filtering(arrived, filters, joined, tables, seq_len):
    padded, inner, outer = sizes_of(seq_len)
    half = outer // 2
    sources, rows, local = arrived.shape
    channels = rows // 2
    tiles = local // LANES
    fold = local // inner
    groups = channels // CPG
    height = sources * channels
    chunk = sources // 4

    def kernel(x_ref, f_ref, table_ref, tr_ref, ti_ref, y_hbm, cross_hbm, y_ref, cross_ref, talls, results, sems):
        second_ref, third_ref = table_ref.at[: 2 * inner], table_ref.at[2 * inner : 4 * inner]
        fourth_ref = table_ref.at[4 * inner : 4 * inner + 2 * half]
        firsts = table_ref[4 * inner + 2 * half :, :]
        first = jnp.concatenate([firsts[:, : 2 * half], firsts[:, 2 * half :]], axis=0)
        tr, ti = tr_ref[...], ti_ref[...]
        for s in range(2):
            for t in range(tiles):
                block = x_ref[:, s * channels : (s + 1) * channels, t * LANES : (t + 1) * LANES]
                talls[s, t * height : (t + 1) * height, :] = block.astype(jnp.float32).reshape(height, LANES)

        def gathered(s, g):
            pieces = []
            for p in range(PAIRS):
                lines = [
                    spread(talls.at[s], sources, channels, g * CPG + 2 * p + part, height, (h * inner, (h + 1) * inner))
                    for part in range(2)
                    for h in range(fold)
                ]
                pieces.append(jnp.concatenate(lines, axis=0).astype(jnp.bfloat16))
            return jnp.concatenate(pieces, axis=1)

        def spectrum(s, g):
            f = dot(first, gathered(s, g))
            turned = []
            for p in range(PAIRS):
                f_re = f[:outer, p * inner : (p + 1) * inner]
                f_im = f[outer:, p * inner : (p + 1) * inner]
                parts = [f_re * tr + f_im * ti, f_im * tr - f_re * ti]
                turned.append(jnp.concatenate([part.astype(jnp.bfloat16) for part in parts], axis=1))
            return dot(jnp.concatenate(turned, axis=0), second_ref[...])

        def back(s, g, products):
            joined = [jnp.concatenate([part.astype(jnp.bfloat16) for part in pair], axis=1) for pair in products]
            h = dot(jnp.concatenate(joined, axis=0), third_ref[...])
            turned = []
            for p in range(PAIRS):
                h_re = h[p * outer : (p + 1) * outer, :inner]
                h_im = h[p * outer : (p + 1) * outer, inner:]
                parts = [h_re * tr - h_im * ti, h_im * tr + h_re * ti]
                turned.append(jnp.concatenate([part.astype(jnp.bfloat16) for part in parts], axis=0))
            y = dot(fourth_ref[...], jnp.concatenate(turned, axis=1))
            for p in range(PAIRS):
                for part in range(2):
                    for h in range(fold):
                        at = part * half + h * sources
                        line = y[at : at + sources, p * inner : (p + 1) * inner]
                        c = g * CPG + 2 * p + part
                        put_spread(results.at[s], line, channels, c, height, (h * inner, (h + 1) * inner))

        for step in range(groups // STEP):
            slots = [step * STEP + slot for slot in range(STEP)]
            spectra = [[spectrum(s, g) for s in range(2)] for g in slots]
            answers = []
            for g, (k, d) in zip(slots, spectra):
                lines = slice(g * outer, (g + 1) * outer)
                s_re = f_ref[lines, :inner].astype(jnp.float32)
                s_im = f_ref[lines, inner:].astype(jnp.float32)
                cross_re = cross_im = 0.0
                conv, dkv = [], []
                for p in range(PAIRS):
                    here = slice(p * outer, (p + 1) * outer)
                    k_re, k_im = k[here, :inner], k[here, inner:]
                    d_re, d_im = d[here, :inner], d[here, inner:]
                    cross_re = cross_re + (k_re * d_re + k_im * d_im)
                    cross_im = cross_im + (k_re * d_im - k_im * d_re)
                    conv.append((s_re * k_re - s_im * k_im, s_re * k_im + s_im * k_re))
                    dkv.append((s_re * d_re + s_im * d_im, s_re * d_im - s_im * d_re))
                cross_ref[lines, :inner] = cross_re.astype(jnp.bfloat16)
                cross_ref[lines, inner:] = cross_im.astype(jnp.bfloat16)
                answers.append((conv, dkv))
            for g, answer in zip(slots, answers):
                for s in range(2):
                    back(s, g, answer[s])

        copies = [pltpu.make_async_copy(cross_ref, cross_hbm, sems.at[4])]
        copies[0].start()
        spot = lax.broadcasted_iota(jnp.int32, (RIM, LANES), 0)
        lane = lax.broadcasted_iota(jnp.int32, (RIM, LANES), 1)
        pick = jnp.where(spot == lane, 1.0, 0.0).astype(jnp.bfloat16)
        rims = []
        for s in range(2):
            front = results[s, :height, :].astype(jnp.bfloat16)
            rims.append(
                lax.dot_general(pick, front, (((1,), (1,)), ((), ())), preferred_element_type=jnp.float32)
            )
        for q in range(4):
            to = slice(q * chunk, (q + 1) * chunk)
            for s in range(2):
                for t in range(tiles):
                    at = t * height + q * chunk * channels
                    block = results[s, at : at + chunk * channels, :].reshape(chunk, channels, LANES)
                    row = (s * tiles + t) * channels
                    y_ref[to, row : row + channels, :] = block.astype(jnp.bfloat16)
            for d in range(q * chunk, (q + 1) * chunk):
                tile, lanes = divmod((d + 1) % sources * channels, LANES)
                edge = jnp.zeros((RIM, LANES), jnp.float32)
                if d < sources - 1:
                    for s in range(2):
                        piece = rims[s][:, tile * LANES : (tile + 1) * LANES]
                        turn_by = (s * channels - lanes) % LANES
                        if turn_by:
                            piece = pltpu.roll(piece, turn_by, 1)
                        edge = piece if s == 0 else jnp.where(lane < channels, edge, piece)
                y_ref[d, 2 * tiles * channels :, :] = edge.astype(jnp.bfloat16)
            copies.append(pltpu.make_async_copy(y_ref.at[to], y_hbm.at[to], sems.at[q]))
            copies[-1].start()
        for copy in copies:
            copy.wait()

    sent = (sources, 2 * tiles * channels + RIM, LANES)
    vmem = pl.BlockSpec(memory_space=pltpu.VMEM)
    hbm = pl.BlockSpec(memory_space=pltpu.HBM)
    return whole_call(
        kernel,
        "joined_filtering",
        (narrow_shape(*sent), narrow_shape(groups * outer, 2 * inner)),
        [arrived, filters, joined, tables["twist_re"], tables["twist_im"]],
        [
            pltpu.VMEM(sent, jnp.bfloat16),
            pltpu.VMEM((groups * outer, 2 * inner), jnp.bfloat16),
            pltpu.VMEM((2, tiles * height, LANES), jnp.float32),
            pltpu.VMEM((2, tiles * height, LANES), jnp.float32),
            pltpu.SemaphoreType.DMA((5,)),
        ],
        flops=4_000_000_000,
        in_specs=[vmem] * 5,
        out_specs=(hbm, hbm),
    )


def joined_gradients(cross, feats, edges, returned, out_grad, short_filter, owned):
    width, local = out_grad.shape
    tiles = local // LANES
    near = LANES // owned
    steps = width // LANES // STEP

    def kernel(_, f_hbm, edge_ref, back_ref, og_ref, w_ref, mixed_ref, out_ref, tall, made, f_ref, sent, fetched):
        def step_rows(part, step):
            return pl.ds(pl.multiple_of(part * width + step * STEP * LANES, STEP * LANES), STEP * LANES)

        def fetch(part, step):
            rows = step_rows(part, step)
            return pltpu.make_async_copy(f_hbm.at[rows, :], f_ref.at[rows, :], fetched.at[part * steps + step])

        @pl.loop(0, steps)
        def _(step):
            for part in range(3):
                fetch(part, step).start()

        def features(part, i):
            rows = lane_block(i, part * width)
            held = [f_ref[rows, t * LANES : (t + 1) * LANES] for t in range(tiles)]
            return jnp.concatenate(held, axis=0).astype(jnp.float32)

        lane = lax.broadcasted_iota(jnp.int32, (RIM, LANES), 1)

        def copy(part, step):
            rows = step_rows(part, step)
            to = out_ref.at[rows, :] if part < 3 else mixed_ref.at[step_rows(0, step), :]
            return pltpu.make_async_copy(made.at[rows, :], to, sent.at[part * steps + step])

        def turned(s, i):
            held = pl.ds(i * near, near)
            pieces = [
                back_ref[held, (s * tiles + t) * owned : (s * tiles + t + 1) * owned, :].reshape(LANES, LANES).T
                for t in range(tiles)
            ]
            return jnp.concatenate(pieces, axis=0).astype(jnp.float32)

        def rim_of(s, i):
            rim = None
            for n in range(near):
                piece = back_ref[i * near + n, 2 * tiles * owned :, :].astype(jnp.float32)
                turn_by = (n - s) * owned % LANES
                if turn_by:
                    piece = pltpu.roll(piece, turn_by, 1)
                rim = jnp.where(lane >= n * owned, piece, rim) if n else piece
            return rim

        def third(part, slot, i, here, rim, other):
            edge = edge_ref[:, lane_block(i, (3 - part) % 3 * width)].astype(jnp.float32)
            total = seven_taps(
                tall.at[3 * slot + part],
                (here * other).astype(jnp.bfloat16).astype(jnp.float32),
                (rim * edge).astype(jnp.bfloat16).astype(jnp.float32),
                w_ref[:, lane_block(i, part * width)].astype(jnp.float32),
                False,
            )
            made[lane_block(i, part * width), :] = total.astype(jnp.bfloat16).T

        @pl.loop(0, steps)
        def _(step):
            for part in range(3):
                fetch(part, step).wait()
            for slot in range(STEP):
                i = step * STEP + slot
                query, key, value = [features(part, i) for part in range(3)]
                conv = turned(0, i)
                made[lane_block(i, 3 * width), :] = (query * conv).astype(jnp.bfloat16).T
                third(0, slot, i, conv, rim_of(0, i), og_ref[lane_block(i), :].T.astype(jnp.float32))
                back, rim = turned(1, i), rim_of(1, i)
                third(1, slot, i, back, rim, value)
                third(2, slot, i, back, rim, key)
            for part in range(4):
                copy(part, step).start()

        @pl.loop(0, steps)
        def _(step):
            for part in range(4):
                copy(part, step).wait()

    vmem = pl.BlockSpec(memory_space=pltpu.VMEM)
    hbm = pl.BlockSpec(memory_space=pltpu.HBM)
    return whole_call(
        kernel,
        "joined_gradients",
        (narrow_shape(width, local), narrow_shape(3 * width, local)),
        (cross, feats, edges, returned, out_grad, short_filter),
        [
            pltpu.VMEM((3 * STEP, local + RIM, LANES), jnp.float32),
            pltpu.VMEM((4 * width, local), jnp.bfloat16),
            pltpu.VMEM((3 * width, local), jnp.bfloat16),
            pltpu.SemaphoreType.DMA((4 * steps,)),
            pltpu.SemaphoreType.DMA((3 * steps,)),
        ],
        in_specs=[hbm, hbm] + [vmem] * 4,
        out_specs=(hbm, hbm),
        input_output_aliases={0: 0, 1: 1},
    )


def query_gradient(grad, rim, short_filter):
    local, width = grad.shape
    steps = width // GRAD_ROWS

    def kernel(d_ref, rim_ref, w_ref, out_ref, tall):
        gradient_block(d_ref, rim_ref, w_ref, out_ref, tall)

    return gradient_call(kernel, "query_gradient", (), grad, rim, short_filter, 1, 0)


def key_value_gradient(whole, grad, rim, short_filter):
    def kernel(_, d_ref, rim_ref, w_ref, out_ref, tall):
        gradient_block(d_ref, rim_ref, w_ref, out_ref, tall)

    return gradient_call(kernel, "key_value_gradient", (whole,), grad, rim, short_filter, 2, 1)


GRAD_ROWS = 512


def gradient_block(d_ref, rim_ref, w_ref, out_ref, tall):
    for c in range(GRAD_ROWS // LANES):
        lanes = slice(c * LANES, (c + 1) * LANES)
        total = seven_taps(
            tall.at[c],
            d_ref[:, lanes].astype(jnp.float32),
            rim_ref[:, lanes].astype(jnp.float32),
            w_ref[:, lanes].astype(jnp.float32),
            False,
        )
        out_ref[lanes, :] = total.astype(jnp.bfloat16).T


def gradient_call(kernel, name, whole, grad, rim, short_filter, parts, first):
    local, lanes = grad.shape
    width = lanes // parts
    steps = width // GRAD_ROWS
    return pl.pallas_call(
        kernel,
        name=name,
        grid=(parts * steps,),
        in_specs=[pl.BlockSpec(memory_space=pl.ANY)] * len(whole)
        + [
            pl.BlockSpec((local, GRAD_ROWS), lambda i: (0, i)),
            pl.BlockSpec((RIM, GRAD_ROWS), lambda i: (0, i)),
            pl.BlockSpec((TAPS, GRAD_ROWS), lambda i: (0, first * steps + i)),
        ],
        out_specs=pl.BlockSpec((GRAD_ROWS, local), lambda i: (first * steps + i, 0)),
        out_shape=narrow_shape(3 * width, local),
        scratch_shapes=[pltpu.VMEM((GRAD_ROWS // LANES, local + RIM, LANES), jnp.float32)],
        input_output_aliases={0: 0} if whole else {},
        cost_estimate=pl.CostEstimate(flops=20_000_000, bytes_accessed=4_000_000, transcendentals=0),
    )(*whole, grad, rim, short_filter)


def shards(projections, short_filter, long_filter, out_grad):
    width, local_len = out_grad.shape
    devices = lax.axis_size(EVERYONE)
    seq_len = local_len * devices
    owned = width // devices
    tables = make_tables(seq_len, devices)

    turned = projections.T
    rim = shifted(turned[local_len - RIM :], EVERYONE, 1)

    _, inner, outer = sizes_of(seq_len)
    twin = owned // CPG * outer == width and 2 * inner == local_len and inner == outer
    if owned % 16 == 0 and LANES % (2 * owned) == 0 and devices % 4 == 0 and twin and width % (STEP * LANES) == owned // CPG % STEP == 0:
        feats, message, edges = joined_features(turned, rim, short_filter, out_grad, owned)
        filters, joined = transform_filters(long_filter, tables, seq_len, jnp.bfloat16, [tables["joined"]])
        arrived = lax.all_to_all(message, EVERYONE, split_axis=0, concat_axis=0, tiled=True)
        edges, filters, joined, arrived = lax.optimization_barrier(
            (shifted(edges, EVERYONE, -1), filters, joined, arrived)
        )
        answer, cross = joined_filtering(arrived, filters, joined, tables, seq_len)
        returned = lax.all_to_all(answer, EVERYONE, split_axis=0, concat_axis=0, tiled=True)
        filter_grad = filter_gradient(cross, tables, seq_len)
        filter_grad, returned, cross = lax.optimization_barrier((filter_grad, returned, cross))
        mixed, grad = joined_gradients(cross, feats, edges, returned, out_grad, short_filter, owned)
        return (mixed, grad, filter_grad)

    cotangent = out_grad.T
    feats, product, conv_grad = features_of(turned, rim, short_filter, cotangent)

    def exchange(block):
        pieces = block.reshape(devices, owned, local_len)
        return lax.all_to_all(pieces, EVERYONE, split_axis=0, concat_axis=0, tiled=True)

    (filters,) = transform_filters(long_filter, tables, seq_len)
    prod_chan = exchange(product)
    conv_grad, prod_chan = lax.optimization_barrier((conv_grad, prod_chan))
    grad_chan = exchange(conv_grad)
    conv_chan, prod_spec = filtered(prod_chan, filters, tables, seq_len)
    conv_chan, grad_chan = lax.optimization_barrier((conv_chan, grad_chan))
    conv_tok = exchange(conv_chan)
    back_chan, cross = filtered(grad_chan, filters, tables, seq_len, prod_spec)
    back_chan, conv_tok = lax.optimization_barrier((back_chan, conv_tok))
    back_tok = exchange(back_chan)

    filter_grad = filter_gradient(cross, tables, seq_len)
    mixed, grad_q, rim_q = query_products(feats, conv_tok.reshape(width, local_len), cotangent)
    grad = query_gradient(grad_q, shifted(rim_q, EVERYONE, -1), short_filter)
    filter_grad, mixed, grad, back_tok = lax.optimization_barrier((filter_grad, mixed, grad, back_tok))

    grad_kv, rim_kv = key_value_products(feats, back_tok.reshape(width, local_len))
    grad = key_value_gradient(grad, grad_kv, shifted(rim_kv, EVERYONE, -1), short_filter)
    return (mixed, grad, filter_grad)


def solution(mesh):
    placed = (P(None, EVERYONE), P(), P(EVERYONE, None), P(None, EVERYONE))
    return jax.shard_map(
        shards,
        mesh=mesh,
        in_specs=placed,
        out_specs=(P(None, EVERYONE), P(None, EVERYONE), P(EVERYONE, None)),
        check_vma=False,
    )
```

```python
import math

import jax
import jax.numpy as jnp
import numpy as np
from jax import lax
from jax.experimental import pallas as pl
from jax.experimental.pallas import tpu as pltpu
from jax.sharding import PartitionSpec as P

CPG = 4
TAPS = 7
PAIRS = CPG // 2
EVERYONE = ("dp", "ctx")
VMEM_LIMIT = 24 * 1024 * 1024


def shifted(value, axis, steps):
    count = lax.axis_size(axis)
    first, last = (max(0, -steps), min(count, count - steps))
    return lax.ppermute(value, axis, [(source, source + steps) for source in range(first, last)])


def sizes_of(seq_len):
    padded = 2 * seq_len
    inner = max(d for d in range(1, seq_len + 1) if seq_len % d == 0 and d * d <= padded)
    return padded, inner, padded // inner


def table(count_out, count_in, period):
    turns = np.arange(count_out, dtype=np.int64)[:, None] * np.arange(count_in, dtype=np.int64)
    angle = (turns % period).astype(np.float64) * (2.0 * math.pi / period)
    return np.cos(angle), np.sin(angle)


def make_tables(seq_len, sources):
    padded, inner, outer = sizes_of(seq_len)
    half = outer // 2
    fold = half // sources
    order = np.arange(half).reshape(sources, fold).T.reshape(-1)
    cos_o, sin_o = table(outer, half, outer)
    cos_i, sin_i = table(inner, inner, inner)
    cos_p, sin_p = cos_o[:, order], sin_o[:, order]
    narrow = lambda blocks: jnp.asarray(np.block(blocks).astype(np.float32)).astype(jnp.bfloat16)
    twist = [jnp.asarray(t.astype(np.float32)) for t in table(outer, inner, padded)]
    return {
        "first": narrow([[cos_p, sin_p], [-sin_p, cos_p]]),
        "second": narrow([[cos_i, -sin_i], [sin_i, cos_i]]),
        "third": narrow([[cos_i, sin_i], [-sin_i, cos_i]]),
        "fourth": narrow([[cos_p.T, -sin_p.T], [sin_p.T, cos_p.T]]),
        "joined": narrow(
            [
                [cos_i, -sin_i],
                [sin_i, cos_i],
                [cos_i, sin_i],
                [-sin_i, cos_i],
                [cos_p.T / padded, -sin_p.T / padded],
                [sin_p.T / padded, cos_p.T / padded],
                [np.hstack([cos_p, sin_p]), np.hstack([-sin_p, cos_p])],
            ]
        )
        if inner == outer
        else None,
        "first_real": narrow([[cos_o], [-sin_o]]),
        "fourth_real": narrow([[cos_o.T, -sin_o.T]]),
        "twist_re": twist[0],
        "twist_im": twist[1],
    }


LANES = 128


def spread(tall, count, stride, first, height, width):
    tiles = [tall[pl.ds(t * height + first, count, stride=stride), :] for t in range(width[0] // LANES, width[1] // LANES)]
    return tiles[0] if len(tiles) == 1 else jnp.concatenate(tiles, axis=1)


def put_spread(tall, values, stride, first, height, width):
    for i, t in enumerate(range(width[0] // LANES, width[1] // LANES)):
        tall[pl.ds(t * height + first, values.shape[0], stride=stride), :] = values[:, i * LANES : (i + 1) * LANES]


def dot(left, right):
    return jnp.dot(left, right, preferred_element_type=jnp.float32)


def transform_filters(long_filter, tables, seq_len, kind=jnp.float32, handed=()):
    padded, inner, outer = sizes_of(seq_len)
    half = outer // 2
    groups = long_filter.shape[0]
    scale = seq_len ** -0.5

    def kernel(x_ref, first_ref, second_ref, tr_ref, ti_ref, *refs):
        count = len(handed)
        out_ref, tall = refs[count], refs[-1]
        for n in range(count):
            refs[count + 1 + n][...] = refs[n][...]
        height = half * groups
        for b in range(half):
            for t in range(inner // LANES):
                at = t * height + b * groups
                lanes = slice(b * inner + t * LANES, b * inner + (t + 1) * LANES)
                tall[at : at + groups, :] = x_ref[:, lanes].astype(jnp.float32)
        for g in range(groups):
            x = spread(tall, half, groups, g, height, (0, inner)).astype(jnp.bfloat16)
            f = dot(first_ref[...], x)
            f_re, f_im = f[:outer], f[outer:]
            g_re = (f_re * tr_ref[...] + f_im * ti_ref[...]).astype(jnp.bfloat16)
            g_im = (f_im * tr_ref[...] - f_re * ti_ref[...]).astype(jnp.bfloat16)
            spec = dot(g_re, second_ref[:inner]) + dot(g_im, second_ref[inner:])
            out_ref[g * outer : (g + 1) * outer, :] = (spec * scale).astype(kind)

    return pl.pallas_call(
        kernel,
        name="filter_dft",
        out_shape=[jax.ShapeDtypeStruct((groups * outer, 2 * inner), kind)]
        + [jax.ShapeDtypeStruct(array.shape, array.dtype) for array in handed],
        scratch_shapes=[pltpu.VMEM((half * groups * inner // LANES, LANES), jnp.float32)],
        compiler_params=pltpu.CompilerParams(vmem_limit_bytes=VMEM_LIMIT),
        cost_estimate=pl.CostEstimate(flops=200_000_000, bytes_accessed=2_000_000, transcendentals=0),
    )(long_filter, tables["first_real"], tables["second"], tables["twist_re"], tables["twist_im"], *handed)


def filtered(arrived, filters, tables, seq_len, other=None):
    padded, inner, outer = sizes_of(seq_len)
    half = outer // 2
    sources, channels, local = arrived.shape
    fold = local // inner
    groups = channels // CPG
    backward = other is not None

    def kernel(*refs):
        if backward:
            (x_ref, f_ref, k_ref, first_ref, second_ref, third_ref, fourth_ref, tr_ref, ti_ref,
             y_ref, cross_ref, tall, wide, stage, turn) = refs
        else:
            (x_ref, f_ref, first_ref, second_ref, third_ref, fourth_ref, tr_ref, ti_ref,
             y_ref, z_ref, tall, wide, stage, turn) = refs
        height = sources * channels
        for t in range(local // LANES):
            block = x_ref[:, :, t * LANES : (t + 1) * LANES].astype(jnp.float32)
            tall[t * height : (t + 1) * height, :] = block.reshape(height, LANES)
        for c in range(channels):
            pair, part = divmod(c, 2)
            for h in range(fold):
                rows = spread(tall, sources, channels, c, height, (h * inner, (h + 1) * inner))
                at = part * half + h * sources
                wide[at : at + sources, pair * inner : (pair + 1) * inner] = rows.astype(jnp.bfloat16)
        for g in range(groups):
            span = PAIRS * inner
            f = dot(first_ref[...], wide[:, g * span : (g + 1) * span])
            for p in range(PAIRS):
                f_re = f[:outer, p * inner : (p + 1) * inner]
                f_im = f[outer:, p * inner : (p + 1) * inner]
                at = (g * PAIRS + p) * outer
                stage[at : at + outer, :inner] = (f_re * tr_ref[...] + f_im * ti_ref[...]).astype(jnp.bfloat16)
                stage[at : at + outer, inner:] = (f_im * tr_ref[...] - f_re * ti_ref[...]).astype(jnp.bfloat16)
        for g in range(groups):
            s_re = f_ref[g * outer : (g + 1) * outer, :inner]
            s_im = f_ref[g * outer : (g + 1) * outer, inner:]
            cross_re = cross_im = None
            for p in range(PAIRS):
                at = (g * PAIRS + p) * outer
                z = dot(stage[at : at + outer, :], second_ref[...])
                z_re, z_im = z[:, :inner], z[:, inner:]
                if backward:
                    k_re = k_ref[at : at + outer, :inner].astype(jnp.float32)
                    k_im = k_ref[at : at + outer, inner:].astype(jnp.float32)
                    part_re = k_re * z_re + k_im * z_im
                    part_im = k_re * z_im - k_im * z_re
                    cross_re = part_re if cross_re is None else cross_re + part_re
                    cross_im = part_im if cross_im is None else cross_im + part_im
                    o_re = s_re * z_re + s_im * z_im
                    o_im = s_re * z_im - s_im * z_re
                else:
                    z_ref[at : at + outer, :] = z
                    o_re = s_re * z_re - s_im * z_im
                    o_im = s_re * z_im + s_im * z_re
                stage[at : at + outer, :inner] = o_re.astype(jnp.bfloat16)
                stage[at : at + outer, inner:] = o_im.astype(jnp.bfloat16)
            if backward:
                cross_ref[g * outer : (g + 1) * outer, :inner] = cross_re.astype(jnp.bfloat16)
                cross_ref[g * outer : (g + 1) * outer, inner:] = cross_im.astype(jnp.bfloat16)
        for pair in range(groups * PAIRS):
            at = pair * outer
            h = dot(stage[at : at + outer, :], third_ref[...])
            h_re, h_im = h[:, :inner], h[:, inner:]
            lanes = slice(pair * inner, (pair + 1) * inner)
            turn[:outer, lanes] = (h_re * tr_ref[...] - h_im * ti_ref[...]).astype(jnp.bfloat16)
            turn[outer:, lanes] = (h_im * tr_ref[...] + h_re * ti_ref[...]).astype(jnp.bfloat16)
        for g in range(groups):
            span = PAIRS * inner
            y = dot(fourth_ref[...], turn[:, g * span : (g + 1) * span]) * (1.0 / padded)
            for p in range(PAIRS):
                for part in range(2):
                    c = (g * PAIRS + p) * 2 + part
                    for h in range(fold):
                        at = part * half + h * sources
                        rows = y[at : at + sources, p * inner : (p + 1) * inner]
                        put_spread(tall, rows, channels, c, height, (h * inner, (h + 1) * inner))
        for t in range(local // LANES):
            block = tall[t * height : (t + 1) * height, :].reshape(sources, channels, LANES)
            y_ref[:, :, t * LANES : (t + 1) * LANES] = block.astype(jnp.bfloat16)

    pairs = groups * PAIRS
    if backward:
        extra = jax.ShapeDtypeStruct((groups * outer, 2 * inner), jnp.bfloat16)
    else:
        extra = jax.ShapeDtypeStruct((pairs * outer, 2 * inner), jnp.float32)
    operands = [arrived, filters] + ([other] if backward else [])
    operands += [tables[n] for n in ("first", "second", "third", "fourth", "twist_re", "twist_im")]
    return pl.pallas_call(
        kernel,
        name="correlate" if backward else "convolve",
        out_shape=(jax.ShapeDtypeStruct(arrived.shape, jnp.bfloat16), extra),
        scratch_shapes=[
            pltpu.VMEM((sources * channels * local // LANES, LANES), jnp.float32),
            pltpu.VMEM((outer, pairs * inner), jnp.bfloat16),
            pltpu.VMEM((pairs * outer, 2 * inner), jnp.bfloat16),
            pltpu.VMEM((2 * outer, pairs * inner), jnp.bfloat16),
        ],
        compiler_params=pltpu.CompilerParams(vmem_limit_bytes=VMEM_LIMIT),
        cost_estimate=pl.CostEstimate(flops=2_000_000_000, bytes_accessed=5_000_000, transcendentals=0),
    )(*operands)


def filter_gradient(cross, tables, seq_len):
    padded, inner, outer = sizes_of(seq_len)
    half = outer // 2
    groups = cross.shape[0] // outer
    scale = seq_len ** -0.5 / padded

    def kernel(s_ref, third_ref, fourth_ref, tr_ref, ti_ref, out_ref, tall, turn):
        for g in range(groups):
            h = dot(s_ref[g * outer : (g + 1) * outer, :], third_ref[...])
            h_re, h_im = h[:, :inner], h[:, inner:]
            turn[:outer, g * inner : (g + 1) * inner] = (h_re * tr_ref[...] - h_im * ti_ref[...]).astype(jnp.bfloat16)
            turn[outer:, g * inner : (g + 1) * inner] = (h_im * tr_ref[...] + h_re * ti_ref[...]).astype(jnp.bfloat16)
        for g in range(groups):
            y = dot(fourth_ref[...], turn[:, g * inner : (g + 1) * inner]) * scale
            put_spread(tall, y, groups, g, half * groups, (0, inner))
        for b in range(half):
            for t in range(inner // LANES):
                at = (t * half + b) * groups
                out_ref[:, b * inner + t * LANES : b * inner + (t + 1) * LANES] = tall[at : at + groups, :]

    return pl.pallas_call(
        kernel,
        name="filter_gradient",
        out_shape=jax.ShapeDtypeStruct((groups, seq_len), jnp.float32),
        scratch_shapes=[
            pltpu.VMEM((half * groups * inner // LANES, LANES), jnp.float32),
            pltpu.VMEM((2 * outer, groups * inner), jnp.bfloat16),
        ],
        compiler_params=pltpu.CompilerParams(vmem_limit_bytes=VMEM_LIMIT),
        cost_estimate=pl.CostEstimate(flops=200_000_000, bytes_accessed=2_000_000, transcendentals=0),
    )(cross, tables["third"], tables["fourth_real"], tables["twist_re"], tables["twist_im"])


RIM = 8
STEP = 2


def seven_taps(tall, value, rim, weights, forward):
    count = value.shape[0]
    if forward:
        tall[:RIM, :] = rim
        tall[RIM : RIM + count, :] = value
    else:
        tall[:count, :] = value
        tall[count : count + RIM, :] = rim
    total = value * weights[:1]
    for lag in range(1, TAPS):
        first = RIM - lag if forward else lag
        total = total + tall[first : first + count, :] * weights[lag : lag + 1]
    return total


def lane_block(i, offset=0):
    return pl.ds(pl.multiple_of(i * LANES + offset, LANES), LANES)


def whole_call(kernel, name, out_shape, operands, scratch=(), flops=10_000_000, **kwargs):
    return pl.pallas_call(
        kernel,
        name=name,
        out_shape=out_shape,
        scratch_shapes=list(scratch),
        compiler_params=pltpu.CompilerParams(vmem_limit_bytes=VMEM_LIMIT),
        cost_estimate=pl.CostEstimate(flops=flops, bytes_accessed=4_000_000, transcendentals=0),
        **kwargs,
    )(*operands)


def narrow_shape(*shape):
    return jax.ShapeDtypeStruct(shape, jnp.bfloat16)


def features_of(turned, rim, short_filter, cotangent):
    local, width = cotangent.shape

    def kernel(x_ref, rim_ref, w_ref, og_ref, f_ref, kv_ref, dconv_ref, tall):
        @pl.loop(0, width // LANES)
        def _(i):
            made = []
            for part in range(3):
                lanes = lane_block(i, part * width)
                total = seven_taps(
                    tall.at[part],
                    x_ref[:, lanes].astype(jnp.float32),
                    rim_ref[:, lanes].astype(jnp.float32),
                    w_ref[:, lanes].astype(jnp.float32),
                    True,
                ).astype(jnp.bfloat16)
                f_ref[:, lanes] = total
                made.append(total.astype(jnp.float32))
            rows = lane_block(i)
            kv_ref[rows, :] = (made[1] * made[2]).astype(jnp.bfloat16).T
            og = og_ref[:, rows].astype(jnp.float32)
            dconv_ref[rows, :] = (og * made[0]).astype(jnp.bfloat16).T

    return whole_call(
        kernel,
        "features",
        (narrow_shape(local, 3 * width), narrow_shape(width, local), narrow_shape(width, local)),
        (turned, rim, short_filter, cotangent),
        [pltpu.VMEM((3, local + RIM, LANES), jnp.float32)],
    )


def query_products(feats, conv, cotangent):
    width, local = conv.shape

    def kernel(f_ref, conv_ref, og_ref, mixed_ref, dq_ref, rim_ref):
        @pl.loop(0, width // LANES)
        def _(i):
            lanes = lane_block(i)
            here = conv_ref[lanes, :].T.astype(jnp.float32)
            mixed_ref[lanes, :] = (f_ref[:, lanes].astype(jnp.float32) * here).astype(jnp.bfloat16).T
            dq = (og_ref[:, lanes].astype(jnp.float32) * here).astype(jnp.bfloat16)
            dq_ref[:, lanes] = dq
            rim_ref[:, lanes] = dq[:RIM]

    return whole_call(
        kernel,
        "query_products",
        (narrow_shape(width, local), narrow_shape(local, width), narrow_shape(RIM, width)),
        (feats, conv, cotangent),
    )


def key_value_products(feats, back):
    width, local = back.shape

    def kernel(f_ref, back_ref, d_ref, rim_ref):
        @pl.loop(0, width // LANES)
        def _(i):
            here = back_ref[lane_block(i), :].T.astype(jnp.float32)
            for part in range(2):
                other = f_ref[:, lane_block(i, (2 - part) * width)].astype(jnp.float32)
                grad = (here * other).astype(jnp.bfloat16)
                d_ref[:, lane_block(i, part * width)] = grad
                rim_ref[:, lane_block(i, part * width)] = grad[:RIM]

    return whole_call(
        kernel,
        "key_value_products",
        (narrow_shape(local, 2 * width), narrow_shape(RIM, 2 * width)),
        (feats, back),
    )


def joined_features(turned, rim, short_filter, out_grad, owned):
    width, local = out_grad.shape
    near = LANES // owned
    blocks = width // LANES

    def kernel(x_ref, rim_ref, w_ref, og_ref, f_hbm, msg_ref, edge_ref, tall, made, f_ref, edge, sent):
        def copy(i):
            to = pl.ds(i * near, near)
            return pltpu.make_async_copy(made.at[to], msg_ref.at[to], sent.at[i])

        def keep(part, i):
            at = part * blocks + i
            to = pl.ds(pl.multiple_of(at * LANES, LANES), LANES)
            return pltpu.make_async_copy(f_ref.at[at], f_hbm.at[to, :], sent.at[blocks + at])

        @pl.loop(0, blocks // STEP)
        def _(step):
            for slot in range(STEP):
                i = step * STEP + slot
                parts = []
                for part in range(3):
                    lanes = lane_block(i, part * width)
                    total = seven_taps(
                        tall.at[3 * slot + part],
                        x_ref[:, lanes].astype(jnp.float32),
                        rim_ref[:, lanes].astype(jnp.float32),
                        w_ref[:, lanes].astype(jnp.float32),
                        True,
                    ).astype(jnp.bfloat16)
                    for t in range(local // LANES):
                        f_ref[part * blocks + i, :, t * LANES : (t + 1) * LANES] = total[t * LANES : (t + 1) * LANES]
                    if part:
                        edge[:, lanes] = total[:RIM]
                    parts.append(total.astype(jnp.float32))
                og = og_ref[lane_block(i), :].T
                edge[:, lane_block(i)] = og[:RIM]
                kv = (parts[1] * parts[2]).astype(jnp.bfloat16).T
                dconv = (og.astype(jnp.float32) * parts[0]).astype(jnp.bfloat16).T
                to = pl.ds(i * near, near)
                made[to, :owned, :] = kv.reshape(near, owned, local)
                made[to, owned:, :] = dconv.reshape(near, owned, local)
            for slot in range(STEP):
                copy(step * STEP + slot).start()
                for part in range(3):
                    keep(part, step * STEP + slot).start()

        last = pltpu.make_async_copy(edge, edge_ref, sent.at[4 * blocks])
        last.start()

        @pl.loop(0, blocks)
        def _(i):
            copy(i).wait()
            for part in range(3):
                keep(part, i).wait()

        last.wait()

    vmem = pl.BlockSpec(memory_space=pltpu.VMEM)
    hbm = pl.BlockSpec(memory_space=pltpu.HBM)
    devices = width // owned
    return whole_call(
        kernel,
        "joined_features",
        (narrow_shape(3 * width, local), narrow_shape(devices, 2 * owned, local), narrow_shape(RIM, 3 * width)),
        (turned, rim, short_filter, out_grad),
        [
            pltpu.VMEM((3 * STEP, local + RIM, LANES), jnp.float32),
            pltpu.VMEM((devices, 2 * owned, local), jnp.bfloat16),
            pltpu.VMEM((3 * blocks, LANES, local), jnp.bfloat16),
            pltpu.VMEM((RIM, 3 * width), jnp.bfloat16),
            pltpu.SemaphoreType.DMA((4 * blocks + 1,)),
        ],
        in_specs=[vmem] * 4,
        out_specs=(hbm, hbm, hbm),
    )


def joined_filtering(arrived, filters, joined, tables, seq_len):
    padded, inner, outer = sizes_of(seq_len)
    half = outer // 2
    sources, rows, local = arrived.shape
    channels = rows // 2
    tiles = local // LANES
    fold = local // inner
    groups = channels // CPG
    pairs = groups * PAIRS
    height = sources * channels
    chunk = sources // 4

    def kernel(x_ref, f_ref, table_ref, tr_ref, ti_ref, y_hbm, cross_hbm, y_ref, cross_ref, talls, wides, stages, turns, sems):
        second_ref, third_ref = table_ref.at[: 2 * inner], table_ref.at[2 * inner : 4 * inner]
        fourth_ref = table_ref.at[4 * inner : 4 * inner + 2 * half]
        firsts = table_ref[4 * inner + 2 * half :, :]
        first = jnp.concatenate([firsts[:, : 2 * half], firsts[:, 2 * half :]], axis=0)
        tr, ti = tr_ref[...], ti_ref[...]
        for s in range(2):
            tall, wide, stage = talls.at[s], wides.at[s], stages.at[s]
            for t in range(tiles):
                block = x_ref[:, s * channels : (s + 1) * channels, t * LANES : (t + 1) * LANES]
                tall[t * height : (t + 1) * height, :] = block.astype(jnp.float32).reshape(height, LANES)
            for c in range(channels):
                pair, part = divmod(c, 2)
                for h in range(fold):
                    line = spread(tall, sources, channels, c, height, (h * inner, (h + 1) * inner))
                    at = part * half + h * sources
                    wide[at : at + sources, pair * inner : (pair + 1) * inner] = line.astype(jnp.bfloat16)
            for g in range(groups):
                span = PAIRS * inner
                f = dot(first, wide[:, g * span : (g + 1) * span])
                for p in range(PAIRS):
                    f_re = f[:outer, p * inner : (p + 1) * inner]
                    f_im = f[outer:, p * inner : (p + 1) * inner]
                    at = (g * PAIRS + p) * outer
                    stage[at : at + outer, :inner] = (f_re * tr + f_im * ti).astype(jnp.bfloat16)
                    stage[at : at + outer, inner:] = (f_im * tr - f_re * ti).astype(jnp.bfloat16)
        for g in range(groups):
            s_re = f_ref[g * outer : (g + 1) * outer, :inner].astype(jnp.float32)
            s_im = f_ref[g * outer : (g + 1) * outer, inner:].astype(jnp.float32)
            cross_re = cross_im = 0.0
            for p in range(PAIRS):
                at = (g * PAIRS + p) * outer
                k = dot(stages[0, at : at + outer, :], second_ref[...])
                d = dot(stages[1, at : at + outer, :], second_ref[...])
                k_re, k_im = k[:, :inner], k[:, inner:]
                d_re, d_im = d[:, :inner], d[:, inner:]
                cross_re = cross_re + (k_re * d_re + k_im * d_im)
                cross_im = cross_im + (k_re * d_im - k_im * d_re)
                stages[0, at : at + outer, :inner] = (s_re * k_re - s_im * k_im).astype(jnp.bfloat16)
                stages[0, at : at + outer, inner:] = (s_re * k_im + s_im * k_re).astype(jnp.bfloat16)
                stages[1, at : at + outer, :inner] = (s_re * d_re + s_im * d_im).astype(jnp.bfloat16)
                stages[1, at : at + outer, inner:] = (s_re * d_im - s_im * d_re).astype(jnp.bfloat16)
            cross_ref[g * outer : (g + 1) * outer, :inner] = cross_re.astype(jnp.bfloat16)
            cross_ref[g * outer : (g + 1) * outer, inner:] = cross_im.astype(jnp.bfloat16)
        copies = [pltpu.make_async_copy(cross_ref, cross_hbm, sems.at[4])]
        copies[0].start()
        spot = lax.broadcasted_iota(jnp.int32, (RIM, LANES), 0)
        lane = lax.broadcasted_iota(jnp.int32, (RIM, LANES), 1)
        pick = jnp.where(spot == lane, 1.0, 0.0).astype(jnp.bfloat16)
        rims = []
        for s in range(2):
            tall, stage, turn = talls.at[s], stages.at[s], turns.at[s]
            for pair in range(pairs):
                at = pair * outer
                h = dot(stage[at : at + outer, :], third_ref[...])
                h_re, h_im = h[:, :inner], h[:, inner:]
                lanes = slice(pair * inner, (pair + 1) * inner)
                turn[:outer, lanes] = (h_re * tr - h_im * ti).astype(jnp.bfloat16)
                turn[outer:, lanes] = (h_im * tr + h_re * ti).astype(jnp.bfloat16)
            for g in range(groups):
                span = PAIRS * inner
                y = dot(fourth_ref[...], turn[:, g * span : (g + 1) * span])
                for p in range(PAIRS):
                    for part in range(2):
                        c = (g * PAIRS + p) * 2 + part
                        for h in range(fold):
                            at = part * half + h * sources
                            line = y[at : at + sources, p * inner : (p + 1) * inner]
                            put_spread(tall, line, channels, c, height, (h * inner, (h + 1) * inner))
            front = tall[:height, :].astype(jnp.bfloat16)
            rims.append(
                lax.dot_general(pick, front, (((1,), (1,)), ((), ())), preferred_element_type=jnp.float32)
            )
        for q in range(4):
            to = slice(q * chunk, (q + 1) * chunk)
            for s in range(2):
                for t in range(tiles):
                    at = t * height + q * chunk * channels
                    block = talls[s, at : at + chunk * channels, :].reshape(chunk, channels, LANES)
                    row = (s * tiles + t) * channels
                    y_ref[to, row : row + channels, :] = block.astype(jnp.bfloat16)
            for d in range(q * chunk, (q + 1) * chunk):
                tile, lanes = divmod((d + 1) % sources * channels, LANES)
                edge = jnp.zeros((RIM, LANES), jnp.float32)
                if d < sources - 1:
                    for s in range(2):
                        piece = rims[s][:, tile * LANES : (tile + 1) * LANES]
                        turn_by = (s * channels - lanes) % LANES
                        if turn_by:
                            piece = pltpu.roll(piece, turn_by, 1)
                        edge = piece if s == 0 else jnp.where(lane < channels, edge, piece)
                y_ref[d, 2 * tiles * channels :, :] = edge.astype(jnp.bfloat16)
            copies.append(pltpu.make_async_copy(y_ref.at[to], y_hbm.at[to], sems.at[q]))
            copies[-1].start()
        for copy in copies:
            copy.wait()

    sent = (sources, 2 * tiles * channels + RIM, LANES)
    vmem = pl.BlockSpec(memory_space=pltpu.VMEM)
    hbm = pl.BlockSpec(memory_space=pltpu.HBM)
    return whole_call(
        kernel,
        "joined_filtering",
        (narrow_shape(*sent), narrow_shape(groups * outer, 2 * inner)),
        [arrived, filters, joined, tables["twist_re"], tables["twist_im"]],
        [
            pltpu.VMEM(sent, jnp.bfloat16),
            pltpu.VMEM((groups * outer, 2 * inner), jnp.bfloat16),
            pltpu.VMEM((2, tiles * height, LANES), jnp.float32),
            pltpu.VMEM((2, outer, pairs * inner), jnp.bfloat16),
            pltpu.VMEM((2, pairs * outer, 2 * inner), jnp.bfloat16),
            pltpu.VMEM((2, 2 * outer, pairs * inner), jnp.bfloat16),
            pltpu.SemaphoreType.DMA((5,)),
        ],
        flops=4_000_000_000,
        in_specs=[vmem] * 5,
        out_specs=(hbm, hbm),
    )


def joined_gradients(cross, feats, edges, returned, out_grad, short_filter, owned):
    width, local = out_grad.shape
    tiles = local // LANES
    near = LANES // owned
    steps = width // LANES // STEP

    def kernel(_, f_hbm, edge_ref, back_ref, og_ref, w_ref, mixed_ref, out_ref, tall, made, f_ref, sent, fetched):
        def step_rows(part, step):
            return pl.ds(pl.multiple_of(part * width + step * STEP * LANES, STEP * LANES), STEP * LANES)

        def fetch(part, step):
            rows = step_rows(part, step)
            return pltpu.make_async_copy(f_hbm.at[rows, :], f_ref.at[rows, :], fetched.at[part * steps + step])

        @pl.loop(0, steps)
        def _(step):
            for part in range(3):
                fetch(part, step).start()

        def features(part, i):
            rows = lane_block(i, part * width)
            held = [f_ref[rows, t * LANES : (t + 1) * LANES] for t in range(tiles)]
            return jnp.concatenate(held, axis=0).astype(jnp.float32)

        lane = lax.broadcasted_iota(jnp.int32, (RIM, LANES), 1)

        def copy(part, step):
            rows = step_rows(part, step)
            to = out_ref.at[rows, :] if part < 3 else mixed_ref.at[step_rows(0, step), :]
            return pltpu.make_async_copy(made.at[rows, :], to, sent.at[part * steps + step])

        def turned(s, i):
            held = pl.ds(i * near, near)
            pieces = [
                back_ref[held, (s * tiles + t) * owned : (s * tiles + t + 1) * owned, :].reshape(LANES, LANES).T
                for t in range(tiles)
            ]
            return jnp.concatenate(pieces, axis=0).astype(jnp.float32)

        def rim_of(s, i):
            rim = None
            for n in range(near):
                piece = back_ref[i * near + n, 2 * tiles * owned :, :].astype(jnp.float32)
                turn_by = (n - s) * owned % LANES
                if turn_by:
                    piece = pltpu.roll(piece, turn_by, 1)
                rim = jnp.where(lane >= n * owned, piece, rim) if n else piece
            return rim

        def third(part, slot, i, here, rim, other):
            edge = edge_ref[:, lane_block(i, (3 - part) % 3 * width)].astype(jnp.float32)
            total = seven_taps(
                tall.at[3 * slot + part],
                (here * other).astype(jnp.bfloat16).astype(jnp.float32),
                (rim * edge).astype(jnp.bfloat16).astype(jnp.float32),
                w_ref[:, lane_block(i, part * width)].astype(jnp.float32),
                False,
            )
            made[lane_block(i, part * width), :] = total.astype(jnp.bfloat16).T

        @pl.loop(0, steps)
        def _(step):
            for part in range(3):
                fetch(part, step).wait()
            for slot in range(STEP):
                i = step * STEP + slot
                query, key, value = [features(part, i) for part in range(3)]
                conv = turned(0, i)
                made[lane_block(i, 3 * width), :] = (query * conv).astype(jnp.bfloat16).T
                third(0, slot, i, conv, rim_of(0, i), og_ref[lane_block(i), :].T.astype(jnp.float32))
                back, rim = turned(1, i), rim_of(1, i)
                third(1, slot, i, back, rim, value)
                third(2, slot, i, back, rim, key)
            for part in range(4):
                copy(part, step).start()

        @pl.loop(0, steps)
        def _(step):
            for part in range(4):
                copy(part, step).wait()

    vmem = pl.BlockSpec(memory_space=pltpu.VMEM)
    hbm = pl.BlockSpec(memory_space=pltpu.HBM)
    return whole_call(
        kernel,
        "joined_gradients",
        (narrow_shape(width, local), narrow_shape(3 * width, local)),
        (cross, feats, edges, returned, out_grad, short_filter),
        [
            pltpu.VMEM((3 * STEP, local + RIM, LANES), jnp.float32),
            pltpu.VMEM((4 * width, local), jnp.bfloat16),
            pltpu.VMEM((3 * width, local), jnp.bfloat16),
            pltpu.SemaphoreType.DMA((4 * steps,)),
            pltpu.SemaphoreType.DMA((3 * steps,)),
        ],
        in_specs=[hbm, hbm] + [vmem] * 4,
        out_specs=(hbm, hbm),
        input_output_aliases={0: 0, 1: 1},
    )


def query_gradient(grad, rim, short_filter):
    local, width = grad.shape
    steps = width // GRAD_ROWS

    def kernel(d_ref, rim_ref, w_ref, out_ref, tall):
        gradient_block(d_ref, rim_ref, w_ref, out_ref, tall)

    return gradient_call(kernel, "query_gradient", (), grad, rim, short_filter, 1, 0)


def key_value_gradient(whole, grad, rim, short_filter):
    def kernel(_, d_ref, rim_ref, w_ref, out_ref, tall):
        gradient_block(d_ref, rim_ref, w_ref, out_ref, tall)

    return gradient_call(kernel, "key_value_gradient", (whole,), grad, rim, short_filter, 2, 1)


GRAD_ROWS = 512


def gradient_block(d_ref, rim_ref, w_ref, out_ref, tall):
    for c in range(GRAD_ROWS // LANES):
        lanes = slice(c * LANES, (c + 1) * LANES)
        total = seven_taps(
            tall.at[c],
            d_ref[:, lanes].astype(jnp.float32),
            rim_ref[:, lanes].astype(jnp.float32),
            w_ref[:, lanes].astype(jnp.float32),
            False,
        )
        out_ref[lanes, :] = total.astype(jnp.bfloat16).T


def gradient_call(kernel, name, whole, grad, rim, short_filter, parts, first):
    local, lanes = grad.shape
    width = lanes // parts
    steps = width // GRAD_ROWS
    return pl.pallas_call(
        kernel,
        name=name,
        grid=(parts * steps,),
        in_specs=[pl.BlockSpec(memory_space=pl.ANY)] * len(whole)
        + [
            pl.BlockSpec((local, GRAD_ROWS), lambda i: (0, i)),
            pl.BlockSpec((RIM, GRAD_ROWS), lambda i: (0, i)),
            pl.BlockSpec((TAPS, GRAD_ROWS), lambda i: (0, first * steps + i)),
        ],
        out_specs=pl.BlockSpec((GRAD_ROWS, local), lambda i: (first * steps + i, 0)),
        out_shape=narrow_shape(3 * width, local),
        scratch_shapes=[pltpu.VMEM((GRAD_ROWS // LANES, local + RIM, LANES), jnp.float32)],
        input_output_aliases={0: 0} if whole else {},
        cost_estimate=pl.CostEstimate(flops=20_000_000, bytes_accessed=4_000_000, transcendentals=0),
    )(*whole, grad, rim, short_filter)


def shards(projections, short_filter, long_filter, out_grad):
    width, local_len = out_grad.shape
    devices = lax.axis_size(EVERYONE)
    seq_len = local_len * devices
    owned = width // devices
    tables = make_tables(seq_len, devices)

    turned = projections.T
    rim = shifted(turned[local_len - RIM :], EVERYONE, 1)

    _, inner, outer = sizes_of(seq_len)
    twin = owned // CPG * outer == width and 2 * inner == local_len and inner == outer
    if owned % 16 == 0 and LANES % (2 * owned) == 0 and devices % 4 == 0 and twin and width % (STEP * LANES) == 0:
        feats, message, edges = joined_features(turned, rim, short_filter, out_grad, owned)
        filters, joined = transform_filters(long_filter, tables, seq_len, jnp.bfloat16, [tables["joined"]])
        arrived = lax.all_to_all(message, EVERYONE, split_axis=0, concat_axis=0, tiled=True)
        edges, filters, joined, arrived = lax.optimization_barrier(
            (shifted(edges, EVERYONE, -1), filters, joined, arrived)
        )
        answer, cross = joined_filtering(arrived, filters, joined, tables, seq_len)
        returned = lax.all_to_all(answer, EVERYONE, split_axis=0, concat_axis=0, tiled=True)
        filter_grad = filter_gradient(cross, tables, seq_len)
        filter_grad, returned, cross = lax.optimization_barrier((filter_grad, returned, cross))
        mixed, grad = joined_gradients(cross, feats, edges, returned, out_grad, short_filter, owned)
        return (mixed, grad, filter_grad)

    cotangent = out_grad.T
    feats, product, conv_grad = features_of(turned, rim, short_filter, cotangent)

    def exchange(block):
        pieces = block.reshape(devices, owned, local_len)
        return lax.all_to_all(pieces, EVERYONE, split_axis=0, concat_axis=0, tiled=True)

    (filters,) = transform_filters(long_filter, tables, seq_len)
    prod_chan = exchange(product)
    conv_grad, prod_chan = lax.optimization_barrier((conv_grad, prod_chan))
    grad_chan = exchange(conv_grad)
    conv_chan, prod_spec = filtered(prod_chan, filters, tables, seq_len)
    conv_chan, grad_chan = lax.optimization_barrier((conv_chan, grad_chan))
    conv_tok = exchange(conv_chan)
    back_chan, cross = filtered(grad_chan, filters, tables, seq_len, prod_spec)
    back_chan, conv_tok = lax.optimization_barrier((back_chan, conv_tok))
    back_tok = exchange(back_chan)

    filter_grad = filter_gradient(cross, tables, seq_len)
    mixed, grad_q, rim_q = query_products(feats, conv_tok.reshape(width, local_len), cotangent)
    grad = query_gradient(grad_q, shifted(rim_q, EVERYONE, -1), short_filter)
    filter_grad, mixed, grad, back_tok = lax.optimization_barrier((filter_grad, mixed, grad, back_tok))

    grad_kv, rim_kv = key_value_products(feats, back_tok.reshape(width, local_len))
    grad = key_value_gradient(grad, grad_kv, shifted(rim_kv, EVERYONE, -1), short_filter)
    return (mixed, grad, filter_grad)


def solution(mesh):
    placed = (P(None, EVERYONE), P(), P(EVERYONE, None), P(None, EVERYONE))
    return jax.shard_map(
        shards,
        mesh=mesh,
        in_specs=placed,
        out_specs=(P(None, EVERYONE), P(None, EVERYONE), P(EVERYONE, None)),
        check_vma=False,
    )
```
